128 devices in a mesh: lon: 16 (over y_hi, z, core), lat: 8 (over y_lo, x).
Axes of the slice: x: 4, y: 4 (y_hi: 2, y_lo: 2; y = y_hi * 2 + y_lo), z: 4, core: 2. Of those that a mesh axis runs over, the one named last changes fastest.
Arguments:
- tracers: float32 [2, 10, 512, 2048], P(None, None, 'lat', 'lon'), may hold values from -6 to 6
- velocity: float32 [2, 10, 512, 2048], P(None, None, 'lat', 'lon'), may hold values from -6 to 6
- active_levels: int32 [512, 2048], P('lat', 'lon'), may hold values from 0 to 10, as said below
- diffusivity: float32 [512, 2048], P('lat', 'lon'), may hold values from 0.02 to 0.2
- viscosity: float32 [512, 2048], P('lat', 'lon'), may hold values from 0.002 to 0.012
- ocean_depth: float32 [512, 2048], P('lat', 'lon'), may hold values from 0.5 to 1.5
- wind_forcing: float32 [2, 512, 2048], P(None, 'lat', 'lon'), may hold values from -5 to 5
Outputs:
- tracers_out: float32 [2, 10, 512, 2048], P(None, None, 'lat', 'lon')
- velocity_out: float32 [2, 10, 512, 2048], P(None, None, 'lat', 'lon')
- surface: float32 [512, 2048], P('lat', 'lon')
The draws below stay inside these ranges and needn't reach their ends.
Inputs may be any that keep to these rules, and one draw needn't show every extreme that they name: `active_levels`: 0 marks land, which covers whole aligned blocks of 8 x 8 cells; every other cell has 1 to 10 wet levels.
All inputs are finite; a program needn't handle non-finite values.
Results may differ from the reference program's by a relative error of at most 0.0003.
Values sent between devices are 32-bit elements; how exact they have to be, the bound alone decides.
No kernel may reach another device: no remote copies, remote signals or barrier semaphores. Data moves between devices by JAX's collectives and lax.ppermute only.
A program may use at most 128 MiB of HBM per device.

```python
import math
import jax
import jax.numpy as jnp
from jax import lax

LEVELS = 10
SUBCYCLES = 8
SOLVE_ITERS = 4
NLAT = 512
NLON = 2048


def draw_active_levels(key, part):
    key = jax.random.fold_in(key, 11)
    land_key, level_key = jax.random.split(key)
    coarse = jax.random.randint(land_key, (NLAT // 8, NLON // 8), 0, 4)
    land_block = jnp.repeat(jnp.repeat(coarse == 0, 8, axis=0), 8, axis=1)
    levels = jax.random.randint(level_key, (NLAT, NLON), 1, LEVELS + 1)
    return jnp.where(land_block, 0, levels).astype(jnp.int32)


def block_levels(own_key, dims, cuts, low, largest):
    level = 1.0
    for dim, blocks in cuts:
        heights = jax.random.uniform(jax.random.fold_in(jax.random.fold_in(own_key, 6), dim), (blocks,), jnp.float32, low / len(cuts), largest / len(cuts))
        level = level * jnp.repeat(jnp.exp(heights), dims[dim] // blocks).reshape((-1,) + (1,) * (len(dims) - 1 - dim))
    return level


def normal_values(key, shape, width, bound, cuts=(), kind=jnp.bfloat16):
    factor_of = block_levels(key, shape, cuts, -0.22, 0.18) if cuts else 1.0
    entries = jax.random.normal(key, shape, jnp.float32) * width * factor_of
    return jnp.minimum(jnp.maximum(entries, -bound), bound).astype(kind)


def setup_inputs(seed: int = 0) -> dict:
    arg_keys = jax.random.split(jax.random.key(seed), 8)
    tracers = normal_values(arg_keys[0], (2, LEVELS, NLAT, NLON), 1.0, 6.0, ((2, 8), (3, 16)), jnp.float32)
    velocity = normal_values(arg_keys[1], (2, LEVELS, NLAT, NLON), 1.0, 6.0, ((2, 8), (3, 16)), jnp.float32)
    active_levels = draw_active_levels(jax.random.fold_in(arg_keys[7], 71), 0)
    diffusivity = jnp.clip(jnp.exp(math.log(0.2) - 2.3025851 * jax.random.uniform(arg_keys[3], (NLAT, NLON), jnp.float32) ** block_levels(arg_keys[3], (NLAT, NLON), ((0, 8), (1, 16)), -0.2, 0.2)), 0.02, 0.2)
    viscosity = jnp.clip(jnp.exp(math.log(0.012) - 1.7917594 * jax.random.uniform(arg_keys[4], (NLAT, NLON), jnp.float32) ** block_levels(arg_keys[4], (NLAT, NLON), ((0, 8), (1, 16)), -0.2, 0.2)), 0.002, 0.012)
    ocean_depth = jnp.clip(0.5 + 1.0 * jax.random.uniform(arg_keys[5], (NLAT, NLON), jnp.float32) ** block_levels(arg_keys[5], (NLAT, NLON), ((0, 8), (1, 16)), -0.2, 0.2), 0.5, 1.5)
    wind_forcing = normal_values(arg_keys[6], (2, NLAT, NLON), 1.0, 5.0, ((1, 8), (2, 16)), jnp.float32)
    return {"tracers": tracers, "velocity": velocity, "active_levels": active_levels, "diffusivity": diffusivity, "viscosity": viscosity, "ocean_depth": ocean_depth, "wind_forcing": wind_forcing}


edge_offsets = ((0, 1), (0, -1), (1, 0), (-1, 0))
corner_offsets = ((1, 1), (1, -1), (-1, 1), (-1, -1))
flow_step = 0.3
slope_step = 0.3
floor_diag = 0.05


def parity_of(values):
    return jnp.array(values, jnp.float32).reshape(-1, 1, 1)


def window(field, row_off, col_off):
    row_count = field.shape[-2] - 2
    col_count = field.shape[-1] - 2
    inner = lax.slice_in_dim(field, 1 + row_off, 1 + row_off + row_count, axis=field.ndim - 2)
    return lax.slice_in_dim(inner, 1 + col_off, 1 + col_off + col_count, axis=field.ndim - 1)


def masked_laplacian(field, coefficient, wet_mask):
    centre = window(field, 0, 0)
    mask_centre = window(wet_mask, 0, 0)
    summed = None
    for row_off, col_off in edge_offsets:
        face_weight = mask_centre * window(wet_mask, row_off, col_off)
        if coefficient is not None:
            face_weight = 0.5 * (window(coefficient, 0, 0) + window(coefficient, row_off, col_off)) * face_weight
        flux_term = face_weight * (window(field, row_off, col_off) - centre)
        summed = flux_term if summed is None else summed + flux_term
    return summed


def extend_global(stacked, margin, parity):
    lon_pad = jnp.concatenate([stacked[..., -margin:], stacked, stacked[..., :margin]], axis=-1)
    south_rows = jnp.zeros_like(lon_pad[:, :margin])
    north_rows = jnp.flip(lon_pad[:, -margin:], (1, 2)) * parity
    return jnp.concatenate([south_rows, lon_pad, north_rows], axis=1)


def nine_weights(statics):
    depth_pad = statics[0]
    ocean_pad = statics[1]
    depth_centre = window(depth_pad, 0, 0)
    ocean_centre = window(ocean_pad, 0, 0)
    weights = []
    for offsets, scale in ((edge_offsets, 1.0), (corner_offsets, 0.5)):
        for row_off, col_off in offsets:
            weights.append(scale * 0.5 * (depth_centre + window(depth_pad, row_off, col_off)) * ocean_centre * window(ocean_pad, row_off, col_off))
    diagonal = floor_diag * ocean_centre + (1.0 - ocean_centre)
    return weights, diagonal


def operate_nine(direction_pad, weights, diagonal):
    centre = window(direction_pad, 0, 0)
    summed = diagonal * centre
    for offset, weight in zip(edge_offsets + corner_offsets, weights):
        summed = summed + weight * (centre - window(direction_pad, offset[0], offset[1]))
    return summed


def barotropic(start_east, start_north, ocean_depth, ocean_mask):
    statics = extend_global(jnp.stack([ocean_depth, ocean_mask]), 1, parity_of([1.0, 1.0]))
    depth_pad = statics[0]
    height = jnp.zeros_like(start_east)
    east_flow, north_flow = start_east, start_north
    for cycle_index in range(SUBCYCLES):
        moved = extend_global(jnp.stack([east_flow, north_flow]), 1, parity_of([-1.0, -1.0]))
        flux_east = depth_pad * moved[0]
        flux_north = depth_pad * moved[1]
        divergence = 0.5 * ((window(flux_east, 0, 1) - window(flux_east, 0, -1)) + (window(flux_north, 1, 0) - window(flux_north, -1, 0)))
        height = height - flow_step * ocean_mask * divergence
        height_pad = extend_global(height[None], 1, parity_of([1.0]))[0]
        east_flow = east_flow - slope_step * ocean_mask * (0.5 * (window(height_pad, 0, 1) - window(height_pad, 0, -1)))
        north_flow = north_flow - slope_step * ocean_mask * (0.5 * (window(height_pad, 1, 0) - window(height_pad, -1, 0)))
    weights, diagonal = nine_weights(statics)
    surface = jnp.zeros_like(height)
    residual = height
    direction = height
    old_norm = jnp.sum(residual * residual)
    for iteration in range(SOLVE_ITERS):
        direction_pad = extend_global(direction[None], 1, parity_of([1.0]))[0]
        image = operate_nine(direction_pad, weights, diagonal)
        step_size = old_norm / jnp.sum(direction * image)
        surface = surface + step_size * direction
        residual = residual - step_size * image
        new_norm = jnp.sum(residual * residual)
        direction = residual + (new_norm / old_norm) * direction
        old_norm = new_norm
    surface_pad = extend_global(surface[None], 1, parity_of([1.0]))[0]
    east_final = east_flow - slope_step * ocean_mask * (0.5 * (window(surface_pad, 0, 1) - window(surface_pad, 0, -1)))
    north_final = north_flow - slope_step * ocean_mask * (0.5 * (window(surface_pad, 1, 0) - window(surface_pad, -1, 0)))
    return east_final, north_final, surface


def reference(tracers, velocity, active_levels, diffusivity, viscosity, ocean_depth, wind_forcing):
    levels_float = active_levels.astype(jnp.float32)
    statics = extend_global(jnp.stack([diffusivity, viscosity, levels_float]), 2, parity_of([1.0, 1.0, 1.0]))
    row_ids = jnp.arange(NLAT, dtype=jnp.float32)[:, None]
    coriolis = 0.25 * jnp.sin(math.pi * ((row_ids + 0.5) / NLAT - 0.5))

    def level_body(level, carry):
        tracer_store, star_store, column_sum = carry
        level_tracer = lax.dynamic_index_in_dim(tracers, level, 1, keepdims=False)
        level_velocity = lax.dynamic_index_in_dim(velocity, level, 1, keepdims=False)
        padded = extend_global(jnp.concatenate([level_tracer, level_velocity]), 2, parity_of([1.0, 1.0, -1.0, -1.0]))
        wet_pad = (level.astype(jnp.float32) < statics[2]).astype(jnp.float32)
        tracer_lap = window(masked_laplacian(padded[:2], statics[0], wet_pad), 0, 0)
        new_tracer = level_tracer + tracer_lap
        first_pass = masked_laplacian(padded[2:], None, wet_pad)
        second_pass = masked_laplacian(first_pass, window(statics[1], 0, 0), window(wet_pad, 0, 0))
        wet = wet_pad[2:-2, 2:-2]
        rotated = jnp.stack([level_velocity[1], -level_velocity[0]])
        star = wet * (level_velocity - second_pass + coriolis * rotated)
        tracer_store = lax.dynamic_update_index_in_dim(tracer_store, new_tracer, level, 1)
        star_store = lax.dynamic_update_index_in_dim(star_store, star, level, 1)
        return tracer_store, star_store, column_sum + star

    init = (jnp.zeros_like(tracers), jnp.zeros_like(velocity), jnp.zeros((2, NLAT, NLON), jnp.float32))
    tracers_out, star_all, column_sum = lax.fori_loop(0, LEVELS, level_body, init)
    column_mean = column_sum / jnp.maximum(levels_float, 1.0)
    ocean_mask = (active_levels > 0).astype(jnp.float32)
    start = column_mean + wind_forcing * ocean_mask
    east_final, north_final, surface = barotropic(start[0], start[1], ocean_depth, ocean_mask)
    corrected = jnp.stack([east_final, north_final])
    wet_all = (jnp.arange(LEVELS, dtype=jnp.float32)[:, None, None] < levels_float).astype(jnp.float32)
    velocity_out = star_all + wet_all * (corrected - column_mean)[:, None]
    return tracers_out, velocity_out, surface
```

```python
import functools
import math

import jax
import jax.numpy as jnp
from jax import lax
from jax.experimental import pallas as pl
from jax.experimental.pallas import tpu as pltpu
from jax.sharding import PartitionSpec as P

SUBCYCLES = 8
SOLVE_ITERS = 4
LEVELS = 10
PLANES = 2 * LEVELS
ROWS = 64
LANES = 128
MARGIN = 24
TALL = ROWS + 2 * MARGIN
RIM = 32
SLOPE = 0.15
CENTRE = 9.0
RADIUS = 9.1
F32 = jnp.float32
BOTH = ("lon", "lat")


def lane_ids(rows):
    return lax.broadcasted_iota(jnp.int32, (rows, LANES), 1)


def row_ids(rows):
    return lax.broadcasted_iota(jnp.int32, (rows, LANES), 0)


def turn(x, shift):
    return pltpu.roll(x, shift, 1)


def flip_lanes(x):
    lanes = lane_ids(x.shape[0])
    for bit in range(7):
        step = 1 << bit
        x = jnp.where((lanes & step) != 0, turn(x, step), turn(x, LANES - step))
    return x


def flip_rows(x):
    rows = x.shape[0]
    ids = row_ids(rows)
    for bit in range(3):
        step = 1 << bit
        x = jnp.where((ids & step) != 0, pltpu.roll(x, step, 0), pltpu.roll(x, rows - step, 0))
    return jnp.concatenate([x[r : r + 8] for r in range(rows - 8, -8, -8)], axis=0)


def odd(axis):
    return lax.rem(lax.axis_index(axis), 2) == 1


def at_fold():
    return lax.axis_index("lat") == lax.axis_size("lat") - 1


def pack_kernel(vel, tra, lev, visc, diff, cols, send_a, send_b, north, south):
    lanes = lane_ids(ROWS)

    def velocity_plane(p, acc):
        x = vel[pl.ds(pl.multiple_of(p * ROWS, ROWS), ROWS), :]
        return jnp.where((lanes >> 2) == p, turn(x, 4 * p + 2), acc)

    def tracer_plane(p, acc):
        x = tra[pl.ds(pl.multiple_of(p * ROWS, ROWS), ROWS), :]
        return jnp.where((lanes >> 1) == 40 + p, turn(x, 2 * p + 81), acc)

    acc = lax.fori_loop(0, PLANES, velocity_plane, jnp.zeros((ROWS, LANES), F32))
    acc = lax.fori_loop(0, PLANES, tracer_plane, acc)
    levels = lev[...].astype(F32)
    acc = jnp.where((lanes >> 2) == 30, turn(levels, 122), acc)
    acc = jnp.where((lanes >> 1) == 62, turn(visc[...], 125), acc)
    acc = jnp.where((lanes >> 1) == 63, turn(diff[...], 127), acc)
    cols[...] = acc
    for edge, step, out in ((ROWS - 1, -1, north), (0, 1, south)):
        out[pl.ds(0, PLANES, stride=2), :] = vel[pl.ds(edge, PLANES, stride=ROWS), :]
        out[pl.ds(1, PLANES, stride=2), :] = vel[pl.ds(edge + step, PLANES, stride=ROWS), :]
        out[pl.ds(40, PLANES), :] = tra[pl.ds(edge, PLANES, stride=ROWS), :]
        out[60:61, :] = levels[edge : edge + 1]
        out[61:62, :] = levels[edge + step : edge + step + 1]
        out[62:63, :] = visc[edge : edge + 1, :]
        out[63:64, :] = diff[edge : edge + 1, :]
    up = north[...]
    down = south[...]
    is_odd = odd("lat")
    send_a[...] = jnp.where(is_odd, down, up)
    send_b[...] = jnp.where(is_odd, up, down)

    @pl.when(at_fold())
    def _():
        turned = flip_lanes(up)
        send_b[...] = jnp.where(row_ids(ROWS) < 2 * PLANES, -turned, turned)


def corner_kernel(cols, recv_a, recv_b, out, rim_north, rim_south, spread):
    is_odd = odd("lat")
    got_a = recv_a[...]
    got_b = recv_b[...]
    rim_north[...] = jnp.where(is_odd, got_b, got_a)
    rim_south[...] = jnp.where(is_odd, got_a, got_b)
    out[0:ROWS, :] = cols[...]
    out[ROWS : ROWS + 8, :] = jnp.zeros((8, LANES), F32)
    phase = lane_ids(1) & 3
    for rim, row in ((rim_south, ROWS), (rim_north, ROWS + 1)):
        spread[...] = jnp.zeros((LANES, LANES), F32)
        spread[pl.ds(0, PLANES, stride=4), :] = rim[pl.ds(0, PLANES, stride=2), :]
        spread[120:121, :] = rim[60:61, :]
        flat = spread[...].T
        total = jnp.zeros((1, LANES), F32)
        for c, col in enumerate((126, 127, 0, 1)):
            total = jnp.where(phase == c, turn(flat[col : col + 1], c), total)
        out[row : row + 1, :] = total


def rim_lanes(own, east, west):
    phase = lane_ids(own.shape[0]) & 3
    return jnp.where(phase < 2, own, east), jnp.where(phase < 2, west, own)


def spread_levels(strip):
    lanes = lane_ids(strip.shape[0])
    x = jnp.where((lanes >> 2) == 30, strip, 0.0)
    for step in (4, 8, 16, 32, 64):
        x = x + turn(x, step)
    return x


def star_kernel(
    vel, lev, visc, depth, wind, rim_north, rim_south, own_cols, recv_a, recv_b,
    star, mean, fields, send_a, send_b,
    own_pad, east_pad, west_pad, level_pad, level_east, level_west, faces, plane_pad, lap_pad, swap, swap_lap, sums,
):
    is_odd = odd("lon")
    inner = pl.ds(8, ROWS)
    for src, dst in ((own_cols[...], own_pad), (jnp.where(is_odd, recv_b[...], recv_a[...]), east_pad),
                     (jnp.where(is_odd, recv_a[...], recv_b[...]), west_pad)):
        dst[8 : 8 + ROWS, :] = src[0:ROWS]
        dst[7:8, :] = src[ROWS : ROWS + 1]
        dst[8 + ROWS : 9 + ROWS, :] = src[ROWS + 1 : ROWS + 2]
    lanes = lane_ids(ROWS)
    group = (lanes >> 2).astype(F32)
    level_of_lane = jnp.where(group >= LEVELS, group - LEVELS, group)

    def strips(rows):
        return rim_lanes(own_pad[rows, :], east_pad[rows, :], west_pad[rows, :])

    laps = []
    for which in range(2):
        centre, north, south = (strips(pl.ds(r, ROWS))[which] for r in (8, 9, 7))

        def wet_of(strip):
            return (level_of_lane < spread_levels(strip)).astype(F32)

        wet = wet_of(centre)
        total = wet_of(north) * (north - centre) + wet_of(south) * (south - centre)
        for shift in (1, LANES - 1):
            total += turn(wet, shift) * (turn(centre, shift) - centre)
        laps.append(wet * total)
    phase = lanes & 3

    def swapped(east, west):
        return jnp.where(phase == 1, turn(east, LANES - 1), turn(west, 1))

    for tall in range(0, 72, 8):
        rows = pl.ds(7 + tall, 8)
        e, w = strips(rows)
        swap[pl.ds(tall, 8), :] = jnp.where((lane_ids(8) & 3) == 1, turn(e, LANES - 1), turn(w, 1))
    swap_lap[...] = swapped(laps[0], laps[1])
    level_pad[inner, :] = lev[...].astype(F32)
    level_pad[7:8, :] = rim_south[60:61, :]
    level_pad[6:7, :] = rim_south[61:62, :]
    level_pad[72:73, :] = rim_north[60:61, :]
    level_pad[73:74, :] = rim_north[61:62, :]
    tall_lanes = lane_ids(72)
    first_lane = tall_lanes == 0
    last_lane = tall_lanes == LANES - 1

    def east_west(x, halo):
        rows = x.shape[0]
        return (
            jnp.where(last_lane[0:rows], halo, turn(x, LANES - 1)),
            jnp.where(first_lane[0:rows], halo, turn(x, 1)),
        )

    level_centre = level_pad[pl.ds(7, 72), :]
    level_east[...], level_west[...] = east_west(level_centre, turn(swap[...], 6))
    v = visc[...]
    halo = turn(jnp.where((lanes & 1) == 0, turn(east_pad[inner, :], LANES - 1), turn(west_pad[inner, :], 1)), 3)
    v_east, v_west = east_west(v, halo)
    ids = row_ids(ROWS)
    v_north = jnp.where(ids == ROWS - 1, rim_north[62:63, :], pltpu.roll(v, ROWS - 1, 0))
    v_south = jnp.where(ids == 0, rim_south[62:63, :], pltpu.roll(v, 1, 0))
    for n, other in enumerate((v_east, v_west, v_north, v_south)):
        faces[n] = 0.5 * (v + other)
    row = (lax.axis_index("lat") * ROWS).astype(F32) + ids.astype(F32)
    turning = 0.25 * jnp.sin(math.pi * ((row + 0.5) / (ROWS * lax.axis_size("lat")) - 0.5))
    sums[...] = jnp.zeros((2, ROWS, LANES), F32)

    def level_step(k, carry):
        level = k.astype(F32)
        wet = (level < level_pad[pl.ds(7, 72), :]).astype(F32)
        wet_n = (level < level_pad[pl.ds(8, 72), :]).astype(F32)
        wet_s = (level < level_pad[pl.ds(6, 72), :]).astype(F32)
        wet_e = (level < level_east[...]).astype(F32)
        wet_w = (level < level_west[...]).astype(F32)
        wet_in = (level < level_pad[inner, :]).astype(F32)
        values = []
        for comp in range(2):
            p = comp * LEVELS + k
            x = vel[pl.ds(pl.multiple_of(p * ROWS, ROWS), ROWS), :]
            values.append(x)
            plane_pad[comp, inner, :] = x
            plane_pad[comp, 7:8, :] = rim_south[pl.ds(2 * p, 1), :]
            plane_pad[comp, 6:7, :] = rim_south[pl.ds(2 * p + 1, 1), :]
            plane_pad[comp, 72:73, :] = rim_north[pl.ds(2 * p, 1), :]
            plane_pad[comp, 73:74, :] = rim_north[pl.ds(2 * p + 1, 1), :]
            centre = plane_pad[comp, pl.ds(7, 72), :]
            east, west = east_west(centre, turn(swap[...], 126 - 4 * p))
            total = wet_e * (east - centre) + wet_w * (west - centre)
            total += wet_n * (plane_pad[comp, pl.ds(8, 72), :] - centre)
            total += wet_s * (plane_pad[comp, pl.ds(6, 72), :] - centre)
            lap_pad[comp, pl.ds(7, 72), :] = wet * total
        for comp in range(2):
            p = comp * LEVELS + k
            centre = lap_pad[comp, inner, :]
            east, west = east_west(centre, turn(swap_lap[...], 126 - 4 * p))
            total = faces[0] * wet_e[1:65] * (east - centre) + faces[1] * wet_w[1:65] * (west - centre)
            total += faces[2] * wet_n[1:65] * (lap_pad[comp, pl.ds(9, ROWS), :] - centre)
            total += faces[3] * wet_s[1:65] * (lap_pad[comp, pl.ds(7, ROWS), :] - centre)
            rotated = values[1] if comp == 0 else -values[0]
            out = wet_in * (values[comp] - total + turning * rotated)
            star[pl.ds(pl.multiple_of(p * ROWS, ROWS), ROWS), :] = out
            sums[comp] += out
        return carry

    lax.fori_loop(0, LEVELS, level_step, 0)
    levels = level_pad[inner, :]
    ocean = levels > 0.0
    for comp in range(2):
        column_mean = sums[comp] / jnp.maximum(levels, 1.0)
        mean[pl.ds(comp * ROWS, ROWS), :] = column_mean
        fields[pl.ds(comp * ROWS, ROWS), :] = column_mean + jnp.where(ocean, wind[pl.ds(comp * ROWS, ROWS), :], 0.0)
    fields[pl.ds(2 * ROWS, ROWS), :] = jnp.where(ocean, depth[...], 0.0)
    lat_odd = odd("lat")
    for f in range(3):
        up = fields[pl.ds(f * ROWS + ROWS - MARGIN, MARGIN), :]
        down = fields[pl.ds(f * ROWS, MARGIN), :]
        here = pl.ds(f * MARGIN, MARGIN)
        send_a[here, :] = jnp.where(lat_odd, down, up)
        send_b[here, :] = jnp.where(lat_odd, up, down)

    @pl.when(at_fold())
    def _():
        for f in range(3):
            up = fields[pl.ds(f * ROWS + ROWS - MARGIN, MARGIN), :]
            turned = flip_rows(flip_lanes(up))
            send_b[pl.ds(f * MARGIN, MARGIN), :] = turned if f == 2 else -turned


def tracer_kernel(tra, lev, diff, rim_north, rim_south, recv_a, recv_b, out, swap, faces, level_sides):
    is_odd = odd("lon")
    lanes = lane_ids(ROWS)
    ids = row_ids(ROWS)
    got_a = recv_a[0:ROWS, :]
    got_b = recv_b[0:ROWS, :]
    east_cols = jnp.where(is_odd, got_b, got_a)
    west_cols = jnp.where(is_odd, got_a, got_b)
    swap[...] = jnp.where((lanes & 1) == 0, turn(east_cols, LANES - 1), turn(west_cols, 1))

    def sides(x, halo, north_row, south_row):
        return (
            jnp.where(lanes == LANES - 1, halo, turn(x, LANES - 1)),
            jnp.where(lanes == 0, halo, turn(x, 1)),
            jnp.where(ids == ROWS - 1, north_row, pltpu.roll(x, ROWS - 1, 0)),
            jnp.where(ids == 0, south_row, pltpu.roll(x, 1, 0)),
        )

    level = lev[...].astype(F32)
    level_halo = jnp.where(lanes == LANES - 1, turn(east_cols, 5), turn(west_cols, 7))
    d = diff[...]
    for n, other in enumerate(sides(level, level_halo, rim_north[60:61, :], rim_south[60:61, :])):
        level_sides[n] = jnp.minimum(level, other)
    for n, other in enumerate(sides(d, turn(swap[...], 1), rim_north[63:64, :], rim_south[63:64, :])):
        faces[n] = 0.5 * (d + other)

    def level_step(k, carry):
        weights = [jnp.where(k.astype(F32) < level_sides[n], faces[n], 0.0) for n in range(4)]
        for comp in range(2):
            p = comp * LEVELS + k
            here = pl.ds(pl.multiple_of(p * ROWS, ROWS), ROWS)
            x = tra[here, :]
            around = sides(x, turn(swap[...], 47 - 2 * p), rim_north[pl.ds(40 + p, 1), :], rim_south[pl.ds(40 + p, 1), :])
            total = weights[0] * (around[0] - x)
            for n in range(1, 4):
                total += weights[n] * (around[n] - x)
            out[here, :] = x + total
        return carry

    lax.fori_loop(0, LEVELS, level_step, 0)


def widen_kernel(fields, recv_a, recv_b, tall, send):
    is_odd = odd("lat")
    group = lane_ids(TALL) >> 5
    east = jnp.zeros((TALL, LANES), F32)
    west = jnp.zeros((TALL, LANES), F32)
    for f in range(3):
        here = pl.ds(f * MARGIN, MARGIN)
        got_a = recv_a[here, :]
        got_b = recv_b[here, :]
        tall[pl.ds(f * TALL, MARGIN), :] = jnp.where(is_odd, got_a, got_b)
        tall[pl.ds(f * TALL + MARGIN, ROWS), :] = fields[pl.ds(f * ROWS, ROWS), :]
        tall[pl.ds(f * TALL + MARGIN + ROWS, MARGIN), :] = jnp.where(is_odd, got_b, got_a)
        x = tall[pl.ds(f * TALL, TALL), :]
        east = jnp.where(group == f, turn(x, 32 * (f + 1)), east)
        west = jnp.where(group == f, turn(x, 32 * f), west)
    send[0:TALL, :] = east
    send[TALL : 2 * TALL, :] = west


def gram_pairs():
    return [(i, j) for i in range(SOLVE_ITERS) for j in range(i, SOLVE_ITERS + 1)]


def surface_kernel(tall, recv_a, recv_b, basis_out, flow, partial, state, height, flux, slope, basis, weights, diagonal):
    is_odd = odd("lon")
    rows = pl.ds(8, TALL)
    lanes = lane_ids(TALL)
    got_a = recv_a[...]
    got_b = recv_b[...]
    from_east = jnp.where(is_odd, got_b, got_a)
    from_west = jnp.where(is_odd, got_a, got_b)
    for f in range(3):
        state[f, 0, rows, :] = tall[pl.ds(f * TALL, TALL), :]
        state[f, 1, rows, :] = jnp.where(
            lanes < 64, turn(from_east, (LANES - 32 * f) % LANES), turn(from_west, 96 - 32 * f)
        )
    last = lanes == LANES - 1
    first = lanes == 0

    def lane_sides(a, b):
        n = a.shape[0]
        ea, eb, wa, wb = turn(a, LANES - 1), turn(b, LANES - 1), turn(a, 1), turn(b, 1)
        return (
            (jnp.where(last[0:n], eb, ea), jnp.where(last[0:n], ea, eb)),
            (jnp.where(first[0:n], wb, wa), jnp.where(first[0:n], wa, wb)),
        )

    for half in range(2):
        slope[half, rows, :] = jnp.where(state[2, half, rows, :] > 0.0, SLOPE, 0.0)
        height[half, rows, :] = jnp.zeros((TALL, LANES), F32)

    def subcycle(step, carry):
        for half in range(2):
            flux[half, rows, :] = state[2, half, rows, :] * state[1, half, rows, :]
        east, west = lane_sides(*(state[2, half, rows, :] * state[0, half, rows, :] for half in range(2)))
        for half in range(2):
            divergence = (east[half] - west[half]) + (flux[half, pl.ds(9, TALL), :] - flux[half, pl.ds(7, TALL), :])
            height[half, rows, :] = height[half, rows, :] - slope[half, rows, :] * divergence
        east, west = lane_sides(height[0, rows, :], height[1, rows, :])
        for half in range(2):
            state[0, half, rows, :] = state[0, half, rows, :] - slope[half, rows, :] * (east[half] - west[half])
            state[1, half, rows, :] = state[1, half, rows, :] - slope[half, rows, :] * (
                height[half, pl.ds(9, TALL), :] - height[half, pl.ds(7, TALL), :]
            )
        return carry

    lax.fori_loop(0, SUBCYCLES, subcycle, 0)
    for comp in range(2):
        flow[pl.ds(comp * ROWS, ROWS), :] = state[comp, 0, pl.ds(8 + MARGIN, ROWS), :]
    scale = 2.0 / RADIUS
    short = ROWS + 16
    base = MARGIN

    def nine(read):
        out = [[], []]
        for off in (0, 1, -1):
            a, b = read(0, pl.ds(base + off, short)), read(1, pl.ds(base + off, short))
            east, west = lane_sides(a, b)
            for half, centre in enumerate((a, b)):
                out[half] += [centre, east[half], west[half]]
        return out

    around = nine(lambda half, where: state[2, half, where, :])
    for half in range(2):
        d = around[half][0]
        wet = d > 0.0
        total = jnp.where(wet, 0.05, 1.0)
        for n in range(1, 9):
            factor = 0.5 if n in (1, 2, 3, 6) else 0.25
            w = jnp.where(wet & (around[half][n] > 0.0), factor * (d + around[half][n]), 0.0)
            weights[n - 1, half] = scale * w
            total += w
        diagonal[half] = scale * (total - CENTRE)
        basis[0, half, pl.ds(base, short), :] = height[half, pl.ds(base, short), :]

    def applied(source):
        around = nine(lambda half, where: basis[source, half, where, :])
        out = []
        for half in range(2):
            total = diagonal[half] * around[half][0]
            for n in range(1, 9):
                total -= weights[n - 1, half] * around[half][n]
            out.append(total)
        return out

    for half, x in enumerate(applied(0)):
        basis[1, half, pl.ds(base, short), :] = 0.5 * x

    def next_basis(k, carry):
        for half, x in enumerate(applied(k)):
            basis[k + 1, half, pl.ds(base, short), :] = x - basis[k - 1, half, pl.ds(base, short), :]
        return carry

    lax.fori_loop(1, SOLVE_ITERS, next_basis, 0)
    lane = lane_ids(1)
    row = jnp.zeros((1, LANES), F32)
    mine = pl.ds(8 + MARGIN, ROWS)
    for n, (i, j) in enumerate(gram_pairs()):
        product = basis[i, 0, mine, :] * basis[j, 0, mine, :]
        row = jnp.where(lane == n, jnp.sum(jnp.sum(product, axis=0, keepdims=True), axis=1, keepdims=True), row)
    partial[...] = jnp.broadcast_to(row, partial.shape)
    for i in range(SOLVE_ITERS):
        for half in range(2):
            basis_out[i, half] = basis[i, half, pl.ds(base, short), :]


def solve_coefficients(gram):
    half = 0.5 * RADIUS

    def image_of(d):
        out = [None] * (len(d) + 1)

        def add(n, term):
            out[n] = term if out[n] is None else out[n] + term

        for j, value in enumerate(d):
            add(j, CENTRE * value)
            if j == 0:
                add(1, RADIUS * value)
            else:
                add(j + 1, half * value)
                add(j - 1, half * value)
        return out

    def inner(a, b):
        total = None
        for i, x in enumerate(a):
            for j, y in enumerate(b):
                term = x * y * gram[(min(i, j), max(i, j))]
                total = term if total is None else total + term
        return total

    one = jnp.ones((8, LANES), F32)
    residual, direction, surface = [one], [one], [0.0 * one]
    norm = gram[(0, 0)]
    for iteration in range(SOLVE_ITERS):
        image = image_of(direction)
        step = norm / inner(direction, image)
        surface = [a + step * b for a, b in zip(surface, direction)] + [0.0 * one]
        if iteration == SOLVE_ITERS - 1:
            break
        residual = [(residual[n] if n < len(residual) else 0.0) - step * x for n, x in enumerate(image)]
        fresh = inner(residual, residual)
        ratio = fresh / norm
        direction = [x + (ratio * direction[n] if n < len(direction) else 0.0) for n, x in enumerate(residual)]
        norm = fresh
    return surface[:SOLVE_ITERS]


def final_kernel(gathered, basis, flow, mean, star, lev, velocity_out, surface_out, pad, change):
    sums = jnp.sum(gathered[...], axis=0, keepdims=True)
    lane = lane_ids(1)
    gram = {}
    for n, pair in enumerate(gram_pairs()):
        value = jnp.sum(jnp.where(lane == n, sums, 0.0), axis=1, keepdims=True)
        gram[pair] = jnp.broadcast_to(value, (8, LANES))
    coefficients = [c[0:1] for c in solve_coefficients(gram)]
    for half in range(2):
        total = coefficients[0] * basis[0, half]
        for i in range(1, SOLVE_ITERS):
            total += coefficients[i] * basis[i, half]
        pad[half] = total
    mine = pl.ds(8, ROWS)
    centre = pad[0, mine, :]
    ghost = pad[1, mine, :]
    surface_out[...] = centre
    lanes = lane_ids(ROWS)
    east = jnp.where(lanes == LANES - 1, turn(ghost, LANES - 1), turn(centre, LANES - 1))
    west = jnp.where(lanes == 0, turn(ghost, 1), turn(centre, 1))
    levels = lev[...]
    slope = jnp.where(levels > 0, SLOPE, 0.0)
    slopes = (east - west, pad[0, pl.ds(9, ROWS), :] - pad[0, pl.ds(7, ROWS), :])
    for comp in range(2):
        here = pl.ds(comp * ROWS, ROWS)
        change[comp] = flow[here, :] - slope * slopes[comp] - mean[here, :]

    def level_step(k, carry):
        wet = k < levels
        for comp in range(2):
            here = pl.ds(pl.multiple_of((comp * LEVELS + k) * ROWS, ROWS), ROWS)
            velocity_out[here, :] = star[here, :] + jnp.where(wet, change[comp], 0.0)
        return carry

    lax.fori_loop(0, LEVELS, level_step, 0)


def call(kernel, shapes, scratch, flops, *args):
    out = tuple(jax.ShapeDtypeStruct(s, F32) for s in shapes)
    moved = sum(4 * math.prod(a.shape) for a in args) + sum(4 * math.prod(s) for s in shapes)
    return pl.pallas_call(
        kernel,
        out_shape=out,
        scratch_shapes=[pltpu.VMEM(s, F32) for s in scratch],
        compiler_params=pltpu.CompilerParams(vmem_limit_bytes=32 * 1024 * 1024),
        cost_estimate=pl.CostEstimate(flops=flops, bytes_accessed=moved, transcendentals=0),
    )(*args)


def pair_tables(lon, lat):
    def index(i, j):
        return j * lat + i

    lat_a, lat_b, lon_a, lon_b = [], [], [], []
    for j in range(lon):
        for i in range(lat):
            lat_a.append((index(i, j), index(i ^ 1, j)))
            if i == lat - 1:
                lat_b.append((index(i, j), index(i, lon - 1 - j)))
            elif i > 0:
                lat_b.append((index(i, j), index(i + 1 if i % 2 else i - 1, j)))
            lon_a.append((index(i, j), index(i, j ^ 1)))
            lon_b.append((index(i, j), index(i, (j + 1 if j % 2 else j - 1) % lon)))
    return lat_a, lat_b, lon_a, lon_b


def per_device(lon, lat, tracers, velocity, active_levels, diffusivity, viscosity, ocean_depth, wind_forcing):
    lat_a, lat_b, lon_a, lon_b = pair_tables(lon, lat)

    def swap(x, pairs):
        return lax.ppermute(x, BOTH, pairs)

    block = (ROWS, LANES)
    tra = tracers.reshape(PLANES * ROWS, LANES)
    vel = velocity.reshape(PLANES * ROWS, LANES)
    wind = wind_forcing.reshape(2 * ROWS, LANES)
    cols, send_a, send_b, _, _ = call(
        pack_kernel, [block] * 5, [], 10**6, vel, tra, active_levels, viscosity, diffusivity
    )
    got_b = swap(send_b, lat_b)
    got_a = swap(send_a, lat_a)
    cols, rim_north, rim_south = call(
        corner_kernel, [(ROWS + 8, LANES), block, block], [(LANES, LANES)], 10**5, cols, got_a, got_b
    )
    got_b = swap(cols, lon_b)
    got_a = swap(cols, lon_a)
    tall_pad = (ROWS + 24, LANES)
    star, mean, fields, send_a, send_b = call(
        star_kernel,
        [(PLANES * ROWS, LANES), (2 * ROWS, LANES), (3 * ROWS, LANES), (3 * MARGIN, LANES), (3 * MARGIN, LANES)],
        [tall_pad, tall_pad, tall_pad, tall_pad, (72, LANES), (72, LANES), (4,) + block, (2,) + tall_pad, (2,) + tall_pad,
         (72, LANES), block, (2,) + block],
        10**7,
        vel, active_levels, viscosity, ocean_depth, wind, rim_north, rim_south, cols, got_a, got_b,
    )
    (tracers_out,) = call(
        tracer_kernel, [(PLANES * ROWS, LANES)], [block, (4,) + block, (4,) + block], 10**6,
        tra, active_levels, diffusivity, rim_north, rim_south, got_a, got_b,
    )
    got_b = swap(send_b, lat_b)
    got_a = swap(send_a, lat_a)
    tall, send = call(widen_kernel, [(3 * TALL, LANES), (2 * TALL, LANES)], [], 10**5, fields, got_a, got_b)
    is_odd = lax.axis_index("lon") % 2 == 1
    east, west = send[:TALL], send[TALL:]
    got_b = swap(jnp.where(is_odd, east, west), lon_b)
    got_a = swap(jnp.where(is_odd, west, east), lon_a)
    padded = (2, TALL + 16, LANES)
    short = (2, ROWS + 16, LANES)
    basis, flow, partial = call(
        surface_kernel,
        [(SOLVE_ITERS,) + short, (2 * ROWS, LANES), (lon * lat, LANES)],
        [(3,) + padded, padded, padded, padded, (SOLVE_ITERS + 1,) + padded, (8,) + short, short],
        10**7,
        tall, got_a, got_b,
    )
    gathered = lax.all_to_all(partial, BOTH, 0, 0, tiled=True)
    velocity_out, surface = call(
        final_kernel, [(PLANES * ROWS, LANES), block], [short, (2,) + block], 10**6,
        gathered, basis, flow, mean, star, active_levels,
    )
    return tracers_out.reshape(tracers.shape), velocity_out.reshape(velocity.shape), surface


def solution(mesh):
    placed = (
        P(None, None, "lat", "lon"),
        P(None, None, "lat", "lon"),
        P("lat", "lon"),
        P("lat", "lon"),
        P("lat", "lon"),
        P("lat", "lon"),
        P(None, "lat", "lon"),
    )
    return jax.shard_map(
        functools.partial(per_device, mesh.shape["lon"], mesh.shape["lat"]),
        mesh=mesh,
        in_specs=placed,
        out_specs=(P(None, None, "lat", "lon"), P(None, None, "lat", "lon"), P("lat", "lon")),
        check_vma=False,
    )
```

```python
import functools
import math

import jax
import jax.numpy as jnp
from jax import lax
from jax.experimental import pallas as pl
from jax.experimental.pallas import tpu as pltpu
from jax.sharding import PartitionSpec as P

SUBCYCLES = 8
SOLVE_ITERS = 4
LEVELS = 10
PLANES = 2 * LEVELS
ROWS = 64
LANES = 128
MARGIN = 24
TALL = ROWS + 2 * MARGIN
RIM = 32
SLOPE = 0.15
CENTRE = 9.0
RADIUS = 9.1
F32 = jnp.float32
BOTH = ("lon", "lat")

STRIP = 24
RIMS = 3 * STRIP
LAT_SEND = 3 * MARGIN + RIMS + MARGIN
LON_SEND = 2 * TALL + 2 * STRIP


def lane_ids(rows):
    return lax.broadcasted_iota(jnp.int32, (rows, LANES), 1)


def row_ids(rows):
    return lax.broadcasted_iota(jnp.int32, (rows, LANES), 0)


def turn(x, shift):
    return pltpu.roll(x, shift, 1)


def flip_lanes(x, bits=7):
    lanes = lane_ids(x.shape[0])
    for bit in range(bits):
        step = 1 << bit
        x = jnp.where((lanes & step) != 0, turn(x, step), turn(x, LANES - step))
    return x


def flip_rows(x):
    rows = x.shape[0]
    ids = row_ids(rows)
    for bit in range(3):
        step = 1 << bit
        x = jnp.where((ids & step) != 0, pltpu.roll(x, step, 0), pltpu.roll(x, rows - step, 0))
    return jnp.concatenate([x[r : r + 8] for r in range(rows - 8, -8, -8)], axis=0)


def odd(axis):
    return lax.rem(lax.axis_index(axis), 2) == 1


def at_fold():
    return lax.axis_index("lat") == lax.axis_size("lat") - 1


def shifted(x):
    rows = x.shape[0]
    return (turn(x, LANES - 1), turn(x, 1), pltpu.roll(x, rows - 1, 0), pltpu.roll(x, 1, 0))


def block_kernel(
    vel, tra, lev, visc, diff, depth, wind,
    star, mean, fields, cols, north, south, send_a, send_b,
    faces, face_levels, sums, turning,
):
    lanes = lane_ids(ROWS)
    ids = row_ids(ROWS)
    levels = lev[...].astype(F32)
    v = visc[...]
    inside = (lanes < LANES - 1, lanes > 0, ids < ROWS - 1, ids > 0)
    for n, (v_n, level_n) in enumerate(zip(shifted(v), shifted(levels))):
        faces[n] = 0.5 * (v + v_n)
        face_levels[n] = jnp.where(inside[n], jnp.minimum(levels, level_n), 0.0)
    row = (lax.axis_index("lat") * ROWS).astype(F32) + ids.astype(F32)
    turning[...] = 0.25 * jnp.sin(math.pi * ((row + 0.5) / (ROWS * lax.axis_size("lat")) - 0.5))
    sums[...] = jnp.zeros((2, ROWS, LANES), F32)
    acc = jnp.where((lanes >> 2) == 20, turn(levels, 82), 0.0)
    cols[...] = jnp.where((lanes >> 2) == 21, turn(v, 86), acc)

    def level_step(k, carry):
        level = k.astype(F32)
        open_faces = [level < face_levels[n] for n in range(4)]
        wet = level < lev[...].astype(F32)
        weights = [jnp.where(o, faces[n], 0.0) for n, o in enumerate(open_faces)]
        values = [
            vel[pl.ds(pl.multiple_of((comp * LEVELS + k) * ROWS, ROWS), ROWS), :] for comp in range(2)
        ]
        packed = cols[...]
        for comp, x in enumerate(values):
            p = comp * LEVELS + k
            lap = jnp.zeros((ROWS, LANES), F32)
            for n, x_n in enumerate(shifted(x)):
                lap += jnp.where(open_faces[n], x_n - x, 0.0)
            second = jnp.zeros((ROWS, LANES), F32)
            for n, lap_n in enumerate(shifted(lap)):
                second += weights[n] * (lap_n - lap)
            rotated = values[1] if comp == 0 else -values[0]
            out = jnp.where(wet, x - second + turning[...] * rotated, 0.0)
            star[pl.ds(pl.multiple_of(p * ROWS, ROWS), ROWS), :] = out
            sums[comp] += out
            packed = jnp.where((lanes >> 2) == p, turn(x, 4 * p + 2), packed)
            t = tra[pl.ds(pl.multiple_of(p * ROWS, ROWS), ROWS), :]
            packed = jnp.where((lanes >> 1) == 44 + p, turn(t, lax.rem(89 + 2 * p, LANES)), packed)
        cols[...] = packed
        return carry

    lax.fori_loop(0, LEVELS, level_step, 0)
    ocean = levels > 0.0
    for comp in range(2):
        here = pl.ds(comp * ROWS, ROWS)
        column_mean = sums[comp] / jnp.maximum(levels, 1.0)
        mean[here, :] = column_mean
        fields[here, :] = column_mean + jnp.where(ocean, wind[here, :], 0.0)
    fields[pl.ds(2 * ROWS, ROWS), :] = jnp.where(ocean, depth[...], 0.0)
    for edge, step, out in ((ROWS - 1, -1, north), (0, 1, south)):
        out[...] = jnp.zeros((RIMS, LANES), F32)
        for d in range(2):
            r = edge + d * step
            out[pl.ds(d * STRIP, PLANES), :] = vel[pl.ds(r, PLANES, stride=ROWS), :]
            out[pl.ds(d * STRIP + 20, 1), :] = levels[r : r + 1]
            out[pl.ds(d * STRIP + 21, 1), :] = visc[pl.ds(r, 1), :]
        out[pl.ds(2 * STRIP, PLANES), :] = tra[pl.ds(edge, PLANES, stride=ROWS), :]
        out[pl.ds(2 * STRIP + 20, 1), :] = diff[pl.ds(edge, 1), :]
    lat_odd = odd("lat")

    def put(start, up, down):
        here = pl.ds(start, up.shape[0])
        send_a[here, :] = jnp.where(lat_odd, down, up)
        send_b[here, :] = jnp.where(lat_odd, up, down)

    for f in range(3):
        put(f * MARGIN, fields[pl.ds((f + 1) * ROWS - MARGIN, MARGIN), :], fields[pl.ds(f * ROWS, MARGIN), :])
    put(3 * MARGIN, north[...], south[...])
    put(3 * MARGIN + RIMS, cols[ROWS - MARGIN : ROWS, :], cols[0:MARGIN, :])

    @pl.when(at_fold())
    def _():
        for f in range(3):
            turned = flip_rows(flip_lanes(fields[pl.ds((f + 1) * ROWS - MARGIN, MARGIN), :]))
            send_b[pl.ds(f * MARGIN, MARGIN), :] = turned if f == 2 else -turned
        turned = flip_lanes(north[...])
        r = row_ids(RIMS)
        is_velocity = (r < PLANES) | ((r >= STRIP) & (r < STRIP + PLANES))
        send_b[pl.ds(3 * MARGIN, RIMS), :] = jnp.where(is_velocity, -turned, turned)
        turned = flip_rows(flip_lanes(cols[ROWS - MARGIN : ROWS, :], 2))
        send_b[pl.ds(3 * MARGIN + RIMS, MARGIN), :] = jnp.where(lane_ids(MARGIN) < 4 * PLANES, -turned, turned)


def widen_kernel(fields, cols, diff, north, south, recv_a, recv_b, tall, strips, tracer_rows, send_a, send_b, east, west):
    lat_odd = odd("lat")
    lon_odd = odd("lon")
    group = lane_ids(TALL) >> 5

    def received(start, count):
        here = pl.ds(start, count)
        got_a = recv_a[here, :]
        got_b = recv_b[here, :]
        return jnp.where(lat_odd, got_b, got_a), jnp.where(lat_odd, got_a, got_b)

    acc_east = jnp.zeros((TALL, LANES), F32)
    acc_west = jnp.zeros((TALL, LANES), F32)
    for f in range(4):
        from_north, from_south = received(f * MARGIN if f < 3 else 3 * MARGIN + RIMS, MARGIN)
        tall[pl.ds(f * TALL, MARGIN), :] = from_south
        tall[pl.ds(f * TALL + MARGIN, ROWS), :] = fields[pl.ds(f * ROWS, ROWS), :] if f < 3 else cols[...]
        tall[pl.ds(f * TALL + MARGIN + ROWS, MARGIN), :] = from_north
        if f < 3:
            x = tall[pl.ds(f * TALL, TALL), :]
            acc_east = jnp.where(group == f, turn(x, 32 * (f + 1)), acc_east)
            acc_west = jnp.where(group == f, turn(x, 32 * f), acc_west)
    for out, acc, shift in ((east, acc_east, 97), (west, acc_west, 96)):
        out[pl.ds(0, TALL), :] = acc
        out[pl.ds(MARGIN, ROWS), :] = jnp.where(lane_ids(ROWS) == 96, turn(diff[...], shift), acc[MARGIN : MARGIN + ROWS])
    rims = received(3 * MARGIN, RIMS)
    for s, (own, rim) in enumerate(((north, rims[0]), (south, rims[1]))):
        pieces = (rim[STRIP : 2 * STRIP], rim[0:STRIP], own[0:STRIP, :], own[STRIP : 2 * STRIP, :])
        acc_east = jnp.zeros((STRIP, LANES), F32)
        acc_west = jnp.zeros((STRIP, LANES), F32)
        for r, x in enumerate(pieces):
            strips[pl.ds((4 * s + r) * STRIP, STRIP), :] = x
            acc_east = jnp.where(group[0:STRIP] == r, turn(x, (32 * (r + 1)) % LANES), acc_east)
            acc_west = jnp.where(group[0:STRIP] == r, turn(x, 32 * r), acc_west)
        east[pl.ds(TALL + s * STRIP, STRIP), :] = acc_east
        west[pl.ds(TALL + s * STRIP, STRIP), :] = acc_west
        tracer_rows[pl.ds(2 * s * STRIP, STRIP), :] = rim[2 * STRIP : 3 * STRIP]
        tracer_rows[pl.ds((2 * s + 1) * STRIP, STRIP), :] = rim[0:STRIP]
    k = tall[pl.ds(3 * TALL, TALL), :]
    send_a[pl.ds(0, TALL), :] = k
    send_b[pl.ds(0, TALL), :] = k
    rest = pl.ds(TALL, TALL + 2 * STRIP)
    e, w = east[...], west[...]
    send_a[rest, :] = jnp.where(lon_odd, w, e)
    send_b[rest, :] = jnp.where(lon_odd, e, w)


def tracer_kernel(tra, lev, diff, tracer_rows, recv_a, recv_b, out, swap, faces, face_levels):
    is_odd = odd("lon")
    lanes = lane_ids(ROWS)
    ids = row_ids(ROWS)

    def received(start):
        here = pl.ds(start + MARGIN, ROWS)
        got_a = recv_a[here, :]
        got_b = recv_b[here, :]
        return jnp.where(is_odd, got_b, got_a), jnp.where(is_odd, got_a, got_b)

    east_cols, west_cols = received(0)
    east_rest, west_rest = received(TALL)
    swap[...] = jnp.where((lanes & 1) == 0, turn(east_cols, LANES - 1), turn(west_cols, 1))

    def sides(x, halo, row):
        east, west, north, south = shifted(x)
        return (
            jnp.where(lanes == LANES - 1, halo, east),
            jnp.where(lanes == 0, halo, west),
            jnp.where(ids == ROWS - 1, tracer_rows[pl.ds(row, 1), :], north),
            jnp.where(ids == 0, tracer_rows[pl.ds(row + 2 * STRIP, 1), :], south),
        )

    level = lev[...].astype(F32)
    level_halo = jnp.where(lanes == LANES - 1, turn(east_cols, 45), turn(west_cols, 47))
    d = diff[...]
    d_halo = jnp.where(lanes == LANES - 1, turn(east_rest, 31), turn(west_rest, 32))
    for n, other in enumerate(sides(level, level_halo, STRIP + 20)):
        face_levels[n] = jnp.minimum(level, other)
    for n, other in enumerate(sides(d, d_halo, 20)):
        faces[n] = 0.5 * (d + other)

    def level_step(k, carry):
        weights = [jnp.where(k.astype(F32) < face_levels[n], faces[n], 0.0) for n in range(4)]
        for comp in range(2):
            p = comp * LEVELS + k
            here = pl.ds(pl.multiple_of(p * ROWS, ROWS), ROWS)
            x = tra[here, :]
            around = sides(x, turn(swap[...], 39 - 2 * p), p)
            total = weights[0] * (around[0] - x)
            for n in range(1, 4):
                total += weights[n] * (around[n] - x)
            out[here, :] = x + total
        return carry

    lax.fori_loop(0, LEVELS, level_step, 0)


def column_strip(strip):
    rows = strip.shape[0]
    lanes = lane_ids(rows)
    ids = row_ids(rows)
    phase = lanes & 3
    group = lanes >> 2

    def spread(which):
        x = jnp.where(group == which, strip, 0.0)
        for step in (4, 8, 16, 32, 64):
            x = x + turn(x, step)
        return x

    levels = spread(20)
    v = spread(21)
    number = jnp.where(group >= LEVELS, group - LEVELS, group).astype(F32)
    wet = jnp.where((number < levels) & (group < PLANES), 1.0, 0.0)
    x = jnp.where(group < PLANES, strip, 0.0)
    open_e = wet * turn(wet, LANES - 1)
    wet_n = pltpu.roll(wet, rows - 1, 0)
    open_n = wet * wet_n
    flux_e = open_e * (turn(x, LANES - 1) - x)
    flux_n = open_n * (pltpu.roll(x, rows - 1, 0) - x)
    lap = flux_e - turn(flux_e, 1) + flux_n - pltpu.roll(flux_n, 1, 0)
    seam = jnp.where(phase == 1, flux_e, 0.0)
    added = seam - turn(seam, 1)
    base = jnp.where(phase == 1, lap, added)
    other = jnp.where(phase == 1, turn(lap, LANES - 1), turn(added, LANES - 1))
    face = 0.5 * (v + turn(v, LANES - 1)) * open_e
    flux_e = jnp.where(phase == 3, 0.0, face * (other - base))
    in_block = (ids != MARGIN - 1) & (ids != MARGIN + ROWS - 1)
    face = jnp.where(in_block, 0.5 * (v + pltpu.roll(v, rows - 1, 0)) * open_n, 0.0)
    flux_n = face * (pltpu.roll(added, rows - 1, 0) - added)
    second = flux_e - turn(flux_e, 1) + flux_n - pltpu.roll(flux_n, 1, 0)
    return wet * second, levels


def gram_pairs():
    return [(i, j) for i in range(SOLVE_ITERS) for j in range(i, SOLVE_ITERS + 1)]


def surface_kernel(
    tall, strips, mean, recv_a, recv_b,
    basis_out, flow, partial, col_patch, row_patch,
    state, height, flux, slope, basis, weights, diagonal,
):
    is_odd = odd("lon")
    rows = pl.ds(8, TALL)
    lanes = lane_ids(TALL)

    def received(start, count):
        here = pl.ds(start, count)
        got_a = recv_a[here, :]
        got_b = recv_b[here, :]
        return jnp.where(is_odd, got_b, got_a), jnp.where(is_odd, got_a, got_b)

    def ghost(east, west, f):
        return jnp.where(
            lane_ids(east.shape[0]) < 64, turn(east, (LANES - 32 * f) % LANES), turn(west, (96 - 32 * f) % LANES)
        )

    from_east, from_west = received(TALL, TALL)
    for f in range(3):
        state[f, 0, rows, :] = tall[pl.ds(f * TALL, TALL), :]
        state[f, 1, rows, :] = ghost(from_east, from_west, f)
    last = lanes == LANES - 1
    first = lanes == 0

    def lane_sides(a, b):
        n = a.shape[0]
        ea, eb, wa, wb = turn(a, LANES - 1), turn(b, LANES - 1), turn(a, 1), turn(b, 1)
        return (
            (jnp.where(last[0:n], eb, ea), jnp.where(last[0:n], ea, eb)),
            (jnp.where(first[0:n], wb, wa), jnp.where(first[0:n], wa, wb)),
        )

    own = tall[pl.ds(3 * TALL, TALL), :]
    phase = lanes & 3
    from_east, from_west = received(0, TALL)
    patches = []
    for side, strip in enumerate((jnp.where(phase < 2, own, from_east), jnp.where(phase < 2, from_west, own))):
        change, levels = column_strip(strip)
        patches.append(change)
        for comp in range(2):
            total = jnp.where((lanes >= 40 * comp) & (lanes < 40 * comp + 40), change, 0.0)
            for step in (4, 8, 16, 32, 64):
                total = total + turn(total, step)
            total = turn(total / jnp.maximum(levels, 1.0), 2)
            for half in range(2):
                here = lanes >= LANES - 2 if half == side else lanes < 2
                state[comp, half, rows, :] = state[comp, half, rows, :] - jnp.where(here, total, 0.0)
    patch = jnp.where(phase < 2, patches[0], patches[1])
    col_patch[...] = patch[MARGIN : MARGIN + ROWS]
    number = lax.broadcasted_iota(jnp.int32, (STRIP, LANES), 0)
    level_of_row = jnp.where(number >= LEVELS, number - LEVELS, number).astype(F32)
    is_plane = number < PLANES
    not_last = lane_ids(STRIP) < LANES - 1
    for s in range(2):
        from_east, from_west = received(2 * TALL + s * STRIP, STRIP)
        x, wet, v, deep = [], [], [], []
        for r in range(4):
            centre = strips[pl.ds((4 * s + r) * STRIP, STRIP), :]
            both = (centre, ghost(from_east, from_west, r))
            deep.append([b[20:21] for b in both])
            v.append([jnp.broadcast_to(b[21:22], (STRIP, LANES)) for b in both])
            wet.append([jnp.where(is_plane & (level_of_row < b[20:21]), 1.0, 0.0) for b in both])
            x.append([jnp.where(is_plane, b, 0.0) for b in both])
        half_range = range(2)
        lap = {}
        added = {}
        seam = [wet[1][h] * wet[2][h] * (x[2][h] - x[1][h]) for h in half_range]
        added[1] = seam
        added[2] = [-t for t in seam]
        along = {}
        for r in (1, 2):
            x_e = lane_sides(*x[r])[0]
            wet_e = lane_sides(*wet[r])[0]
            v_e = lane_sides(*v[r])[0]
            added_e = lane_sides(*added[r])[0]
            open_e = [wet[r][h] * wet_e[h] for h in half_range]
            edge = [open_e[h] * (x_e[h] - x[r][h]) for h in half_range]
            edge_w = lane_sides(*edge)[1]
            lap[r] = [
                edge[h]
                - edge_w[h]
                + wet[r][h] * (wet[r + 1][h] * (x[r + 1][h] - x[r][h]) + wet[r - 1][h] * (x[r - 1][h] - x[r][h]))
                for h in half_range
            ]
            edge = [
                jnp.where(not_last, 0.5 * (v[r][h] + v_e[h]) * open_e[h] * (added_e[h] - added[r][h]), 0.0)
                for h in half_range
            ]
            edge_w = lane_sides(*edge)[1]
            along[r] = [edge[h] - edge_w[h] for h in half_range]
        for h in half_range:
            face = [0.5 * (v[r][h] + v[r + 1][h]) * wet[r][h] * wet[r + 1][h] for r in range(3)]
            across = (face[0] * added[1][h], face[1] * (lap[2][h] - lap[1][h]), -face[2] * added[2][h])
            second = (
                across[0],
                across[1] - across[0] + along[1][h],
                across[2] - across[1] + along[2][h],
                -across[2],
            )
            for r in range(4):
                change = wet[r][h] * second[r]
                if h == 0 and r >= 2:
                    row_patch[pl.ds((2 * s + r - 2) * STRIP, STRIP), :] = change
                where = 8 + MARGIN + ((ROWS + 1 - r) if s == 0 else (r - 2))
                for comp in range(2):
                    mine = (number >= comp * LEVELS) & (number < (comp + 1) * LEVELS)
                    total = jnp.sum(jnp.where(mine, change, 0.0), axis=0, keepdims=True)
                    total = total / jnp.maximum(deep[r][h], 1.0)
                    state[comp, h, where : where + 1, :] = state[comp, h, where : where + 1, :] - total
    for comp in range(2):
        here = pl.ds(comp * ROWS, ROWS)
        started = state[comp, 0, pl.ds(8 + MARGIN, ROWS), :] - tall[pl.ds(comp * TALL + MARGIN, ROWS), :]
        flow[here, :] = -(started + mean[here, :])

    for half in range(2):
        slope[half, rows, :] = jnp.where(state[2, half, rows, :] > 0.0, SLOPE, 0.0)
        height[half, rows, :] = jnp.zeros((TALL, LANES), F32)

    def subcycle(step, carry):
        for half in range(2):
            flux[half, rows, :] = state[2, half, rows, :] * state[1, half, rows, :]
        east, west = lane_sides(*(state[2, half, rows, :] * state[0, half, rows, :] for half in range(2)))
        for half in range(2):
            divergence = (east[half] - west[half]) + (flux[half, pl.ds(9, TALL), :] - flux[half, pl.ds(7, TALL), :])
            height[half, rows, :] = height[half, rows, :] - slope[half, rows, :] * divergence
        east, west = lane_sides(height[0, rows, :], height[1, rows, :])
        for half in range(2):
            state[0, half, rows, :] = state[0, half, rows, :] - slope[half, rows, :] * (east[half] - west[half])
            state[1, half, rows, :] = state[1, half, rows, :] - slope[half, rows, :] * (
                height[half, pl.ds(9, TALL), :] - height[half, pl.ds(7, TALL), :]
            )
        return carry

    lax.fori_loop(0, SUBCYCLES, subcycle, 0)
    for comp in range(2):
        here = pl.ds(comp * ROWS, ROWS)
        flow[here, :] = flow[here, :] + state[comp, 0, pl.ds(8 + MARGIN, ROWS), :]
    scale = 2.0 / RADIUS
    short = ROWS + 16
    base = MARGIN

    def nine(read):
        out = [[], []]
        for off in (0, 1, -1):
            a, b = read(0, pl.ds(base + off, short)), read(1, pl.ds(base + off, short))
            east, west = lane_sides(a, b)
            for half, centre in enumerate((a, b)):
                out[half] += [centre, east[half], west[half]]
        return out

    around = nine(lambda half, where: state[2, half, where, :])
    for half in range(2):
        d = around[half][0]
        wet = d > 0.0
        total = jnp.where(wet, 0.05, 1.0)
        for n in range(1, 9):
            factor = 0.5 if n in (1, 2, 3, 6) else 0.25
            w = jnp.where(wet & (around[half][n] > 0.0), factor * (d + around[half][n]), 0.0)
            weights[n - 1, half] = scale * w
            total += w
        diagonal[half] = scale * (total - CENTRE)
        basis[0, half, pl.ds(base, short), :] = height[half, pl.ds(base, short), :]

    def applied(source):
        around = nine(lambda half, where: basis[source, half, where, :])
        out = []
        for half in range(2):
            total = diagonal[half] * around[half][0]
            for n in range(1, 9):
                total -= weights[n - 1, half] * around[half][n]
            out.append(total)
        return out

    for half, x in enumerate(applied(0)):
        basis[1, half, pl.ds(base, short), :] = 0.5 * x

    def next_basis(k, carry):
        for half, x in enumerate(applied(k)):
            basis[k + 1, half, pl.ds(base, short), :] = x - basis[k - 1, half, pl.ds(base, short), :]
        return carry

    lax.fori_loop(1, SOLVE_ITERS, next_basis, 0)
    lane = lane_ids(1)
    row = jnp.zeros((1, LANES), F32)
    mine = pl.ds(8 + MARGIN, ROWS)
    for n, (i, j) in enumerate(gram_pairs()):
        product = basis[i, 0, mine, :] * basis[j, 0, mine, :]
        row = jnp.where(lane == n, jnp.sum(jnp.sum(product, axis=0, keepdims=True), axis=1, keepdims=True), row)
    partial[...] = jnp.broadcast_to(row, partial.shape)
    for i in range(SOLVE_ITERS):
        for half in range(2):
            basis_out[i, half] = basis[i, half, pl.ds(base, short), :]


def solve_coefficients(gram):
    half = 0.5 * RADIUS

    def image_of(d):
        out = [None] * (len(d) + 1)

        def add(n, term):
            out[n] = term if out[n] is None else out[n] + term

        for j, value in enumerate(d):
            add(j, CENTRE * value)
            if j == 0:
                add(1, RADIUS * value)
            else:
                add(j + 1, half * value)
                add(j - 1, half * value)
        return out

    def inner(a, b):
        total = None
        for i, x in enumerate(a):
            for j, y in enumerate(b):
                term = x * y * gram[(min(i, j), max(i, j))]
                total = term if total is None else total + term
        return total

    one = jnp.ones((8, LANES), F32)
    residual, direction, surface = [one], [one], [0.0 * one]
    norm = gram[(0, 0)]
    for iteration in range(SOLVE_ITERS):
        image = image_of(direction)
        step = norm / inner(direction, image)
        surface = [a + step * b for a, b in zip(surface, direction)] + [0.0 * one]
        if iteration == SOLVE_ITERS - 1:
            break
        residual = [(residual[n] if n < len(residual) else 0.0) - step * x for n, x in enumerate(image)]
        fresh = inner(residual, residual)
        ratio = fresh / norm
        direction = [x + (ratio * direction[n] if n < len(direction) else 0.0) for n, x in enumerate(residual)]
        norm = fresh
    return surface[:SOLVE_ITERS]


def final_kernel(gathered, basis, flow, star, lev, col_patch, row_patch, velocity_out, surface_out, pad, change):
    sums = jnp.sum(gathered[...], axis=0, keepdims=True)
    lane = lane_ids(1)
    gram = {}
    for n, pair in enumerate(gram_pairs()):
        value = jnp.sum(jnp.where(lane == n, sums, 0.0), axis=1, keepdims=True)
        gram[pair] = jnp.broadcast_to(value, (8, LANES))
    coefficients = [c[0:1] for c in solve_coefficients(gram)]
    for half in range(2):
        total = coefficients[0] * basis[0, half]
        for i in range(1, SOLVE_ITERS):
            total += coefficients[i] * basis[i, half]
        pad[half] = total
    mine = pl.ds(8, ROWS)
    centre = pad[0, mine, :]
    ghost = pad[1, mine, :]
    surface_out[...] = centre
    lanes = lane_ids(ROWS)
    east = jnp.where(lanes == LANES - 1, turn(ghost, LANES - 1), turn(centre, LANES - 1))
    west = jnp.where(lanes == 0, turn(ghost, 1), turn(centre, 1))
    levels = lev[...]
    slope = jnp.where(levels > 0, SLOPE, 0.0)
    slopes = (east - west, pad[0, pl.ds(9, ROWS), :] - pad[0, pl.ds(7, ROWS), :])
    for comp in range(2):
        here = pl.ds(comp * ROWS, ROWS)
        change[comp] = flow[here, :] - slope * slopes[comp]

    rims = (lanes < 2) | (lanes >= LANES - 2)
    ids = row_ids(ROWS)

    def level_step(k, carry):
        wet = k < levels
        for comp in range(2):
            p = comp * LEVELS + k
            here = pl.ds(pl.multiple_of(p * ROWS, ROWS), ROWS)
            x = star[here, :] - jnp.where(rims, turn(col_patch[...], 126 - 4 * p), 0.0)
            for n, row in enumerate((ROWS - 1, ROWS - 2, 0, 1)):
                x = x - jnp.where(ids == row, row_patch[pl.ds(n * STRIP + p, 1), :], 0.0)
            velocity_out[here, :] = x + jnp.where(wet, change[comp], 0.0)
        return carry

    lax.fori_loop(0, LEVELS, level_step, 0)


def call(kernel, shapes, scratch, flops, *args):
    out = tuple(jax.ShapeDtypeStruct(s, F32) for s in shapes)
    moved = sum(4 * math.prod(a.shape) for a in args) + sum(4 * math.prod(s) for s in shapes)
    return pl.pallas_call(
        kernel,
        out_shape=out,
        scratch_shapes=[pltpu.VMEM(s, F32) for s in scratch],
        compiler_params=pltpu.CompilerParams(vmem_limit_bytes=32 * 1024 * 1024),
        cost_estimate=pl.CostEstimate(flops=flops, bytes_accessed=moved, transcendentals=0),
    )(*args)


def pair_tables(lon, lat):
    def index(i, j):
        return j * lat + i

    lat_a, lat_b, lon_a, lon_b = [], [], [], []
    for j in range(lon):
        for i in range(lat):
            lat_a.append((index(i, j), index(i ^ 1, j)))
            if i == lat - 1:
                lat_b.append((index(i, j), index(i, lon - 1 - j)))
            elif i > 0:
                lat_b.append((index(i, j), index(i + 1 if i % 2 else i - 1, j)))
            lon_a.append((index(i, j), index(i, j ^ 1)))
            lon_b.append((index(i, j), index(i, (j + 1 if j % 2 else j - 1) % lon)))
    return lat_a, lat_b, lon_a, lon_b


def per_device(lon, lat, tracers, velocity, active_levels, diffusivity, viscosity, ocean_depth, wind_forcing):
    lat_a, lat_b, lon_a, lon_b = pair_tables(lon, lat)

    def swap(x, pairs):
        return lax.ppermute(x, BOTH, pairs)

    block = (ROWS, LANES)
    tra = tracers.reshape(PLANES * ROWS, LANES)
    vel = velocity.reshape(PLANES * ROWS, LANES)
    wind = wind_forcing.reshape(2 * ROWS, LANES)
    rim = (RIMS, LANES)
    star, mean, fields, cols, north, south, send_a, send_b = call(
        block_kernel,
        [(PLANES * ROWS, LANES), (2 * ROWS, LANES), (3 * ROWS, LANES), block, rim, rim, (LAT_SEND, LANES), (LAT_SEND, LANES)],
        [(4,) + block, (4,) + block, (2,) + block, block],
        10**7,
        vel, tra, active_levels, viscosity, diffusivity, ocean_depth, wind,
    )
    got_b = swap(send_b, lat_b)
    got_a = swap(send_a, lat_a)
    tall, strips, tracer_rows, send_a, send_b = call(
        widen_kernel,
        [(4 * TALL, LANES), (8 * STRIP, LANES), (4 * STRIP, LANES), (LON_SEND, LANES), (LON_SEND, LANES)],
        [(TALL + 2 * STRIP, LANES)] * 2,
        10**6,
        fields, cols, diffusivity, north, south, got_a, got_b,
    )
    got_b = swap(send_b, lon_b)
    got_a = swap(send_a, lon_a)
    (tracers_out,) = call(
        tracer_kernel, [(PLANES * ROWS, LANES)], [block, (4,) + block, (4,) + block], 10**6,
        tra, active_levels, diffusivity, tracer_rows, got_a, got_b,
    )
    padded = (2, TALL + 16, LANES)
    short = (2, ROWS + 16, LANES)
    basis, flow, partial, col_patch, row_patch = call(
        surface_kernel,
        [(SOLVE_ITERS,) + short, (2 * ROWS, LANES), (lon * lat, LANES), block, (4 * STRIP, LANES)],
        [(3,) + padded, padded, padded, padded, (SOLVE_ITERS + 1,) + padded, (8,) + short, short],
        10**7,
        tall, strips, mean, got_a, got_b,
    )
    gathered = lax.all_to_all(partial, BOTH, 0, 0, tiled=True)
    velocity_out, surface = call(
        final_kernel, [(PLANES * ROWS, LANES), block], [short, (2,) + block], 10**6,
        gathered, basis, flow, star, active_levels, col_patch, row_patch,
    )
    return tracers_out.reshape(tracers.shape), velocity_out.reshape(velocity.shape), surface


def solution(mesh):
    placed = (
        P(None, None, "lat", "lon"),
        P(None, None, "lat", "lon"),
        P("lat", "lon"),
        P("lat", "lon"),
        P("lat", "lon"),
        P("lat", "lon"),
        P(None, "lat", "lon"),
    )
    return jax.shard_map(
        functools.partial(per_device, mesh.shape["lon"], mesh.shape["lat"]),
        mesh=mesh,
        in_specs=placed,
        out_specs=(P(None, None, "lat", "lon"), P(None, None, "lat", "lon"), P("lat", "lon")),
        check_vma=False,
    )
```

```python
import functools
import math

import jax
import jax.numpy as jnp
from jax import lax
from jax.experimental import pallas as pl
from jax.experimental.pallas import tpu as pltpu
from jax.sharding import PartitionSpec as P

SUBCYCLES = 8
SOLVE_ITERS = 4
LEVELS = 10
PLANES = 2 * LEVELS
ROWS = 64
LANES = 128
MARGIN = 24
TALL = ROWS + 2 * MARGIN
RIM = 32
SLOPE = 0.15
CENTRE = 5.0
RADIUS = 5.0
F32 = jnp.float32
BOTH = ("lon", "lat")

STRIP = 24
RIMS = 3 * STRIP
LAT_SEND = 3 * MARGIN + RIMS + MARGIN
LON_SEND = 2 * TALL + 2 * STRIP


def lane_ids(rows):
    return lax.broadcasted_iota(jnp.int32, (rows, LANES), 1)


def row_ids(rows):
    return lax.broadcasted_iota(jnp.int32, (rows, LANES), 0)


def turn(x, shift):
    return pltpu.roll(x, shift, 1)


def flip_lanes(x, bits=7):
    lanes = lane_ids(x.shape[0])
    for bit in range(bits):
        step = 1 << bit
        x = jnp.where((lanes & step) != 0, turn(x, step), turn(x, LANES - step))
    return x


def flip_rows(x):
    rows = x.shape[0]
    ids = row_ids(rows)
    for bit in range(3):
        step = 1 << bit
        x = jnp.where((ids & step) != 0, pltpu.roll(x, step, 0), pltpu.roll(x, rows - step, 0))
    return jnp.concatenate([x[r : r + 8] for r in range(rows - 8, -8, -8)], axis=0)


def odd(axis):
    return lax.rem(lax.axis_index(axis), 2) == 1


def at_fold():
    return lax.axis_index("lat") == lax.axis_size("lat") - 1


def shifted(x):
    rows = x.shape[0]
    return (turn(x, LANES - 1), turn(x, 1), pltpu.roll(x, rows - 1, 0), pltpu.roll(x, 1, 0))


def block_kernel(
    vel_far, tra_far, lev_far, visc_far, diff_far, depth_far, wind_far,
    star, mean, fields, cols, north, south, send_a, send_b,
    faces, face_levels, sums, turning, vel, tra, visc, diff, depth, wind, lev, done,
):
    pairs = ((lev_far, lev), (visc_far, visc), (vel_far, vel), (tra_far, tra), (wind_far, wind), (depth_far, depth), (diff_far, diff))
    copies = [pltpu.make_async_copy(far, near, done.at[n]) for n, (far, near) in enumerate(pairs)]
    for copy in copies:
        copy.start()
    for copy in copies[:2]:
        copy.wait()
    lanes = lane_ids(ROWS)
    ids = row_ids(ROWS)
    levels = lev[...].astype(F32)
    v = visc[...]
    inside = (lanes < LANES - 1, lanes > 0, ids < ROWS - 1, ids > 0)
    for n, (v_n, level_n) in enumerate(zip(shifted(v), shifted(levels))):
        faces[n] = 0.5 * (v + v_n)
        face_levels[n] = jnp.where(inside[n], jnp.minimum(levels, level_n), 0.0)
    row = (lax.axis_index("lat") * ROWS).astype(F32) + ids.astype(F32)
    turning[...] = 0.25 * jnp.sin(math.pi * ((row + 0.5) / (ROWS * lax.axis_size("lat")) - 0.5))
    sums[...] = jnp.zeros((2, ROWS, LANES), F32)
    acc = jnp.where((lanes >> 2) == 20, turn(levels, 82), 0.0)
    cols[...] = jnp.where((lanes >> 2) == 21, turn(v, 86), acc)
    for copy in copies[2:]:
        copy.wait()

    def level_step(k, carry):
        level = k.astype(F32)
        open_faces = [level < face_levels[n] for n in range(4)]
        wet = level < lev[...].astype(F32)
        weights = [jnp.where(o, faces[n], 0.0) for n, o in enumerate(open_faces)]
        values = [
            vel[pl.ds(pl.multiple_of((comp * LEVELS + k) * ROWS, ROWS), ROWS), :] for comp in range(2)
        ]
        packed = cols[...]
        for comp, x in enumerate(values):
            p = comp * LEVELS + k
            lap = jnp.zeros((ROWS, LANES), F32)
            for n, x_n in enumerate(shifted(x)):
                lap += jnp.where(open_faces[n], x_n - x, 0.0)
            second = jnp.zeros((ROWS, LANES), F32)
            for n, lap_n in enumerate(shifted(lap)):
                second += weights[n] * (lap_n - lap)
            rotated = values[1] if comp == 0 else -values[0]
            out = jnp.where(wet, x - second + turning[...] * rotated, 0.0)
            star[pl.ds(pl.multiple_of(p * ROWS, ROWS), ROWS), :] = out
            sums[comp] += out
            packed = jnp.where((lanes >> 2) == p, turn(x, 4 * p + 2), packed)
            t = tra[pl.ds(pl.multiple_of(p * ROWS, ROWS), ROWS), :]
            packed = jnp.where((lanes >> 1) == 44 + p, turn(t, lax.rem(89 + 2 * p, LANES)), packed)
        cols[...] = packed
        return carry

    lax.fori_loop(0, LEVELS, level_step, 0)
    ocean = levels > 0.0
    for comp in range(2):
        here = pl.ds(comp * ROWS, ROWS)
        column_mean = sums[comp] / jnp.maximum(levels, 1.0)
        mean[here, :] = column_mean
        fields[here, :] = column_mean + jnp.where(ocean, wind[here, :], 0.0)
    fields[pl.ds(2 * ROWS, ROWS), :] = jnp.where(ocean, depth[...], 0.0)
    for edge, step, out in ((ROWS - 1, -1, north), (0, 1, south)):
        out[...] = jnp.zeros((RIMS, LANES), F32)
        for d in range(2):
            r = edge + d * step
            out[pl.ds(d * STRIP, PLANES), :] = vel[pl.ds(r, PLANES, stride=ROWS), :]
            out[pl.ds(d * STRIP + 20, 1), :] = levels[r : r + 1]
            out[pl.ds(d * STRIP + 21, 1), :] = visc[pl.ds(r, 1), :]
        out[pl.ds(2 * STRIP, PLANES), :] = tra[pl.ds(edge, PLANES, stride=ROWS), :]
        out[pl.ds(2 * STRIP + 20, 1), :] = diff[pl.ds(edge, 1), :]
    lat_odd = odd("lat")

    def put(start, up, down):
        here = pl.ds(start, up.shape[0])
        send_a[here, :] = jnp.where(lat_odd, down, up)
        send_b[here, :] = jnp.where(lat_odd, up, down)

    for f in range(3):
        put(f * MARGIN, fields[pl.ds((f + 1) * ROWS - MARGIN, MARGIN), :], fields[pl.ds(f * ROWS, MARGIN), :])
    put(3 * MARGIN, north[...], south[...])
    put(3 * MARGIN + RIMS, cols[ROWS - MARGIN : ROWS, :], cols[0:MARGIN, :])

    @pl.when(at_fold())
    def _():
        for f in range(3):
            turned = flip_rows(flip_lanes(fields[pl.ds((f + 1) * ROWS - MARGIN, MARGIN), :]))
            send_b[pl.ds(f * MARGIN, MARGIN), :] = turned if f == 2 else -turned
        turned = flip_lanes(north[...])
        r = row_ids(RIMS)
        is_velocity = (r < PLANES) | ((r >= STRIP) & (r < STRIP + PLANES))
        send_b[pl.ds(3 * MARGIN, RIMS), :] = jnp.where(is_velocity, -turned, turned)
        turned = flip_rows(flip_lanes(cols[ROWS - MARGIN : ROWS, :], 2))
        send_b[pl.ds(3 * MARGIN + RIMS, MARGIN), :] = jnp.where(lane_ids(MARGIN) < 4 * PLANES, -turned, turned)


def widen_kernel(fields, cols, diff, north, south, recv_a, recv_b, tall, strips, tracer_rows, send_a, send_b, east, west):
    lat_odd = odd("lat")
    lon_odd = odd("lon")
    group = lane_ids(TALL) >> 5

    def received(start, count):
        here = pl.ds(start, count)
        got_a = recv_a[here, :]
        got_b = recv_b[here, :]
        return jnp.where(lat_odd, got_b, got_a), jnp.where(lat_odd, got_a, got_b)

    acc_east = jnp.zeros((TALL, LANES), F32)
    acc_west = jnp.zeros((TALL, LANES), F32)
    for f in range(4):
        from_north, from_south = received(f * MARGIN if f < 3 else 3 * MARGIN + RIMS, MARGIN)
        tall[pl.ds(f * TALL, MARGIN), :] = from_south
        tall[pl.ds(f * TALL + MARGIN, ROWS), :] = fields[pl.ds(f * ROWS, ROWS), :] if f < 3 else cols[...]
        tall[pl.ds(f * TALL + MARGIN + ROWS, MARGIN), :] = from_north
        if f < 3:
            x = tall[pl.ds(f * TALL, TALL), :]
            acc_east = jnp.where(group == f, turn(x, 32 * (f + 1)), acc_east)
            acc_west = jnp.where(group == f, turn(x, 32 * f), acc_west)
    for out, acc, shift in ((east, acc_east, 97), (west, acc_west, 96)):
        out[pl.ds(0, TALL), :] = acc
        out[pl.ds(MARGIN, ROWS), :] = jnp.where(lane_ids(ROWS) == 96, turn(diff[...], shift), acc[MARGIN : MARGIN + ROWS])
    rims = received(3 * MARGIN, RIMS)
    for s, (own, rim) in enumerate(((north, rims[0]), (south, rims[1]))):
        pieces = (rim[STRIP : 2 * STRIP], rim[0:STRIP], own[0:STRIP, :], own[STRIP : 2 * STRIP, :])
        acc_east = jnp.zeros((STRIP, LANES), F32)
        acc_west = jnp.zeros((STRIP, LANES), F32)
        for r, x in enumerate(pieces):
            strips[pl.ds((4 * s + r) * STRIP, STRIP), :] = x
            acc_east = jnp.where(group[0:STRIP] == r, turn(x, (32 * (r + 1)) % LANES), acc_east)
            acc_west = jnp.where(group[0:STRIP] == r, turn(x, 32 * r), acc_west)
        east[pl.ds(TALL + s * STRIP, STRIP), :] = acc_east
        west[pl.ds(TALL + s * STRIP, STRIP), :] = acc_west
        tracer_rows[pl.ds(2 * s * STRIP, STRIP), :] = rim[2 * STRIP : 3 * STRIP]
        tracer_rows[pl.ds((2 * s + 1) * STRIP, STRIP), :] = rim[0:STRIP]
    k = tall[pl.ds(3 * TALL, TALL), :]
    send_a[pl.ds(0, TALL), :] = k
    send_b[pl.ds(0, TALL), :] = k
    rest = pl.ds(TALL, TALL + 2 * STRIP)
    e, w = east[...], west[...]
    send_a[rest, :] = jnp.where(lon_odd, w, e)
    send_b[rest, :] = jnp.where(lon_odd, e, w)


def tracer_kernel(tra, lev, diff, tracer_rows, recv_a, recv_b, out, swap, faces, face_levels):
    is_odd = odd("lon")
    lanes = lane_ids(ROWS)
    ids = row_ids(ROWS)

    def received(start):
        here = pl.ds(start + MARGIN, ROWS)
        got_a = recv_a[here, :]
        got_b = recv_b[here, :]
        return jnp.where(is_odd, got_b, got_a), jnp.where(is_odd, got_a, got_b)

    east_cols, west_cols = received(0)
    east_rest, west_rest = received(TALL)
    swap[...] = jnp.where((lanes & 1) == 0, turn(east_cols, LANES - 1), turn(west_cols, 1))

    def sides(x, halo, row):
        east, west, north, south = shifted(x)
        return (
            jnp.where(lanes == LANES - 1, halo, east),
            jnp.where(lanes == 0, halo, west),
            jnp.where(ids == ROWS - 1, tracer_rows[pl.ds(row, 1), :], north),
            jnp.where(ids == 0, tracer_rows[pl.ds(row + 2 * STRIP, 1), :], south),
        )

    level = lev[...].astype(F32)
    level_halo = jnp.where(lanes == LANES - 1, turn(east_cols, 45), turn(west_cols, 47))
    d = diff[...]
    d_halo = jnp.where(lanes == LANES - 1, turn(east_rest, 31), turn(west_rest, 32))
    for n, other in enumerate(sides(level, level_halo, STRIP + 20)):
        face_levels[n] = jnp.minimum(level, other)
    for n, other in enumerate(sides(d, d_halo, 20)):
        faces[n] = 0.5 * (d + other)

    def level_step(k, carry):
        weights = [jnp.where(k.astype(F32) < face_levels[n], faces[n], 0.0) for n in range(4)]
        for comp in range(2):
            p = comp * LEVELS + k
            here = pl.ds(pl.multiple_of(p * ROWS, ROWS), ROWS)
            x = tra[here, :]
            around = sides(x, turn(swap[...], 39 - 2 * p), p)
            total = weights[0] * (around[0] - x)
            for n in range(1, 4):
                total += weights[n] * (around[n] - x)
            out[here, :] = x + total
        return carry

    lax.fori_loop(0, LEVELS, level_step, 0)


def column_strip(strip):
    rows = strip.shape[0]
    lanes = lane_ids(rows)
    ids = row_ids(rows)
    phase = lanes & 3
    group = lanes >> 2

    def spread(which):
        x = jnp.where(group == which, strip, 0.0)
        for step in (4, 8, 16, 32, 64):
            x = x + turn(x, step)
        return x

    levels = spread(20)
    v = spread(21)
    number = jnp.where(group >= LEVELS, group - LEVELS, group).astype(F32)
    wet = jnp.where((number < levels) & (group < PLANES), 1.0, 0.0)
    x = jnp.where(group < PLANES, strip, 0.0)
    open_e = wet * turn(wet, LANES - 1)
    wet_n = pltpu.roll(wet, rows - 1, 0)
    open_n = wet * wet_n
    flux_e = open_e * (turn(x, LANES - 1) - x)
    flux_n = open_n * (pltpu.roll(x, rows - 1, 0) - x)
    lap = flux_e - turn(flux_e, 1) + flux_n - pltpu.roll(flux_n, 1, 0)
    seam = jnp.where(phase == 1, flux_e, 0.0)
    added = seam - turn(seam, 1)
    base = jnp.where(phase == 1, lap, added)
    other = jnp.where(phase == 1, turn(lap, LANES - 1), turn(added, LANES - 1))
    face = 0.5 * (v + turn(v, LANES - 1)) * open_e
    flux_e = jnp.where(phase == 3, 0.0, face * (other - base))
    in_block = (ids != MARGIN - 1) & (ids != MARGIN + ROWS - 1)
    face = jnp.where(in_block, 0.5 * (v + pltpu.roll(v, rows - 1, 0)) * open_n, 0.0)
    flux_n = face * (pltpu.roll(added, rows - 1, 0) - added)
    second = flux_e - turn(flux_e, 1) + flux_n - pltpu.roll(flux_n, 1, 0)
    return wet * second, levels


def gram_pairs():
    return [(i, j) for i in range(SOLVE_ITERS) for j in range(i, SOLVE_ITERS + 1)]


def surface_kernel(
    tall, strips, mean, recv_a, recv_b,
    basis_out, flow, partial, col_patch, row_patch,
    state, height, flux, slope, basis, weights, diagonal,
):
    is_odd = odd("lon")
    rows = pl.ds(8, TALL)
    lanes = lane_ids(TALL)

    def received(start, count):
        here = pl.ds(start, count)
        got_a = recv_a[here, :]
        got_b = recv_b[here, :]
        return jnp.where(is_odd, got_b, got_a), jnp.where(is_odd, got_a, got_b)

    def ghost(east, west, f):
        return jnp.where(
            lane_ids(east.shape[0]) < 64, turn(east, (LANES - 32 * f) % LANES), turn(west, (96 - 32 * f) % LANES)
        )

    from_east, from_west = received(TALL, TALL)
    for f in range(3):
        state[f, 0, rows, :] = tall[pl.ds(f * TALL, TALL), :]
        state[f, 1, rows, :] = ghost(from_east, from_west, f)
    last = lanes == LANES - 1
    first = lanes == 0

    def lane_sides(a, b):
        n = a.shape[0]
        ea, eb, wa, wb = turn(a, LANES - 1), turn(b, LANES - 1), turn(a, 1), turn(b, 1)
        return (
            (jnp.where(last[0:n], eb, ea), jnp.where(last[0:n], ea, eb)),
            (jnp.where(first[0:n], wb, wa), jnp.where(first[0:n], wa, wb)),
        )

    own = tall[pl.ds(3 * TALL, TALL), :]
    phase = lanes & 3
    from_east, from_west = received(0, TALL)
    patches = []
    for side, strip in enumerate((jnp.where(phase < 2, own, from_east), jnp.where(phase < 2, from_west, own))):
        change, levels = column_strip(strip)
        patches.append(change)
        for comp in range(2):
            total = jnp.where((lanes >= 40 * comp) & (lanes < 40 * comp + 40), change, 0.0)
            for step in (4, 8, 16, 32, 64):
                total = total + turn(total, step)
            total = turn(total / jnp.maximum(levels, 1.0), 2)
            for half in range(2):
                here = lanes >= LANES - 2 if half == side else lanes < 2
                state[comp, half, rows, :] = state[comp, half, rows, :] - jnp.where(here, total, 0.0)
    patch = jnp.where(phase < 2, patches[0], patches[1])
    col_patch[...] = patch[MARGIN : MARGIN + ROWS]
    number = lax.broadcasted_iota(jnp.int32, (STRIP, LANES), 0)
    level_of_row = jnp.where(number >= LEVELS, number - LEVELS, number).astype(F32)
    is_plane = number < PLANES
    not_last = lane_ids(STRIP) < LANES - 1
    for s in range(2):
        from_east, from_west = received(2 * TALL + s * STRIP, STRIP)
        x, wet, v, deep = [], [], [], []
        for r in range(4):
            centre = strips[pl.ds((4 * s + r) * STRIP, STRIP), :]
            both = (centre, ghost(from_east, from_west, r))
            deep.append([b[20:21] for b in both])
            v.append([jnp.broadcast_to(b[21:22], (STRIP, LANES)) for b in both])
            wet.append([jnp.where(is_plane & (level_of_row < b[20:21]), 1.0, 0.0) for b in both])
            x.append([jnp.where(is_plane, b, 0.0) for b in both])
        half_range = range(2)
        lap = {}
        added = {}
        seam = [wet[1][h] * wet[2][h] * (x[2][h] - x[1][h]) for h in half_range]
        added[1] = seam
        added[2] = [-t for t in seam]
        along = {}
        for r in (1, 2):
            x_e = lane_sides(*x[r])[0]
            wet_e = lane_sides(*wet[r])[0]
            v_e = lane_sides(*v[r])[0]
            added_e = lane_sides(*added[r])[0]
            open_e = [wet[r][h] * wet_e[h] for h in half_range]
            edge = [open_e[h] * (x_e[h] - x[r][h]) for h in half_range]
            edge_w = lane_sides(*edge)[1]
            lap[r] = [
                edge[h]
                - edge_w[h]
                + wet[r][h] * (wet[r + 1][h] * (x[r + 1][h] - x[r][h]) + wet[r - 1][h] * (x[r - 1][h] - x[r][h]))
                for h in half_range
            ]
            edge = [
                jnp.where(not_last, 0.5 * (v[r][h] + v_e[h]) * open_e[h] * (added_e[h] - added[r][h]), 0.0)
                for h in half_range
            ]
            edge_w = lane_sides(*edge)[1]
            along[r] = [edge[h] - edge_w[h] for h in half_range]
        for h in half_range:
            face = [0.5 * (v[r][h] + v[r + 1][h]) * wet[r][h] * wet[r + 1][h] for r in range(3)]
            across = (face[0] * added[1][h], face[1] * (lap[2][h] - lap[1][h]), -face[2] * added[2][h])
            second = (
                across[0],
                across[1] - across[0] + along[1][h],
                across[2] - across[1] + along[2][h],
                -across[2],
            )
            for r in range(4):
                change = wet[r][h] * second[r]
                if h == 0 and r >= 2:
                    row_patch[pl.ds((2 * s + r - 2) * STRIP, STRIP), :] = change
                where = 8 + MARGIN + ((ROWS + 1 - r) if s == 0 else (r - 2))
                for comp in range(2):
                    mine = (number >= comp * LEVELS) & (number < (comp + 1) * LEVELS)
                    total = jnp.sum(jnp.where(mine, change, 0.0), axis=0, keepdims=True)
                    total = total / jnp.maximum(deep[r][h], 1.0)
                    state[comp, h, where : where + 1, :] = state[comp, h, where : where + 1, :] - total
    for comp in range(2):
        here = pl.ds(comp * ROWS, ROWS)
        started = state[comp, 0, pl.ds(8 + MARGIN, ROWS), :] - tall[pl.ds(comp * TALL + MARGIN, ROWS), :]
        flow[here, :] = -(started + mean[here, :])

    for half in range(2):
        slope[half, rows, :] = jnp.where(state[2, half, rows, :] > 0.0, SLOPE, 0.0)
        height[half, rows, :] = jnp.zeros((TALL, LANES), F32)

    halves = range(2)

    def subcycle(step, carry):
        for tile in range(8, 8 + TALL, 8):
            here, above, below = (pl.ds(tile + off, 8) for off in (0, 1, -1))
            east, west = lane_sides(*(state[2, h, here, :] * state[0, h, here, :] for h in halves))
            for h in halves:
                north = state[2, h, above, :] * state[1, h, above, :]
                south = state[2, h, below, :] * state[1, h, below, :]
                divergence = (east[h] - west[h]) + (north - south)
                height[h, here, :] = height[h, here, :] - slope[h, here, :] * divergence
        for tile in range(8, 8 + TALL, 8):
            here, above, below = (pl.ds(tile + off, 8) for off in (0, 1, -1))
            east, west = lane_sides(height[0, here, :], height[1, here, :])
            for h in halves:
                factor = slope[h, here, :]
                state[0, h, here, :] = state[0, h, here, :] - factor * (east[h] - west[h])
                state[1, h, here, :] = state[1, h, here, :] - factor * (height[h, above, :] - height[h, below, :])
        return carry

    lax.fori_loop(0, SUBCYCLES, subcycle, 0)
    for comp in range(2):
        here = pl.ds(comp * ROWS, ROWS)
        flow[here, :] = flow[here, :] + state[comp, 0, pl.ds(8 + MARGIN, ROWS), :]
    scale = 2.0 / RADIUS
    short = ROWS + 16
    base = MARGIN

    tiles = range(0, short, 8)

    def nine(read, tile):
        out = [[], []]
        for off in (0, 1, -1):
            a, b = (read(h, pl.ds(base + tile + off, 8)) for h in halves)
            east, west = lane_sides(a, b)
            for h, centre in enumerate((a, b)):
                out[h] += [centre, east[h], west[h]]
        return out

    for tile in tiles:
        here = pl.ds(tile, 8)
        around = nine(lambda h, where: state[2, h, where, :], tile)
        for h in halves:
            d = around[h][0]
            wet = d > 0.0
            total = jnp.where(wet, 0.05, 1.0)
            for n in range(1, 9):
                factor = 0.5 if n in (1, 2, 3, 6) else 0.25
                w = jnp.where(wet & (around[h][n] > 0.0), factor * (d + around[h][n]), 0.0)
                weights[n - 1, h, here, :] = scale * w
                total += w
            diagonal[h, here, :] = scale * (total - CENTRE)
            basis[0, h, pl.ds(base + tile, 8), :] = height[h, pl.ds(base + tile, 8), :]

    def applied(source, tile):
        around = nine(lambda h, where: basis[source, h, where, :], tile)
        out = []
        for h in halves:
            here = pl.ds(tile, 8)
            total = diagonal[h, here, :] * around[h][0]
            for n in range(1, 9):
                total -= weights[n - 1, h, here, :] * around[h][n]
            out.append(total)
        return out

    for tile in tiles:
        for h, x in enumerate(applied(0, tile)):
            basis[1, h, pl.ds(base + tile, 8), :] = 0.5 * x

    def next_basis(k, carry):
        for tile in tiles:
            here = pl.ds(base + tile, 8)
            for h, x in enumerate(applied(k, tile)):
                basis[k + 1, h, here, :] = x - basis[k - 1, h, here, :]
        return carry

    lax.fori_loop(1, SOLVE_ITERS, next_basis, 0)
    lane = lane_ids(1)
    row = jnp.zeros((1, LANES), F32)
    mine = pl.ds(8 + MARGIN, ROWS)
    for n, (i, j) in enumerate(gram_pairs()):
        product = basis[i, 0, mine, :] * basis[j, 0, mine, :]
        row = jnp.where(lane == n, jnp.sum(jnp.sum(product, axis=0, keepdims=True), axis=1, keepdims=True), row)
    partial[...] = jnp.broadcast_to(row, partial.shape)
    for i in range(SOLVE_ITERS):
        for half in range(2):
            basis_out[i, half] = basis[i, half, pl.ds(base, short), :]


def solve_coefficients(gram):
    half = 0.5 * RADIUS

    def image_of(d):
        out = [None] * (len(d) + 1)

        def add(n, term):
            out[n] = term if out[n] is None else out[n] + term

        for j, value in enumerate(d):
            add(j, CENTRE * value)
            if j == 0:
                add(1, RADIUS * value)
            else:
                add(j + 1, half * value)
                add(j - 1, half * value)
        return out

    def inner(a, b):
        total = None
        for i, x in enumerate(a):
            for j, y in enumerate(b):
                term = x * y * gram[(min(i, j), max(i, j))]
                total = term if total is None else total + term
        return total

    one = jnp.ones((8, LANES), F32)
    residual, direction, surface = [one], [one], [0.0 * one]
    norm = gram[(0, 0)]
    for iteration in range(SOLVE_ITERS):
        image = image_of(direction)
        step = norm / inner(direction, image)
        surface = [a + step * b for a, b in zip(surface, direction)] + [0.0 * one]
        if iteration == SOLVE_ITERS - 1:
            break
        residual = [(residual[n] if n < len(residual) else 0.0) - step * x for n, x in enumerate(image)]
        fresh = inner(residual, residual)
        ratio = fresh / norm
        direction = [x + (ratio * direction[n] if n < len(direction) else 0.0) for n, x in enumerate(residual)]
        norm = fresh
    return surface[:SOLVE_ITERS]


def final_kernel(gathered, basis, flow, star, lev, velocity_out, surface_out, pad, change):
    sums = jnp.sum(gathered[...], axis=0, keepdims=True)
    lane = lane_ids(1)
    gram = {}
    for n, pair in enumerate(gram_pairs()):
        value = jnp.sum(jnp.where(lane == n, sums, 0.0), axis=1, keepdims=True)
        gram[pair] = jnp.broadcast_to(value, (8, LANES))
    coefficients = [c[0:1] for c in solve_coefficients(gram)]
    for half in range(2):
        total = coefficients[0] * basis[0, half]
        for i in range(1, SOLVE_ITERS):
            total += coefficients[i] * basis[i, half]
        pad[half] = total
    mine = pl.ds(8, ROWS)
    centre = pad[0, mine, :]
    ghost = pad[1, mine, :]
    surface_out[...] = centre
    lanes = lane_ids(ROWS)
    east = jnp.where(lanes == LANES - 1, turn(ghost, LANES - 1), turn(centre, LANES - 1))
    west = jnp.where(lanes == 0, turn(ghost, 1), turn(centre, 1))
    levels = lev[...]
    slope = jnp.where(levels > 0, SLOPE, 0.0)
    slopes = (east - west, pad[0, pl.ds(9, ROWS), :] - pad[0, pl.ds(7, ROWS), :])
    for comp in range(2):
        here = pl.ds(comp * ROWS, ROWS)
        change[comp] = flow[here, :] - slope * slopes[comp]


    def level_step(k, carry):
        wet = k < levels
        for comp in range(2):
            here = pl.ds(pl.multiple_of((comp * LEVELS + k) * ROWS, ROWS), ROWS)
            velocity_out[here, :] = star[here, :] + jnp.where(wet, change[comp], 0.0)
        return carry

    lax.fori_loop(0, LEVELS, level_step, 0)


def patch_kernel(star, col_patch, row_patch, out):
    lanes = lane_ids(ROWS)
    rims = (lanes < 2) | (lanes >= LANES - 2)
    ids = row_ids(8)

    def plane(p, carry):
        here = pl.ds(pl.multiple_of(p * ROWS, ROWS), ROWS)
        out[here, :] = star[here, :] - jnp.where(rims, turn(col_patch[...], 126 - 4 * p), 0.0)
        for first, pieces in ((ROWS - 8, ((7, 0), (6, 1))), (0, ((0, 2), (1, 3)))):
            here = pl.ds(pl.multiple_of(p * ROWS + first, 8), 8)
            x = out[here, :]
            for row, n in pieces:
                x = x - jnp.where(ids == row, row_patch[pl.ds(n * STRIP + p, 1), :], 0.0)
            out[here, :] = x
        return carry

    lax.fori_loop(0, PLANES, plane, 0)


def call(kernel, shapes, scratch, flops, *args, far=False):
    out = tuple(jax.ShapeDtypeStruct(s, F32) for s in shapes)
    moved = sum(4 * math.prod(a.shape) for a in args) + sum(4 * math.prod(s) for s in shapes)
    if far:
        args = [pltpu.with_memory_space_constraint(a, pltpu.HBM) for a in args]
    return pl.pallas_call(
        kernel,
        out_shape=out,
        in_specs=[pl.BlockSpec(memory_space=pltpu.HBM if far else pltpu.VMEM)] * len(args),
        scratch_shapes=[pltpu.VMEM(s, F32) if isinstance(s, tuple) else s for s in scratch],
        compiler_params=pltpu.CompilerParams(vmem_limit_bytes=32 * 1024 * 1024),
        cost_estimate=pl.CostEstimate(flops=flops, bytes_accessed=moved, transcendentals=0),
    )(*args)


def pair_tables(lon, lat):
    def index(i, j):
        return j * lat + i

    lat_a, lat_b, lon_a, lon_b = [], [], [], []
    for j in range(lon):
        for i in range(lat):
            lat_a.append((index(i, j), index(i ^ 1, j)))
            if i == lat - 1:
                lat_b.append((index(i, j), index(i, lon - 1 - j)))
            elif i > 0:
                lat_b.append((index(i, j), index(i + 1 if i % 2 else i - 1, j)))
            lon_a.append((index(i, j), index(i, j ^ 1)))
            lon_b.append((index(i, j), index(i, (j + 1 if j % 2 else j - 1) % lon)))
    return lat_a, lat_b, lon_a, lon_b


def per_device(lon, lat, tracers, velocity, active_levels, diffusivity, viscosity, ocean_depth, wind_forcing):
    lat_a, lat_b, lon_a, lon_b = pair_tables(lon, lat)

    def swap(x, pairs):
        return lax.ppermute(x, BOTH, pairs)

    block = (ROWS, LANES)
    tra = tracers.reshape(PLANES * ROWS, LANES)
    vel = velocity.reshape(PLANES * ROWS, LANES)
    wind = wind_forcing.reshape(2 * ROWS, LANES)
    rim = (RIMS, LANES)
    star, mean, fields, cols, north, south, send_a, send_b = call(
        block_kernel,
        [(PLANES * ROWS, LANES), (2 * ROWS, LANES), (3 * ROWS, LANES), block, rim, rim, (LAT_SEND, LANES), (LAT_SEND, LANES)],
        [(4,) + block, (4,) + block, (2,) + block, block, vel.shape, vel.shape, block, block, block, wind.shape,
         pltpu.VMEM(block, jnp.int32), pltpu.SemaphoreType.DMA((7,))],
        10**7,
        vel, tra, active_levels, viscosity, diffusivity, ocean_depth, wind,
        far=True,
    )
    got_b = swap(send_b, lat_b)
    got_a = swap(send_a, lat_a)
    tall, strips, tracer_rows, send_a, send_b = call(
        widen_kernel,
        [(4 * TALL, LANES), (8 * STRIP, LANES), (4 * STRIP, LANES), (LON_SEND, LANES), (LON_SEND, LANES)],
        [(TALL + 2 * STRIP, LANES)] * 2,
        10**6,
        fields, cols, diffusivity, north, south, got_a, got_b,
    )
    got_b = swap(send_b, lon_b)
    got_a = swap(send_a, lon_a)
    (tracers_out,) = call(
        tracer_kernel, [(PLANES * ROWS, LANES)], [block, (4,) + block, (4,) + block], 10**6,
        tra, active_levels, diffusivity, tracer_rows, got_a, got_b,
    )
    padded = (2, TALL + 16, LANES)
    short = (2, ROWS + 16, LANES)
    basis, flow, partial, col_patch, row_patch = call(
        surface_kernel,
        [(SOLVE_ITERS,) + short, (2 * ROWS, LANES), (lon * lat, LANES), block, (4 * STRIP, LANES)],
        [(3,) + padded, padded, padded, padded, (SOLVE_ITERS + 1,) + padded, (8,) + short, short],
        10**7,
        tall, strips, mean, got_a, got_b,
    )
    gathered = lax.all_to_all(partial, BOTH, 0, 0, tiled=True)
    (star,) = call(patch_kernel, [(PLANES * ROWS, LANES)], [], 10**6, star, col_patch, row_patch)
    velocity_out, surface = call(
        final_kernel, [(PLANES * ROWS, LANES), block], [short, (2,) + block], 10**6,
        gathered, basis, flow, star, active_levels,
    )
    return tracers_out.reshape(tracers.shape), velocity_out.reshape(velocity.shape), surface


def solution(mesh):
    placed = (
        P(None, None, "lat", "lon"),
        P(None, None, "lat", "lon"),
        P("lat", "lon"),
        P("lat", "lon"),
        P("lat", "lon"),
        P("lat", "lon"),
        P(None, "lat", "lon"),
    )
    return jax.shard_map(
        functools.partial(per_device, mesh.shape["lon"], mesh.shape["lat"]),
        mesh=mesh,
        in_specs=placed,
        out_specs=(P(None, None, "lat", "lon"), P(None, None, "lat", "lon"), P("lat", "lon")),
        check_vma=False,
    )
```

```python
import functools
import math

import jax
import jax.numpy as jnp
from jax import lax
from jax.experimental import pallas as pl
from jax.experimental.pallas import tpu as pltpu
from jax.sharding import PartitionSpec as P

SUBCYCLES = 8
SOLVE_ITERS = 4
LEVELS = 10
PLANES = 2 * LEVELS
ROWS = 64
LANES = 128
MARGIN = 24
TALL = ROWS + 2 * MARGIN
RIM = 32
SLOPE = 0.15
CENTRE = 5.0
RADIUS = 5.0
F32 = jnp.float32
BOTH = ("lon", "lat")

STRIP = 24
RIMS = 3 * STRIP
LAT_SEND = 3 * MARGIN + RIMS + MARGIN
LON_SEND = 2 * TALL + 2 * STRIP


def lane_ids(rows):
    return lax.broadcasted_iota(jnp.int32, (rows, LANES), 1)


def row_ids(rows):
    return lax.broadcasted_iota(jnp.int32, (rows, LANES), 0)


def turn(x, shift):
    return pltpu.roll(x, shift, 1)


def pick(x, index):
    return jnp.take_along_axis(x, index, axis=1)


def flip_lanes(x, mask=LANES - 1):
    return pick(x, lane_ids(x.shape[0]) ^ mask)


def flip_rows(x):
    rows = x.shape[0]
    ids = row_ids(rows)
    for bit in range(3):
        step = 1 << bit
        x = jnp.where((ids & step) != 0, pltpu.roll(x, step, 0), pltpu.roll(x, rows - step, 0))
    return jnp.concatenate([x[r : r + 8] for r in range(rows - 8, -8, -8)], axis=0)


def odd(axis):
    return lax.rem(lax.axis_index(axis), 2) == 1


def at_fold():
    return lax.axis_index("lat") == lax.axis_size("lat") - 1


def shifted(x):
    rows = x.shape[0]
    return (turn(x, LANES - 1), turn(x, 1), pltpu.roll(x, rows - 1, 0), pltpu.roll(x, 1, 0))


def block_kernel(
    vel_far, tra_far, lev_far, visc_far, diff_far, depth_far, wind_far,
    star, mean, fields, cols, north, south, send_a, send_b,
    faces, face_levels, sums, turning, vel, tra, visc, diff, depth, wind, levels_kept, lap_pad, lev, done,
):
    pairs = ((lev_far, lev), (visc_far, visc), (vel_far, vel), (tra_far, tra), (wind_far, wind), (depth_far, depth), (diff_far, diff))
    copies = [
        pltpu.make_async_copy(far, near.at[pl.ds(8, PLANES * ROWS)] if near is vel else near, done.at[n])
        for n, (far, near) in enumerate(pairs)
    ]
    for copy in copies:
        copy.start()
    for copy in copies[:2]:
        copy.wait()
    lanes = lane_ids(ROWS)
    ids = row_ids(ROWS)
    levels = lev[...].astype(F32)
    v = visc[...]
    inside = (lanes < LANES - 1, lanes > 0, ids < ROWS - 1, ids > 0)
    for n, (v_n, level_n) in enumerate(zip(shifted(v), shifted(levels))):
        faces[n] = 0.5 * (v + v_n)
        face_levels[n] = jnp.where(inside[n], jnp.minimum(levels, level_n), 0.0)
    row = (lax.axis_index("lat") * ROWS).astype(F32) + ids.astype(F32)
    turning[...] = 0.25 * jnp.sin(math.pi * ((row + 0.5) / (ROWS * lax.axis_size("lat")) - 0.5))
    sums[...] = jnp.zeros((2, ROWS, LANES), F32)
    levels_kept[...] = levels
    for comp in range(2):
        lap_pad[comp, 0:8, :] = jnp.zeros((8, LANES), F32)
        lap_pad[comp, ROWS + 8 : ROWS + 16, :] = jnp.zeros((8, LANES), F32)
    vel[0:8, :] = jnp.zeros((8, LANES), F32)
    vel[PLANES * ROWS + 8 : PLANES * ROWS + 16, :] = jnp.zeros((8, LANES), F32)
    acc = jnp.where((lanes >> 2) == 20, turn(levels, 82), 0.0)
    cols[...] = jnp.where((lanes >> 2) == 21, turn(v, 86), acc)
    copies[2].wait()

    def level_step(k, carry):
        level = k.astype(F32)
        open_faces = [level < face_levels[n] for n in range(4)]
        wet = level < levels_kept[...]
        weights = [jnp.where(o, faces[n], 0.0) for n, o in enumerate(open_faces)]
        starts = [8 + pl.multiple_of((comp * LEVELS + k) * ROWS, ROWS) for comp in range(2)]
        values = [vel[pl.ds(s, ROWS), :] for s in starts]
        packed = cols[...]
        for comp, x in enumerate(values):
            p = comp * LEVELS + k
            around = (turn(x, LANES - 1), turn(x, 1), vel[pl.ds(starts[comp] + 1, ROWS), :], vel[pl.ds(starts[comp] - 1, ROWS), :])
            lap = jnp.where(open_faces[0], around[0] - x, 0.0)
            for n in range(1, 4):
                lap += jnp.where(open_faces[n], around[n] - x, 0.0)
            lap_pad[comp, pl.ds(8, ROWS), :] = lap
            around = (turn(lap, LANES - 1), turn(lap, 1), lap_pad[comp, pl.ds(9, ROWS), :], lap_pad[comp, pl.ds(7, ROWS), :])
            second = weights[0] * (around[0] - lap)
            for n in range(1, 4):
                second += weights[n] * (around[n] - lap)
            rotated = values[1] if comp == 0 else -values[0]
            out = jnp.where(wet, x - second + turning[...] * rotated, 0.0)
            star[pl.ds(pl.multiple_of(p * ROWS, ROWS), ROWS), :] = out
            sums[comp] += out
            packed = jnp.where((lanes >> 2) == p, turn(x, 4 * p + 2), packed)
        cols[...] = packed
        return carry

    lax.fori_loop(0, LEVELS, level_step, 0, unroll=2)
    for copy in copies[3:]:
        copy.wait()

    def tracer_step(p, acc):
        t = tra[pl.ds(pl.multiple_of(p * ROWS, ROWS), ROWS), :]
        return jnp.where((lanes >> 1) == 44 + p, turn(t, lax.rem(89 + 2 * p, LANES)), acc)

    cols[...] = lax.fori_loop(0, PLANES, tracer_step, cols[...], unroll=True)
    ocean = levels > 0.0
    for comp in range(2):
        here = pl.ds(comp * ROWS, ROWS)
        column_mean = sums[comp] / jnp.maximum(levels, 1.0)
        mean[here, :] = column_mean
        fields[here, :] = column_mean + jnp.where(ocean, wind[here, :], 0.0)
    fields[pl.ds(2 * ROWS, ROWS), :] = jnp.where(ocean, depth[...], 0.0)
    for edge, step, out in ((ROWS - 1, -1, north), (0, 1, south)):
        out[...] = jnp.zeros((RIMS, LANES), F32)
        for d in range(2):
            r = edge + d * step
            out[pl.ds(d * STRIP, PLANES), :] = vel[pl.ds(8 + r, PLANES, stride=ROWS), :]
            out[pl.ds(d * STRIP + 20, 1), :] = levels[r : r + 1]
            out[pl.ds(d * STRIP + 21, 1), :] = visc[pl.ds(r, 1), :]
        out[pl.ds(2 * STRIP, PLANES), :] = tra[pl.ds(edge, PLANES, stride=ROWS), :]
        out[pl.ds(2 * STRIP + 20, 1), :] = diff[pl.ds(edge, 1), :]
    lat_odd = odd("lat")

    def put(start, up, down):
        here = pl.ds(start, up.shape[0])
        send_a[here, :] = jnp.where(lat_odd, down, up)
        send_b[here, :] = jnp.where(lat_odd, up, down)

    for f in range(3):
        put(f * MARGIN, fields[pl.ds((f + 1) * ROWS - MARGIN, MARGIN), :], fields[pl.ds(f * ROWS, MARGIN), :])
    put(3 * MARGIN, north[...], south[...])
    put(3 * MARGIN + RIMS, cols[ROWS - MARGIN : ROWS, :], cols[0:MARGIN, :])

    @pl.when(at_fold())
    def _():
        for f in range(3):
            turned = flip_rows(flip_lanes(fields[pl.ds((f + 1) * ROWS - MARGIN, MARGIN), :]))
            send_b[pl.ds(f * MARGIN, MARGIN), :] = turned if f == 2 else -turned
        turned = flip_lanes(north[...])
        r = row_ids(RIMS)
        is_velocity = (r < PLANES) | ((r >= STRIP) & (r < STRIP + PLANES))
        send_b[pl.ds(3 * MARGIN, RIMS), :] = jnp.where(is_velocity, -turned, turned)
        turned = flip_rows(flip_lanes(cols[ROWS - MARGIN : ROWS, :], 3))
        send_b[pl.ds(3 * MARGIN + RIMS, MARGIN), :] = jnp.where(lane_ids(MARGIN) < 4 * PLANES, -turned, turned)


def widen_kernel(fields, cols, diff, north, south, recv_b, recv_a, tall, strips, tracer_rows, send_a, send_b, east, west):
    lat_odd = odd("lat")
    lon_odd = odd("lon")
    group = lane_ids(TALL) >> 5

    def received(start, count):
        here = pl.ds(start, count)
        got_a = recv_a[here, :]
        got_b = recv_b[here, :]
        return jnp.where(lat_odd, got_b, got_a), jnp.where(lat_odd, got_a, got_b)

    acc_east = jnp.zeros((TALL, LANES), F32)
    acc_west = jnp.zeros((TALL, LANES), F32)
    for f in range(4):
        from_north, from_south = received(f * MARGIN if f < 3 else 3 * MARGIN + RIMS, MARGIN)
        tall[pl.ds(f * TALL, MARGIN), :] = from_south
        tall[pl.ds(f * TALL + MARGIN, ROWS), :] = fields[pl.ds(f * ROWS, ROWS), :] if f < 3 else cols[...]
        tall[pl.ds(f * TALL + MARGIN + ROWS, MARGIN), :] = from_north
        if f < 3:
            x = tall[pl.ds(f * TALL, TALL), :]
            acc_east = jnp.where(group == f, turn(x, 32 * (f + 1)), acc_east)
            acc_west = jnp.where(group == f, turn(x, 32 * f), acc_west)
    for out, acc, shift in ((east, acc_east, 97), (west, acc_west, 96)):
        out[pl.ds(0, TALL), :] = acc
        out[pl.ds(MARGIN, ROWS), :] = jnp.where(lane_ids(ROWS) == 96, turn(diff[...], shift), acc[MARGIN : MARGIN + ROWS])
    rims = received(3 * MARGIN, RIMS)
    for s, (own, rim) in enumerate(((north, rims[0]), (south, rims[1]))):
        pieces = (rim[STRIP : 2 * STRIP], rim[0:STRIP], own[0:STRIP, :], own[STRIP : 2 * STRIP, :])
        acc_east = jnp.zeros((STRIP, LANES), F32)
        acc_west = jnp.zeros((STRIP, LANES), F32)
        for r, x in enumerate(pieces):
            strips[pl.ds((4 * s + r) * STRIP, STRIP), :] = x
            acc_east = jnp.where(group[0:STRIP] == r, turn(x, (32 * (r + 1)) % LANES), acc_east)
            acc_west = jnp.where(group[0:STRIP] == r, turn(x, 32 * r), acc_west)
        east[pl.ds(TALL + s * STRIP, STRIP), :] = acc_east
        west[pl.ds(TALL + s * STRIP, STRIP), :] = acc_west
        tracer_rows[pl.ds(2 * s * STRIP, STRIP), :] = rim[2 * STRIP : 3 * STRIP]
        tracer_rows[pl.ds((2 * s + 1) * STRIP, STRIP), :] = rim[0:STRIP]
    k = tall[pl.ds(3 * TALL, TALL), :]
    send_a[pl.ds(0, TALL), :] = k
    send_b[pl.ds(0, TALL), :] = k
    rest = pl.ds(TALL, TALL + 2 * STRIP)
    e, w = east[...], west[...]
    send_a[rest, :] = jnp.where(lon_odd, w, e)
    send_b[rest, :] = jnp.where(lon_odd, e, w)


def tracer_kernel(tra, lev, diff, tracer_rows, recv_b, recv_a, out, swap, faces, face_levels):
    is_odd = odd("lon")
    lanes = lane_ids(ROWS)
    ids = row_ids(ROWS)

    def received(start):
        here = pl.ds(start + MARGIN, ROWS)
        got_a = recv_a[here, :]
        got_b = recv_b[here, :]
        return jnp.where(is_odd, got_b, got_a), jnp.where(is_odd, got_a, got_b)

    east_cols, west_cols = received(0)
    east_rest, west_rest = received(TALL)
    swap[...] = jnp.where((lanes & 1) == 0, turn(east_cols, LANES - 1), turn(west_cols, 1))

    def sides(x, halo, row):
        east, west, north, south = shifted(x)
        return (
            jnp.where(lanes == LANES - 1, halo, east),
            jnp.where(lanes == 0, halo, west),
            jnp.where(ids == ROWS - 1, tracer_rows[pl.ds(row, 1), :], north),
            jnp.where(ids == 0, tracer_rows[pl.ds(row + 2 * STRIP, 1), :], south),
        )

    level = lev[...].astype(F32)
    level_halo = jnp.where(lanes == LANES - 1, turn(east_cols, 45), turn(west_cols, 47))
    d = diff[...]
    d_halo = jnp.where(lanes == LANES - 1, turn(east_rest, 31), turn(west_rest, 32))
    for n, other in enumerate(sides(level, level_halo, STRIP + 20)):
        face_levels[n] = jnp.minimum(level, other)
    for n, other in enumerate(sides(d, d_halo, 20)):
        faces[n] = 0.5 * (d + other)

    def level_step(k, carry):
        weights = [jnp.where(k.astype(F32) < face_levels[n], faces[n], 0.0) for n in range(4)]
        for comp in range(2):
            p = comp * LEVELS + k
            here = pl.ds(pl.multiple_of(p * ROWS, ROWS), ROWS)
            x = tra[here, :]
            around = sides(x, turn(swap[...], 39 - 2 * p), p)
            total = weights[0] * (around[0] - x)
            for n in range(1, 4):
                total += weights[n] * (around[n] - x)
            out[here, :] = x + total
        return carry

    lax.fori_loop(0, LEVELS, level_step, 0, unroll=2)


def column_strip(strip):
    rows = strip.shape[0]
    lanes = lane_ids(rows)
    ids = row_ids(rows)
    phase = lanes & 3
    group = lanes >> 2

    levels = pick(strip, phase + 80)
    v = pick(strip, phase + 84)
    number = jnp.where(group >= LEVELS, group - LEVELS, group).astype(F32)
    wet = jnp.where((number < levels) & (group < PLANES), 1.0, 0.0)
    x = jnp.where(group < PLANES, strip, 0.0)
    open_e = wet * turn(wet, LANES - 1)
    wet_n = pltpu.roll(wet, rows - 1, 0)
    open_n = wet * wet_n
    flux_e = open_e * (turn(x, LANES - 1) - x)
    flux_n = open_n * (pltpu.roll(x, rows - 1, 0) - x)
    lap = flux_e - turn(flux_e, 1) + flux_n - pltpu.roll(flux_n, 1, 0)
    seam = jnp.where(phase == 1, flux_e, 0.0)
    added = seam - turn(seam, 1)
    base = jnp.where(phase == 1, lap, added)
    other = jnp.where(phase == 1, turn(lap, LANES - 1), turn(added, LANES - 1))
    face = 0.5 * (v + turn(v, LANES - 1)) * open_e
    flux_e = jnp.where(phase == 3, 0.0, face * (other - base))
    in_block = (ids != MARGIN - 1) & (ids != MARGIN + ROWS - 1)
    face = jnp.where(in_block, 0.5 * (v + pltpu.roll(v, rows - 1, 0)) * open_n, 0.0)
    flux_n = face * (pltpu.roll(added, rows - 1, 0) - added)
    second = flux_e - turn(flux_e, 1) + flux_n - pltpu.roll(flux_n, 1, 0)
    return wet * second


def gram_pairs():
    return [(i, j) for i in range(SOLVE_ITERS) for j in range(i, SOLVE_ITERS + 1)]


def surface_kernel(
    tall, strips, mean, recv_b, recv_a,
    basis_out, flow, partial, col_patch, row_patch,
    state, height, flux, slope, basis, weights, diagonal,
):
    is_odd = odd("lon")
    rows = pl.ds(8, TALL)
    lanes = lane_ids(TALL)

    def received(start, count):
        here = pl.ds(start, count)
        got_a = recv_a[here, :]
        got_b = recv_b[here, :]
        return jnp.where(is_odd, got_b, got_a), jnp.where(is_odd, got_a, got_b)

    def ghost(east, west, f):
        return jnp.where(
            lane_ids(east.shape[0]) < 64, turn(east, (LANES - 32 * f) % LANES), turn(west, (96 - 32 * f) % LANES)
        )

    from_east, from_west = received(TALL, TALL)
    for f in range(3):
        state[f, 0, rows, :] = tall[pl.ds(f * TALL, TALL), :]
        state[f, 1, rows, :] = ghost(from_east, from_west, f)
    last = lanes == LANES - 1
    first = lanes == 0

    def lane_sides(a, b):
        n = a.shape[0]
        ea, eb, wa, wb = turn(a, LANES - 1), turn(b, LANES - 1), turn(a, 1), turn(b, 1)
        return (
            (jnp.where(last[0:n], eb, ea), jnp.where(last[0:n], ea, eb)),
            (jnp.where(first[0:n], wb, wa), jnp.where(first[0:n], wa, wb)),
        )

    own = tall[pl.ds(3 * TALL, TALL), :]
    phase = lanes & 3
    from_east, from_west = received(0, TALL)
    to_east = column_strip(jnp.where(phase < 2, own, from_east))
    to_west = column_strip(jnp.where(phase < 2, from_west, own))
    changes = (jnp.where(phase < 2, to_east, to_west), jnp.where(phase < 2, to_west, to_east))
    deep = (own, jnp.where(phase < 2, from_west, from_east))
    col_patch[...] = changes[0][MARGIN : MARGIN + ROWS]
    rims = (lanes < 2) | (lanes >= LANES - 2)
    for half in range(2):
        pairs = changes[half] + turn(changes[half], LANES - 4)
        fours = pairs + turn(pairs, LANES - 8)
        total = fours + turn(fours, LANES - 16) + turn(pairs, LANES - 32)
        total = total / jnp.maximum(pick(deep[half], phase + 80), 1.0)
        for comp in range(2):
            here = turn(total, LANES - 2 - 40 * comp)
            state[comp, half, rows, :] = state[comp, half, rows, :] - jnp.where(rims, here, 0.0)
    number = lax.broadcasted_iota(jnp.int32, (STRIP, LANES), 0)
    level_of_row = jnp.where(number >= LEVELS, number - LEVELS, number).astype(F32)
    is_plane = number < PLANES
    not_last = lane_ids(STRIP) < LANES - 1
    for s in range(2):
        from_east, from_west = received(2 * TALL + s * STRIP, STRIP)
        x, wet, v, deep = [], [], [], []
        for r in range(4):
            centre = strips[pl.ds((4 * s + r) * STRIP, STRIP), :]
            both = (centre, ghost(from_east, from_west, r))
            deep.append([b[20:21] for b in both])
            v.append([jnp.broadcast_to(b[21:22], (STRIP, LANES)) for b in both])
            wet.append([jnp.where(is_plane & (level_of_row < b[20:21]), 1.0, 0.0) for b in both])
            x.append([jnp.where(is_plane, b, 0.0) for b in both])
        half_range = range(2)
        lap = {}
        added = {}
        seam = [wet[1][h] * wet[2][h] * (x[2][h] - x[1][h]) for h in half_range]
        added[1] = seam
        added[2] = [-t for t in seam]
        along = {}
        for r in (1, 2):
            x_e = lane_sides(*x[r])[0]
            wet_e = lane_sides(*wet[r])[0]
            v_e = lane_sides(*v[r])[0]
            added_e = lane_sides(*added[r])[0]
            open_e = [wet[r][h] * wet_e[h] for h in half_range]
            edge = [open_e[h] * (x_e[h] - x[r][h]) for h in half_range]
            edge_w = lane_sides(*edge)[1]
            lap[r] = [
                edge[h]
                - edge_w[h]
                + wet[r][h] * (wet[r + 1][h] * (x[r + 1][h] - x[r][h]) + wet[r - 1][h] * (x[r - 1][h] - x[r][h]))
                for h in half_range
            ]
            edge = [
                jnp.where(not_last, 0.5 * (v[r][h] + v_e[h]) * open_e[h] * (added_e[h] - added[r][h]), 0.0)
                for h in half_range
            ]
            edge_w = lane_sides(*edge)[1]
            along[r] = [edge[h] - edge_w[h] for h in half_range]
        for h in half_range:
            face = [0.5 * (v[r][h] + v[r + 1][h]) * wet[r][h] * wet[r + 1][h] for r in range(3)]
            across = (face[0] * added[1][h], face[1] * (lap[2][h] - lap[1][h]), -face[2] * added[2][h])
            second = (
                across[0],
                across[1] - across[0] + along[1][h],
                across[2] - across[1] + along[2][h],
                -across[2],
            )
            for r in range(4):
                change = wet[r][h] * second[r]
                if h == 0 and r >= 2:
                    row_patch[pl.ds((2 * s + r - 2) * STRIP, STRIP), :] = change
                where = 8 + MARGIN + ((ROWS + 1 - r) if s == 0 else (r - 2))
                for comp in range(2):
                    mine = (number >= comp * LEVELS) & (number < (comp + 1) * LEVELS)
                    total = jnp.sum(jnp.where(mine, change, 0.0), axis=0, keepdims=True)
                    total = total / jnp.maximum(deep[r][h], 1.0)
                    state[comp, h, where : where + 1, :] = state[comp, h, where : where + 1, :] - total
    for comp in range(2):
        here = pl.ds(comp * ROWS, ROWS)
        started = state[comp, 0, pl.ds(8 + MARGIN, ROWS), :] - tall[pl.ds(comp * TALL + MARGIN, ROWS), :]
        flow[here, :] = -(started + mean[here, :])

    for half in range(2):
        slope[half, rows, :] = jnp.where(state[2, half, rows, :] > 0.0, SLOPE, 0.0)
        height[half, rows, :] = jnp.zeros((TALL, LANES), F32)

    halves = range(2)

    def subcycle(cut, step, carry):
        for tile in range(8 + cut, 8 + TALL - cut, 8):
            here, above, below = (pl.ds(tile + off, 8) for off in (0, 1, -1))
            east, west = lane_sides(*(state[2, h, here, :] * state[0, h, here, :] for h in halves))
            for h in halves:
                north = state[2, h, above, :] * state[1, h, above, :]
                south = state[2, h, below, :] * state[1, h, below, :]
                divergence = (east[h] - west[h]) + (north - south)
                height[h, here, :] = height[h, here, :] - slope[h, here, :] * divergence
        for tile in range(8 + cut, 8 + TALL - cut, 8):
            here, above, below = (pl.ds(tile + off, 8) for off in (0, 1, -1))
            east, west = lane_sides(height[0, here, :], height[1, here, :])
            for h in halves:
                factor = slope[h, here, :]
                state[0, h, here, :] = state[0, h, here, :] - factor * (east[h] - west[h])
                state[1, h, here, :] = state[1, h, here, :] - factor * (height[h, above, :] - height[h, below, :])
        return carry

    for cut, start, stop in ((0, 0, 1), (8, 1, 5), (16, 5, SUBCYCLES)):
        lax.fori_loop(start, stop, functools.partial(subcycle, cut), 0, unroll=True)
    for comp in range(2):
        here = pl.ds(comp * ROWS, ROWS)
        flow[here, :] = flow[here, :] + state[comp, 0, pl.ds(8 + MARGIN, ROWS), :]
    scale = 2.0 / RADIUS
    short = ROWS + 16
    base = MARGIN

    tiles = range(0, short, 8)

    def nine(read, tile):
        out = [[], []]
        for off in (0, 1, -1):
            a, b = (read(h, pl.ds(base + tile + off, 8)) for h in halves)
            east, west = lane_sides(a, b)
            for h, centre in enumerate((a, b)):
                out[h] += [centre, east[h], west[h]]
        return out

    for tile in tiles:
        here = pl.ds(tile, 8)
        around = nine(lambda h, where: state[2, h, where, :], tile)
        for h in halves:
            d = around[h][0]
            wet = d > 0.0
            total = jnp.where(wet, 0.05, 1.0)
            for n in range(1, 9):
                factor = 0.5 if n in (1, 2, 3, 6) else 0.25
                w = jnp.where(wet & (around[h][n] > 0.0), factor * (d + around[h][n]), 0.0)
                weights[n - 1, h, here, :] = scale * w
                total += w
            diagonal[h, here, :] = scale * (total - CENTRE)
            basis[0, h, pl.ds(base + tile, 8), :] = height[h, pl.ds(base + tile, 8), :]

    def applied(source, tile):
        around = nine(lambda h, where: basis[source, h, where, :], tile)
        out = []
        for h in halves:
            here = pl.ds(tile, 8)
            total = diagonal[h, here, :] * around[h][0]
            for n in range(1, 9):
                total -= weights[n - 1, h, here, :] * around[h][n]
            out.append(total)
        return out

    for tile in tiles:
        for h, x in enumerate(applied(0, tile)):
            basis[1, h, pl.ds(base + tile, 8), :] = 0.5 * x

    def next_basis(k, carry):
        for tile in tiles:
            here = pl.ds(base + tile, 8)
            for h, x in enumerate(applied(k, tile)):
                basis[k + 1, h, here, :] = x - basis[k - 1, h, here, :]
        return carry

    lax.fori_loop(1, SOLVE_ITERS, next_basis, 0, unroll=True)
    lane = lane_ids(1)
    row = jnp.zeros((1, LANES), F32)
    mine = pl.ds(8 + MARGIN, ROWS)
    for n, (i, j) in enumerate(gram_pairs()):
        product = basis[i, 0, mine, :] * basis[j, 0, mine, :]
        row = jnp.where(lane == n, jnp.sum(jnp.sum(product, axis=0, keepdims=True), axis=1, keepdims=True), row)
    partial[...] = jnp.broadcast_to(row, partial.shape)
    for i in range(SOLVE_ITERS):
        for half in range(2):
            basis_out[i, half] = basis[i, half, pl.ds(base, short), :]


def solve_coefficients(gram):
    half = 0.5 * RADIUS

    def image_of(d):
        out = [None] * (len(d) + 1)

        def add(n, term):
            out[n] = term if out[n] is None else out[n] + term

        for j, value in enumerate(d):
            add(j, CENTRE * value)
            if j == 0:
                add(1, RADIUS * value)
            else:
                add(j + 1, half * value)
                add(j - 1, half * value)
        return out

    def inner(a, b):
        total = None
        for i, x in enumerate(a):
            for j, y in enumerate(b):
                term = x * y * gram[(min(i, j), max(i, j))]
                total = term if total is None else total + term
        return total

    one = jnp.ones((8, LANES), F32)
    residual, direction, surface = [one], [one], [0.0 * one]
    norm = gram[(0, 0)]
    for iteration in range(SOLVE_ITERS):
        image = image_of(direction)
        step = norm / inner(direction, image)
        surface = [a + step * b for a, b in zip(surface, direction)] + [0.0 * one]
        if iteration == SOLVE_ITERS - 1:
            break
        residual = [(residual[n] if n < len(residual) else 0.0) - step * x for n, x in enumerate(image)]
        fresh = inner(residual, residual)
        ratio = fresh / norm
        direction = [x + (ratio * direction[n] if n < len(direction) else 0.0) for n, x in enumerate(residual)]
        norm = fresh
    return surface[:SOLVE_ITERS]


def final_kernel(gathered, basis, flow, star, lev, velocity_out, surface_out, pad, change):
    sums = jnp.sum(gathered[...], axis=0, keepdims=True)
    lane = lane_ids(1)
    gram = {}
    for n, pair in enumerate(gram_pairs()):
        value = jnp.sum(jnp.where(lane == n, sums, 0.0), axis=1, keepdims=True)
        gram[pair] = jnp.broadcast_to(value, (8, LANES))
    coefficients = [c[0:1] for c in solve_coefficients(gram)]
    for half in range(2):
        total = coefficients[0] * basis[0, half]
        for i in range(1, SOLVE_ITERS):
            total += coefficients[i] * basis[i, half]
        pad[half] = total
    mine = pl.ds(8, ROWS)
    centre = pad[0, mine, :]
    ghost = pad[1, mine, :]
    surface_out[...] = centre
    lanes = lane_ids(ROWS)
    east = jnp.where(lanes == LANES - 1, turn(ghost, LANES - 1), turn(centre, LANES - 1))
    west = jnp.where(lanes == 0, turn(ghost, 1), turn(centre, 1))
    levels = lev[...]
    slope = jnp.where(levels > 0, SLOPE, 0.0)
    slopes = (east - west, pad[0, pl.ds(9, ROWS), :] - pad[0, pl.ds(7, ROWS), :])
    for comp in range(2):
        here = pl.ds(comp * ROWS, ROWS)
        change[comp] = flow[here, :] - slope * slopes[comp]


    def level_step(k, carry):
        wet = k < levels
        for comp in range(2):
            here = pl.ds(pl.multiple_of((comp * LEVELS + k) * ROWS, ROWS), ROWS)
            velocity_out[here, :] = star[here, :] + jnp.where(wet, change[comp], 0.0)
        return carry

    lax.fori_loop(0, LEVELS, level_step, 0, unroll=True)


def patch_kernel(star, col_patch, row_patch, out):
    lanes = lane_ids(ROWS)
    rims = (lanes < 2) | (lanes >= LANES - 2)
    ids = row_ids(8)

    def plane(p, carry):
        here = pl.ds(pl.multiple_of(p * ROWS, ROWS), ROWS)
        out[here, :] = star[here, :] - jnp.where(rims, turn(col_patch[...], 126 - 4 * p), 0.0)
        for first, pieces in ((ROWS - 8, ((7, 0), (6, 1))), (0, ((0, 2), (1, 3)))):
            here = pl.ds(pl.multiple_of(p * ROWS + first, 8), 8)
            x = out[here, :]
            for row, n in pieces:
                x = x - jnp.where(ids == row, row_patch[pl.ds(n * STRIP + p, 1), :], 0.0)
            out[here, :] = x
        return carry

    lax.fori_loop(0, PLANES, plane, 0, unroll=10)


def call(kernel, shapes, scratch, flops, *args, far=False):
    out = tuple(jax.ShapeDtypeStruct(s, F32) for s in shapes)
    moved = sum(4 * math.prod(a.shape) for a in args) + sum(4 * math.prod(s) for s in shapes)
    if far:
        args = [pltpu.with_memory_space_constraint(a, pltpu.HBM) for a in args]
    return pl.pallas_call(
        kernel,
        out_shape=out,
        in_specs=[pl.BlockSpec(memory_space=pltpu.HBM if far else pltpu.VMEM)] * len(args),
        scratch_shapes=[pltpu.VMEM(s, F32) if isinstance(s, tuple) else s for s in scratch],
        compiler_params=pltpu.CompilerParams(vmem_limit_bytes=32 * 1024 * 1024),
        cost_estimate=pl.CostEstimate(flops=flops, bytes_accessed=moved, transcendentals=0),
    )(*args)


def pair_tables(lon, lat):
    def index(i, j):
        return j * lat + i

    lat_a, lat_b, lon_a, lon_b = [], [], [], []
    for j in range(lon):
        for i in range(lat):
            lat_a.append((index(i, j), index(i ^ 1, j)))
            if i == lat - 1:
                lat_b.append((index(i, j), index(i, lon - 1 - j)))
            elif i > 0:
                lat_b.append((index(i, j), index(i + 1 if i % 2 else i - 1, j)))
            lon_a.append((index(i, j), index(i, j ^ 1)))
            lon_b.append((index(i, j), index(i, (j + 1 if j % 2 else j - 1) % lon)))
    return lat_a, lat_b, lon_a, lon_b


def per_device(lon, lat, tracers, velocity, active_levels, diffusivity, viscosity, ocean_depth, wind_forcing):
    lat_a, lat_b, lon_a, lon_b = pair_tables(lon, lat)

    def swap(x, pairs):
        return lax.ppermute(x, BOTH, pairs)

    block = (ROWS, LANES)
    tra = tracers.reshape(PLANES * ROWS, LANES)
    vel = velocity.reshape(PLANES * ROWS, LANES)
    wind = wind_forcing.reshape(2 * ROWS, LANES)
    rim = (RIMS, LANES)
    star, mean, fields, cols, north, south, send_a, send_b = call(
        block_kernel,
        [(PLANES * ROWS, LANES), (2 * ROWS, LANES), (3 * ROWS, LANES), block, rim, rim, (LAT_SEND, LANES), (LAT_SEND, LANES)],
        [(4,) + block, (4,) + block, (2,) + block, block, (PLANES * ROWS + 16, LANES), vel.shape, block, block, block, wind.shape,
         block, (2, ROWS + 16, LANES),
         pltpu.VMEM(block, jnp.int32), pltpu.SemaphoreType.DMA((7,))],
        10**7,
        vel, tra, active_levels, viscosity, diffusivity, ocean_depth, wind,
        far=True,
    )
    got_a = swap(send_a, lat_a)
    got_b = swap(send_b, lat_b)
    tall, strips, tracer_rows, send_a, send_b = call(
        widen_kernel,
        [(4 * TALL, LANES), (8 * STRIP, LANES), (4 * STRIP, LANES), (LON_SEND, LANES), (LON_SEND, LANES)],
        [(TALL + 2 * STRIP, LANES)] * 2,
        10**6,
        fields, cols, diffusivity, north, south, got_b, got_a,
    )
    got_a = swap(send_a, lon_a)
    got_b = swap(send_b, lon_b)
    (tracers_out,) = call(
        tracer_kernel, [(PLANES * ROWS, LANES)], [block, (4,) + block, (4,) + block], 10**6,
        tra, active_levels, diffusivity, tracer_rows, got_b, got_a,
    )
    padded = (2, TALL + 16, LANES)
    short = (2, ROWS + 16, LANES)
    basis, flow, partial, col_patch, row_patch = call(
        surface_kernel,
        [(SOLVE_ITERS,) + short, (2 * ROWS, LANES), (lon * lat, LANES), block, (4 * STRIP, LANES)],
        [(3,) + padded, padded, padded, padded, (SOLVE_ITERS + 1,) + padded, (8,) + short, short],
        10**7,
        tall, strips, mean, got_b, got_a,
    )
    gathered = lax.all_to_all(partial, BOTH, 0, 0, tiled=True)
    (star,) = call(patch_kernel, [(PLANES * ROWS, LANES)], [], 10**6, star, col_patch, row_patch)
    velocity_out, surface = call(
        final_kernel, [(PLANES * ROWS, LANES), block],
        [short, (2,) + block], 10**6,
        gathered, basis, flow, star, active_levels,
    )
    return tracers_out.reshape(tracers.shape), velocity_out.reshape(velocity.shape), surface


def solution(mesh):
    placed = (
        P(None, None, "lat", "lon"),
        P(None, None, "lat", "lon"),
        P("lat", "lon"),
        P("lat", "lon"),
        P("lat", "lon"),
        P("lat", "lon"),
        P(None, "lat", "lon"),
    )
    return jax.shard_map(
        functools.partial(per_device, mesh.shape["lon"], mesh.shape["lat"]),
        mesh=mesh,
        in_specs=placed,
        out_specs=(P(None, None, "lat", "lon"), P(None, None, "lat", "lon"), P("lat", "lon")),
        check_vma=False,
    )
```

```python
import functools
import math

import jax
import jax.numpy as jnp
from jax import lax
from jax.experimental import pallas as pl
from jax.experimental.pallas import tpu as pltpu
from jax.sharding import PartitionSpec as P

SUBCYCLES = 8
SOLVE_ITERS = 4
LEVELS = 10
PLANES = 2 * LEVELS
ROWS = 64
LANES = 128
MARGIN = 24
TALL = ROWS + 2 * MARGIN
RIM = 32
SLOPE = 0.15
CENTRE = 5.0
RADIUS = 5.0
F32 = jnp.float32
BOTH = ("lon", "lat")

STRIP = 24
RIMS = 3 * STRIP
LAT_SEND = 3 * MARGIN + RIMS + MARGIN
LON_SEND = 2 * TALL + 2 * STRIP


def lane_ids(rows):
    return lax.broadcasted_iota(jnp.int32, (rows, LANES), 1)


def row_ids(rows):
    return lax.broadcasted_iota(jnp.int32, (rows, LANES), 0)


def turn(x, shift):
    return pltpu.roll(x, shift, 1)


def pick(x, index):
    return jnp.take_along_axis(x, index, axis=1)


def flip_lanes(x, mask=LANES - 1):
    return pick(x, lane_ids(x.shape[0]) ^ mask)


def flip_rows(x):
    rows = x.shape[0]
    ids = row_ids(rows)
    for bit in range(3):
        step = 1 << bit
        x = jnp.where((ids & step) != 0, pltpu.roll(x, step, 0), pltpu.roll(x, rows - step, 0))
    return jnp.concatenate([x[r : r + 8] for r in range(rows - 8, -8, -8)], axis=0)


def odd(axis):
    return lax.rem(lax.axis_index(axis), 2) == 1


def at_fold():
    return lax.axis_index("lat") == lax.axis_size("lat") - 1


def shifted(x):
    rows = x.shape[0]
    return (turn(x, LANES - 1), turn(x, 1), pltpu.roll(x, rows - 1, 0), pltpu.roll(x, 1, 0))


def block_kernel(
    vel_far, tra_far, lev_far, visc_far, diff_far, depth_far, wind_far,
    star, mean, fields, cols, north, south, send_a, send_b,
    faces, face_levels, sums, turning, vel, tra, visc, diff, depth, wind, levels_kept, laps, lev, done,
):
    pairs = ((lev_far, lev), (visc_far, visc), (vel_far, vel), (tra_far, tra), (wind_far, wind), (depth_far, depth), (diff_far, diff))
    copies = [
        pltpu.make_async_copy(far, near.at[pl.ds(8, PLANES * ROWS)] if near is vel else near, done.at[n])
        for n, (far, near) in enumerate(pairs)
    ]
    for copy in copies:
        copy.start()
    for copy in copies[:2]:
        copy.wait()
    lanes = lane_ids(ROWS)
    ids = row_ids(ROWS)
    levels = lev[...].astype(F32)
    v = visc[...]
    inside = (lanes < LANES - 1, lanes > 0, ids < ROWS - 1, ids > 0)
    for n, (v_n, level_n) in enumerate(zip(shifted(v), shifted(levels))):
        faces[n] = 0.5 * (v + v_n)
        face_levels[n] = jnp.where(inside[n], jnp.minimum(levels, level_n), 0.0)
    row = (lax.axis_index("lat") * ROWS).astype(F32) + ids.astype(F32)
    turning[...] = 0.25 * jnp.sin(math.pi * ((row + 0.5) / (ROWS * lax.axis_size("lat")) - 0.5))
    sums[...] = jnp.zeros((2, ROWS, LANES), F32)
    levels_kept[...] = levels
    for padded in (vel, laps):
        padded[0:8, :] = jnp.zeros((8, LANES), F32)
        padded[PLANES * ROWS + 8 : PLANES * ROWS + 16, :] = jnp.zeros((8, LANES), F32)
    acc = jnp.where((lanes >> 2) == 20, turn(levels, 82), 0.0)
    cols[...] = jnp.where((lanes >> 2) == 21, turn(v, 86), acc)
    copies[2].wait()

    def lap_step(k, carry):
        level = k.astype(F32)
        open_faces = [level < face_levels[n] for n in range(4)]
        ones = [jnp.where(o, 1.0, 0.0) for o in open_faces]
        count = (ones[0] + ones[1]) + (ones[2] + ones[3])
        packed = cols[...]
        for comp in range(2):
            p = comp * LEVELS + k
            start = 8 + pl.multiple_of(p * ROWS, ROWS)
            x = vel[pl.ds(start, ROWS), :]
            around = (turn(x, LANES - 1), turn(x, 1), vel[pl.ds(start + 1, ROWS), :], vel[pl.ds(start - 1, ROWS), :])
            picked = [jnp.where(open_faces[n], around[n], 0.0) for n in range(4)]
            laps[pl.ds(start, ROWS), :] = (picked[0] + picked[1]) + (picked[2] + picked[3]) - count * x
            packed = jnp.where((lanes >> 2) == p, turn(x, 4 * p + 2), packed)
        cols[...] = packed
        return carry

    def star_step(k, carry):
        level = k.astype(F32)
        wet = level < levels_kept[...]
        weights = [jnp.where(level < face_levels[n], faces[n], 0.0) for n in range(4)]
        weight = (weights[0] + weights[1]) + (weights[2] + weights[3])
        starts = [8 + pl.multiple_of((comp * LEVELS + k) * ROWS, ROWS) for comp in range(2)]
        values = [vel[pl.ds(s, ROWS), :] for s in starts]
        for comp, x in enumerate(values):
            start = starts[comp]
            lap = laps[pl.ds(start, ROWS), :]
            around = (turn(lap, LANES - 1), turn(lap, 1), laps[pl.ds(start + 1, ROWS), :], laps[pl.ds(start - 1, ROWS), :])
            terms = [weights[n] * around[n] for n in range(4)]
            second = (terms[0] + terms[1]) + (terms[2] + terms[3]) - weight * lap
            rotated = values[1] if comp == 0 else -values[0]
            out = jnp.where(wet, x - second + turning[...] * rotated, 0.0)
            star[pl.ds(pl.multiple_of((comp * LEVELS + k) * ROWS, ROWS), ROWS), :] = out
            sums[comp] += out
        return carry

    lax.fori_loop(0, LEVELS, lap_step, 0, unroll=10)
    lax.fori_loop(0, LEVELS, star_step, 0, unroll=10)
    for copy in copies[3:]:
        copy.wait()

    def tracer_step(p, acc):
        t = tra[pl.ds(pl.multiple_of(p * ROWS, ROWS), ROWS), :]
        return jnp.where((lanes >> 1) == 44 + p, turn(t, lax.rem(89 + 2 * p, LANES)), acc)

    cols[...] = lax.fori_loop(0, PLANES, tracer_step, cols[...], unroll=True)
    ocean = levels > 0.0
    for comp in range(2):
        here = pl.ds(comp * ROWS, ROWS)
        column_mean = sums[comp] / jnp.maximum(levels, 1.0)
        mean[here, :] = column_mean
        fields[here, :] = column_mean + jnp.where(ocean, wind[here, :], 0.0)
    fields[pl.ds(2 * ROWS, ROWS), :] = jnp.where(ocean, depth[...], 0.0)
    for edge, step, out in ((ROWS - 1, -1, north), (0, 1, south)):
        out[...] = jnp.zeros((RIMS, LANES), F32)
        for d in range(2):
            r = edge + d * step
            out[pl.ds(d * STRIP, PLANES), :] = vel[pl.ds(8 + r, PLANES, stride=ROWS), :]
            out[pl.ds(d * STRIP + 20, 1), :] = levels[r : r + 1]
            out[pl.ds(d * STRIP + 21, 1), :] = visc[pl.ds(r, 1), :]
        out[pl.ds(2 * STRIP, PLANES), :] = tra[pl.ds(edge, PLANES, stride=ROWS), :]
        out[pl.ds(2 * STRIP + 20, 1), :] = diff[pl.ds(edge, 1), :]
    lat_odd = odd("lat")

    def put(start, up, down):
        here = pl.ds(start, up.shape[0])
        send_a[here, :] = jnp.where(lat_odd, down, up)
        send_b[here, :] = jnp.where(lat_odd, up, down)

    for f in range(3):
        put(f * MARGIN, fields[pl.ds((f + 1) * ROWS - MARGIN, MARGIN), :], fields[pl.ds(f * ROWS, MARGIN), :])
    put(3 * MARGIN, north[...], south[...])
    put(3 * MARGIN + RIMS, cols[ROWS - MARGIN : ROWS, :], cols[0:MARGIN, :])

    @pl.when(at_fold())
    def _():
        for f in range(3):
            turned = flip_rows(flip_lanes(fields[pl.ds((f + 1) * ROWS - MARGIN, MARGIN), :]))
            send_b[pl.ds(f * MARGIN, MARGIN), :] = turned if f == 2 else -turned
        turned = flip_lanes(north[...])
        r = row_ids(RIMS)
        is_velocity = (r < PLANES) | ((r >= STRIP) & (r < STRIP + PLANES))
        send_b[pl.ds(3 * MARGIN, RIMS), :] = jnp.where(is_velocity, -turned, turned)
        turned = flip_rows(flip_lanes(cols[ROWS - MARGIN : ROWS, :], 3))
        send_b[pl.ds(3 * MARGIN + RIMS, MARGIN), :] = jnp.where(lane_ids(MARGIN) < 4 * PLANES, -turned, turned)


def widen_kernel(fields, cols, diff, north, south, recv_b, recv_a, tall, strips, tracer_rows, send_a, send_b, east, west):
    lat_odd = odd("lat")
    lon_odd = odd("lon")
    group = lane_ids(TALL) >> 5

    def received(start, count):
        here = pl.ds(start, count)
        got_a = recv_a[here, :]
        got_b = recv_b[here, :]
        return jnp.where(lat_odd, got_b, got_a), jnp.where(lat_odd, got_a, got_b)

    acc_east = jnp.zeros((TALL, LANES), F32)
    acc_west = jnp.zeros((TALL, LANES), F32)
    for f in range(4):
        from_north, from_south = received(f * MARGIN if f < 3 else 3 * MARGIN + RIMS, MARGIN)
        tall[pl.ds(f * TALL, MARGIN), :] = from_south
        tall[pl.ds(f * TALL + MARGIN, ROWS), :] = fields[pl.ds(f * ROWS, ROWS), :] if f < 3 else cols[...]
        tall[pl.ds(f * TALL + MARGIN + ROWS, MARGIN), :] = from_north
        if f < 3:
            x = tall[pl.ds(f * TALL, TALL), :]
            acc_east = jnp.where(group == f, turn(x, 32 * (f + 1)), acc_east)
            acc_west = jnp.where(group == f, turn(x, 32 * f), acc_west)
    for out, acc, shift in ((east, acc_east, 97), (west, acc_west, 96)):
        out[pl.ds(0, TALL), :] = acc
        out[pl.ds(MARGIN, ROWS), :] = jnp.where(lane_ids(ROWS) == 96, turn(diff[...], shift), acc[MARGIN : MARGIN + ROWS])
    rims = received(3 * MARGIN, RIMS)
    for s, (own, rim) in enumerate(((north, rims[0]), (south, rims[1]))):
        pieces = (rim[STRIP : 2 * STRIP], rim[0:STRIP], own[0:STRIP, :], own[STRIP : 2 * STRIP, :])
        acc_east = jnp.zeros((STRIP, LANES), F32)
        acc_west = jnp.zeros((STRIP, LANES), F32)
        for r, x in enumerate(pieces):
            strips[pl.ds((4 * s + r) * STRIP, STRIP), :] = x
            acc_east = jnp.where(group[0:STRIP] == r, turn(x, (32 * (r + 1)) % LANES), acc_east)
            acc_west = jnp.where(group[0:STRIP] == r, turn(x, 32 * r), acc_west)
        east[pl.ds(TALL + s * STRIP, STRIP), :] = acc_east
        west[pl.ds(TALL + s * STRIP, STRIP), :] = acc_west
        tracer_rows[pl.ds(2 * s * STRIP, STRIP), :] = rim[2 * STRIP : 3 * STRIP]
        tracer_rows[pl.ds((2 * s + 1) * STRIP, STRIP), :] = rim[0:STRIP]
    k = tall[pl.ds(3 * TALL, TALL), :]
    send_a[pl.ds(0, TALL), :] = k
    send_b[pl.ds(0, TALL), :] = k
    rest = pl.ds(TALL, TALL + 2 * STRIP)
    e, w = east[...], west[...]
    send_a[rest, :] = jnp.where(lon_odd, w, e)
    send_b[rest, :] = jnp.where(lon_odd, e, w)


def tracer_kernel(tra, lev, diff, tracer_rows, recv_b, recv_a, out, swap, faces, face_levels):
    is_odd = odd("lon")
    lanes = lane_ids(ROWS)
    ids = row_ids(ROWS)

    def received(start):
        here = pl.ds(start + MARGIN, ROWS)
        got_a = recv_a[here, :]
        got_b = recv_b[here, :]
        return jnp.where(is_odd, got_b, got_a), jnp.where(is_odd, got_a, got_b)

    east_cols, west_cols = received(0)
    east_rest, west_rest = received(TALL)
    swap[...] = jnp.where((lanes & 1) == 0, turn(east_cols, LANES - 1), turn(west_cols, 1))

    def sides(x, halo, row):
        east, west, north, south = shifted(x)
        return (
            jnp.where(lanes == LANES - 1, halo, east),
            jnp.where(lanes == 0, halo, west),
            jnp.where(ids == ROWS - 1, tracer_rows[pl.ds(row, 1), :], north),
            jnp.where(ids == 0, tracer_rows[pl.ds(row + 2 * STRIP, 1), :], south),
        )

    level = lev[...].astype(F32)
    level_halo = jnp.where(lanes == LANES - 1, turn(east_cols, 45), turn(west_cols, 47))
    d = diff[...]
    d_halo = jnp.where(lanes == LANES - 1, turn(east_rest, 31), turn(west_rest, 32))
    for n, other in enumerate(sides(level, level_halo, STRIP + 20)):
        face_levels[n] = jnp.minimum(level, other)
    for n, other in enumerate(sides(d, d_halo, 20)):
        faces[n] = 0.5 * (d + other)

    def level_step(k, carry):
        weights = [jnp.where(k.astype(F32) < face_levels[n], faces[n], 0.0) for n in range(4)]
        for comp in range(2):
            p = comp * LEVELS + k
            here = pl.ds(pl.multiple_of(p * ROWS, ROWS), ROWS)
            x = tra[here, :]
            around = sides(x, turn(swap[...], 39 - 2 * p), p)
            total = weights[0] * (around[0] - x)
            for n in range(1, 4):
                total += weights[n] * (around[n] - x)
            out[here, :] = x + total
        return carry

    lax.fori_loop(0, LEVELS, level_step, 0, unroll=2)


def column_strip(strip):
    rows = strip.shape[0]
    lanes = lane_ids(rows)
    ids = row_ids(rows)
    phase = lanes & 3
    group = lanes >> 2

    levels = pick(strip, phase + 80)
    v = pick(strip, phase + 84)
    number = jnp.where(group >= LEVELS, group - LEVELS, group).astype(F32)
    wet = jnp.where((number < levels) & (group < PLANES), 1.0, 0.0)
    x = jnp.where(group < PLANES, strip, 0.0)
    open_e = wet * turn(wet, LANES - 1)
    wet_n = pltpu.roll(wet, rows - 1, 0)
    open_n = wet * wet_n
    flux_e = open_e * (turn(x, LANES - 1) - x)
    flux_n = open_n * (pltpu.roll(x, rows - 1, 0) - x)
    lap = flux_e - turn(flux_e, 1) + flux_n - pltpu.roll(flux_n, 1, 0)
    seam = jnp.where(phase == 1, flux_e, 0.0)
    added = seam - turn(seam, 1)
    base = jnp.where(phase == 1, lap, added)
    other = jnp.where(phase == 1, turn(lap, LANES - 1), turn(added, LANES - 1))
    face = 0.5 * (v + turn(v, LANES - 1)) * open_e
    flux_e = jnp.where(phase == 3, 0.0, face * (other - base))
    in_block = (ids != MARGIN - 1) & (ids != MARGIN + ROWS - 1)
    face = jnp.where(in_block, 0.5 * (v + pltpu.roll(v, rows - 1, 0)) * open_n, 0.0)
    flux_n = face * (pltpu.roll(added, rows - 1, 0) - added)
    second = flux_e - turn(flux_e, 1) + flux_n - pltpu.roll(flux_n, 1, 0)
    return wet * second


def gram_pairs():
    return [(i, j) for i in range(SOLVE_ITERS) for j in range(i, SOLVE_ITERS + 1)]


def surface_kernel(
    tall, strips, mean, recv_b, recv_a,
    basis_out, flow, partial, col_patch, row_patch,
    state, height, flux, slope, basis, weights, diagonal,
):
    is_odd = odd("lon")
    rows = pl.ds(8, TALL)
    lanes = lane_ids(TALL)

    def received(start, count):
        here = pl.ds(start, count)
        got_a = recv_a[here, :]
        got_b = recv_b[here, :]
        return jnp.where(is_odd, got_b, got_a), jnp.where(is_odd, got_a, got_b)

    def ghost(east, west, f):
        return jnp.where(
            lane_ids(east.shape[0]) < 64, turn(east, (LANES - 32 * f) % LANES), turn(west, (96 - 32 * f) % LANES)
        )

    from_east, from_west = received(TALL, TALL)
    for f in range(3):
        state[f, 0, rows, :] = tall[pl.ds(f * TALL, TALL), :]
        state[f, 1, rows, :] = ghost(from_east, from_west, f)
    last = lanes == LANES - 1
    first = lanes == 0

    def lane_sides(a, b):
        n = a.shape[0]
        ea, eb, wa, wb = turn(a, LANES - 1), turn(b, LANES - 1), turn(a, 1), turn(b, 1)
        return (
            (jnp.where(last[0:n], eb, ea), jnp.where(last[0:n], ea, eb)),
            (jnp.where(first[0:n], wb, wa), jnp.where(first[0:n], wa, wb)),
        )

    own = tall[pl.ds(3 * TALL, TALL), :]
    phase = lanes & 3
    from_east, from_west = received(0, TALL)
    to_east = column_strip(jnp.where(phase < 2, own, from_east))
    to_west = column_strip(jnp.where(phase < 2, from_west, own))
    changes = (jnp.where(phase < 2, to_east, to_west), jnp.where(phase < 2, to_west, to_east))
    deep = (own, jnp.where(phase < 2, from_west, from_east))
    col_patch[...] = changes[0][MARGIN : MARGIN + ROWS]
    to_lane = lax.broadcasted_iota(jnp.int32, (LANES, 2 * LANES), 1)
    from_lane = lax.broadcasted_iota(jnp.int32, (LANES, 2 * LANES), 0)
    column = to_lane & (LANES - 1)
    comp_of = jnp.where(from_lane < 4 * LEVELS, 0, 1)
    chosen = (
        ((column < 2) | (column >= LANES - 2))
        & ((from_lane & 3) == ((to_lane + 2) & 3))
        & (comp_of == (to_lane >> 7))
        & (from_lane < 4 * PLANES)
    )
    chooser = jnp.where(chosen, 1.0, 0.0)
    for half in range(2):
        total = lax.dot_general(
            changes[half], chooser, (((1,), (0,)), ((), ())),
            precision=lax.Precision.HIGHEST, preferred_element_type=F32,
        )
        share = 1.0 / jnp.maximum(pick(deep[half], ((lanes + 2) & 3) + 80), 1.0)
        for comp in range(2):
            change = total[:, comp * LANES : (comp + 1) * LANES] * share
            state[comp, half, rows, :] = state[comp, half, rows, :] - change
    number = lax.broadcasted_iota(jnp.int32, (STRIP, LANES), 0)
    level_of_row = jnp.where(number >= LEVELS, number - LEVELS, number).astype(F32)
    is_plane = number < PLANES
    not_last = lane_ids(STRIP) < LANES - 1
    for s in range(2):
        from_east, from_west = received(2 * TALL + s * STRIP, STRIP)
        x, wet, v, deep = [], [], [], []
        for r in range(4):
            centre = strips[pl.ds((4 * s + r) * STRIP, STRIP), :]
            both = (centre, ghost(from_east, from_west, r))
            deep.append([b[20:21] for b in both])
            v.append([jnp.broadcast_to(b[21:22], (STRIP, LANES)) for b in both])
            wet.append([jnp.where(is_plane & (level_of_row < b[20:21]), 1.0, 0.0) for b in both])
            x.append([jnp.where(is_plane, b, 0.0) for b in both])
        half_range = range(2)
        lap = {}
        added = {}
        seam = [wet[1][h] * wet[2][h] * (x[2][h] - x[1][h]) for h in half_range]
        added[1] = seam
        added[2] = [-t for t in seam]
        along = {}
        for r in (1, 2):
            x_e = lane_sides(*x[r])[0]
            wet_e = lane_sides(*wet[r])[0]
            v_e = lane_sides(*v[r])[0]
            added_e = lane_sides(*added[r])[0]
            open_e = [wet[r][h] * wet_e[h] for h in half_range]
            edge = [open_e[h] * (x_e[h] - x[r][h]) for h in half_range]
            edge_w = lane_sides(*edge)[1]
            lap[r] = [
                edge[h]
                - edge_w[h]
                + wet[r][h] * (wet[r + 1][h] * (x[r + 1][h] - x[r][h]) + wet[r - 1][h] * (x[r - 1][h] - x[r][h]))
                for h in half_range
            ]
            edge = [
                jnp.where(not_last, 0.5 * (v[r][h] + v_e[h]) * open_e[h] * (added_e[h] - added[r][h]), 0.0)
                for h in half_range
            ]
            edge_w = lane_sides(*edge)[1]
            along[r] = [edge[h] - edge_w[h] for h in half_range]
        for h in half_range:
            face = [0.5 * (v[r][h] + v[r + 1][h]) * wet[r][h] * wet[r + 1][h] for r in range(3)]
            across = (face[0] * added[1][h], face[1] * (lap[2][h] - lap[1][h]), -face[2] * added[2][h])
            second = (
                across[0],
                across[1] - across[0] + along[1][h],
                across[2] - across[1] + along[2][h],
                -across[2],
            )
            for r in range(4):
                change = wet[r][h] * second[r]
                if h == 0 and r >= 2:
                    row_patch[pl.ds((2 * s + r - 2) * STRIP, STRIP), :] = change
                where = 8 + MARGIN + ((ROWS + 1 - r) if s == 0 else (r - 2))
                for comp in range(2):
                    mine = (number >= comp * LEVELS) & (number < (comp + 1) * LEVELS)
                    total = jnp.sum(jnp.where(mine, change, 0.0), axis=0, keepdims=True)
                    total = total / jnp.maximum(deep[r][h], 1.0)
                    state[comp, h, where : where + 1, :] = state[comp, h, where : where + 1, :] - total
    for comp in range(2):
        here = pl.ds(comp * ROWS, ROWS)
        started = state[comp, 0, pl.ds(8 + MARGIN, ROWS), :] - tall[pl.ds(comp * TALL + MARGIN, ROWS), :]
        flow[here, :] = -(started + mean[here, :])

    for half in range(2):
        slope[half, rows, :] = jnp.where(state[2, half, rows, :] > 0.0, SLOPE, 0.0)
        height[half, rows, :] = jnp.zeros((TALL, LANES), F32)

    halves = range(2)

    def subcycle(cut, step, carry):
        for tile in range(8 + cut, 8 + TALL - cut, 8):
            here, above, below = (pl.ds(tile + off, 8) for off in (0, 1, -1))
            east, west = lane_sides(*(state[2, h, here, :] * state[0, h, here, :] for h in halves))
            for h in halves:
                north = state[2, h, above, :] * state[1, h, above, :]
                south = state[2, h, below, :] * state[1, h, below, :]
                divergence = (east[h] - west[h]) + (north - south)
                height[h, here, :] = height[h, here, :] - slope[h, here, :] * divergence
        for tile in range(8 + cut, 8 + TALL - cut, 8):
            here, above, below = (pl.ds(tile + off, 8) for off in (0, 1, -1))
            east, west = lane_sides(height[0, here, :], height[1, here, :])
            for h in halves:
                factor = slope[h, here, :]
                state[0, h, here, :] = state[0, h, here, :] - factor * (east[h] - west[h])
                state[1, h, here, :] = state[1, h, here, :] - factor * (height[h, above, :] - height[h, below, :])
        return carry

    for cut, start, stop in ((0, 0, 1), (8, 1, 5), (16, 5, SUBCYCLES)):
        lax.fori_loop(start, stop, functools.partial(subcycle, cut), 0, unroll=True)
    for comp in range(2):
        here = pl.ds(comp * ROWS, ROWS)
        flow[here, :] = flow[here, :] + state[comp, 0, pl.ds(8 + MARGIN, ROWS), :]
    scale = 2.0 / RADIUS
    short = ROWS + 16
    base = MARGIN

    tiles = range(0, short, 8)

    def nine(read, tile):
        out = [[], []]
        for off in (0, 1, -1):
            a, b = (read(h, pl.ds(base + tile + off, 8)) for h in halves)
            east, west = lane_sides(a, b)
            for h, centre in enumerate((a, b)):
                out[h] += [centre, east[h], west[h]]
        return out

    for tile in tiles:
        here = pl.ds(tile, 8)
        around = nine(lambda h, where: state[2, h, where, :], tile)
        for h in halves:
            d = around[h][0]
            wet = d > 0.0
            total = jnp.where(wet, 0.05, 1.0)
            for n in range(1, 9):
                factor = 0.5 if n in (1, 2, 3, 6) else 0.25
                w = jnp.where(wet & (around[h][n] > 0.0), factor * (d + around[h][n]), 0.0)
                weights[n - 1, h, here, :] = scale * w
                total += w
            diagonal[h, here, :] = scale * (total - CENTRE)
            basis[0, h, pl.ds(base + tile, 8), :] = height[h, pl.ds(base + tile, 8), :]

    def applied(source, tile, count=2):
        around = nine(lambda h, where: basis[source, h, where, :], tile)
        out = []
        for h in range(count):
            here = pl.ds(tile, 8)
            total = diagonal[h, here, :] * around[h][0]
            for n in range(1, 9):
                total -= weights[n - 1, h, here, :] * around[h][n]
            out.append(total)
        return out

    for tile in tiles:
        for h, x in enumerate(applied(0, tile)):
            basis[1, h, pl.ds(base + tile, 8), :] = 0.5 * x

    for k in range(1, SOLVE_ITERS - 1):
        for tile in tiles:
            here = pl.ds(base + tile, 8)
            for h, x in enumerate(applied(k, tile)):
                basis[k + 1, h, here, :] = x - basis[k - 1, h, here, :]
    for tile in tiles[1:-1]:
        here = pl.ds(base + tile, 8)
        basis[SOLVE_ITERS, 0, here, :] = applied(SOLVE_ITERS - 1, tile, 1)[0] - basis[SOLVE_ITERS - 2, 0, here, :]
    lane = lane_ids(1)
    row = jnp.zeros((1, LANES), F32)
    mine = pl.ds(8 + MARGIN, ROWS)
    for n, (i, j) in enumerate(gram_pairs()):
        product = basis[i, 0, mine, :] * basis[j, 0, mine, :]
        row = jnp.where(lane == n, jnp.sum(jnp.sum(product, axis=0, keepdims=True), axis=1, keepdims=True), row)
    partial[...] = jnp.broadcast_to(row, partial.shape)
    for i in range(SOLVE_ITERS):
        for half in range(2):
            basis_out[i, half] = basis[i, half, pl.ds(base, short), :]


def solve_coefficients(gram):
    half = 0.5 * RADIUS

    def image_of(d):
        out = [None] * (len(d) + 1)

        def add(n, term):
            out[n] = term if out[n] is None else out[n] + term

        for j, value in enumerate(d):
            add(j, CENTRE * value)
            if j == 0:
                add(1, RADIUS * value)
            else:
                add(j + 1, half * value)
                add(j - 1, half * value)
        return out

    def inner(a, b):
        total = None
        for i, x in enumerate(a):
            for j, y in enumerate(b):
                term = x * y * gram[(min(i, j), max(i, j))]
                total = term if total is None else total + term
        return total

    one = jnp.ones((8, LANES), F32)
    residual, direction, surface = [one], [one], [0.0 * one]
    norm = gram[(0, 0)]
    for iteration in range(SOLVE_ITERS):
        image = image_of(direction)
        step = norm / inner(direction, image)
        surface = [a + step * b for a, b in zip(surface, direction)] + [0.0 * one]
        if iteration == SOLVE_ITERS - 1:
            break
        residual = [(residual[n] if n < len(residual) else 0.0) - step * x for n, x in enumerate(image)]
        fresh = inner(residual, residual)
        ratio = fresh / norm
        direction = [x + (ratio * direction[n] if n < len(direction) else 0.0) for n, x in enumerate(residual)]
        norm = fresh
    return surface[:SOLVE_ITERS]


def final_kernel(gathered, basis, flow, star, lev, velocity_out, surface_out, pad, change):
    sums = jnp.sum(gathered[...], axis=0, keepdims=True)
    lane = lane_ids(1)
    gram = {}
    for n, pair in enumerate(gram_pairs()):
        value = jnp.sum(jnp.where(lane == n, sums, 0.0), axis=1, keepdims=True)
        gram[pair] = jnp.broadcast_to(value, (8, LANES))
    coefficients = [c[0:1] for c in solve_coefficients(gram)]
    for half in range(2):
        total = coefficients[0] * basis[0, half]
        for i in range(1, SOLVE_ITERS):
            total += coefficients[i] * basis[i, half]
        pad[half] = total
    mine = pl.ds(8, ROWS)
    centre = pad[0, mine, :]
    ghost = pad[1, mine, :]
    surface_out[...] = centre
    lanes = lane_ids(ROWS)
    east = jnp.where(lanes == LANES - 1, turn(ghost, LANES - 1), turn(centre, LANES - 1))
    west = jnp.where(lanes == 0, turn(ghost, 1), turn(centre, 1))
    levels = lev[...]
    slope = jnp.where(levels > 0, SLOPE, 0.0)
    slopes = (east - west, pad[0, pl.ds(9, ROWS), :] - pad[0, pl.ds(7, ROWS), :])
    for comp in range(2):
        here = pl.ds(comp * ROWS, ROWS)
        change[comp] = flow[here, :] - slope * slopes[comp]


    def level_step(k, carry):
        wet = k < levels
        for comp in range(2):
            here = pl.ds(pl.multiple_of((comp * LEVELS + k) * ROWS, ROWS), ROWS)
            velocity_out[here, :] = star[here, :] + jnp.where(wet, change[comp], 0.0)
        return carry

    lax.fori_loop(0, LEVELS, level_step, 0, unroll=True)


def patch_kernel(star, col_patch, row_patch, out):
    lanes = lane_ids(ROWS)
    rims = (lanes < 2) | (lanes >= LANES - 2)
    ids = row_ids(8)

    def plane(p, carry):
        here = pl.ds(pl.multiple_of(p * ROWS, ROWS), ROWS)
        out[here, :] = star[here, :] - jnp.where(rims, turn(col_patch[...], 126 - 4 * p), 0.0)
        for first, pieces in ((ROWS - 8, ((7, 0), (6, 1))), (0, ((0, 2), (1, 3)))):
            here = pl.ds(pl.multiple_of(p * ROWS + first, 8), 8)
            x = out[here, :]
            for row, n in pieces:
                x = x - jnp.where(ids == row, row_patch[pl.ds(n * STRIP + p, 1), :], 0.0)
            out[here, :] = x
        return carry

    lax.fori_loop(0, PLANES, plane, 0, unroll=10)


def call(kernel, shapes, scratch, flops, *args, far=False):
    out = tuple(jax.ShapeDtypeStruct(s, F32) for s in shapes)
    moved = sum(4 * math.prod(a.shape) for a in args) + sum(4 * math.prod(s) for s in shapes)
    if far:
        args = [pltpu.with_memory_space_constraint(a, pltpu.HBM) for a in args]
    return pl.pallas_call(
        kernel,
        out_shape=out,
        in_specs=[pl.BlockSpec(memory_space=pltpu.HBM if far else pltpu.VMEM)] * len(args),
        scratch_shapes=[pltpu.VMEM(s, F32) if isinstance(s, tuple) else s for s in scratch],
        compiler_params=pltpu.CompilerParams(vmem_limit_bytes=32 * 1024 * 1024),
        cost_estimate=pl.CostEstimate(flops=flops, bytes_accessed=moved, transcendentals=0),
    )(*args)


def pair_tables(lon, lat):
    def index(i, j):
        return j * lat + i

    lat_a, lat_b, lon_a, lon_b = [], [], [], []
    for j in range(lon):
        for i in range(lat):
            lat_a.append((index(i, j), index(i ^ 1, j)))
            if i == lat - 1:
                lat_b.append((index(i, j), index(i, lon - 1 - j)))
            elif i > 0:
                lat_b.append((index(i, j), index(i + 1 if i % 2 else i - 1, j)))
            lon_a.append((index(i, j), index(i, j ^ 1)))
            lon_b.append((index(i, j), index(i, (j + 1 if j % 2 else j - 1) % lon)))
    return lat_a, lat_b, lon_a, lon_b


def per_device(lon, lat, tracers, velocity, active_levels, diffusivity, viscosity, ocean_depth, wind_forcing):
    lat_a, lat_b, lon_a, lon_b = pair_tables(lon, lat)

    def swap(x, pairs):
        return lax.ppermute(x, BOTH, pairs)

    block = (ROWS, LANES)
    tra = tracers.reshape(PLANES * ROWS, LANES)
    vel = velocity.reshape(PLANES * ROWS, LANES)
    wind = wind_forcing.reshape(2 * ROWS, LANES)
    rim = (RIMS, LANES)
    star, mean, fields, cols, north, south, send_a, send_b = call(
        block_kernel,
        [(PLANES * ROWS, LANES), (2 * ROWS, LANES), (3 * ROWS, LANES), block, rim, rim, (LAT_SEND, LANES), (LAT_SEND, LANES)],
        [(4,) + block, (4,) + block, (2,) + block, block, (PLANES * ROWS + 16, LANES), vel.shape, block, block, block, wind.shape,
         block, (PLANES * ROWS + 16, LANES),
         pltpu.VMEM(block, jnp.int32), pltpu.SemaphoreType.DMA((7,))],
        10**7,
        vel, tra, active_levels, viscosity, diffusivity, ocean_depth, wind,
        far=True,
    )
    got_a = swap(send_a, lat_a)
    got_b = swap(send_b, lat_b)
    tall, strips, tracer_rows, send_a, send_b = call(
        widen_kernel,
        [(4 * TALL, LANES), (8 * STRIP, LANES), (4 * STRIP, LANES), (LON_SEND, LANES), (LON_SEND, LANES)],
        [(TALL + 2 * STRIP, LANES)] * 2,
        10**6,
        fields, cols, diffusivity, north, south, got_b, got_a,
    )
    got_a = swap(send_a, lon_a)
    got_b = swap(send_b, lon_b)
    (tracers_out,) = call(
        tracer_kernel, [(PLANES * ROWS, LANES)], [block, (4,) + block, (4,) + block], 10**6,
        tra, active_levels, diffusivity, tracer_rows, got_b, got_a,
    )
    padded = (2, TALL + 16, LANES)
    short = (2, ROWS + 16, LANES)
    basis, flow, partial, col_patch, row_patch = call(
        surface_kernel,
        [(SOLVE_ITERS,) + short, (2 * ROWS, LANES), (lon * lat, LANES), block, (4 * STRIP, LANES)],
        [(3,) + padded, padded, padded, padded, (SOLVE_ITERS + 1,) + padded, (8,) + short, short],
        10**7,
        tall, strips, mean, got_b, got_a,
    )
    gathered = lax.all_to_all(partial, BOTH, 0, 0, tiled=True)
    (star,) = call(patch_kernel, [(PLANES * ROWS, LANES)], [], 10**6, star, col_patch, row_patch)
    velocity_out, surface = call(
        final_kernel, [(PLANES * ROWS, LANES), block],
        [short, (2,) + block], 10**6,
        gathered, basis, flow, star, active_levels,
    )
    return tracers_out.reshape(tracers.shape), velocity_out.reshape(velocity.shape), surface


def solution(mesh):
    placed = (
        P(None, None, "lat", "lon"),
        P(None, None, "lat", "lon"),
        P("lat", "lon"),
        P("lat", "lon"),
        P("lat", "lon"),
        P("lat", "lon"),
        P(None, "lat", "lon"),
    )
    return jax.shard_map(
        functools.partial(per_device, mesh.shape["lon"], mesh.shape["lat"]),
        mesh=mesh,
        in_specs=placed,
        out_specs=(P(None, None, "lat", "lon"), P(None, None, "lat", "lon"), P("lat", "lon")),
        check_vma=False,
    )
```

```python
import functools
import math

import jax
import jax.numpy as jnp
from jax import lax
from jax.experimental import pallas as pl
from jax.experimental.pallas import tpu as pltpu
from jax.sharding import PartitionSpec as P

SUBCYCLES = 8
SOLVE_ITERS = 4
LEVELS = 10
PLANES = 2 * LEVELS
ROWS = 64
LANES = 128
MARGIN = 24
TALL = ROWS + 2 * MARGIN
RIM = 32
SLOPE = 0.15
CENTRE = 5.0
RADIUS = 5.0
F32 = jnp.float32
BOTH = ("lon", "lat")

STRIP = 24
RIMS = 3 * STRIP
SENT = 20
FULL = 22
EDGE = 21
NEAR, NEXT, LAST, COLS = 3 * SENT, 3 * SENT + FULL, 3 * SENT + 2 * FULL, 128
LAT_SEND = COLS + MARGIN
LON_SEND = 2 * TALL
WIDE = 21


def lane_ids(rows):
    return lax.broadcasted_iota(jnp.int32, (rows, LANES), 1)


def row_ids(rows):
    return lax.broadcasted_iota(jnp.int32, (rows, LANES), 0)


def turn(x, shift):
    return pltpu.roll(x, shift, 1)


def pick(x, index):
    return jnp.take_along_axis(x, index, axis=1)


def flip_lanes(x, mask=LANES - 1):
    return pick(x, lane_ids(x.shape[0]) ^ mask)


def flip_rows(x):
    rows = x.shape[0]
    ids = row_ids(rows)
    for bit in range(3):
        step = 1 << bit
        x = jnp.where((ids & step) != 0, pltpu.roll(x, step, 0), pltpu.roll(x, rows - step, 0))
    return jnp.concatenate([x[r : r + 8] for r in range(rows - 8, -8, -8)], axis=0)


def odd(axis):
    return lax.rem(lax.axis_index(axis), 2) == 1


def at_fold():
    return lax.axis_index("lat") == lax.axis_size("lat") - 1


def shifted(x):
    rows = x.shape[0]
    return (turn(x, LANES - 1), turn(x, 1), pltpu.roll(x, rows - 1, 0), pltpu.roll(x, 1, 0))


def block_kernel(
    vel_far, tra_far, lev_far, visc_far, diff_far, depth_far, wind_far,
    star, mean, fields, cols, north, south, send_a, send_b,
    faces, face_levels, sums, turning, vel, tra, visc, diff, depth, wind, levels_kept, laps, lev, done,
):
    pairs = ((lev_far, lev), (visc_far, visc), (vel_far, vel), (tra_far, tra), (wind_far, wind), (depth_far, depth), (diff_far, diff))
    copies = [
        pltpu.make_async_copy(far, near.at[pl.ds(8, PLANES * ROWS)] if near is vel else near, done.at[n])
        for n, (far, near) in enumerate(pairs)
    ]
    for copy in copies:
        copy.start()
    for copy in copies[:2]:
        copy.wait()
    lanes = lane_ids(ROWS)
    ids = row_ids(ROWS)
    levels = lev[...].astype(F32)
    v = visc[...]
    inside = (lanes < LANES - 1, lanes > 0, ids < ROWS - 1, ids > 0)
    for n, (v_n, level_n) in enumerate(zip(shifted(v), shifted(levels))):
        faces[n] = 0.5 * (v + v_n)
        face_levels[n] = jnp.where(inside[n], jnp.minimum(levels, level_n), 0.0)
    row = (lax.axis_index("lat") * ROWS).astype(F32) + ids.astype(F32)
    turning[...] = 0.25 * jnp.sin(math.pi * ((row + 0.5) / (ROWS * lax.axis_size("lat")) - 0.5))
    sums[...] = jnp.zeros((2, ROWS, LANES), F32)
    levels_kept[...] = levels
    for padded in (vel, laps):
        padded[0:8, :] = jnp.zeros((8, LANES), F32)
        padded[PLANES * ROWS + 8 : PLANES * ROWS + 16, :] = jnp.zeros((8, LANES), F32)
    acc = jnp.where((lanes >> 2) == 20, turn(levels, 82), 0.0)
    cols[...] = jnp.where((lanes >> 2) == 21, turn(v, 86), acc)
    copies[2].wait()

    def lap_step(k, carry):
        level = k.astype(F32)
        open_faces = [level < face_levels[n] for n in range(4)]
        ones = [jnp.where(o, 1.0, 0.0) for o in open_faces]
        count = (ones[0] + ones[1]) + (ones[2] + ones[3])
        packed = cols[...]
        for comp in range(2):
            p = comp * LEVELS + k
            start = 8 + pl.multiple_of(p * ROWS, ROWS)
            x = vel[pl.ds(start, ROWS), :]
            around = (turn(x, LANES - 1), turn(x, 1), vel[pl.ds(start + 1, ROWS), :], vel[pl.ds(start - 1, ROWS), :])
            picked = [jnp.where(open_faces[n], around[n], 0.0) for n in range(4)]
            laps[pl.ds(start, ROWS), :] = (picked[0] + picked[1]) + (picked[2] + picked[3]) - count * x
            packed = jnp.where((lanes >> 2) == p, turn(x, 4 * p + 2), packed)
        cols[...] = packed
        return carry

    def star_step(k, carry):
        level = k.astype(F32)
        wet = level < levels_kept[...]
        weights = [jnp.where(level < face_levels[n], faces[n], 0.0) for n in range(4)]
        weight = (weights[0] + weights[1]) + (weights[2] + weights[3])
        starts = [8 + pl.multiple_of((comp * LEVELS + k) * ROWS, ROWS) for comp in range(2)]
        values = [vel[pl.ds(s, ROWS), :] for s in starts]
        for comp, x in enumerate(values):
            start = starts[comp]
            lap = laps[pl.ds(start, ROWS), :]
            around = (turn(lap, LANES - 1), turn(lap, 1), laps[pl.ds(start + 1, ROWS), :], laps[pl.ds(start - 1, ROWS), :])
            terms = [weights[n] * around[n] for n in range(4)]
            second = (terms[0] + terms[1]) + (terms[2] + terms[3]) - weight * lap
            rotated = values[1] if comp == 0 else -values[0]
            out = jnp.where(wet, x - second + turning[...] * rotated, 0.0)
            star[pl.ds(pl.multiple_of((comp * LEVELS + k) * ROWS, ROWS), ROWS), :] = out
            sums[comp] += out
        return carry

    lax.fori_loop(0, LEVELS, lap_step, 0, unroll=10)
    lax.fori_loop(0, LEVELS, star_step, 0, unroll=10)
    for copy in copies[3:]:
        copy.wait()

    def tracer_step(p, acc):
        t = tra[pl.ds(pl.multiple_of(p * ROWS, ROWS), ROWS), :]
        return jnp.where((lanes >> 1) == 44 + p, turn(t, lax.rem(89 + 2 * p, LANES)), acc)

    cols[...] = lax.fori_loop(0, PLANES, tracer_step, cols[...], unroll=True)
    ocean = levels > 0.0
    for comp in range(2):
        here = pl.ds(comp * ROWS, ROWS)
        column_mean = sums[comp] / jnp.maximum(levels, 1.0)
        mean[here, :] = column_mean
        fields[here, :] = column_mean + jnp.where(ocean, wind[here, :], 0.0)
    fields[pl.ds(2 * ROWS, ROWS), :] = jnp.where(ocean, depth[...], 0.0)
    for edge, step, out in ((ROWS - 1, -1, north), (0, 1, south)):
        out[...] = jnp.zeros((RIMS, LANES), F32)
        for d in range(2):
            r = edge + d * step
            out[pl.ds(d * STRIP, PLANES), :] = vel[pl.ds(8 + r, PLANES, stride=ROWS), :]
            out[pl.ds(d * STRIP + 20, 1), :] = levels[r : r + 1]
            out[pl.ds(d * STRIP + 21, 1), :] = visc[pl.ds(r, 1), :]
        out[pl.ds(2 * STRIP, PLANES), :] = tra[pl.ds(edge, PLANES, stride=ROWS), :]
        out[pl.ds(2 * STRIP + 20, 1), :] = diff[pl.ds(edge, 1), :]
    lat_odd = odd("lat")

    def put(start, up, down):
        here = pl.ds(start, up.shape[0])
        send_a[here, :] = jnp.where(lat_odd, down, up)
        send_b[here, :] = jnp.where(lat_odd, up, down)

    for f in range(3):
        put(f * SENT, fields[pl.ds((f + 1) * ROWS - SENT, SENT), :], fields[pl.ds(f * ROWS, SENT), :])
    for start, first, count in ((NEAR, 0, FULL), (NEXT, STRIP, FULL), (LAST, 2 * STRIP, EDGE)):
        put(start, north[pl.ds(first, count), :], south[pl.ds(first, count), :])
    put(COLS, cols[ROWS - MARGIN : ROWS, :], cols[0:MARGIN, :])
    for send in (send_a, send_b):
        send[LAST + EDGE : COLS, :] = jnp.zeros((COLS - LAST - EDGE, LANES), F32)

    @pl.when(at_fold())
    def _():
        for f in range(3):
            turned = flip_rows(flip_lanes(fields[pl.ds((f + 1) * ROWS - MARGIN, MARGIN), :]))[0:SENT]
            send_b[pl.ds(f * SENT, SENT), :] = turned if f == 2 else -turned
        turned = flip_lanes(north[...])
        r = row_ids(RIMS)
        is_velocity = (r < PLANES) | ((r >= STRIP) & (r < STRIP + PLANES))
        turned = jnp.where(is_velocity, -turned, turned)
        for start, first, count in ((NEAR, 0, FULL), (NEXT, STRIP, FULL), (LAST, 2 * STRIP, EDGE)):
            send_b[pl.ds(start, count), :] = turned[first : first + count]
        turned = flip_rows(flip_lanes(cols[ROWS - MARGIN : ROWS, :], 3))
        send_b[pl.ds(COLS, MARGIN), :] = jnp.where(lane_ids(MARGIN) < 4 * PLANES, -turned, turned)


def widen_kernel(fields, cols, diff, north, south, recv_b, recv_a, tall, strips, tracer_rows, send_a, send_b, east, west):
    lat_odd = odd("lat")
    lon_odd = odd("lon")
    def received(start, count):
        here = pl.ds(start, count)
        got_a = recv_a[here, :]
        got_b = recv_b[here, :]
        return jnp.where(lat_odd, got_b, got_a), jnp.where(lat_odd, got_a, got_b)

    lanes = lane_ids(TALL)
    acc_east = jnp.zeros((TALL, LANES), F32)
    acc_west = jnp.zeros((TALL, LANES), F32)
    for f in range(3):
        from_north, from_south = received(f * SENT, SENT)
        unused = jnp.zeros((MARGIN - SENT, LANES), F32)
        tall[pl.ds(f * TALL, MARGIN - SENT), :] = unused
        tall[pl.ds(f * TALL + MARGIN - SENT, SENT), :] = from_south
        tall[pl.ds(f * TALL + MARGIN, ROWS), :] = fields[pl.ds(f * ROWS, ROWS), :]
        tall[pl.ds(f * TALL + MARGIN + ROWS, SENT), :] = from_north
        tall[pl.ds(f * TALL + MARGIN + ROWS + SENT, MARGIN - SENT), :] = unused
        x = tall[pl.ds(f * TALL, TALL), :]
        here = (lanes >= f * WIDE) & (lanes < (f + 1) * WIDE)
        acc_east = jnp.where(here, turn(x, (f + 1) * WIDE), acc_east)
        acc_west = jnp.where(here, turn(x, f * WIDE), acc_west)
    from_north, from_south = received(COLS, MARGIN)
    tall[pl.ds(3 * TALL, MARGIN), :] = from_south
    tall[pl.ds(3 * TALL + MARGIN, ROWS), :] = cols[...]
    tall[pl.ds(3 * TALL + MARGIN + ROWS, MARGIN), :] = from_north
    for out, acc, shift in ((east, acc_east, 64), (west, acc_west, 63)):
        out[...] = acc
        out[pl.ds(MARGIN, ROWS), :] = jnp.where(lane_ids(ROWS) == 63, turn(diff[...], shift), acc[MARGIN : MARGIN + ROWS])
    near, next_to, last = received(NEAR, FULL), received(NEXT, FULL), received(LAST, EDGE)
    unused = jnp.zeros((STRIP - FULL, LANES), F32)
    group = lane_ids(STRIP) >> 5
    for s, own in enumerate((north, south)):
        pieces = (
            jnp.concatenate([next_to[s], unused], axis=0),
            jnp.concatenate([near[s], unused], axis=0),
            own[0:STRIP, :],
            own[STRIP : 2 * STRIP, :],
        )
        for r, x in enumerate(pieces):
            strips[pl.ds((4 * s + r) * STRIP, STRIP), :] = x
            block, g = divmod(4 * s + r, 2)
            here = pl.ds(block * STRIP, STRIP)
            east[here, :] = jnp.where(group == 2 + g, turn(x, (96 + 32 * g) % LANES), east[here, :])
            west[here, :] = jnp.where(group == 2 + g, turn(x, 64 + 32 * g), west[here, :])
        tracer_rows[pl.ds(2 * s * STRIP, EDGE), :] = last[s]
        tracer_rows[pl.ds((2 * s + 1) * STRIP, STRIP), :] = pieces[1]
    k = tall[pl.ds(3 * TALL, TALL), :]
    send_a[pl.ds(0, TALL), :] = k
    send_b[pl.ds(0, TALL), :] = k
    rest = pl.ds(TALL, TALL)
    e, w = east[...], west[...]
    send_a[rest, :] = jnp.where(lon_odd, w, e)
    send_b[rest, :] = jnp.where(lon_odd, e, w)


def tracer_kernel(tra, lev, diff, tracer_rows, recv_b, recv_a, out, swap, faces, face_levels):
    is_odd = odd("lon")
    lanes = lane_ids(ROWS)
    ids = row_ids(ROWS)

    def received(start):
        here = pl.ds(start + MARGIN, ROWS)
        got_a = recv_a[here, :]
        got_b = recv_b[here, :]
        return jnp.where(is_odd, got_b, got_a), jnp.where(is_odd, got_a, got_b)

    east_cols, west_cols = received(0)
    east_rest, west_rest = received(TALL)
    swap[...] = jnp.where((lanes & 1) == 0, turn(east_cols, LANES - 1), turn(west_cols, 1))

    def sides(x, halo, row):
        east, west, north, south = shifted(x)
        return (
            jnp.where(lanes == LANES - 1, halo, east),
            jnp.where(lanes == 0, halo, west),
            jnp.where(ids == ROWS - 1, tracer_rows[pl.ds(row, 1), :], north),
            jnp.where(ids == 0, tracer_rows[pl.ds(row + 2 * STRIP, 1), :], south),
        )

    level = lev[...].astype(F32)
    level_halo = jnp.where(lanes == LANES - 1, turn(east_cols, 45), turn(west_cols, 47))
    d = diff[...]
    d_halo = jnp.where(lanes == LANES - 1, turn(east_rest, 64), turn(west_rest, 65))
    for n, other in enumerate(sides(level, level_halo, STRIP + 20)):
        face_levels[n] = jnp.minimum(level, other)
    for n, other in enumerate(sides(d, d_halo, 20)):
        faces[n] = 0.5 * (d + other)

    def level_step(k, carry):
        weights = [jnp.where(k.astype(F32) < face_levels[n], faces[n], 0.0) for n in range(4)]
        for comp in range(2):
            p = comp * LEVELS + k
            here = pl.ds(pl.multiple_of(p * ROWS, ROWS), ROWS)
            x = tra[here, :]
            around = sides(x, turn(swap[...], 39 - 2 * p), p)
            total = weights[0] * (around[0] - x)
            for n in range(1, 4):
                total += weights[n] * (around[n] - x)
            out[here, :] = x + total
        return carry

    lax.fori_loop(0, LEVELS, level_step, 0, unroll=2)


def column_strip(strip):
    rows = strip.shape[0]
    lanes = lane_ids(rows)
    ids = row_ids(rows)
    phase = lanes & 3
    group = lanes >> 2

    levels = pick(strip, phase + 80)
    v = pick(strip, phase + 84)
    number = jnp.where(group >= LEVELS, group - LEVELS, group).astype(F32)
    wet = jnp.where((number < levels) & (group < PLANES), 1.0, 0.0)
    x = jnp.where(group < PLANES, strip, 0.0)
    open_e = wet * turn(wet, LANES - 1)
    wet_n = pltpu.roll(wet, rows - 1, 0)
    open_n = wet * wet_n
    flux_e = open_e * (turn(x, LANES - 1) - x)
    flux_n = open_n * (pltpu.roll(x, rows - 1, 0) - x)
    lap = flux_e - turn(flux_e, 1) + flux_n - pltpu.roll(flux_n, 1, 0)
    seam = jnp.where(phase == 1, flux_e, 0.0)
    added = seam - turn(seam, 1)
    base = jnp.where(phase == 1, lap, added)
    other = jnp.where(phase == 1, turn(lap, LANES - 1), turn(added, LANES - 1))
    face = 0.5 * (v + turn(v, LANES - 1)) * open_e
    flux_e = jnp.where(phase == 3, 0.0, face * (other - base))
    in_block = (ids != MARGIN - 1) & (ids != MARGIN + ROWS - 1)
    face = jnp.where(in_block, 0.5 * (v + pltpu.roll(v, rows - 1, 0)) * open_n, 0.0)
    flux_n = face * (pltpu.roll(added, rows - 1, 0) - added)
    second = flux_e - turn(flux_e, 1) + flux_n - pltpu.roll(flux_n, 1, 0)
    return wet * second


def gram_pairs():
    return [(i, j) for i in range(SOLVE_ITERS) for j in range(i, SOLVE_ITERS + 1)]


def surface_kernel(
    tall, strips, mean, recv_b, recv_a,
    basis_out, flow, partial, col_patch, row_patch,
    state, height, heights, transport, force, faces, slope, basis, weights, diagonal,
):
    is_odd = odd("lon")
    rows = pl.ds(8, TALL)
    lanes = lane_ids(TALL)

    def received(start, count):
        here = pl.ds(start, count)
        got_a = recv_a[here, :]
        got_b = recv_b[here, :]
        return jnp.where(is_odd, got_b, got_a), jnp.where(is_odd, got_a, got_b)

    def ghost(east, west, first, count):
        return jnp.where(
            lane_ids(east.shape[0]) < 64, turn(east, (LANES - first) % LANES), turn(west, LANES - first - count)
        )

    from_east, from_west = received(TALL, TALL)
    for f in range(3):
        state[f, 0, rows, :] = tall[pl.ds(f * TALL, TALL), :]
        state[f, 1, rows, :] = ghost(from_east, from_west, f * WIDE, WIDE)
    last = lanes == LANES - 1
    first = lanes == 0

    def lane_sides(a, b):
        n = a.shape[0]
        ea, eb, wa, wb = turn(a, LANES - 1), turn(b, LANES - 1), turn(a, 1), turn(b, 1)
        return (
            (jnp.where(last[0:n], eb, ea), jnp.where(last[0:n], ea, eb)),
            (jnp.where(first[0:n], wb, wa), jnp.where(first[0:n], wa, wb)),
        )

    own = tall[pl.ds(3 * TALL, TALL), :]
    phase = lanes & 3
    from_east, from_west = received(0, TALL)
    to_east = column_strip(jnp.where(phase < 2, own, from_east))
    to_west = column_strip(jnp.where(phase < 2, from_west, own))
    changes = (jnp.where(phase < 2, to_east, to_west), jnp.where(phase < 2, to_west, to_east))
    deep = (own, jnp.where(phase < 2, from_west, from_east))
    col_patch[...] = changes[0][MARGIN : MARGIN + ROWS]
    to_lane = lax.broadcasted_iota(jnp.int32, (LANES, 2 * LANES), 1)
    from_lane = lax.broadcasted_iota(jnp.int32, (LANES, 2 * LANES), 0)
    column = to_lane & (LANES - 1)
    comp_of = jnp.where(from_lane < 4 * LEVELS, 0, 1)
    chosen = (
        ((column < 2) | (column >= LANES - 2))
        & ((from_lane & 3) == ((to_lane + 2) & 3))
        & (comp_of == (to_lane >> 7))
        & (from_lane < 4 * PLANES)
    )
    chooser = jnp.where(chosen, 1.0, 0.0)
    for half in range(2):
        total = lax.dot_general(
            changes[half], chooser, (((1,), (0,)), ((), ())),
            precision=lax.Precision.HIGHEST, preferred_element_type=F32,
        )
        share = 1.0 / jnp.maximum(pick(deep[half], ((lanes + 2) & 3) + 80), 1.0)
        for comp in range(2):
            change = total[:, comp * LANES : (comp + 1) * LANES] * share
            state[comp, half, rows, :] = state[comp, half, rows, :] - change
    number = lax.broadcasted_iota(jnp.int32, (STRIP, LANES), 0)
    level_of_row = jnp.where(number >= LEVELS, number - LEVELS, number).astype(F32)
    is_plane = number < PLANES
    not_last = lane_ids(STRIP) < LANES - 1
    for s in range(2):
        x, wet, v, deep = [], [], [], []
        for r in range(4):
            centre = strips[pl.ds((4 * s + r) * STRIP, STRIP), :]
            block, g = divmod(4 * s + r, 2)
            both = (centre, ghost(*received(TALL + block * STRIP, STRIP), 64 + 32 * g, 32))
            deep.append([b[20:21] for b in both])
            v.append([jnp.broadcast_to(b[21:22], (STRIP, LANES)) for b in both])
            wet.append([jnp.where(is_plane & (level_of_row < b[20:21]), 1.0, 0.0) for b in both])
            x.append([jnp.where(is_plane, b, 0.0) for b in both])
        half_range = range(2)
        lap = {}
        added = {}
        seam = [wet[1][h] * wet[2][h] * (x[2][h] - x[1][h]) for h in half_range]
        added[1] = seam
        added[2] = [-t for t in seam]
        along = {}
        for r in (1, 2):
            x_e = lane_sides(*x[r])[0]
            wet_e = lane_sides(*wet[r])[0]
            v_e = lane_sides(*v[r])[0]
            added_e = lane_sides(*added[r])[0]
            open_e = [wet[r][h] * wet_e[h] for h in half_range]
            edge = [open_e[h] * (x_e[h] - x[r][h]) for h in half_range]
            edge_w = lane_sides(*edge)[1]
            lap[r] = [
                edge[h]
                - edge_w[h]
                + wet[r][h] * (wet[r + 1][h] * (x[r + 1][h] - x[r][h]) + wet[r - 1][h] * (x[r - 1][h] - x[r][h]))
                for h in half_range
            ]
            edge = [
                jnp.where(not_last, 0.5 * (v[r][h] + v_e[h]) * open_e[h] * (added_e[h] - added[r][h]), 0.0)
                for h in half_range
            ]
            edge_w = lane_sides(*edge)[1]
            along[r] = [edge[h] - edge_w[h] for h in half_range]
        for h in half_range:
            face = [0.5 * (v[r][h] + v[r + 1][h]) * wet[r][h] * wet[r + 1][h] for r in range(3)]
            across = (face[0] * added[1][h], face[1] * (lap[2][h] - lap[1][h]), -face[2] * added[2][h])
            second = (
                across[0],
                across[1] - across[0] + along[1][h],
                across[2] - across[1] + along[2][h],
                -across[2],
            )
            for r in range(4):
                change = wet[r][h] * second[r]
                if h == 0 and r >= 2:
                    row_patch[pl.ds((2 * s + r - 2) * STRIP, STRIP), :] = change
                where = 8 + MARGIN + ((ROWS + 1 - r) if s == 0 else (r - 2))
                for comp in range(2):
                    mine = (number >= comp * LEVELS) & (number < (comp + 1) * LEVELS)
                    total = jnp.sum(jnp.where(mine, change, 0.0), axis=0, keepdims=True)
                    total = total / jnp.maximum(deep[r][h], 1.0)
                    state[comp, h, where : where + 1, :] = state[comp, h, where : where + 1, :] - total
    for comp in range(2):
        here = pl.ds(comp * ROWS, ROWS)
        started = state[comp, 0, pl.ds(8 + MARGIN, ROWS), :] - tall[pl.ds(comp * TALL + MARGIN, ROWS), :]
        flow[here, :] = -(started + mean[here, :])

    halves = range(2)
    ahead = lanes[0:8] >= LANES - 2
    behind = lanes[0:8] < 2

    def far_sides(a, b):
        ea, eb, wa, wb = turn(a, LANES - 2), turn(b, LANES - 2), turn(a, 2), turn(b, 2)
        return (
            (jnp.where(ahead, eb, ea), jnp.where(ahead, ea, eb)),
            (jnp.where(behind, wb, wa), jnp.where(behind, wa, wb)),
        )

    for half in halves:
        d = state[2, half, rows, :]
        slope[half, rows, :] = jnp.where(d > 0.0, SLOPE, 0.0)
        force[half, rows, :] = SLOPE * d
        transport[half, rows, :] = d * state[1, half, rows, :]
    tiles = range(8, 8 + TALL, 8)
    for tile in tiles:
        here, above, below = (pl.ds(tile + off, 8) for off in (0, 1, -1))
        east, west = lane_sides(force[0, here, :], force[1, here, :])
        for h in halves:
            faces[0, h, here, :] = east[h]
            faces[1, h, here, :] = west[h]
            faces[2, h, here, :] = force[h, above, :]
            faces[3, h, here, :] = force[h, below, :]
    for tile in tiles:
        here, above, below = (pl.ds(tile + off, 8) for off in (0, 1, -1))
        east, west = lane_sides(*(state[2, h, here, :] * state[0, h, here, :] for h in halves))
        for h in halves:
            divergence = (east[h] - west[h]) + (transport[h, above, :] - transport[h, below, :])
            force[h, here, :] = divergence
            new = -slope[h, here, :] * divergence
            heights[0, h, here, :] = new
            height[h, here, :] = new
    for step in range(1, SUBCYCLES):
        cut = min(8 * ((6 + 2 * step) // 8), 16)
        now, later = heights.at[(step - 1) % 2], heights.at[step % 2]
        for tile in range(8 + cut, 8 + TALL - cut, 8):
            here, above, below = (pl.ds(tile + off, 8) for off in (0, 2, -2))
            centres = [now[h, here, :] for h in halves]
            east, west = far_sides(*centres)
            for h, x in enumerate(centres):
                along = faces[0, h, here, :] * (east[h] - x) - faces[1, h, here, :] * (x - west[h])
                across = faces[2, h, here, :] * (now[h, above, :] - x) - faces[3, h, here, :] * (x - now[h, below, :])
                change = force[h, here, :] - (along + across)
                force[h, here, :] = change
                new = x - slope[h, here, :] * change
                later[h, here, :] = new
                height[h, here, :] = height[h, here, :] + new
    mine = pl.ds(8 + MARGIN, ROWS)
    east, west = lane_sides(height[0, mine, :], height[1, mine, :])
    inner = slope[0, mine, :]
    north, south = (height[0, pl.ds(8 + MARGIN + off, ROWS), :] for off in (1, -1))
    for comp, gradient in enumerate((east[0] - west[0], north - south)):
        here = pl.ds(comp * ROWS, ROWS)
        flow[here, :] = flow[here, :] + (state[comp, 0, mine, :] - inner * gradient)
    final = heights.at[(SUBCYCLES - 1) % 2]
    scale = 2.0 / RADIUS
    short = ROWS + 16
    base = MARGIN

    tiles = range(0, short, 8)

    def nine(read, tile):
        out = [[], []]
        for off in (0, 1, -1):
            a, b = (read(h, pl.ds(base + tile + off, 8)) for h in halves)
            east, west = lane_sides(a, b)
            for h, centre in enumerate((a, b)):
                out[h] += [centre, east[h], west[h]]
        return out

    for tile in tiles:
        here = pl.ds(tile, 8)
        around = nine(lambda h, where: state[2, h, where, :], tile)
        for h in halves:
            d = around[h][0]
            wet = d > 0.0
            total = jnp.where(wet, 0.05, 1.0)
            for n in range(1, 9):
                factor = 0.5 if n in (1, 2, 3, 6) else 0.25
                w = jnp.where(wet & (around[h][n] > 0.0), factor * (d + around[h][n]), 0.0)
                weights[n - 1, h, here, :] = scale * w
                total += w
            diagonal[h, here, :] = scale * (total - CENTRE)
            basis[0, h, pl.ds(base + tile, 8), :] = final[h, pl.ds(base + tile, 8), :]

    def applied(source, tile, count=2):
        around = nine(lambda h, where: basis[source, h, where, :], tile)
        out = []
        for h in range(count):
            here = pl.ds(tile, 8)
            terms = [weights[n - 1, h, here, :] * around[h][n] for n in range(1, 9)]
            while len(terms) > 1:
                terms = [a + b for a, b in zip(terms[::2], terms[1::2])]
            out.append(diagonal[h, here, :] * around[h][0] - terms[0])
        return out

    for tile in tiles:
        for h, x in enumerate(applied(0, tile)):
            basis[1, h, pl.ds(base + tile, 8), :] = 0.5 * x

    for k in range(1, SOLVE_ITERS - 1):
        for tile in tiles:
            here = pl.ds(base + tile, 8)
            for h, x in enumerate(applied(k, tile)):
                basis[k + 1, h, here, :] = x - basis[k - 1, h, here, :]
    for tile in tiles[1:-1]:
        here = pl.ds(base + tile, 8)
        basis[SOLVE_ITERS, 0, here, :] = applied(SOLVE_ITERS - 1, tile, 1)[0] - basis[SOLVE_ITERS - 2, 0, here, :]
    lane = lane_ids(1)
    row = jnp.zeros((1, LANES), F32)
    mine = pl.ds(8 + MARGIN, ROWS)
    for n, (i, j) in enumerate(gram_pairs()):
        product = basis[i, 0, mine, :] * basis[j, 0, mine, :]
        row = jnp.where(lane == n, jnp.sum(jnp.sum(product, axis=0, keepdims=True), axis=1, keepdims=True), row)
    partial[...] = jnp.broadcast_to(row, partial.shape)
    for i in range(SOLVE_ITERS):
        for half in range(2):
            basis_out[i, half] = basis[i, half, pl.ds(base, short), :]


def solve_coefficients(gram):
    half = 0.5 * RADIUS

    def image_of(d):
        out = [None] * (len(d) + 1)

        def add(n, term):
            out[n] = term if out[n] is None else out[n] + term

        for j, value in enumerate(d):
            add(j, CENTRE * value)
            if j == 0:
                add(1, RADIUS * value)
            else:
                add(j + 1, half * value)
                add(j - 1, half * value)
        return out

    def inner(a, b):
        total = None
        for i, x in enumerate(a):
            for j, y in enumerate(b):
                term = x * y * gram[(min(i, j), max(i, j))]
                total = term if total is None else total + term
        return total

    one = jnp.ones((8, LANES), F32)
    residual, direction, surface = [one], [one], [0.0 * one]
    norm = gram[(0, 0)]
    for iteration in range(SOLVE_ITERS):
        image = image_of(direction)
        step = norm / inner(direction, image)
        surface = [a + step * b for a, b in zip(surface, direction)] + [0.0 * one]
        if iteration == SOLVE_ITERS - 1:
            break
        residual = [(residual[n] if n < len(residual) else 0.0) - step * x for n, x in enumerate(image)]
        fresh = inner(residual, residual)
        ratio = fresh / norm
        direction = [x + (ratio * direction[n] if n < len(direction) else 0.0) for n, x in enumerate(residual)]
        norm = fresh
    return surface[:SOLVE_ITERS]


def final_kernel(gathered, basis, flow, star, lev, velocity_out, surface_out, pad, change):
    sums = jnp.sum(gathered[...], axis=0, keepdims=True)
    lane = lane_ids(1)
    gram = {}
    for n, pair in enumerate(gram_pairs()):
        value = jnp.sum(jnp.where(lane == n, sums, 0.0), axis=1, keepdims=True)
        gram[pair] = jnp.broadcast_to(value, (8, LANES))
    coefficients = [c[0:1] for c in solve_coefficients(gram)]
    for half in range(2):
        total = coefficients[0] * basis[0, half]
        for i in range(1, SOLVE_ITERS):
            total += coefficients[i] * basis[i, half]
        pad[half] = total
    mine = pl.ds(8, ROWS)
    centre = pad[0, mine, :]
    ghost = pad[1, mine, :]
    surface_out[...] = centre
    lanes = lane_ids(ROWS)
    east = jnp.where(lanes == LANES - 1, turn(ghost, LANES - 1), turn(centre, LANES - 1))
    west = jnp.where(lanes == 0, turn(ghost, 1), turn(centre, 1))
    levels = lev[...]
    slope = jnp.where(levels > 0, SLOPE, 0.0)
    slopes = (east - west, pad[0, pl.ds(9, ROWS), :] - pad[0, pl.ds(7, ROWS), :])
    for comp in range(2):
        here = pl.ds(comp * ROWS, ROWS)
        change[comp] = flow[here, :] - slope * slopes[comp]


    def level_step(k, carry):
        wet = k < levels
        for comp in range(2):
            here = pl.ds(pl.multiple_of((comp * LEVELS + k) * ROWS, ROWS), ROWS)
            velocity_out[here, :] = star[here, :] + jnp.where(wet, change[comp], 0.0)
        return carry

    lax.fori_loop(0, LEVELS, level_step, 0, unroll=True)


def patch_kernel(star, col_patch, row_patch, out):
    lanes = lane_ids(ROWS)
    rims = (lanes < 2) | (lanes >= LANES - 2)
    ids = row_ids(8)

    def plane(p, carry):
        here = pl.ds(pl.multiple_of(p * ROWS, ROWS), ROWS)
        out[here, :] = star[here, :] - jnp.where(rims, turn(col_patch[...], 126 - 4 * p), 0.0)
        for first, pieces in ((ROWS - 8, ((7, 0), (6, 1))), (0, ((0, 2), (1, 3)))):
            here = pl.ds(pl.multiple_of(p * ROWS + first, 8), 8)
            x = out[here, :]
            for row, n in pieces:
                x = x - jnp.where(ids == row, row_patch[pl.ds(n * STRIP + p, 1), :], 0.0)
            out[here, :] = x
        return carry

    lax.fori_loop(0, PLANES, plane, 0, unroll=10)


def call(kernel, shapes, scratch, flops, *args, far=False):
    out = tuple(jax.ShapeDtypeStruct(s, F32) for s in shapes)
    moved = sum(4 * math.prod(a.shape) for a in args) + sum(4 * math.prod(s) for s in shapes)
    if far:
        args = [pltpu.with_memory_space_constraint(a, pltpu.HBM) for a in args]
    return pl.pallas_call(
        kernel,
        out_shape=out,
        in_specs=[pl.BlockSpec(memory_space=pltpu.HBM if far else pltpu.VMEM)] * len(args),
        scratch_shapes=[pltpu.VMEM(s, F32) if isinstance(s, tuple) else s for s in scratch],
        compiler_params=pltpu.CompilerParams(vmem_limit_bytes=32 * 1024 * 1024),
        cost_estimate=pl.CostEstimate(flops=flops, bytes_accessed=moved, transcendentals=0),
    )(*args)


def pair_tables(lon, lat):
    def index(i, j):
        return j * lat + i

    lat_a, lat_b, lon_a, lon_b = [], [], [], []
    for j in range(lon):
        for i in range(lat):
            lat_a.append((index(i, j), index(i ^ 1, j)))
            if i == lat - 1:
                lat_b.append((index(i, j), index(i, lon - 1 - j)))
            elif i > 0:
                lat_b.append((index(i, j), index(i + 1 if i % 2 else i - 1, j)))
            lon_a.append((index(i, j), index(i, j ^ 1)))
            lon_b.append((index(i, j), index(i, (j + 1 if j % 2 else j - 1) % lon)))
    return lat_a, lat_b, lon_a, lon_b


def per_device(lon, lat, tracers, velocity, active_levels, diffusivity, viscosity, ocean_depth, wind_forcing):
    lat_a, lat_b, lon_a, lon_b = pair_tables(lon, lat)

    def swap(x, pairs):
        return lax.ppermute(x, BOTH, pairs)

    block = (ROWS, LANES)
    tra = tracers.reshape(PLANES * ROWS, LANES)
    vel = velocity.reshape(PLANES * ROWS, LANES)
    wind = wind_forcing.reshape(2 * ROWS, LANES)
    rim = (RIMS, LANES)
    star, mean, fields, cols, north, south, send_a, send_b = call(
        block_kernel,
        [(PLANES * ROWS, LANES), (2 * ROWS, LANES), (3 * ROWS, LANES), block, rim, rim, (LAT_SEND, LANES), (LAT_SEND, LANES)],
        [(4,) + block, (4,) + block, (2,) + block, block, (PLANES * ROWS + 16, LANES), vel.shape, block, block, block, wind.shape,
         block, (PLANES * ROWS + 16, LANES),
         pltpu.VMEM(block, jnp.int32), pltpu.SemaphoreType.DMA((7,))],
        10**7,
        vel, tra, active_levels, viscosity, diffusivity, ocean_depth, wind,
        far=True,
    )
    got_a = swap(send_a, lat_a)
    got_b = swap(send_b, lat_b)
    tall, strips, tracer_rows, send_a, send_b = call(
        widen_kernel,
        [(4 * TALL, LANES), (8 * STRIP, LANES), (4 * STRIP, LANES), (LON_SEND, LANES), (LON_SEND, LANES)],
        [(TALL, LANES)] * 2,
        10**6,
        fields, cols, diffusivity, north, south, got_b, got_a,
    )
    got_a = swap(send_a, lon_a)
    got_b = swap(send_b, lon_b)
    (tracers_out,) = call(
        tracer_kernel, [(PLANES * ROWS, LANES)], [block, (4,) + block, (4,) + block], 10**6,
        tra, active_levels, diffusivity, tracer_rows, got_b, got_a,
    )
    padded = (2, TALL + 16, LANES)
    short = (2, ROWS + 16, LANES)
    basis, flow, partial, col_patch, row_patch = call(
        surface_kernel,
        [(SOLVE_ITERS,) + short, (2 * ROWS, LANES), (lon * lat, LANES), block, (4 * STRIP, LANES)],
        [(3,) + padded, padded, (2,) + padded, padded, padded, (4,) + padded, padded, (SOLVE_ITERS + 1,) + padded, (8,) + short, short],
        10**7,
        tall, strips, mean, got_b, got_a,
    )
    gathered = lax.all_to_all(partial, BOTH, 0, 0, tiled=True)
    (star,) = call(patch_kernel, [(PLANES * ROWS, LANES)], [], 10**6, star, col_patch, row_patch)
    velocity_out, surface = call(
        final_kernel, [(PLANES * ROWS, LANES), block],
        [short, (2,) + block], 10**6,
        gathered, basis, flow, star, active_levels,
    )
    return tracers_out.reshape(tracers.shape), velocity_out.reshape(velocity.shape), surface


def solution(mesh):
    placed = (
        P(None, None, "lat", "lon"),
        P(None, None, "lat", "lon"),
        P("lat", "lon"),
        P("lat", "lon"),
        P("lat", "lon"),
        P("lat", "lon"),
        P(None, "lat", "lon"),
    )
    return jax.shard_map(
        functools.partial(per_device, mesh.shape["lon"], mesh.shape["lat"]),
        mesh=mesh,
        in_specs=placed,
        out_specs=(P(None, None, "lat", "lon"), P(None, None, "lat", "lon"), P("lat", "lon")),
        check_vma=False,
    )
```

```python
import functools
import math

import jax
import jax.numpy as jnp
from jax import lax
from jax.experimental import pallas as pl
from jax.experimental.pallas import tpu as pltpu
from jax.sharding import PartitionSpec as P

SUBCYCLES = 8
SOLVE_ITERS = 4
LEVELS = 10
PLANES = 2 * LEVELS
ROWS = 64
LANES = 128
MARGIN = 24
TALL = ROWS + 2 * MARGIN
RIM = 32
SLOPE = 0.15
CENTRE = 5.0
RADIUS = 5.0
F32 = jnp.float32
BOTH = ("lon", "lat")

STRIP = 24
RIMS = 3 * STRIP
SENT = 20
FULL = 22
EDGE = 21
NEAR, NEXT, LAST, COLS = 3 * SENT, 3 * SENT + FULL, 3 * SENT + 2 * FULL, 128
LAT_SEND = COLS + MARGIN
LON_SEND = 2 * TALL
WIDE = 21


def lane_ids(rows):
    return lax.broadcasted_iota(jnp.int32, (rows, LANES), 1)


def row_ids(rows):
    return lax.broadcasted_iota(jnp.int32, (rows, LANES), 0)


def turn(x, shift):
    return pltpu.roll(x, shift, 1)


def pick(x, index):
    return jnp.take_along_axis(x, index, axis=1)


def flip_lanes(x, mask=LANES - 1):
    return pick(x, lane_ids(x.shape[0]) ^ mask)


def flip_rows(x):
    rows = x.shape[0]
    ids = row_ids(rows)
    for bit in range(3):
        step = 1 << bit
        x = jnp.where((ids & step) != 0, pltpu.roll(x, step, 0), pltpu.roll(x, rows - step, 0))
    return jnp.concatenate([x[r : r + 8] for r in range(rows - 8, -8, -8)], axis=0)


def odd(axis):
    return lax.rem(lax.axis_index(axis), 2) == 1


def at_fold():
    return lax.axis_index("lat") == lax.axis_size("lat") - 1


def shifted(x):
    rows = x.shape[0]
    return (turn(x, LANES - 1), turn(x, 1), pltpu.roll(x, rows - 1, 0), pltpu.roll(x, 1, 0))


def block_kernel(
    vel_far, tra_far, lev_far, visc_far, diff_far, depth_far, wind_far,
    star, mean, fields, cols, north, south, send_a, send_b,
    faces, face_levels, sums, turning, vel, tra_north, tra_south, visc, diff, depth, wind, levels_kept, laps, lev, done,
):
    pairs = (
        (lev_far, lev), (visc_far, visc), (vel_far, vel), (tra_far.at[:, pl.ds(ROWS - 8, 8)], tra_north),
        (tra_far.at[:, pl.ds(0, 8)], tra_south), (wind_far, wind), (depth_far, depth), (diff_far, diff),
    )
    copies = [
        pltpu.make_async_copy(far, near.at[pl.ds(8, PLANES * ROWS)] if near is vel else near, done.at[n])
        for n, (far, near) in enumerate(pairs)
    ]
    for copy in copies:
        copy.start()
    for copy in copies[:2]:
        copy.wait()
    lanes = lane_ids(ROWS)
    ids = row_ids(ROWS)
    levels = lev[...].astype(F32)
    v = visc[...]
    inside = (lanes < LANES - 1, lanes > 0, ids < ROWS - 1, ids > 0)
    for n, (v_n, level_n) in enumerate(zip(shifted(v), shifted(levels))):
        faces[n] = 0.5 * (v + v_n)
        face_levels[n] = jnp.where(inside[n], jnp.minimum(levels, level_n), 0.0)
    row = (lax.axis_index("lat") * ROWS).astype(F32) + ids.astype(F32)
    turning[...] = 0.25 * jnp.sin(math.pi * ((row + 0.5) / (ROWS * lax.axis_size("lat")) - 0.5))
    sums[...] = jnp.zeros((2, ROWS, LANES), F32)
    levels_kept[...] = levels
    for padded in (vel, laps):
        padded[0:8, :] = jnp.zeros((8, LANES), F32)
        padded[PLANES * ROWS + 8 : PLANES * ROWS + 16, :] = jnp.zeros((8, LANES), F32)
    acc = jnp.where((lanes >> 2) == 20, turn(levels, 82), 0.0)
    cols[...] = jnp.where((lanes >> 2) == 21, turn(v, 86), acc)
    copies[2].wait()

    def lap_step(k, carry):
        level = k.astype(F32)
        open_faces = [level < face_levels[n] for n in range(4)]
        ones = [jnp.where(o, 1.0, 0.0) for o in open_faces]
        count = (ones[0] + ones[1]) + (ones[2] + ones[3])
        packed = cols[...]
        for comp in range(2):
            p = comp * LEVELS + k
            start = 8 + pl.multiple_of(p * ROWS, ROWS)
            x = vel[pl.ds(start, ROWS), :]
            around = (turn(x, LANES - 1), turn(x, 1), vel[pl.ds(start + 1, ROWS), :], vel[pl.ds(start - 1, ROWS), :])
            picked = [jnp.where(open_faces[n], around[n], 0.0) for n in range(4)]
            laps[pl.ds(start, ROWS), :] = (picked[0] + picked[1]) + (picked[2] + picked[3]) - count * x
            packed = jnp.where((lanes >> 2) == p, turn(x, 4 * p + 2), packed)
        cols[...] = packed
        return carry

    def star_step(k, carry):
        level = k.astype(F32)
        wet = level < levels_kept[...]
        weights = [jnp.where(level < face_levels[n], faces[n], 0.0) for n in range(4)]
        weight = (weights[0] + weights[1]) + (weights[2] + weights[3])
        starts = [8 + pl.multiple_of((comp * LEVELS + k) * ROWS, ROWS) for comp in range(2)]
        values = [vel[pl.ds(s, ROWS), :] for s in starts]
        for comp, x in enumerate(values):
            start = starts[comp]
            lap = laps[pl.ds(start, ROWS), :]
            around = (turn(lap, LANES - 1), turn(lap, 1), laps[pl.ds(start + 1, ROWS), :], laps[pl.ds(start - 1, ROWS), :])
            terms = [weights[n] * around[n] for n in range(4)]
            second = (terms[0] + terms[1]) + (terms[2] + terms[3]) - weight * lap
            rotated = values[1] if comp == 0 else -values[0]
            out = jnp.where(wet, x - second + turning[...] * rotated, 0.0)
            star[pl.ds(pl.multiple_of((comp * LEVELS + k) * ROWS, ROWS), ROWS), :] = out
            sums[comp] += out
        return carry

    lax.fori_loop(0, LEVELS, lap_step, 0, unroll=10)
    lax.fori_loop(0, LEVELS, star_step, 0, unroll=10)
    for copy in copies[3:]:
        copy.wait()

    ocean = levels > 0.0
    for comp in range(2):
        here = pl.ds(comp * ROWS, ROWS)
        column_mean = sums[comp] / jnp.maximum(levels, 1.0)
        mean[here, :] = column_mean
        fields[here, :] = column_mean + jnp.where(ocean, wind[here, :], 0.0)
    fields[pl.ds(2 * ROWS, ROWS), :] = jnp.where(ocean, depth[...], 0.0)
    for edge, step, out, tra in ((ROWS - 1, -1, north, tra_north), (0, 1, south, tra_south)):
        out[...] = jnp.zeros((RIMS, LANES), F32)
        for d in range(2):
            r = edge + d * step
            out[pl.ds(d * STRIP, PLANES), :] = vel[pl.ds(8 + r, PLANES, stride=ROWS), :]
            out[pl.ds(d * STRIP + 20, 1), :] = levels[r : r + 1]
            out[pl.ds(d * STRIP + 21, 1), :] = visc[pl.ds(r, 1), :]
        out[pl.ds(2 * STRIP, PLANES), :] = tra[:, edge % 8, :]
        out[pl.ds(2 * STRIP + 20, 1), :] = diff[pl.ds(edge, 1), :]
    lat_odd = odd("lat")

    def put(start, up, down):
        here = pl.ds(start, up.shape[0])
        send_a[here, :] = jnp.where(lat_odd, down, up)
        send_b[here, :] = jnp.where(lat_odd, up, down)

    for f in range(3):
        put(f * SENT, fields[pl.ds((f + 1) * ROWS - SENT, SENT), :], fields[pl.ds(f * ROWS, SENT), :])
    for start, first, count in ((NEAR, 0, FULL), (NEXT, STRIP, FULL), (LAST, 2 * STRIP, EDGE)):
        put(start, north[pl.ds(first, count), :], south[pl.ds(first, count), :])
    put(COLS, cols[ROWS - MARGIN : ROWS, :], cols[0:MARGIN, :])
    for send in (send_a, send_b):
        send[LAST + EDGE : COLS, :] = jnp.zeros((COLS - LAST - EDGE, LANES), F32)

    @pl.when(at_fold())
    def _():
        for f in range(3):
            turned = flip_rows(flip_lanes(fields[pl.ds((f + 1) * ROWS - MARGIN, MARGIN), :]))[0:SENT]
            send_b[pl.ds(f * SENT, SENT), :] = turned if f == 2 else -turned
        turned = flip_lanes(north[...])
        r = row_ids(RIMS)
        is_velocity = (r < PLANES) | ((r >= STRIP) & (r < STRIP + PLANES))
        turned = jnp.where(is_velocity, -turned, turned)
        for start, first, count in ((NEAR, 0, FULL), (NEXT, STRIP, FULL), (LAST, 2 * STRIP, EDGE)):
            send_b[pl.ds(start, count), :] = turned[first : first + count]
        turned = flip_rows(flip_lanes(cols[ROWS - MARGIN : ROWS, :], 3))
        send_b[pl.ds(COLS, MARGIN), :] = jnp.where(lane_ids(MARGIN) < 4 * PLANES, -turned, turned)


def tracer_rim_kernel(tra, out):
    lanes = lane_ids(ROWS)

    def tracer_step(p, acc):
        t = tra[pl.ds(pl.multiple_of(p * ROWS, ROWS), ROWS), :]
        return jnp.where((lanes >> 1) == 44 + p, turn(t, lax.rem(89 + 2 * p, LANES)), acc)

    out[...] = lax.fori_loop(0, PLANES, tracer_step, jnp.zeros((ROWS, LANES), F32), unroll=True)


def widen_kernel(fields, cols, tracer_cols, diff, north, south, recv_b, recv_a, tall, strips, tracer_rows, send_a, send_b, east, west):
    lat_odd = odd("lat")
    lon_odd = odd("lon")
    def received(start, count):
        here = pl.ds(start, count)
        got_a = recv_a[here, :]
        got_b = recv_b[here, :]
        return jnp.where(lat_odd, got_b, got_a), jnp.where(lat_odd, got_a, got_b)

    lanes = lane_ids(TALL)
    acc_east = jnp.zeros((TALL, LANES), F32)
    acc_west = jnp.zeros((TALL, LANES), F32)
    for f in range(3):
        from_north, from_south = received(f * SENT, SENT)
        unused = jnp.zeros((MARGIN - SENT, LANES), F32)
        tall[pl.ds(f * TALL, MARGIN - SENT), :] = unused
        tall[pl.ds(f * TALL + MARGIN - SENT, SENT), :] = from_south
        tall[pl.ds(f * TALL + MARGIN, ROWS), :] = fields[pl.ds(f * ROWS, ROWS), :]
        tall[pl.ds(f * TALL + MARGIN + ROWS, SENT), :] = from_north
        tall[pl.ds(f * TALL + MARGIN + ROWS + SENT, MARGIN - SENT), :] = unused
        x = tall[pl.ds(f * TALL, TALL), :]
        here = (lanes >= f * WIDE) & (lanes < (f + 1) * WIDE)
        acc_east = jnp.where(here, turn(x, (f + 1) * WIDE), acc_east)
        acc_west = jnp.where(here, turn(x, f * WIDE), acc_west)
    from_north, from_south = received(COLS, MARGIN)
    tall[pl.ds(3 * TALL, MARGIN), :] = from_south
    tall[pl.ds(3 * TALL + MARGIN, ROWS), :] = jnp.where(lane_ids(ROWS) < 88, cols[...], tracer_cols[...])
    tall[pl.ds(3 * TALL + MARGIN + ROWS, MARGIN), :] = from_north
    for out, acc, shift in ((east, acc_east, 64), (west, acc_west, 63)):
        out[...] = acc
        out[pl.ds(MARGIN, ROWS), :] = jnp.where(lane_ids(ROWS) == 63, turn(diff[...], shift), acc[MARGIN : MARGIN + ROWS])
    near, next_to, last = received(NEAR, FULL), received(NEXT, FULL), received(LAST, EDGE)
    unused = jnp.zeros((STRIP - FULL, LANES), F32)
    group = lane_ids(STRIP) >> 5
    for s, own in enumerate((north, south)):
        pieces = (
            jnp.concatenate([next_to[s], unused], axis=0),
            jnp.concatenate([near[s], unused], axis=0),
            own[0:STRIP, :],
            own[STRIP : 2 * STRIP, :],
        )
        for r, x in enumerate(pieces):
            strips[pl.ds((4 * s + r) * STRIP, STRIP), :] = x
            block, g = divmod(4 * s + r, 2)
            here = pl.ds(block * STRIP, STRIP)
            east[here, :] = jnp.where(group == 2 + g, turn(x, (96 + 32 * g) % LANES), east[here, :])
            west[here, :] = jnp.where(group == 2 + g, turn(x, 64 + 32 * g), west[here, :])
        tracer_rows[pl.ds(2 * s * STRIP, EDGE), :] = last[s]
        tracer_rows[pl.ds((2 * s + 1) * STRIP, STRIP), :] = pieces[1]
    k = tall[pl.ds(3 * TALL, TALL), :]
    send_a[pl.ds(0, TALL), :] = k
    send_b[pl.ds(0, TALL), :] = k
    rest = pl.ds(TALL, TALL)
    e, w = east[...], west[...]
    send_a[rest, :] = jnp.where(lon_odd, w, e)
    send_b[rest, :] = jnp.where(lon_odd, e, w)


def tracer_kernel(tra, lev, diff, tracer_rows, recv_b, recv_a, out, swap, faces, face_levels):
    is_odd = odd("lon")
    lanes = lane_ids(ROWS)
    ids = row_ids(ROWS)

    def received(start):
        here = pl.ds(start + MARGIN, ROWS)
        got_a = recv_a[here, :]
        got_b = recv_b[here, :]
        return jnp.where(is_odd, got_b, got_a), jnp.where(is_odd, got_a, got_b)

    east_cols, west_cols = received(0)
    east_rest, west_rest = received(TALL)
    swap[...] = jnp.where((lanes & 1) == 0, turn(east_cols, LANES - 1), turn(west_cols, 1))

    def sides(x, halo, row):
        east, west, north, south = shifted(x)
        return (
            jnp.where(lanes == LANES - 1, halo, east),
            jnp.where(lanes == 0, halo, west),
            jnp.where(ids == ROWS - 1, tracer_rows[pl.ds(row, 1), :], north),
            jnp.where(ids == 0, tracer_rows[pl.ds(row + 2 * STRIP, 1), :], south),
        )

    level = lev[...].astype(F32)
    level_halo = jnp.where(lanes == LANES - 1, turn(east_cols, 45), turn(west_cols, 47))
    d = diff[...]
    d_halo = jnp.where(lanes == LANES - 1, turn(east_rest, 64), turn(west_rest, 65))
    for n, other in enumerate(sides(level, level_halo, STRIP + 20)):
        face_levels[n] = jnp.minimum(level, other)
    for n, other in enumerate(sides(d, d_halo, 20)):
        faces[n] = 0.5 * (d + other)

    def level_step(k, carry):
        weights = [jnp.where(k.astype(F32) < face_levels[n], faces[n], 0.0) for n in range(4)]
        for comp in range(2):
            p = comp * LEVELS + k
            here = pl.ds(pl.multiple_of(p * ROWS, ROWS), ROWS)
            x = tra[here, :]
            around = sides(x, turn(swap[...], 39 - 2 * p), p)
            total = weights[0] * (around[0] - x)
            for n in range(1, 4):
                total += weights[n] * (around[n] - x)
            out[here, :] = x + total
        return carry

    lax.fori_loop(0, LEVELS, level_step, 0, unroll=2)


def column_strip(strip):
    rows = strip.shape[0]
    lanes = lane_ids(rows)
    ids = row_ids(rows)
    phase = lanes & 3
    group = lanes >> 2

    levels = pick(strip, phase + 80)
    v = 0.5 * pick(strip, phase + 84)
    number = jnp.where(group >= LEVELS, group - LEVELS, group)
    number = jnp.where(group < PLANES, number, LEVELS).astype(F32)
    wet = jnp.where(number < levels, 1.0, 0.0)
    x = strip
    open_e = wet * turn(wet, LANES - 1)
    open_n = wet * pltpu.roll(wet, rows - 1, 0)
    flux_e = open_e * (turn(x, LANES - 1) - x)
    flux_n = open_n * (pltpu.roll(x, rows - 1, 0) - x)
    lap = (flux_e - turn(flux_e, 1)) + (flux_n - pltpu.roll(flux_n, 1, 0))
    seam = jnp.where(phase == 1, flux_e, 0.0)
    seam_west = turn(seam, 1)
    added = seam - seam_west
    step = jnp.where(phase == 1, turn(lap, LANES - 1) - lap, turn(seam, LANES - 1) + seam_west)
    flux_e = (v + turn(v, LANES - 1)) * open_e * step
    in_block = (ids != MARGIN - 1) & (ids != MARGIN + ROWS - 1)
    face = jnp.where(in_block, (v + pltpu.roll(v, rows - 1, 0)) * open_n, 0.0)
    flux_n = face * (pltpu.roll(added, rows - 1, 0) - added)
    return (flux_e - turn(flux_e, 1)) + (flux_n - pltpu.roll(flux_n, 1, 0))


def gram_pairs():
    return [(i, j) for i in range(SOLVE_ITERS) for j in range(i, SOLVE_ITERS + 1)]


def surface_kernel(
    tall, strips, mean, recv_b, recv_a,
    basis_out, flow, partial, col_patch, row_patch,
    state, height, heights, transport, force, faces, slope, basis, weights, diagonal, sides,
):
    is_odd = odd("lon")
    rows = pl.ds(8, TALL)
    lanes = lane_ids(TALL)

    def received(start, count):
        here = pl.ds(start, count)
        got_a = recv_a[here, :]
        got_b = recv_b[here, :]
        return jnp.where(is_odd, got_b, got_a), jnp.where(is_odd, got_a, got_b)

    def ghost(east, west, first, count):
        return jnp.where(
            lane_ids(east.shape[0]) < 64, turn(east, (LANES - first) % LANES), turn(west, LANES - first - count)
        )

    from_east, from_west = received(TALL, TALL)
    for f in range(3):
        state[f, 0, rows, :] = tall[pl.ds(f * TALL, TALL), :]
        state[f, 1, rows, :] = ghost(from_east, from_west, f * WIDE, WIDE)
    last = lanes == LANES - 1
    first = lanes == 0

    def lane_sides(a, b):
        n = a.shape[0]
        ea, eb, wa, wb = turn(a, LANES - 1), turn(b, LANES - 1), turn(a, 1), turn(b, 1)
        return (
            (jnp.where(last[0:n], eb, ea), jnp.where(last[0:n], ea, eb)),
            (jnp.where(first[0:n], wb, wa), jnp.where(first[0:n], wa, wb)),
        )

    own = tall[pl.ds(3 * TALL, TALL), :]
    phase = lanes & 3
    from_east, from_west = received(0, TALL)
    to_east = column_strip(jnp.where(phase < 2, own, from_east))
    to_west = column_strip(jnp.where(phase < 2, from_west, own))
    changes = (jnp.where(phase < 2, to_east, to_west), jnp.where(phase < 2, to_west, to_east))
    deep = (own, jnp.where(phase < 2, from_west, from_east))
    col_patch[...] = changes[0][MARGIN : MARGIN + ROWS]
    to_lane = lax.broadcasted_iota(jnp.int32, (LANES, 2 * LANES), 1)
    from_lane = lax.broadcasted_iota(jnp.int32, (LANES, 2 * LANES), 0)
    column = to_lane & (LANES - 1)
    comp_of = jnp.where(from_lane < 4 * LEVELS, 0, 1)
    chosen = (
        ((column < 2) | (column >= LANES - 2))
        & ((from_lane & 3) == ((to_lane + 2) & 3))
        & (comp_of == (to_lane >> 7))
        & (from_lane < 4 * PLANES)
    )
    chooser = jnp.where(chosen, 1.0, 0.0)
    for half in range(2):
        total = lax.dot_general(
            changes[half], chooser, (((1,), (0,)), ((), ())),
            precision=lax.Precision.HIGHEST, preferred_element_type=F32,
        )
        share = 1.0 / jnp.maximum(pick(deep[half], ((lanes + 2) & 3) + 80), 1.0)
        for comp in range(2):
            change = total[:, comp * LANES : (comp + 1) * LANES] * share
            state[comp, half, rows, :] = state[comp, half, rows, :] - change
    number = lax.broadcasted_iota(jnp.int32, (STRIP, LANES), 0)
    level_of_row = jnp.where(number >= LEVELS, number - LEVELS, number).astype(F32)
    is_plane = number < PLANES
    not_last = lane_ids(STRIP) < LANES - 1
    for s in range(2):
        x, wet, v, deep = [], [], [], []
        for r in range(4):
            centre = strips[pl.ds((4 * s + r) * STRIP, STRIP), :]
            block, g = divmod(4 * s + r, 2)
            both = (centre, ghost(*received(TALL + block * STRIP, STRIP), 64 + 32 * g, 32))
            deep.append([b[20:21] for b in both])
            v.append([jnp.broadcast_to(b[21:22], (STRIP, LANES)) for b in both])
            wet.append([jnp.where(is_plane & (level_of_row < b[20:21]), 1.0, 0.0) for b in both])
            x.append([jnp.where(is_plane, b, 0.0) for b in both])
        half_range = range(2)
        lap = {}
        added = {}
        seam = [wet[1][h] * wet[2][h] * (x[2][h] - x[1][h]) for h in half_range]
        added[1] = seam
        added[2] = [-t for t in seam]
        along = {}
        for r in (1, 2):
            x_e = lane_sides(*x[r])[0]
            wet_e = lane_sides(*wet[r])[0]
            v_e = lane_sides(*v[r])[0]
            added_e = lane_sides(*added[r])[0]
            open_e = [wet[r][h] * wet_e[h] for h in half_range]
            edge = [open_e[h] * (x_e[h] - x[r][h]) for h in half_range]
            edge_w = lane_sides(*edge)[1]
            lap[r] = [
                edge[h]
                - edge_w[h]
                + wet[r][h] * (wet[r + 1][h] * (x[r + 1][h] - x[r][h]) + wet[r - 1][h] * (x[r - 1][h] - x[r][h]))
                for h in half_range
            ]
            edge = [
                jnp.where(not_last, 0.5 * (v[r][h] + v_e[h]) * open_e[h] * (added_e[h] - added[r][h]), 0.0)
                for h in half_range
            ]
            edge_w = lane_sides(*edge)[1]
            along[r] = [edge[h] - edge_w[h] for h in half_range]
        for h in half_range:
            face = [0.5 * (v[r][h] + v[r + 1][h]) * wet[r][h] * wet[r + 1][h] for r in range(3)]
            across = (face[0] * added[1][h], face[1] * (lap[2][h] - lap[1][h]), -face[2] * added[2][h])
            second = (
                across[0],
                across[1] - across[0] + along[1][h],
                across[2] - across[1] + along[2][h],
                -across[2],
            )
            for r in range(4):
                change = second[r]
                if h == 0 and r >= 2:
                    row_patch[pl.ds((2 * s + r - 2) * STRIP, STRIP), :] = change
                where = 8 + MARGIN + ((ROWS + 1 - r) if s == 0 else (r - 2))
                for comp in range(2):
                    mine = (number >= comp * LEVELS) & (number < (comp + 1) * LEVELS)
                    total = jnp.sum(jnp.where(mine, change, 0.0), axis=0, keepdims=True)
                    total = total / jnp.maximum(deep[r][h], 1.0)
                    state[comp, h, where : where + 1, :] = state[comp, h, where : where + 1, :] - total
    for comp in range(2):
        here = pl.ds(comp * ROWS, ROWS)
        started = state[comp, 0, pl.ds(8 + MARGIN, ROWS), :] - tall[pl.ds(comp * TALL + MARGIN, ROWS), :]
        flow[here, :] = -(started + mean[here, :])

    halves = range(2)
    ahead = lanes[0:8] >= LANES - 2
    behind = lanes[0:8] < 2

    def far_sides(a, b):
        ea, eb, wa, wb = turn(a, LANES - 2), turn(b, LANES - 2), turn(a, 2), turn(b, 2)
        return (
            (jnp.where(ahead, eb, ea), jnp.where(ahead, ea, eb)),
            (jnp.where(behind, wb, wa), jnp.where(behind, wa, wb)),
        )

    for half in halves:
        d = state[2, half, rows, :]
        slope[half, rows, :] = jnp.where(d > 0.0, SLOPE, 0.0)
        force[half, rows, :] = SLOPE * d
        transport[half, rows, :] = d * state[1, half, rows, :]
    tiles = range(8, 8 + TALL, 8)
    for tile in tiles:
        here, above, below = (pl.ds(tile + off, 8) for off in (0, 1, -1))
        east, west = lane_sides(force[0, here, :], force[1, here, :])
        for h in halves:
            faces[0, h, here, :] = east[h]
            faces[1, h, here, :] = west[h]
            faces[2, h, here, :] = force[h, above, :]
            faces[3, h, here, :] = force[h, below, :]
    for tile in tiles:
        here, above, below = (pl.ds(tile + off, 8) for off in (0, 1, -1))
        east, west = lane_sides(*(state[2, h, here, :] * state[0, h, here, :] for h in halves))
        for h in halves:
            divergence = (east[h] - west[h]) + (transport[h, above, :] - transport[h, below, :])
            force[h, here, :] = divergence
            new = -slope[h, here, :] * divergence
            heights[0, h, here, :] = new
            height[h, here, :] = new
    for step in range(1, SUBCYCLES):
        cut = min(8 * ((6 + 2 * step) // 8), 16)
        now, later = heights.at[(step - 1) % 2], heights.at[step % 2]
        for tile in range(8 + cut, 8 + TALL - cut, 8):
            here, above, below = (pl.ds(tile + off, 8) for off in (0, 2, -2))
            centres = [now[h, here, :] for h in halves]
            east, west = far_sides(*centres)
            for h, x in enumerate(centres):
                along = faces[0, h, here, :] * (east[h] - x) - faces[1, h, here, :] * (x - west[h])
                across = faces[2, h, here, :] * (now[h, above, :] - x) - faces[3, h, here, :] * (x - now[h, below, :])
                change = force[h, here, :] - (along + across)
                force[h, here, :] = change
                new = x - slope[h, here, :] * change
                later[h, here, :] = new
                height[h, here, :] = height[h, here, :] + new
    mine = pl.ds(8 + MARGIN, ROWS)
    east, west = lane_sides(height[0, mine, :], height[1, mine, :])
    inner = slope[0, mine, :]
    north, south = (height[0, pl.ds(8 + MARGIN + off, ROWS), :] for off in (1, -1))
    for comp, gradient in enumerate((east[0] - west[0], north - south)):
        here = pl.ds(comp * ROWS, ROWS)
        flow[here, :] = flow[here, :] + (state[comp, 0, mine, :] - inner * gradient)
    final = heights.at[(SUBCYCLES - 1) % 2]
    scale = 2.0 / RADIUS
    short = ROWS + 16
    base = MARGIN

    tiles = range(0, short, 8)

    def spin(tile, a, b):
        here = pl.ds(base + tile, 8)
        for n, pair in enumerate(lane_sides(a, b)):
            for h in halves:
                sides[n, h, here, :] = pair[h]

    def nine(read, tile, h):
        out = []
        for off in (0, 1, -1):
            where = pl.ds(base + tile + off, 8)
            out += [read(h, where), sides[0, h, where, :], sides[1, h, where, :]]
        return out

    for tile in tiles:
        here = pl.ds(base + tile, 8)
        spin(tile, state[2, 0, here, :], state[2, 1, here, :])
    for tile in tiles:
        here = pl.ds(tile, 8)
        for h in halves:
            around = nine(lambda h, where: state[2, h, where, :], tile, h)
            d = around[0]
            wet = d > 0.0
            total = jnp.where(wet, 0.05, 1.0)
            for n in range(1, 9):
                factor = 0.5 if n in (1, 2, 3, 6) else 0.25
                w = jnp.where(wet & (around[n] > 0.0), factor * (d + around[n]), 0.0)
                weights[n - 1, h, here, :] = scale * w
                total += w
            diagonal[h, here, :] = scale * (total - CENTRE)

    def applied(source, tile, h):
        around = nine(lambda h, where: basis[source, h, where, :], tile, h)
        here = pl.ds(tile, 8)
        terms = [weights[n - 1, h, here, :] * around[n] for n in range(1, 9)]
        while len(terms) > 1:
            terms = [a + b for a, b in zip(terms[::2], terms[1::2])]
        return diagonal[h, here, :] * around[0] - terms[0]

    for tile in tiles:
        here = pl.ds(base + tile, 8)
        pair = [final[h, here, :] for h in halves]
        for h in halves:
            basis[0, h, here, :] = pair[h]
        spin(tile, *pair)
    for k in range(1, SOLVE_ITERS):
        for tile in tiles:
            here = pl.ds(base + tile, 8)
            for h in halves:
                x = applied(k - 1, tile, h)
                basis[k, h, here, :] = 0.5 * x if k == 1 else x - basis[k - 2, h, here, :]
        for tile in tiles:
            here = pl.ds(base + tile, 8)
            spin(tile, basis[k, 0, here, :], basis[k, 1, here, :])
    for tile in tiles[1:-1]:
        here = pl.ds(base + tile, 8)
        basis[SOLVE_ITERS, 0, here, :] = applied(SOLVE_ITERS - 1, tile, 0) - basis[SOLVE_ITERS - 2, 0, here, :]
    lane = lane_ids(1)
    row = jnp.zeros((1, LANES), F32)
    mine = pl.ds(8 + MARGIN, ROWS)
    for n, (i, j) in enumerate(gram_pairs()):
        product = basis[i, 0, mine, :] * basis[j, 0, mine, :]
        row = jnp.where(lane == n, jnp.sum(jnp.sum(product, axis=0, keepdims=True), axis=1, keepdims=True), row)
    partial[...] = jnp.broadcast_to(row, partial.shape)
    for i in range(SOLVE_ITERS):
        for half in range(2):
            basis_out[i, half] = basis[i, half, pl.ds(base, short), :]


def solve_coefficients(gram):
    half = 0.5 * RADIUS

    def image_of(d):
        out = [None] * (len(d) + 1)

        def add(n, term):
            out[n] = term if out[n] is None else out[n] + term

        for j, value in enumerate(d):
            add(j, CENTRE * value)
            if j == 0:
                add(1, RADIUS * value)
            else:
                add(j + 1, half * value)
                add(j - 1, half * value)
        return out

    def inner(a, b):
        total = None
        for i, x in enumerate(a):
            for j, y in enumerate(b):
                term = x * y * gram[(min(i, j), max(i, j))]
                total = term if total is None else total + term
        return total

    one = jnp.ones((8, LANES), F32)
    residual, direction, surface = [one], [one], [0.0 * one]
    norm = gram[(0, 0)]
    for iteration in range(SOLVE_ITERS):
        image = image_of(direction)
        step = norm / inner(direction, image)
        surface = [a + step * b for a, b in zip(surface, direction)] + [0.0 * one]
        if iteration == SOLVE_ITERS - 1:
            break
        residual = [(residual[n] if n < len(residual) else 0.0) - step * x for n, x in enumerate(image)]
        fresh = inner(residual, residual)
        ratio = fresh / norm
        direction = [x + (ratio * direction[n] if n < len(direction) else 0.0) for n, x in enumerate(residual)]
        norm = fresh
    return surface[:SOLVE_ITERS]


def final_kernel(gathered, basis, flow, star, lev, velocity_out, surface_out, pad, change):
    sums = jnp.sum(gathered[...], axis=0, keepdims=True)
    lane = lane_ids(1)
    gram = {}
    for n, pair in enumerate(gram_pairs()):
        value = jnp.sum(jnp.where(lane == n, sums, 0.0), axis=1, keepdims=True)
        gram[pair] = jnp.broadcast_to(value, (8, LANES))
    coefficients = [c[0:1] for c in solve_coefficients(gram)]
    for half in range(2):
        total = coefficients[0] * basis[0, half]
        for i in range(1, SOLVE_ITERS):
            total += coefficients[i] * basis[i, half]
        pad[half] = total
    mine = pl.ds(8, ROWS)
    centre = pad[0, mine, :]
    ghost = pad[1, mine, :]
    surface_out[...] = centre
    lanes = lane_ids(ROWS)
    east = jnp.where(lanes == LANES - 1, turn(ghost, LANES - 1), turn(centre, LANES - 1))
    west = jnp.where(lanes == 0, turn(ghost, 1), turn(centre, 1))
    levels = lev[...]
    slope = jnp.where(levels > 0, SLOPE, 0.0)
    slopes = (east - west, pad[0, pl.ds(9, ROWS), :] - pad[0, pl.ds(7, ROWS), :])
    for comp in range(2):
        here = pl.ds(comp * ROWS, ROWS)
        change[comp] = flow[here, :] - slope * slopes[comp]


    def level_step(k, carry):
        wet = k < levels
        for comp in range(2):
            here = pl.ds(pl.multiple_of((comp * LEVELS + k) * ROWS, ROWS), ROWS)
            velocity_out[here, :] = star[here, :] + jnp.where(wet, change[comp], 0.0)
        return carry

    lax.fori_loop(0, LEVELS, level_step, 0, unroll=True)


def patch_kernel(star, col_patch, row_patch, out):
    lanes = lane_ids(ROWS)
    rims = (lanes < 2) | (lanes >= LANES - 2)
    ids = row_ids(8)

    def plane(p, carry):
        here = pl.ds(pl.multiple_of(p * ROWS, ROWS), ROWS)
        out[here, :] = star[here, :] - jnp.where(rims, turn(col_patch[...], 126 - 4 * p), 0.0)
        for first, pieces in ((ROWS - 8, ((7, 0), (6, 1))), (0, ((0, 2), (1, 3)))):
            here = pl.ds(pl.multiple_of(p * ROWS + first, 8), 8)
            x = out[here, :]
            for row, n in pieces:
                x = x - jnp.where(ids == row, row_patch[pl.ds(n * STRIP + p, 1), :], 0.0)
            out[here, :] = x
        return carry

    lax.fori_loop(0, PLANES, plane, 0, unroll=10)


def call(kernel, shapes, scratch, flops, *args, far=False):
    out = tuple(jax.ShapeDtypeStruct(s, F32) for s in shapes)
    moved = sum(4 * math.prod(a.shape) for a in args) + sum(4 * math.prod(s) for s in shapes)
    if far:
        args = [pltpu.with_memory_space_constraint(a, pltpu.HBM) for a in args]
    return pl.pallas_call(
        kernel,
        out_shape=out,
        in_specs=[pl.BlockSpec(memory_space=pltpu.HBM if far else pltpu.VMEM)] * len(args),
        scratch_shapes=[pltpu.VMEM(s, F32) if isinstance(s, tuple) else s for s in scratch],
        compiler_params=pltpu.CompilerParams(vmem_limit_bytes=32 * 1024 * 1024),
        cost_estimate=pl.CostEstimate(flops=flops, bytes_accessed=moved, transcendentals=0),
    )(*args)


def pair_tables(lon, lat):
    def index(i, j):
        return j * lat + i

    lat_a, lat_b, lon_a, lon_b = [], [], [], []
    for j in range(lon):
        for i in range(lat):
            lat_a.append((index(i, j), index(i ^ 1, j)))
            if i == lat - 1:
                lat_b.append((index(i, j), index(i, lon - 1 - j)))
            elif i > 0:
                lat_b.append((index(i, j), index(i + 1 if i % 2 else i - 1, j)))
            lon_a.append((index(i, j), index(i, j ^ 1)))
            lon_b.append((index(i, j), index(i, (j + 1 if j % 2 else j - 1) % lon)))
    return lat_a, lat_b, lon_a, lon_b


def per_device(lon, lat, tracers, velocity, active_levels, diffusivity, viscosity, ocean_depth, wind_forcing):
    lat_a, lat_b, lon_a, lon_b = pair_tables(lon, lat)

    def swap(x, pairs):
        return lax.ppermute(x, BOTH, pairs)

    block = (ROWS, LANES)
    tra = tracers.reshape(PLANES * ROWS, LANES)
    vel = velocity.reshape(PLANES * ROWS, LANES)
    wind = wind_forcing.reshape(2 * ROWS, LANES)
    rim = (RIMS, LANES)
    star, mean, fields, cols, north, south, send_a, send_b = call(
        block_kernel,
        [(PLANES * ROWS, LANES), (2 * ROWS, LANES), (3 * ROWS, LANES), block, rim, rim, (LAT_SEND, LANES), (LAT_SEND, LANES)],
        [(4,) + block, (4,) + block, (2,) + block, block, (PLANES * ROWS + 16, LANES), (PLANES, 8, LANES), (PLANES, 8, LANES), block, block, block, wind.shape,
         block, (PLANES * ROWS + 16, LANES),
         pltpu.VMEM(block, jnp.int32), pltpu.SemaphoreType.DMA((8,))],
        10**7,
        vel, tra.reshape(PLANES, ROWS, LANES), active_levels, viscosity, diffusivity, ocean_depth, wind,
        far=True,
    )
    got_a = swap(send_a, lat_a)
    got_b = swap(send_b, lat_b)
    (tracer_cols,) = call(tracer_rim_kernel, [block], [], 10**5, tra)
    tall, strips, tracer_rows, send_a, send_b = call(
        widen_kernel,
        [(4 * TALL, LANES), (8 * STRIP, LANES), (4 * STRIP, LANES), (LON_SEND, LANES), (LON_SEND, LANES)],
        [(TALL, LANES)] * 2,
        10**6,
        fields, cols, tracer_cols, diffusivity, north, south, got_b, got_a,
    )
    got_a = swap(send_a, lon_a)
    got_b = swap(send_b, lon_b)
    (tracers_out,) = call(
        tracer_kernel, [(PLANES * ROWS, LANES)], [block, (4,) + block, (4,) + block], 10**6,
        tra, active_levels, diffusivity, tracer_rows, got_b, got_a,
    )
    padded = (2, TALL + 16, LANES)
    short = (2, ROWS + 16, LANES)
    basis, flow, partial, col_patch, row_patch = call(
        surface_kernel,
        [(SOLVE_ITERS,) + short, (2 * ROWS, LANES), (lon * lat, LANES), block, (4 * STRIP, LANES)],
        [(3,) + padded, padded, (2,) + padded, padded, padded, (4,) + padded, padded, (SOLVE_ITERS + 1,) + padded, (8,) + short, short, (2,) + padded],
        10**7,
        tall, strips, mean, got_b, got_a,
    )
    gathered = lax.all_to_all(partial, BOTH, 0, 0, tiled=True)
    (star,) = call(patch_kernel, [(PLANES * ROWS, LANES)], [], 10**6, star, col_patch, row_patch)
    velocity_out, surface = call(
        final_kernel, [(PLANES * ROWS, LANES), block],
        [short, (2,) + block], 10**6,
        gathered, basis, flow, star, active_levels,
    )
    return tracers_out.reshape(tracers.shape), velocity_out.reshape(velocity.shape), surface


def solution(mesh):
    placed = (
        P(None, None, "lat", "lon"),
        P(None, None, "lat", "lon"),
        P("lat", "lon"),
        P("lat", "lon"),
        P("lat", "lon"),
        P("lat", "lon"),
        P(None, "lat", "lon"),
    )
    return jax.shard_map(
        functools.partial(per_device, mesh.shape["lon"], mesh.shape["lat"]),
        mesh=mesh,
        in_specs=placed,
        out_specs=(P(None, None, "lat", "lon"), P(None, None, "lat", "lon"), P("lat", "lon")),
        check_vma=False,
    )
```

```python
import functools
import math

import jax
import jax.numpy as jnp
from jax import lax
from jax.experimental import pallas as pl
from jax.experimental.pallas import tpu as pltpu
from jax.sharding import PartitionSpec as P

SUBCYCLES = 8
SOLVE_ITERS = 4
LEVELS = 10
PLANES = 2 * LEVELS
ROWS = 64
LANES = 128
MARGIN = 24
TALL = ROWS + 2 * MARGIN
RIM = 32
SLOPE = 0.15
CENTRE = 5.0
RADIUS = 5.0
F32 = jnp.float32
BOTH = ("lon", "lat")

STRIP = 24
RIMS = 3 * STRIP
SENT = 20
FULL = 22
EDGE = 21
NEAR, NEXT, LAST, COLS = 3 * SENT, 3 * SENT + FULL, 3 * SENT + 2 * FULL, 128
LAT_SEND = COLS + MARGIN
LON_SEND = 2 * TALL
WIDE = 21


def lane_ids(rows):
    return lax.broadcasted_iota(jnp.int32, (rows, LANES), 1)


def row_ids(rows):
    return lax.broadcasted_iota(jnp.int32, (rows, LANES), 0)


def turn(x, shift):
    return pltpu.roll(x, shift, 1)


def pick(x, index):
    return jnp.take_along_axis(x, index, axis=1)


def flip_lanes(x, mask=LANES - 1):
    return pick(x, lane_ids(x.shape[0]) ^ mask)


def flip_rows(x):
    rows = x.shape[0]
    ids = row_ids(rows)
    for bit in range(3):
        step = 1 << bit
        x = jnp.where((ids & step) != 0, pltpu.roll(x, step, 0), pltpu.roll(x, rows - step, 0))
    return jnp.concatenate([x[r : r + 8] for r in range(rows - 8, -8, -8)], axis=0)


def odd(axis):
    return lax.rem(lax.axis_index(axis), 2) == 1


def at_fold():
    return lax.axis_index("lat") == lax.axis_size("lat") - 1


def shifted(x):
    rows = x.shape[0]
    return (turn(x, LANES - 1), turn(x, 1), pltpu.roll(x, rows - 1, 0), pltpu.roll(x, 1, 0))


def block_kernel(
    vel_far, tra_far, lev_far, visc_far, diff_far, depth_far, wind_far,
    star, mean, fields, cols, north, south, send_a, send_b,
    faces, face_levels, sums, turning, vel, tra_north, tra_south, visc, diff, depth, wind, levels_kept, laps, lev, done,
):
    pairs = (
        (lev_far, lev), (visc_far, visc), (vel_far, vel), (tra_far.at[:, pl.ds(ROWS - 8, 8)], tra_north),
        (tra_far.at[:, pl.ds(0, 8)], tra_south), (wind_far, wind), (depth_far, depth), (diff_far, diff),
    )
    copies = [
        pltpu.make_async_copy(far, near.at[pl.ds(8, PLANES * ROWS)] if near is vel else near, done.at[n])
        for n, (far, near) in enumerate(pairs)
    ]
    for copy in copies:
        copy.start()
    for copy in copies[:2]:
        copy.wait()
    lanes = lane_ids(ROWS)
    ids = row_ids(ROWS)
    levels = lev[...].astype(F32)
    v = visc[...]
    inside = (lanes < LANES - 1, lanes > 0, ids < ROWS - 1, ids > 0)
    for n, (v_n, level_n) in enumerate(zip(shifted(v), shifted(levels))):
        faces[n] = 0.5 * (v + v_n)
        face_levels[n] = jnp.where(inside[n], jnp.minimum(levels, level_n), 0.0)
    row = (lax.axis_index("lat") * ROWS).astype(F32) + ids.astype(F32)
    turning[...] = 0.25 * jnp.sin(math.pi * ((row + 0.5) / (ROWS * lax.axis_size("lat")) - 0.5))
    sums[...] = jnp.zeros((2, ROWS, LANES), F32)
    levels_kept[...] = levels
    for padded in (vel, laps):
        padded[0:8, :] = jnp.zeros((8, LANES), F32)
        padded[PLANES * ROWS + 8 : PLANES * ROWS + 16, :] = jnp.zeros((8, LANES), F32)
    acc = jnp.where((lanes >> 2) == 20, turn(levels, 82), 0.0)
    cols[...] = jnp.where((lanes >> 2) == 21, turn(v, 86), acc)
    copies[2].wait()

    def lap_step(k, carry):
        level = k.astype(F32)
        open_faces = [level < face_levels[n] for n in range(4)]
        ones = [jnp.where(o, 1.0, 0.0) for o in open_faces]
        count = (ones[0] + ones[1]) + (ones[2] + ones[3])
        packed = cols[...]
        for comp in range(2):
            p = comp * LEVELS + k
            start = 8 + pl.multiple_of(p * ROWS, ROWS)
            x = vel[pl.ds(start, ROWS), :]
            around = (turn(x, LANES - 1), turn(x, 1), vel[pl.ds(start + 1, ROWS), :], vel[pl.ds(start - 1, ROWS), :])
            picked = [jnp.where(open_faces[n], around[n], 0.0) for n in range(4)]
            laps[pl.ds(start, ROWS), :] = (picked[0] + picked[1]) + (picked[2] + picked[3]) - count * x
            packed = jnp.where((lanes >> 2) == p, turn(x, 4 * p + 2), packed)
        cols[...] = packed
        return carry

    def star_step(k, carry):
        level = k.astype(F32)
        wet = level < levels_kept[...]
        weights = [jnp.where(level < face_levels[n], faces[n], 0.0) for n in range(4)]
        weight = (weights[0] + weights[1]) + (weights[2] + weights[3])
        starts = [8 + pl.multiple_of((comp * LEVELS + k) * ROWS, ROWS) for comp in range(2)]
        values = [vel[pl.ds(s, ROWS), :] for s in starts]
        for comp, x in enumerate(values):
            start = starts[comp]
            lap = laps[pl.ds(start, ROWS), :]
            around = (turn(lap, LANES - 1), turn(lap, 1), laps[pl.ds(start + 1, ROWS), :], laps[pl.ds(start - 1, ROWS), :])
            terms = [weights[n] * around[n] for n in range(4)]
            second = (terms[0] + terms[1]) + (terms[2] + terms[3]) - weight * lap
            rotated = values[1] if comp == 0 else -values[0]
            out = jnp.where(wet, x - second + turning[...] * rotated, 0.0)
            star[pl.ds(pl.multiple_of((comp * LEVELS + k) * ROWS, ROWS), ROWS), :] = out
            sums[comp] += out
        return carry

    lax.fori_loop(0, LEVELS, lap_step, 0, unroll=10)
    lax.fori_loop(0, LEVELS, star_step, 0, unroll=10)
    for copy in copies[3:]:
        copy.wait()

    ocean = levels > 0.0
    for comp in range(2):
        here = pl.ds(comp * ROWS, ROWS)
        column_mean = sums[comp] / jnp.maximum(levels, 1.0)
        mean[here, :] = column_mean
        fields[here, :] = column_mean + jnp.where(ocean, wind[here, :], 0.0)
    fields[pl.ds(2 * ROWS, ROWS), :] = jnp.where(ocean, depth[...], 0.0)
    for edge, step, out, tra in ((ROWS - 1, -1, north, tra_north), (0, 1, south, tra_south)):
        out[...] = jnp.zeros((RIMS, LANES), F32)
        for d in range(2):
            r = edge + d * step
            out[pl.ds(d * STRIP, PLANES), :] = vel[pl.ds(8 + r, PLANES, stride=ROWS), :]
            out[pl.ds(d * STRIP + 20, 1), :] = levels[r : r + 1]
            out[pl.ds(d * STRIP + 21, 1), :] = visc[pl.ds(r, 1), :]
        out[pl.ds(2 * STRIP, PLANES), :] = tra[:, edge % 8, :]
        out[pl.ds(2 * STRIP + 20, 1), :] = diff[pl.ds(edge, 1), :]
    lat_odd = odd("lat")

    def put(start, up, down):
        here = pl.ds(start, up.shape[0])
        send_a[here, :] = jnp.where(lat_odd, down, up)
        send_b[here, :] = jnp.where(lat_odd, up, down)

    for f in range(3):
        put(f * SENT, fields[pl.ds((f + 1) * ROWS - SENT, SENT), :], fields[pl.ds(f * ROWS, SENT), :])
    for start, first, count in ((NEAR, 0, FULL), (NEXT, STRIP, FULL), (LAST, 2 * STRIP, EDGE)):
        put(start, north[pl.ds(first, count), :], south[pl.ds(first, count), :])
    put(COLS, cols[ROWS - MARGIN : ROWS, :], cols[0:MARGIN, :])
    for send in (send_a, send_b):
        send[LAST + EDGE : COLS, :] = jnp.zeros((COLS - LAST - EDGE, LANES), F32)

    @pl.when(at_fold())
    def _():
        for f in range(3):
            turned = flip_rows(flip_lanes(fields[pl.ds((f + 1) * ROWS - MARGIN, MARGIN), :]))[0:SENT]
            send_b[pl.ds(f * SENT, SENT), :] = turned if f == 2 else -turned
        turned = flip_lanes(north[...])
        r = row_ids(RIMS)
        is_velocity = (r < PLANES) | ((r >= STRIP) & (r < STRIP + PLANES))
        turned = jnp.where(is_velocity, -turned, turned)
        for start, first, count in ((NEAR, 0, FULL), (NEXT, STRIP, FULL), (LAST, 2 * STRIP, EDGE)):
            send_b[pl.ds(start, count), :] = turned[first : first + count]
        turned = flip_rows(flip_lanes(cols[ROWS - MARGIN : ROWS, :], 3))
        send_b[pl.ds(COLS, MARGIN), :] = jnp.where(lane_ids(MARGIN) < 4 * PLANES, -turned, turned)


def tracer_rim_kernel(tra, out):
    lanes = lane_ids(ROWS)

    def tracer_step(p, acc):
        t = tra[pl.ds(pl.multiple_of(p * ROWS, ROWS), ROWS), :]
        return jnp.where((lanes >> 1) == 44 + p, turn(t, lax.rem(89 + 2 * p, LANES)), acc)

    out[...] = lax.fori_loop(0, PLANES, tracer_step, jnp.zeros((ROWS, LANES), F32), unroll=True)


def widen_kernel(fields, cols, tracer_cols, diff, north, south, recv_b, recv_a, tall, strips, tracer_rows, send_a, send_b, east, west):
    lat_odd = odd("lat")
    lon_odd = odd("lon")
    at_south = lax.axis_index("lat") == 0
    def received(start, count):
        here = pl.ds(start, count)
        got_a = recv_a[here, :]
        got_b = jnp.where(at_south, 0.0, recv_b[here, :])
        return jnp.where(lat_odd, got_b, got_a), jnp.where(lat_odd, got_a, got_b)

    lanes = lane_ids(TALL)
    acc_east = jnp.zeros((TALL, LANES), F32)
    acc_west = jnp.zeros((TALL, LANES), F32)
    for f in range(3):
        from_north, from_south = received(f * SENT, SENT)
        unused = jnp.zeros((MARGIN - SENT, LANES), F32)
        tall[pl.ds(f * TALL, MARGIN - SENT), :] = unused
        tall[pl.ds(f * TALL + MARGIN - SENT, SENT), :] = from_south
        tall[pl.ds(f * TALL + MARGIN, ROWS), :] = fields[pl.ds(f * ROWS, ROWS), :]
        tall[pl.ds(f * TALL + MARGIN + ROWS, SENT), :] = from_north
        tall[pl.ds(f * TALL + MARGIN + ROWS + SENT, MARGIN - SENT), :] = unused
        x = tall[pl.ds(f * TALL, TALL), :]
        here = (lanes >= f * WIDE) & (lanes < (f + 1) * WIDE)
        acc_east = jnp.where(here, turn(x, (f + 1) * WIDE), acc_east)
        acc_west = jnp.where(here, turn(x, f * WIDE), acc_west)
    from_north, from_south = received(COLS, MARGIN)
    tall[pl.ds(3 * TALL, MARGIN), :] = from_south
    tall[pl.ds(3 * TALL + MARGIN, ROWS), :] = jnp.where(lane_ids(ROWS) < 88, cols[...], tracer_cols[...])
    tall[pl.ds(3 * TALL + MARGIN + ROWS, MARGIN), :] = from_north
    for out, acc, shift in ((east, acc_east, 64), (west, acc_west, 63)):
        out[...] = acc
        out[pl.ds(MARGIN, ROWS), :] = jnp.where(lane_ids(ROWS) == 63, turn(diff[...], shift), acc[MARGIN : MARGIN + ROWS])
    near, next_to, last = received(NEAR, FULL), received(NEXT, FULL), received(LAST, EDGE)
    unused = jnp.zeros((STRIP - FULL, LANES), F32)
    group = lane_ids(STRIP) >> 5
    for s, own in enumerate((north, south)):
        pieces = (
            jnp.concatenate([next_to[s], unused], axis=0),
            jnp.concatenate([near[s], unused], axis=0),
            own[0:STRIP, :],
            own[STRIP : 2 * STRIP, :],
        )
        for r, x in enumerate(pieces):
            strips[pl.ds((4 * s + r) * STRIP, STRIP), :] = x
            block, g = divmod(4 * s + r, 2)
            here = pl.ds(block * STRIP, STRIP)
            east[here, :] = jnp.where(group == 2 + g, turn(x, (96 + 32 * g) % LANES), east[here, :])
            west[here, :] = jnp.where(group == 2 + g, turn(x, 64 + 32 * g), west[here, :])
        tracer_rows[pl.ds(2 * s * STRIP, EDGE), :] = last[s]
        tracer_rows[pl.ds((2 * s + 1) * STRIP, STRIP), :] = pieces[1]
    k = tall[pl.ds(3 * TALL, TALL), :]
    send_a[pl.ds(0, TALL), :] = k
    send_b[pl.ds(0, TALL), :] = k
    rest = pl.ds(TALL, TALL)
    e, w = east[...], west[...]
    send_a[rest, :] = jnp.where(lon_odd, w, e)
    send_b[rest, :] = jnp.where(lon_odd, e, w)


def tracer_kernel(tra, lev, diff, tracer_rows, recv_b, recv_a, out, swap, faces, face_levels):
    is_odd = odd("lon")
    lanes = lane_ids(ROWS)
    ids = row_ids(ROWS)

    def received(start):
        here = pl.ds(start + MARGIN, ROWS)
        got_a = recv_a[here, :]
        got_b = recv_b[here, :]
        return jnp.where(is_odd, got_b, got_a), jnp.where(is_odd, got_a, got_b)

    east_cols, west_cols = received(0)
    east_rest, west_rest = received(TALL)
    swap[...] = jnp.where((lanes & 1) == 0, turn(east_cols, LANES - 1), turn(west_cols, 1))

    def sides(x, halo, row):
        east, west, north, south = shifted(x)
        return (
            jnp.where(lanes == LANES - 1, halo, east),
            jnp.where(lanes == 0, halo, west),
            jnp.where(ids == ROWS - 1, tracer_rows[pl.ds(row, 1), :], north),
            jnp.where(ids == 0, tracer_rows[pl.ds(row + 2 * STRIP, 1), :], south),
        )

    level = lev[...].astype(F32)
    level_halo = jnp.where(lanes == LANES - 1, turn(east_cols, 45), turn(west_cols, 47))
    d = diff[...]
    d_halo = jnp.where(lanes == LANES - 1, turn(east_rest, 64), turn(west_rest, 65))
    for n, other in enumerate(sides(level, level_halo, STRIP + 20)):
        face_levels[n] = jnp.minimum(level, other)
    for n, other in enumerate(sides(d, d_halo, 20)):
        faces[n] = 0.5 * (d + other)

    def level_step(k, carry):
        weights = [jnp.where(k.astype(F32) < face_levels[n], faces[n], 0.0) for n in range(4)]
        for comp in range(2):
            p = comp * LEVELS + k
            here = pl.ds(pl.multiple_of(p * ROWS, ROWS), ROWS)
            x = tra[here, :]
            around = sides(x, turn(swap[...], 39 - 2 * p), p)
            total = weights[0] * (around[0] - x)
            for n in range(1, 4):
                total += weights[n] * (around[n] - x)
            out[here, :] = x + total
        return carry

    lax.fori_loop(0, LEVELS, level_step, 0, unroll=2)


def column_strip(strip):
    rows = strip.shape[0]
    lanes = lane_ids(rows)
    ids = row_ids(rows)
    phase = lanes & 3
    group = lanes >> 2

    levels = pick(strip, phase + 80)
    v = 0.5 * pick(strip, phase + 84)
    number = jnp.where(group >= LEVELS, group - LEVELS, group)
    number = jnp.where(group < PLANES, number, LEVELS).astype(F32)
    wet = jnp.where(number < levels, 1.0, 0.0)
    x = strip
    open_e = wet * turn(wet, LANES - 1)
    open_n = wet * pltpu.roll(wet, rows - 1, 0)
    flux_e = open_e * (turn(x, LANES - 1) - x)
    flux_n = open_n * (pltpu.roll(x, rows - 1, 0) - x)
    lap = (flux_e - turn(flux_e, 1)) + (flux_n - pltpu.roll(flux_n, 1, 0))
    seam = jnp.where(phase == 1, flux_e, 0.0)
    seam_west = turn(seam, 1)
    added = seam - seam_west
    step = jnp.where(phase == 1, turn(lap, LANES - 1) - lap, turn(seam, LANES - 1) + seam_west)
    flux_e = (v + turn(v, LANES - 1)) * open_e * step
    in_block = (ids != MARGIN - 1) & (ids != MARGIN + ROWS - 1)
    face = jnp.where(in_block, (v + pltpu.roll(v, rows - 1, 0)) * open_n, 0.0)
    flux_n = face * (pltpu.roll(added, rows - 1, 0) - added)
    return (flux_e - turn(flux_e, 1)) + (flux_n - pltpu.roll(flux_n, 1, 0))


def gram_pairs():
    return [(i, j) for i in range(SOLVE_ITERS) for j in range(i, SOLVE_ITERS + 1)]


def surface_kernel(
    tall, strips, mean, recv_b, recv_a,
    basis_out, flow, partial, col_patch, row_patch,
    state, height, heights, transport, force, faces, slope, basis, weights, diagonal, sides,
):
    is_odd = odd("lon")
    rows = pl.ds(8, TALL)
    lanes = lane_ids(TALL)

    def received(start, count):
        here = pl.ds(start, count)
        got_a = recv_a[here, :]
        got_b = recv_b[here, :]
        return jnp.where(is_odd, got_b, got_a), jnp.where(is_odd, got_a, got_b)

    def ghost(east, west, first, count):
        return jnp.where(
            lane_ids(east.shape[0]) < 64, turn(east, (LANES - first) % LANES), turn(west, LANES - first - count)
        )

    from_east, from_west = received(TALL, TALL)
    for f in range(3):
        state[f, 0, rows, :] = tall[pl.ds(f * TALL, TALL), :]
        state[f, 1, rows, :] = ghost(from_east, from_west, f * WIDE, WIDE)
    last = lanes == LANES - 1
    first = lanes == 0

    def lane_sides(a, b):
        n = a.shape[0]
        ea, eb, wa, wb = turn(a, LANES - 1), turn(b, LANES - 1), turn(a, 1), turn(b, 1)
        return (
            (jnp.where(last[0:n], eb, ea), jnp.where(last[0:n], ea, eb)),
            (jnp.where(first[0:n], wb, wa), jnp.where(first[0:n], wa, wb)),
        )

    own = tall[pl.ds(3 * TALL, TALL), :]
    phase = lanes & 3
    from_east, from_west = received(0, TALL)
    to_east = column_strip(jnp.where(phase < 2, own, from_east))
    to_west = column_strip(jnp.where(phase < 2, from_west, own))
    changes = (jnp.where(phase < 2, to_east, to_west), jnp.where(phase < 2, to_west, to_east))
    deep = (own, jnp.where(phase < 2, from_west, from_east))
    col_patch[...] = changes[0][MARGIN : MARGIN + ROWS]
    to_lane = lax.broadcasted_iota(jnp.int32, (LANES, 2 * LANES), 1)
    from_lane = lax.broadcasted_iota(jnp.int32, (LANES, 2 * LANES), 0)
    column = to_lane & (LANES - 1)
    comp_of = jnp.where(from_lane < 4 * LEVELS, 0, 1)
    chosen = (
        ((column < 2) | (column >= LANES - 2))
        & ((from_lane & 3) == ((to_lane + 2) & 3))
        & (comp_of == (to_lane >> 7))
        & (from_lane < 4 * PLANES)
    )
    chooser = jnp.where(chosen, 1.0, 0.0)
    for half in range(2):
        total = lax.dot_general(
            changes[half], chooser, (((1,), (0,)), ((), ())),
            precision=lax.Precision.HIGHEST, preferred_element_type=F32,
        )
        share = 1.0 / jnp.maximum(pick(deep[half], ((lanes + 2) & 3) + 80), 1.0)
        for comp in range(2):
            change = total[:, comp * LANES : (comp + 1) * LANES] * share
            state[comp, half, rows, :] = state[comp, half, rows, :] - change
    number = lax.broadcasted_iota(jnp.int32, (STRIP, LANES), 0)
    level_of_row = jnp.where(number >= LEVELS, number - LEVELS, number).astype(F32)
    is_plane = number < PLANES
    not_last = lane_ids(STRIP) < LANES - 1
    for s in range(2):
        x, wet, v, deep = [], [], [], []
        for r in range(4):
            centre = strips[pl.ds((4 * s + r) * STRIP, STRIP), :]
            block, g = divmod(4 * s + r, 2)
            both = (centre, ghost(*received(TALL + block * STRIP, STRIP), 64 + 32 * g, 32))
            deep.append([b[20:21] for b in both])
            v.append([jnp.broadcast_to(b[21:22], (STRIP, LANES)) for b in both])
            wet.append([jnp.where(is_plane & (level_of_row < b[20:21]), 1.0, 0.0) for b in both])
            x.append([jnp.where(is_plane, b, 0.0) for b in both])
        half_range = range(2)
        lap = {}
        added = {}
        seam = [wet[1][h] * wet[2][h] * (x[2][h] - x[1][h]) for h in half_range]
        added[1] = seam
        added[2] = [-t for t in seam]
        along = {}
        for r in (1, 2):
            x_e = lane_sides(*x[r])[0]
            wet_e = lane_sides(*wet[r])[0]
            v_e = lane_sides(*v[r])[0]
            added_e = lane_sides(*added[r])[0]
            open_e = [wet[r][h] * wet_e[h] for h in half_range]
            edge = [open_e[h] * (x_e[h] - x[r][h]) for h in half_range]
            edge_w = lane_sides(*edge)[1]
            lap[r] = [
                edge[h]
                - edge_w[h]
                + wet[r][h] * (wet[r + 1][h] * (x[r + 1][h] - x[r][h]) + wet[r - 1][h] * (x[r - 1][h] - x[r][h]))
                for h in half_range
            ]
            edge = [
                jnp.where(not_last, 0.5 * (v[r][h] + v_e[h]) * open_e[h] * (added_e[h] - added[r][h]), 0.0)
                for h in half_range
            ]
            edge_w = lane_sides(*edge)[1]
            along[r] = [edge[h] - edge_w[h] for h in half_range]
        for h in half_range:
            face = [0.5 * (v[r][h] + v[r + 1][h]) * wet[r][h] * wet[r + 1][h] for r in range(3)]
            across = (face[0] * added[1][h], face[1] * (lap[2][h] - lap[1][h]), -face[2] * added[2][h])
            second = (
                across[0],
                across[1] - across[0] + along[1][h],
                across[2] - across[1] + along[2][h],
                -across[2],
            )
            for r in range(4):
                change = second[r]
                if h == 0 and r >= 2:
                    row_patch[pl.ds((2 * s + r - 2) * STRIP, STRIP), :] = change
                where = 8 + MARGIN + ((ROWS + 1 - r) if s == 0 else (r - 2))
                for comp in range(2):
                    mine = (number >= comp * LEVELS) & (number < (comp + 1) * LEVELS)
                    total = jnp.sum(jnp.where(mine, change, 0.0), axis=0, keepdims=True)
                    total = total / jnp.maximum(deep[r][h], 1.0)
                    state[comp, h, where : where + 1, :] = state[comp, h, where : where + 1, :] - total
    for comp in range(2):
        here = pl.ds(comp * ROWS, ROWS)
        started = state[comp, 0, pl.ds(8 + MARGIN, ROWS), :] - tall[pl.ds(comp * TALL + MARGIN, ROWS), :]
        flow[here, :] = -(started + mean[here, :])

    halves = range(2)
    ahead = lanes[0:8] >= LANES - 2
    behind = lanes[0:8] < 2

    def far_sides(a, b):
        ea, eb, wa, wb = turn(a, LANES - 2), turn(b, LANES - 2), turn(a, 2), turn(b, 2)
        return (
            (jnp.where(ahead, eb, ea), jnp.where(ahead, ea, eb)),
            (jnp.where(behind, wb, wa), jnp.where(behind, wa, wb)),
        )

    for half in halves:
        d = state[2, half, rows, :]
        slope[half, rows, :] = jnp.where(d > 0.0, SLOPE, 0.0)
        force[half, rows, :] = SLOPE * d
        transport[half, rows, :] = d * state[1, half, rows, :]
    tiles = range(8, 8 + TALL, 8)
    for tile in tiles:
        here, above, below = (pl.ds(tile + off, 8) for off in (0, 1, -1))
        east, west = lane_sides(force[0, here, :], force[1, here, :])
        for h in halves:
            faces[0, h, here, :] = east[h]
            faces[1, h, here, :] = west[h]
            faces[2, h, here, :] = force[h, above, :]
            faces[3, h, here, :] = force[h, below, :]
    for tile in tiles:
        here, above, below = (pl.ds(tile + off, 8) for off in (0, 1, -1))
        east, west = lane_sides(*(state[2, h, here, :] * state[0, h, here, :] for h in halves))
        for h in halves:
            divergence = (east[h] - west[h]) + (transport[h, above, :] - transport[h, below, :])
            force[h, here, :] = divergence
            new = -slope[h, here, :] * divergence
            heights[0, h, here, :] = new
            height[h, here, :] = new
    for step in range(1, SUBCYCLES):
        cut = min(8 * ((6 + 2 * step) // 8), 16)
        now, later = heights.at[(step - 1) % 2], heights.at[step % 2]
        for tile in range(8 + cut, 8 + TALL - cut, 8):
            here, above, below = (pl.ds(tile + off, 8) for off in (0, 2, -2))
            centres = [now[h, here, :] for h in halves]
            east, west = far_sides(*centres)
            for h, x in enumerate(centres):
                along = faces[0, h, here, :] * (east[h] - x) - faces[1, h, here, :] * (x - west[h])
                across = faces[2, h, here, :] * (now[h, above, :] - x) - faces[3, h, here, :] * (x - now[h, below, :])
                change = force[h, here, :] - (along + across)
                force[h, here, :] = change
                new = x - slope[h, here, :] * change
                later[h, here, :] = new
                height[h, here, :] = height[h, here, :] + new
    mine = pl.ds(8 + MARGIN, ROWS)
    east, west = lane_sides(height[0, mine, :], height[1, mine, :])
    inner = slope[0, mine, :]
    north, south = (height[0, pl.ds(8 + MARGIN + off, ROWS), :] for off in (1, -1))
    for comp, gradient in enumerate((east[0] - west[0], north - south)):
        here = pl.ds(comp * ROWS, ROWS)
        flow[here, :] = flow[here, :] + (state[comp, 0, mine, :] - inner * gradient)
    final = heights.at[(SUBCYCLES - 1) % 2]
    scale = 2.0 / RADIUS
    short = ROWS + 16
    base = MARGIN

    tiles = range(0, short, 8)

    def spin(tile, a, b):
        here = pl.ds(base + tile, 8)
        for n, pair in enumerate(lane_sides(a, b)):
            for h in halves:
                sides[n, h, here, :] = pair[h]

    def nine(read, tile, h):
        out = []
        for off in (0, 1, -1):
            where = pl.ds(base + tile + off, 8)
            out += [read(h, where), sides[0, h, where, :], sides[1, h, where, :]]
        return out

    for tile in tiles:
        here = pl.ds(base + tile, 8)
        spin(tile, state[2, 0, here, :], state[2, 1, here, :])
    for tile in tiles:
        here = pl.ds(tile, 8)
        for h in halves:
            around = nine(lambda h, where: state[2, h, where, :], tile, h)
            d = around[0]
            wet = d > 0.0
            total = jnp.where(wet, 0.05, 1.0)
            for n in range(1, 9):
                factor = 0.5 if n in (1, 2, 3, 6) else 0.25
                w = jnp.where(wet & (around[n] > 0.0), factor * (d + around[n]), 0.0)
                weights[n - 1, h, here, :] = scale * w
                total += w
            diagonal[h, here, :] = scale * (total - CENTRE)

    def applied(source, tile, h):
        around = nine(lambda h, where: basis[source, h, where, :], tile, h)
        here = pl.ds(tile, 8)
        terms = [weights[n - 1, h, here, :] * around[n] for n in range(1, 9)]
        while len(terms) > 1:
            terms = [a + b for a, b in zip(terms[::2], terms[1::2])]
        return diagonal[h, here, :] * around[0] - terms[0]

    for tile in tiles:
        here = pl.ds(base + tile, 8)
        pair = [final[h, here, :] for h in halves]
        for h in halves:
            basis[0, h, here, :] = pair[h]
        spin(tile, *pair)
    for k in range(1, SOLVE_ITERS):
        for tile in tiles:
            here = pl.ds(base + tile, 8)
            for h in halves:
                x = applied(k - 1, tile, h)
                basis[k, h, here, :] = 0.5 * x if k == 1 else x - basis[k - 2, h, here, :]
        for tile in tiles:
            here = pl.ds(base + tile, 8)
            spin(tile, basis[k, 0, here, :], basis[k, 1, here, :])
    for tile in tiles[1:-1]:
        here = pl.ds(base + tile, 8)
        basis[SOLVE_ITERS, 0, here, :] = applied(SOLVE_ITERS - 1, tile, 0) - basis[SOLVE_ITERS - 2, 0, here, :]
    lane = lane_ids(1)
    row = jnp.zeros((1, LANES), F32)
    mine = pl.ds(8 + MARGIN, ROWS)
    for n, (i, j) in enumerate(gram_pairs()):
        product = basis[i, 0, mine, :] * basis[j, 0, mine, :]
        row = jnp.where(lane == n, jnp.sum(jnp.sum(product, axis=0, keepdims=True), axis=1, keepdims=True), row)
    partial[...] = jnp.broadcast_to(row, partial.shape)
    for i in range(SOLVE_ITERS):
        for half in range(2):
            basis_out[i, half] = basis[i, half, pl.ds(base, short), :]


def solve_coefficients(gram):
    half = 0.5 * RADIUS

    def image_of(d):
        out = [None] * (len(d) + 1)

        def add(n, term):
            out[n] = term if out[n] is None else out[n] + term

        for j, value in enumerate(d):
            add(j, CENTRE * value)
            if j == 0:
                add(1, RADIUS * value)
            else:
                add(j + 1, half * value)
                add(j - 1, half * value)
        return out

    def inner(a, b):
        total = None
        for i, x in enumerate(a):
            for j, y in enumerate(b):
                term = x * y * gram[(min(i, j), max(i, j))]
                total = term if total is None else total + term
        return total

    one = jnp.ones((8, LANES), F32)
    residual, direction, surface = [one], [one], [0.0 * one]
    norm = gram[(0, 0)]
    for iteration in range(SOLVE_ITERS):
        image = image_of(direction)
        step = norm / inner(direction, image)
        surface = [a + step * b for a, b in zip(surface, direction)] + [0.0 * one]
        if iteration == SOLVE_ITERS - 1:
            break
        residual = [(residual[n] if n < len(residual) else 0.0) - step * x for n, x in enumerate(image)]
        fresh = inner(residual, residual)
        ratio = fresh / norm
        direction = [x + (ratio * direction[n] if n < len(direction) else 0.0) for n, x in enumerate(residual)]
        norm = fresh
    return surface[:SOLVE_ITERS]


def final_kernel(gathered, basis, flow, star, lev, velocity_out, surface_out, pad, change):
    sums = jnp.sum(gathered[...], axis=0, keepdims=True)
    lane = lane_ids(1)
    gram = {}
    for n, pair in enumerate(gram_pairs()):
        value = jnp.sum(jnp.where(lane == n, sums, 0.0), axis=1, keepdims=True)
        gram[pair] = jnp.broadcast_to(value, (8, LANES))
    coefficients = [c[0:1] for c in solve_coefficients(gram)]
    for half in range(2):
        total = coefficients[0] * basis[0, half]
        for i in range(1, SOLVE_ITERS):
            total += coefficients[i] * basis[i, half]
        pad[half] = total
    mine = pl.ds(8, ROWS)
    centre = pad[0, mine, :]
    ghost = pad[1, mine, :]
    surface_out[...] = centre
    lanes = lane_ids(ROWS)
    east = jnp.where(lanes == LANES - 1, turn(ghost, LANES - 1), turn(centre, LANES - 1))
    west = jnp.where(lanes == 0, turn(ghost, 1), turn(centre, 1))
    levels = lev[...]
    slope = jnp.where(levels > 0, SLOPE, 0.0)
    slopes = (east - west, pad[0, pl.ds(9, ROWS), :] - pad[0, pl.ds(7, ROWS), :])
    for comp in range(2):
        here = pl.ds(comp * ROWS, ROWS)
        change[comp] = flow[here, :] - slope * slopes[comp]


    def level_step(k, carry):
        wet = k < levels
        for comp in range(2):
            here = pl.ds(pl.multiple_of((comp * LEVELS + k) * ROWS, ROWS), ROWS)
            velocity_out[here, :] = star[here, :] + jnp.where(wet, change[comp], 0.0)
        return carry

    lax.fori_loop(0, LEVELS, level_step, 0, unroll=True)


def patch_kernel(star, col_patch, row_patch, out):
    lanes = lane_ids(ROWS)
    rims = (lanes < 2) | (lanes >= LANES - 2)
    ids = row_ids(8)

    def plane(p, carry):
        here = pl.ds(pl.multiple_of(p * ROWS, ROWS), ROWS)
        out[here, :] = star[here, :] - jnp.where(rims, turn(col_patch[...], 126 - 4 * p), 0.0)
        for first, pieces in ((ROWS - 8, ((7, 0), (6, 1))), (0, ((0, 2), (1, 3)))):
            here = pl.ds(pl.multiple_of(p * ROWS + first, 8), 8)
            x = out[here, :]
            for row, n in pieces:
                x = x - jnp.where(ids == row, row_patch[pl.ds(n * STRIP + p, 1), :], 0.0)
            out[here, :] = x
        return carry

    lax.fori_loop(0, PLANES, plane, 0, unroll=10)


def call(kernel, shapes, scratch, flops, *args, far=False):
    out = tuple(jax.ShapeDtypeStruct(s, F32) for s in shapes)
    moved = sum(4 * math.prod(a.shape) for a in args) + sum(4 * math.prod(s) for s in shapes)
    if far:
        args = [pltpu.with_memory_space_constraint(a, pltpu.HBM) for a in args]
    return pl.pallas_call(
        kernel,
        out_shape=out,
        in_specs=[pl.BlockSpec(memory_space=pltpu.HBM if far else pltpu.VMEM)] * len(args),
        scratch_shapes=[pltpu.VMEM(s, F32) if isinstance(s, tuple) else s for s in scratch],
        compiler_params=pltpu.CompilerParams(vmem_limit_bytes=32 * 1024 * 1024),
        cost_estimate=pl.CostEstimate(flops=flops, bytes_accessed=moved, transcendentals=0),
    )(*args)


def pair_tables(lon, lat):
    def index(i, j):
        return j * lat + i

    lat_a, lat_b, lon_a, lon_b = [], [], [], []
    for j in range(lon):
        for i in range(lat):
            lat_a.append((index(i, j), index(i ^ 1, j)))
            if i == lat - 1:
                lat_b.append((index(i, j), index(i, lon - 1 - j)))
            elif i > 0:
                lat_b.append((index(i, j), index(i + 1 if i % 2 else i - 1, j)))
            else:
                lat_b.append((index(i, j), index(i, j ^ 1)))
            lon_a.append((index(i, j), index(i, j ^ 1)))
            lon_b.append((index(i, j), index(i, (j + 1 if j % 2 else j - 1) % lon)))
    return lat_a, lat_b, lon_a, lon_b


def per_device(lon, lat, tracers, velocity, active_levels, diffusivity, viscosity, ocean_depth, wind_forcing):
    lat_a, lat_b, lon_a, lon_b = pair_tables(lon, lat)

    def swap(x, pairs):
        return lax.ppermute(x, BOTH, pairs)

    block = (ROWS, LANES)
    tra = tracers.reshape(PLANES * ROWS, LANES)
    vel = velocity.reshape(PLANES * ROWS, LANES)
    wind = wind_forcing.reshape(2 * ROWS, LANES)
    rim = (RIMS, LANES)
    star, mean, fields, cols, north, south, send_a, send_b = call(
        block_kernel,
        [(PLANES * ROWS, LANES), (2 * ROWS, LANES), (3 * ROWS, LANES), block, rim, rim, (LAT_SEND, LANES), (LAT_SEND, LANES)],
        [(4,) + block, (4,) + block, (2,) + block, block, (PLANES * ROWS + 16, LANES), (PLANES, 8, LANES), (PLANES, 8, LANES), block, block, block, wind.shape,
         block, (PLANES * ROWS + 16, LANES),
         pltpu.VMEM(block, jnp.int32), pltpu.SemaphoreType.DMA((8,))],
        10**7,
        vel, tra.reshape(PLANES, ROWS, LANES), active_levels, viscosity, diffusivity, ocean_depth, wind,
        far=True,
    )
    got_a = swap(send_a, lat_a)
    got_b = swap(send_b, lat_b)
    (tracer_cols,) = call(tracer_rim_kernel, [block], [], 10**5, tra)
    tall, strips, tracer_rows, send_a, send_b = call(
        widen_kernel,
        [(4 * TALL, LANES), (8 * STRIP, LANES), (4 * STRIP, LANES), (LON_SEND, LANES), (LON_SEND, LANES)],
        [(TALL, LANES)] * 2,
        10**6,
        fields, cols, tracer_cols, diffusivity, north, south, got_b, got_a,
    )
    got_a = swap(send_a, lon_a)
    got_b = swap(send_b, lon_b)
    (tracers_out,) = call(
        tracer_kernel, [(PLANES * ROWS, LANES)], [block, (4,) + block, (4,) + block], 10**6,
        tra, active_levels, diffusivity, tracer_rows, got_b, got_a,
    )
    padded = (2, TALL + 16, LANES)
    short = (2, ROWS + 16, LANES)
    basis, flow, partial, col_patch, row_patch = call(
        surface_kernel,
        [(SOLVE_ITERS,) + short, (2 * ROWS, LANES), (lon * lat, LANES), block, (4 * STRIP, LANES)],
        [(3,) + padded, padded, (2,) + padded, padded, padded, (4,) + padded, padded, (SOLVE_ITERS + 1,) + padded, (8,) + short, short, (2,) + padded],
        10**7,
        tall, strips, mean, got_b, got_a,
    )
    gathered = lax.all_to_all(partial, BOTH, 0, 0, tiled=True)
    (star,) = call(patch_kernel, [(PLANES * ROWS, LANES)], [], 10**6, star, col_patch, row_patch)
    velocity_out, surface = call(
        final_kernel, [(PLANES * ROWS, LANES), block],
        [short, (2,) + block], 10**6,
        gathered, basis, flow, star, active_levels,
    )
    return tracers_out.reshape(tracers.shape), velocity_out.reshape(velocity.shape), surface


def solution(mesh):
    placed = (
        P(None, None, "lat", "lon"),
        P(None, None, "lat", "lon"),
        P("lat", "lon"),
        P("lat", "lon"),
        P("lat", "lon"),
        P("lat", "lon"),
        P(None, "lat", "lon"),
    )
    return jax.shard_map(
        functools.partial(per_device, mesh.shape["lon"], mesh.shape["lat"]),
        mesh=mesh,
        in_specs=placed,
        out_specs=(P(None, None, "lat", "lon"), P(None, None, "lat", "lon"), P("lat", "lon")),
        check_vma=False,
    )
```

```python
import functools
import math

import jax
import jax.numpy as jnp
from jax import lax
from jax.experimental import pallas as pl
from jax.experimental.pallas import tpu as pltpu
from jax.sharding import PartitionSpec as P

SUBCYCLES = 8
SOLVE_ITERS = 4
LEVELS = 10
PLANES = 2 * LEVELS
ROWS = 64
LANES = 128
MARGIN = 24
TALL = ROWS + 2 * MARGIN
RIM = 32
SLOPE = 0.15
CENTRE = 5.0
RADIUS = 5.0
F32 = jnp.float32
BOTH = ("lon", "lat")

STRIP = 24
RIMS = 3 * STRIP
SENT = 20
FULL = 22
EDGE = 21
NEAR, NEXT, COLS = 3 * SENT, 3 * SENT + FULL, 3 * SENT + 2 * FULL
LAT_SEND = COLS + MARGIN
LON_SEND = 2 * TALL
WIDE = 21


def lane_ids(rows):
    return lax.broadcasted_iota(jnp.int32, (rows, LANES), 1)


def row_ids(rows):
    return lax.broadcasted_iota(jnp.int32, (rows, LANES), 0)


def turn(x, shift):
    return pltpu.roll(x, shift, 1)


def pick(x, index):
    return jnp.take_along_axis(x, index, axis=1)


def flip_lanes(x, mask=LANES - 1):
    return pick(x, lane_ids(x.shape[0]) ^ mask)


def flip_rows(x):
    rows = x.shape[0]
    ids = row_ids(rows)
    for bit in range(3):
        step = 1 << bit
        x = jnp.where((ids & step) != 0, pltpu.roll(x, step, 0), pltpu.roll(x, rows - step, 0))
    return jnp.concatenate([x[r : r + 8] for r in range(rows - 8, -8, -8)], axis=0)


def odd(axis):
    return lax.rem(lax.axis_index(axis), 2) == 1


def at_fold():
    return lax.axis_index("lat") == lax.axis_size("lat") - 1


def shifted(x):
    rows = x.shape[0]
    return (turn(x, LANES - 1), turn(x, 1), pltpu.roll(x, rows - 1, 0), pltpu.roll(x, 1, 0))


def block_kernel(
    vel_far, tra_far, lev_far, visc_far, diff_far, depth_far, wind_far,
    star, mean, fields, cols, north, south, send_a, send_b, edge_a, edge_b,
    faces, face_levels, sums, turning, vel, tra_north, tra_south, visc, diff, depth, wind, levels_kept, laps, lev, done,
):
    pairs = (
        (lev_far, lev), (visc_far, visc), (vel_far, vel), (tra_far.at[:, pl.ds(ROWS - 8, 8)], tra_north),
        (tra_far.at[:, pl.ds(0, 8)], tra_south), (wind_far, wind), (depth_far, depth), (diff_far, diff),
    )
    copies = [
        pltpu.make_async_copy(far, near.at[pl.ds(8, PLANES * ROWS)] if near is vel else near, done.at[n])
        for n, (far, near) in enumerate(pairs)
    ]
    for copy in copies:
        copy.start()
    for copy in copies[:2]:
        copy.wait()
    lanes = lane_ids(ROWS)
    ids = row_ids(ROWS)
    levels = lev[...].astype(F32)
    v = visc[...]
    inside = (lanes < LANES - 1, lanes > 0, ids < ROWS - 1, ids > 0)
    for n, (v_n, level_n) in enumerate(zip(shifted(v), shifted(levels))):
        faces[n] = 0.5 * (v + v_n)
        face_levels[n] = jnp.where(inside[n], jnp.minimum(levels, level_n), 0.0)
    row = (lax.axis_index("lat") * ROWS).astype(F32) + ids.astype(F32)
    turning[...] = 0.25 * jnp.sin(math.pi * ((row + 0.5) / (ROWS * lax.axis_size("lat")) - 0.5))
    sums[...] = jnp.zeros((2, ROWS, LANES), F32)
    levels_kept[...] = levels
    for padded in (vel, laps):
        padded[0:8, :] = jnp.zeros((8, LANES), F32)
        padded[PLANES * ROWS + 8 : PLANES * ROWS + 16, :] = jnp.zeros((8, LANES), F32)
    acc = jnp.where((lanes >> 2) == 20, turn(levels, 82), 0.0)
    cols[...] = jnp.where((lanes >> 2) == 21, turn(v, 86), acc)
    copies[2].wait()

    def lap_step(k, carry):
        level = k.astype(F32)
        open_faces = [level < face_levels[n] for n in range(4)]
        ones = [jnp.where(o, 1.0, 0.0) for o in open_faces]
        count = (ones[0] + ones[1]) + (ones[2] + ones[3])
        packed = cols[...]
        for comp in range(2):
            p = comp * LEVELS + k
            start = 8 + pl.multiple_of(p * ROWS, ROWS)
            x = vel[pl.ds(start, ROWS), :]
            around = (turn(x, LANES - 1), turn(x, 1), vel[pl.ds(start + 1, ROWS), :], vel[pl.ds(start - 1, ROWS), :])
            picked = [jnp.where(open_faces[n], around[n], 0.0) for n in range(4)]
            laps[pl.ds(start, ROWS), :] = (picked[0] + picked[1]) + (picked[2] + picked[3]) - count * x
            packed = jnp.where((lanes >> 2) == p, turn(x, 4 * p + 2), packed)
        cols[...] = packed
        return carry

    def star_step(k, carry):
        level = k.astype(F32)
        wet = level < levels_kept[...]
        weights = [jnp.where(level < face_levels[n], faces[n], 0.0) for n in range(4)]
        weight = (weights[0] + weights[1]) + (weights[2] + weights[3])
        starts = [8 + pl.multiple_of((comp * LEVELS + k) * ROWS, ROWS) for comp in range(2)]
        values = [vel[pl.ds(s, ROWS), :] for s in starts]
        for comp, x in enumerate(values):
            start = starts[comp]
            lap = laps[pl.ds(start, ROWS), :]
            around = (turn(lap, LANES - 1), turn(lap, 1), laps[pl.ds(start + 1, ROWS), :], laps[pl.ds(start - 1, ROWS), :])
            terms = [weights[n] * around[n] for n in range(4)]
            second = (terms[0] + terms[1]) + (terms[2] + terms[3]) - weight * lap
            rotated = values[1] if comp == 0 else -values[0]
            out = jnp.where(wet, x - second + turning[...] * rotated, 0.0)
            star[pl.ds(pl.multiple_of((comp * LEVELS + k) * ROWS, ROWS), ROWS), :] = out
            sums[comp] += out
        return carry

    lax.fori_loop(0, LEVELS, lap_step, 0, unroll=10)
    lax.fori_loop(0, LEVELS, star_step, 0, unroll=10)
    for copy in copies[3:]:
        copy.wait()

    ocean = levels > 0.0
    for comp in range(2):
        here = pl.ds(comp * ROWS, ROWS)
        column_mean = sums[comp] / jnp.maximum(levels, 1.0)
        mean[here, :] = column_mean
        fields[here, :] = column_mean + jnp.where(ocean, wind[here, :], 0.0)
    fields[pl.ds(2 * ROWS, ROWS), :] = jnp.where(ocean, depth[...], 0.0)
    for edge, step, out, tra in ((ROWS - 1, -1, north, tra_north), (0, 1, south, tra_south)):
        out[...] = jnp.zeros((RIMS, LANES), F32)
        for d in range(2):
            r = edge + d * step
            out[pl.ds(d * STRIP, PLANES), :] = vel[pl.ds(8 + r, PLANES, stride=ROWS), :]
            out[pl.ds(d * STRIP + 20, 1), :] = levels[r : r + 1]
            out[pl.ds(d * STRIP + 21, 1), :] = visc[pl.ds(r, 1), :]
        out[pl.ds(2 * STRIP, PLANES), :] = tra[:, edge % 8, :]
        out[pl.ds(2 * STRIP + 20, 1), :] = diff[pl.ds(edge, 1), :]
    lat_odd = odd("lat")

    def put(start, up, down):
        here = pl.ds(start, up.shape[0])
        send_a[here, :] = jnp.where(lat_odd, down, up)
        send_b[here, :] = jnp.where(lat_odd, up, down)

    for f in range(3):
        put(f * SENT, fields[pl.ds((f + 1) * ROWS - SENT, SENT), :], fields[pl.ds(f * ROWS, SENT), :])
    edge_a[...] = jnp.where(lat_odd, south[2 * STRIP : RIMS, :], north[2 * STRIP : RIMS, :])
    edge_b[...] = jnp.where(lat_odd, north[2 * STRIP : RIMS, :], south[2 * STRIP : RIMS, :])
    for start, first, count in ((NEAR, 0, FULL), (NEXT, STRIP, FULL)):
        put(start, north[pl.ds(first, count), :], south[pl.ds(first, count), :])
    put(COLS, cols[ROWS - MARGIN : ROWS, :], cols[0:MARGIN, :])

    @pl.when(at_fold())
    def _():
        for f in range(3):
            turned = flip_rows(flip_lanes(fields[pl.ds((f + 1) * ROWS - MARGIN, MARGIN), :]))[0:SENT]
            send_b[pl.ds(f * SENT, SENT), :] = turned if f == 2 else -turned
        turned = flip_lanes(north[...])
        r = row_ids(RIMS)
        is_velocity = (r < PLANES) | ((r >= STRIP) & (r < STRIP + PLANES))
        turned = jnp.where(is_velocity, -turned, turned)
        edge_b[...] = turned[2 * STRIP : RIMS]
        for start, first, count in ((NEAR, 0, FULL), (NEXT, STRIP, FULL)):
            send_b[pl.ds(start, count), :] = turned[first : first + count]
        turned = flip_rows(flip_lanes(cols[ROWS - MARGIN : ROWS, :], 3))
        send_b[pl.ds(COLS, MARGIN), :] = jnp.where(lane_ids(MARGIN) < 4 * PLANES, -turned, turned)


def tracer_rim_kernel(tra, out):
    lanes = lane_ids(ROWS)

    def tracer_step(p, acc):
        t = tra[pl.ds(pl.multiple_of(p * ROWS, ROWS), ROWS), :]
        return jnp.where((lanes >> 1) == 44 + p, turn(t, lax.rem(89 + 2 * p, LANES)), acc)

    out[...] = lax.fori_loop(0, PLANES, tracer_step, jnp.zeros((ROWS, LANES), F32), unroll=True)


def widen_kernel(fields, cols, tracer_cols, diff, north, south, recv_b, recv_a, tall, strips, level_rows, send_a, send_b, east, west):
    lat_odd = odd("lat")
    lon_odd = odd("lon")
    at_south = lax.axis_index("lat") == 0
    def received(start, count):
        here = pl.ds(start, count)
        got_a = recv_a[here, :]
        got_b = jnp.where(at_south, 0.0, recv_b[here, :])
        return jnp.where(lat_odd, got_b, got_a), jnp.where(lat_odd, got_a, got_b)

    lanes = lane_ids(TALL)
    acc_east = jnp.zeros((TALL, LANES), F32)
    acc_west = jnp.zeros((TALL, LANES), F32)
    for f in range(3):
        from_north, from_south = received(f * SENT, SENT)
        unused = jnp.zeros((MARGIN - SENT, LANES), F32)
        tall[pl.ds(f * TALL, MARGIN - SENT), :] = unused
        tall[pl.ds(f * TALL + MARGIN - SENT, SENT), :] = from_south
        tall[pl.ds(f * TALL + MARGIN, ROWS), :] = fields[pl.ds(f * ROWS, ROWS), :]
        tall[pl.ds(f * TALL + MARGIN + ROWS, SENT), :] = from_north
        tall[pl.ds(f * TALL + MARGIN + ROWS + SENT, MARGIN - SENT), :] = unused
        x = tall[pl.ds(f * TALL, TALL), :]
        here = (lanes >= f * WIDE) & (lanes < (f + 1) * WIDE)
        acc_east = jnp.where(here, turn(x, (f + 1) * WIDE), acc_east)
        acc_west = jnp.where(here, turn(x, f * WIDE), acc_west)
    from_north, from_south = received(COLS, MARGIN)
    tall[pl.ds(3 * TALL, MARGIN), :] = from_south
    tall[pl.ds(3 * TALL + MARGIN, ROWS), :] = jnp.where(lane_ids(ROWS) < 88, cols[...], tracer_cols[...])
    tall[pl.ds(3 * TALL + MARGIN + ROWS, MARGIN), :] = from_north
    for out, acc, shift in ((east, acc_east, 64), (west, acc_west, 63)):
        out[...] = acc
        out[pl.ds(MARGIN, ROWS), :] = jnp.where(lane_ids(ROWS) == 63, turn(diff[...], shift), acc[MARGIN : MARGIN + ROWS])
    near, next_to = received(NEAR, FULL), received(NEXT, FULL)
    unused = jnp.zeros((STRIP - FULL, LANES), F32)
    group = lane_ids(STRIP) >> 5
    for s, own in enumerate((north, south)):
        pieces = (
            jnp.concatenate([next_to[s], unused], axis=0),
            jnp.concatenate([near[s], unused], axis=0),
            own[0:STRIP, :],
            own[STRIP : 2 * STRIP, :],
        )
        for r, x in enumerate(pieces):
            strips[pl.ds((4 * s + r) * STRIP, STRIP), :] = x
            block, g = divmod(4 * s + r, 2)
            here = pl.ds(block * STRIP, STRIP)
            east[here, :] = jnp.where(group == 2 + g, turn(x, (96 + 32 * g) % LANES), east[here, :])
            west[here, :] = jnp.where(group == 2 + g, turn(x, 64 + 32 * g), west[here, :])
        level_rows[pl.ds(8 * s, 8), :] = jnp.broadcast_to(near[s][20:21], (8, LANES))
    k = tall[pl.ds(3 * TALL, TALL), :]
    send_a[pl.ds(0, TALL), :] = k
    send_b[pl.ds(0, TALL), :] = k
    rest = pl.ds(TALL, TALL)
    e, w = east[...], west[...]
    send_a[rest, :] = jnp.where(lon_odd, w, e)
    send_b[rest, :] = jnp.where(lon_odd, e, w)


def tracer_kernel(tra, lev, diff, level_rows, edge_b, edge_a, recv_b, recv_a, out, swap, faces, face_levels, rim_rows):
    is_odd = odd("lon")
    lat_odd = odd("lat")
    from_a = edge_a[...]
    from_b = jnp.where(lax.axis_index("lat") == 0, 0.0, edge_b[...])
    rim_rows[0:STRIP, :] = jnp.where(lat_odd, from_b, from_a)
    rim_rows[STRIP : 2 * STRIP, :] = jnp.where(lat_odd, from_a, from_b)
    lanes = lane_ids(ROWS)
    ids = row_ids(ROWS)

    def received(start):
        here = pl.ds(start + MARGIN, ROWS)
        got_a = recv_a[here, :]
        got_b = recv_b[here, :]
        return jnp.where(is_odd, got_b, got_a), jnp.where(is_odd, got_a, got_b)

    east_cols, west_cols = received(0)
    east_rest, west_rest = received(TALL)
    swap[...] = jnp.where((lanes & 1) == 0, turn(east_cols, LANES - 1), turn(west_cols, 1))

    def sides(x, halo, row, rows=rim_rows, apart=STRIP):
        east, west, north, south = shifted(x)
        return (
            jnp.where(lanes == LANES - 1, halo, east),
            jnp.where(lanes == 0, halo, west),
            jnp.where(ids == ROWS - 1, rows[pl.ds(row, 1), :], north),
            jnp.where(ids == 0, rows[pl.ds(row + apart, 1), :], south),
        )

    level = lev[...].astype(F32)
    level_halo = jnp.where(lanes == LANES - 1, turn(east_cols, 45), turn(west_cols, 47))
    d = diff[...]
    d_halo = jnp.where(lanes == LANES - 1, turn(east_rest, 64), turn(west_rest, 65))
    for n, other in enumerate(sides(level, level_halo, 0, level_rows, 8)):
        face_levels[n] = jnp.minimum(level, other)
    for n, other in enumerate(sides(d, d_halo, 20)):
        faces[n] = 0.5 * (d + other)

    def level_step(k, carry):
        weights = [jnp.where(k.astype(F32) < face_levels[n], faces[n], 0.0) for n in range(4)]
        for comp in range(2):
            p = comp * LEVELS + k
            here = pl.ds(pl.multiple_of(p * ROWS, ROWS), ROWS)
            x = tra[here, :]
            around = sides(x, turn(swap[...], 39 - 2 * p), p)
            total = weights[0] * (around[0] - x)
            for n in range(1, 4):
                total += weights[n] * (around[n] - x)
            out[here, :] = x + total
        return carry

    lax.fori_loop(0, LEVELS, level_step, 0, unroll=2)


def column_strip(strip):
    rows = strip.shape[0]
    lanes = lane_ids(rows)
    ids = row_ids(rows)
    phase = lanes & 3
    group = lanes >> 2

    levels = pick(strip, phase + 80)
    v = 0.5 * pick(strip, phase + 84)
    number = jnp.where(group >= LEVELS, group - LEVELS, group)
    number = jnp.where(group < PLANES, number, LEVELS).astype(F32)
    wet = jnp.where(number < levels, 1.0, 0.0)
    x = strip
    open_e = wet * turn(wet, LANES - 1)
    open_n = wet * pltpu.roll(wet, rows - 1, 0)
    flux_e = open_e * (turn(x, LANES - 1) - x)
    flux_n = open_n * (pltpu.roll(x, rows - 1, 0) - x)
    lap = (flux_e - turn(flux_e, 1)) + (flux_n - pltpu.roll(flux_n, 1, 0))
    seam = jnp.where(phase == 1, flux_e, 0.0)
    seam_west = turn(seam, 1)
    added = seam - seam_west
    step = jnp.where(phase == 1, turn(lap, LANES - 1) - lap, turn(seam, LANES - 1) + seam_west)
    flux_e = (v + turn(v, LANES - 1)) * open_e * step
    in_block = (ids != MARGIN - 1) & (ids != MARGIN + ROWS - 1)
    face = jnp.where(in_block, (v + pltpu.roll(v, rows - 1, 0)) * open_n, 0.0)
    flux_n = face * (pltpu.roll(added, rows - 1, 0) - added)
    return (flux_e - turn(flux_e, 1)) + (flux_n - pltpu.roll(flux_n, 1, 0))


def gram_pairs():
    return [(i, j) for i in range(SOLVE_ITERS) for j in range(i, SOLVE_ITERS + 1)]


def surface_kernel(
    tall, strips, mean, recv_b, recv_a,
    basis_out, flow, partial, col_patch, row_patch,
    state, height, heights, transport, force, faces, slope, basis, weights, diagonal, sides,
):
    is_odd = odd("lon")
    rows = pl.ds(8, TALL)
    lanes = lane_ids(TALL)

    def received(start, count):
        here = pl.ds(start, count)
        got_a = recv_a[here, :]
        got_b = recv_b[here, :]
        return jnp.where(is_odd, got_b, got_a), jnp.where(is_odd, got_a, got_b)

    def ghost(east, west, first, count):
        return jnp.where(
            lane_ids(east.shape[0]) < 64, turn(east, (LANES - first) % LANES), turn(west, LANES - first - count)
        )

    from_east, from_west = received(TALL, TALL)
    for f in range(3):
        state[f, 0, rows, :] = tall[pl.ds(f * TALL, TALL), :]
        state[f, 1, rows, :] = ghost(from_east, from_west, f * WIDE, WIDE)
    last = lanes == LANES - 1
    first = lanes == 0

    def lane_sides(a, b):
        n = a.shape[0]
        ea, eb, wa, wb = turn(a, LANES - 1), turn(b, LANES - 1), turn(a, 1), turn(b, 1)
        return (
            (jnp.where(last[0:n], eb, ea), jnp.where(last[0:n], ea, eb)),
            (jnp.where(first[0:n], wb, wa), jnp.where(first[0:n], wa, wb)),
        )

    own = tall[pl.ds(3 * TALL, TALL), :]
    phase = lanes & 3
    from_east, from_west = received(0, TALL)
    to_east = column_strip(jnp.where(phase < 2, own, from_east))
    to_west = column_strip(jnp.where(phase < 2, from_west, own))
    changes = (jnp.where(phase < 2, to_east, to_west), jnp.where(phase < 2, to_west, to_east))
    deep = (own, jnp.where(phase < 2, from_west, from_east))
    col_patch[...] = changes[0][MARGIN : MARGIN + ROWS]
    to_lane = lax.broadcasted_iota(jnp.int32, (LANES, 2 * LANES), 1)
    from_lane = lax.broadcasted_iota(jnp.int32, (LANES, 2 * LANES), 0)
    column = to_lane & (LANES - 1)
    comp_of = jnp.where(from_lane < 4 * LEVELS, 0, 1)
    chosen = (
        ((column < 2) | (column >= LANES - 2))
        & ((from_lane & 3) == ((to_lane + 2) & 3))
        & (comp_of == (to_lane >> 7))
        & (from_lane < 4 * PLANES)
    )
    chooser = jnp.where(chosen, 1.0, 0.0)
    for half in range(2):
        total = lax.dot_general(
            changes[half], chooser, (((1,), (0,)), ((), ())),
            precision=lax.Precision.HIGHEST, preferred_element_type=F32,
        )
        share = 1.0 / jnp.maximum(pick(deep[half], ((lanes + 2) & 3) + 80), 1.0)
        for comp in range(2):
            change = total[:, comp * LANES : (comp + 1) * LANES] * share
            state[comp, half, rows, :] = state[comp, half, rows, :] - change
    number = lax.broadcasted_iota(jnp.int32, (STRIP, LANES), 0)
    level_of_row = jnp.where(number >= LEVELS, number - LEVELS, number).astype(F32)
    is_plane = number < PLANES
    not_last = lane_ids(STRIP) < LANES - 1
    for s in range(2):
        x, wet, v, deep = [], [], [], []
        for r in range(4):
            centre = strips[pl.ds((4 * s + r) * STRIP, STRIP), :]
            block, g = divmod(4 * s + r, 2)
            both = (centre, ghost(*received(TALL + block * STRIP, STRIP), 64 + 32 * g, 32))
            deep.append([b[20:21] for b in both])
            v.append([jnp.broadcast_to(b[21:22], (STRIP, LANES)) for b in both])
            wet.append([jnp.where(is_plane & (level_of_row < b[20:21]), 1.0, 0.0) for b in both])
            x.append([jnp.where(is_plane, b, 0.0) for b in both])
        half_range = range(2)
        lap = {}
        added = {}
        seam = [wet[1][h] * wet[2][h] * (x[2][h] - x[1][h]) for h in half_range]
        added[1] = seam
        added[2] = [-t for t in seam]
        along = {}
        for r in (1, 2):
            x_e = lane_sides(*x[r])[0]
            wet_e = lane_sides(*wet[r])[0]
            v_e = lane_sides(*v[r])[0]
            added_e = lane_sides(*added[r])[0]
            open_e = [wet[r][h] * wet_e[h] for h in half_range]
            edge = [open_e[h] * (x_e[h] - x[r][h]) for h in half_range]
            edge_w = lane_sides(*edge)[1]
            lap[r] = [
                edge[h]
                - edge_w[h]
                + wet[r][h] * (wet[r + 1][h] * (x[r + 1][h] - x[r][h]) + wet[r - 1][h] * (x[r - 1][h] - x[r][h]))
                for h in half_range
            ]
            edge = [
                jnp.where(not_last, 0.5 * (v[r][h] + v_e[h]) * open_e[h] * (added_e[h] - added[r][h]), 0.0)
                for h in half_range
            ]
            edge_w = lane_sides(*edge)[1]
            along[r] = [edge[h] - edge_w[h] for h in half_range]
        for h in half_range:
            face = [0.5 * (v[r][h] + v[r + 1][h]) * wet[r][h] * wet[r + 1][h] for r in range(3)]
            across = (face[0] * added[1][h], face[1] * (lap[2][h] - lap[1][h]), -face[2] * added[2][h])
            second = (
                across[0],
                across[1] - across[0] + along[1][h],
                across[2] - across[1] + along[2][h],
                -across[2],
            )
            for r in range(4):
                change = second[r]
                if h == 0 and r >= 2:
                    row_patch[pl.ds((2 * s + r - 2) * STRIP, STRIP), :] = change
                where = 8 + MARGIN + ((ROWS + 1 - r) if s == 0 else (r - 2))
                for comp in range(2):
                    mine = (number >= comp * LEVELS) & (number < (comp + 1) * LEVELS)
                    total = jnp.sum(jnp.where(mine, change, 0.0), axis=0, keepdims=True)
                    total = total / jnp.maximum(deep[r][h], 1.0)
                    state[comp, h, where : where + 1, :] = state[comp, h, where : where + 1, :] - total
    for comp in range(2):
        here = pl.ds(comp * ROWS, ROWS)
        started = state[comp, 0, pl.ds(8 + MARGIN, ROWS), :] - tall[pl.ds(comp * TALL + MARGIN, ROWS), :]
        flow[here, :] = -(started + mean[here, :])

    halves = range(2)
    ahead = lanes[0:8] >= LANES - 2
    behind = lanes[0:8] < 2

    def far_sides(a, b):
        ea, eb, wa, wb = turn(a, LANES - 2), turn(b, LANES - 2), turn(a, 2), turn(b, 2)
        return (
            (jnp.where(ahead, eb, ea), jnp.where(ahead, ea, eb)),
            (jnp.where(behind, wb, wa), jnp.where(behind, wa, wb)),
        )

    for half in halves:
        d = state[2, half, rows, :]
        slope[half, rows, :] = jnp.where(d > 0.0, SLOPE, 0.0)
        force[half, rows, :] = SLOPE * d
        transport[half, rows, :] = d * state[1, half, rows, :]
    tiles = range(8, 8 + TALL, 8)
    for tile in tiles:
        here, above, below = (pl.ds(tile + off, 8) for off in (0, 1, -1))
        east, west = lane_sides(force[0, here, :], force[1, here, :])
        for h in halves:
            faces[0, h, here, :] = east[h]
            faces[1, h, here, :] = west[h]
            faces[2, h, here, :] = force[h, above, :]
            faces[3, h, here, :] = force[h, below, :]
    for tile in tiles:
        here, above, below = (pl.ds(tile + off, 8) for off in (0, 1, -1))
        east, west = lane_sides(*(state[2, h, here, :] * state[0, h, here, :] for h in halves))
        for h in halves:
            divergence = (east[h] - west[h]) + (transport[h, above, :] - transport[h, below, :])
            force[h, here, :] = divergence
            new = -slope[h, here, :] * divergence
            heights[0, h, here, :] = new
            height[h, here, :] = new
    for step in range(1, SUBCYCLES):
        cut = min(8 * ((6 + 2 * step) // 8), 16)
        now, later = heights.at[(step - 1) % 2], heights.at[step % 2]
        for tile in range(8 + cut, 8 + TALL - cut, 8):
            here, above, below = (pl.ds(tile + off, 8) for off in (0, 2, -2))
            centres = [now[h, here, :] for h in halves]
            east, west = far_sides(*centres)
            for h, x in enumerate(centres):
                along = faces[0, h, here, :] * (east[h] - x) - faces[1, h, here, :] * (x - west[h])
                across = faces[2, h, here, :] * (now[h, above, :] - x) - faces[3, h, here, :] * (x - now[h, below, :])
                change = force[h, here, :] - (along + across)
                force[h, here, :] = change
                new = x - slope[h, here, :] * change
                later[h, here, :] = new
                height[h, here, :] = height[h, here, :] + new
    mine = pl.ds(8 + MARGIN, ROWS)
    east, west = lane_sides(height[0, mine, :], height[1, mine, :])
    inner = slope[0, mine, :]
    north, south = (height[0, pl.ds(8 + MARGIN + off, ROWS), :] for off in (1, -1))
    for comp, gradient in enumerate((east[0] - west[0], north - south)):
        here = pl.ds(comp * ROWS, ROWS)
        flow[here, :] = flow[here, :] + (state[comp, 0, mine, :] - inner * gradient)
    final = heights.at[(SUBCYCLES - 1) % 2]
    scale = 2.0 / RADIUS
    short = ROWS + 16
    base = MARGIN

    tiles = range(0, short, 8)

    def spin(tile, a, b):
        here = pl.ds(base + tile, 8)
        for n, pair in enumerate(lane_sides(a, b)):
            for h in halves:
                sides[n, h, here, :] = pair[h]

    def nine(read, tile, h):
        out = []
        for off in (0, 1, -1):
            where = pl.ds(base + tile + off, 8)
            out += [read(h, where), sides[0, h, where, :], sides[1, h, where, :]]
        return out

    for tile in tiles:
        here = pl.ds(base + tile, 8)
        spin(tile, state[2, 0, here, :], state[2, 1, here, :])
    for tile in tiles:
        here = pl.ds(tile, 8)
        for h in halves:
            around = nine(lambda h, where: state[2, h, where, :], tile, h)
            d = around[0]
            wet = d > 0.0
            total = jnp.where(wet, 0.05, 1.0)
            for n in range(1, 9):
                factor = 0.5 if n in (1, 2, 3, 6) else 0.25
                w = jnp.where(wet & (around[n] > 0.0), factor * (d + around[n]), 0.0)
                weights[n - 1, h, here, :] = scale * w
                total += w
            diagonal[h, here, :] = scale * (total - CENTRE)

    def applied(source, tile, h):
        around = nine(lambda h, where: basis[source, h, where, :], tile, h)
        here = pl.ds(tile, 8)
        terms = [weights[n - 1, h, here, :] * around[n] for n in range(1, 9)]
        while len(terms) > 1:
            terms = [a + b for a, b in zip(terms[::2], terms[1::2])]
        return diagonal[h, here, :] * around[0] - terms[0]

    for tile in tiles:
        here = pl.ds(base + tile, 8)
        pair = [final[h, here, :] for h in halves]
        for h in halves:
            basis[0, h, here, :] = pair[h]
        spin(tile, *pair)
    for k in range(1, SOLVE_ITERS):
        for tile in tiles:
            here = pl.ds(base + tile, 8)
            for h in halves:
                x = applied(k - 1, tile, h)
                basis[k, h, here, :] = 0.5 * x if k == 1 else x - basis[k - 2, h, here, :]
        for tile in tiles:
            here = pl.ds(base + tile, 8)
            spin(tile, basis[k, 0, here, :], basis[k, 1, here, :])
    for tile in tiles[1:-1]:
        here = pl.ds(base + tile, 8)
        basis[SOLVE_ITERS, 0, here, :] = applied(SOLVE_ITERS - 1, tile, 0) - basis[SOLVE_ITERS - 2, 0, here, :]
    lane = lane_ids(1)
    row = jnp.zeros((1, LANES), F32)
    mine = pl.ds(8 + MARGIN, ROWS)
    for n, (i, j) in enumerate(gram_pairs()):
        product = basis[i, 0, mine, :] * basis[j, 0, mine, :]
        row = jnp.where(lane == n, jnp.sum(jnp.sum(product, axis=0, keepdims=True), axis=1, keepdims=True), row)
    partial[...] = jnp.broadcast_to(row, partial.shape)
    for i in range(SOLVE_ITERS):
        for half in range(2):
            basis_out[i, half] = basis[i, half, pl.ds(base, short), :]


def solve_coefficients(gram):
    half = 0.5 * RADIUS

    def image_of(d):
        out = [None] * (len(d) + 1)

        def add(n, term):
            out[n] = term if out[n] is None else out[n] + term

        for j, value in enumerate(d):
            add(j, CENTRE * value)
            if j == 0:
                add(1, RADIUS * value)
            else:
                add(j + 1, half * value)
                add(j - 1, half * value)
        return out

    def inner(a, b):
        total = None
        for i, x in enumerate(a):
            for j, y in enumerate(b):
                term = x * y * gram[(min(i, j), max(i, j))]
                total = term if total is None else total + term
        return total

    one = jnp.ones((8, LANES), F32)
    residual, direction, surface = [one], [one], [0.0 * one]
    norm = gram[(0, 0)]
    for iteration in range(SOLVE_ITERS):
        image = image_of(direction)
        step = norm / inner(direction, image)
        surface = [a + step * b for a, b in zip(surface, direction)] + [0.0 * one]
        if iteration == SOLVE_ITERS - 1:
            break
        residual = [(residual[n] if n < len(residual) else 0.0) - step * x for n, x in enumerate(image)]
        fresh = inner(residual, residual)
        ratio = fresh / norm
        direction = [x + (ratio * direction[n] if n < len(direction) else 0.0) for n, x in enumerate(residual)]
        norm = fresh
    return surface[:SOLVE_ITERS]


def final_kernel(gathered, basis, flow, star, lev, velocity_out, surface_out, pad, change):
    sums = jnp.sum(gathered[...], axis=0, keepdims=True)
    lane = lane_ids(1)
    gram = {}
    for n, pair in enumerate(gram_pairs()):
        value = jnp.sum(jnp.where(lane == n, sums, 0.0), axis=1, keepdims=True)
        gram[pair] = jnp.broadcast_to(value, (8, LANES))
    coefficients = [c[0:1] for c in solve_coefficients(gram)]
    for half in range(2):
        total = coefficients[0] * basis[0, half]
        for i in range(1, SOLVE_ITERS):
            total += coefficients[i] * basis[i, half]
        pad[half] = total
    mine = pl.ds(8, ROWS)
    centre = pad[0, mine, :]
    ghost = pad[1, mine, :]
    surface_out[...] = centre
    lanes = lane_ids(ROWS)
    east = jnp.where(lanes == LANES - 1, turn(ghost, LANES - 1), turn(centre, LANES - 1))
    west = jnp.where(lanes == 0, turn(ghost, 1), turn(centre, 1))
    levels = lev[...]
    slope = jnp.where(levels > 0, SLOPE, 0.0)
    slopes = (east - west, pad[0, pl.ds(9, ROWS), :] - pad[0, pl.ds(7, ROWS), :])
    for comp in range(2):
        here = pl.ds(comp * ROWS, ROWS)
        change[comp] = flow[here, :] - slope * slopes[comp]


    def level_step(k, carry):
        wet = k < levels
        for comp in range(2):
            here = pl.ds(pl.multiple_of((comp * LEVELS + k) * ROWS, ROWS), ROWS)
            velocity_out[here, :] = star[here, :] + jnp.where(wet, change[comp], 0.0)
        return carry

    lax.fori_loop(0, LEVELS, level_step, 0, unroll=True)


def patch_kernel(star, col_patch, row_patch, out):
    lanes = lane_ids(ROWS)
    rims = (lanes < 2) | (lanes >= LANES - 2)
    ids = row_ids(8)

    def plane(p, carry):
        here = pl.ds(pl.multiple_of(p * ROWS, ROWS), ROWS)
        out[here, :] = star[here, :] - jnp.where(rims, turn(col_patch[...], 126 - 4 * p), 0.0)
        for first, pieces in ((ROWS - 8, ((7, 0), (6, 1))), (0, ((0, 2), (1, 3)))):
            here = pl.ds(pl.multiple_of(p * ROWS + first, 8), 8)
            x = out[here, :]
            for row, n in pieces:
                x = x - jnp.where(ids == row, row_patch[pl.ds(n * STRIP + p, 1), :], 0.0)
            out[here, :] = x
        return carry

    lax.fori_loop(0, PLANES, plane, 0, unroll=10)


def call(kernel, shapes, scratch, flops, *args, far=False):
    out = tuple(jax.ShapeDtypeStruct(s, F32) for s in shapes)
    moved = sum(4 * math.prod(a.shape) for a in args) + sum(4 * math.prod(s) for s in shapes)
    if far:
        args = [pltpu.with_memory_space_constraint(a, pltpu.HBM) for a in args]
    return pl.pallas_call(
        kernel,
        out_shape=out,
        in_specs=[pl.BlockSpec(memory_space=pltpu.HBM if far else pltpu.VMEM)] * len(args),
        scratch_shapes=[pltpu.VMEM(s, F32) if isinstance(s, tuple) else s for s in scratch],
        compiler_params=pltpu.CompilerParams(vmem_limit_bytes=32 * 1024 * 1024),
        cost_estimate=pl.CostEstimate(flops=flops, bytes_accessed=moved, transcendentals=0),
    )(*args)


def pair_tables(lon, lat):
    def index(i, j):
        return j * lat + i

    lat_a, lat_b, lon_a, lon_b = [], [], [], []
    for j in range(lon):
        for i in range(lat):
            lat_a.append((index(i, j), index(i ^ 1, j)))
            if i == lat - 1:
                lat_b.append((index(i, j), index(i, lon - 1 - j)))
            elif i > 0:
                lat_b.append((index(i, j), index(i + 1 if i % 2 else i - 1, j)))
            else:
                lat_b.append((index(i, j), index(i, j ^ 1)))
            lon_a.append((index(i, j), index(i, j ^ 1)))
            lon_b.append((index(i, j), index(i, (j + 1 if j % 2 else j - 1) % lon)))
    return lat_a, lat_b, lon_a, lon_b


def per_device(lon, lat, tracers, velocity, active_levels, diffusivity, viscosity, ocean_depth, wind_forcing):
    lat_a, lat_b, lon_a, lon_b = pair_tables(lon, lat)

    def swap(x, pairs):
        return lax.ppermute(x, BOTH, pairs)

    block = (ROWS, LANES)
    tra = tracers.reshape(PLANES * ROWS, LANES)
    vel = velocity.reshape(PLANES * ROWS, LANES)
    wind = wind_forcing.reshape(2 * ROWS, LANES)
    rim = (RIMS, LANES)
    star, mean, fields, cols, north, south, send_a, send_b, edge_a, edge_b = call(
        block_kernel,
        [(PLANES * ROWS, LANES), (2 * ROWS, LANES), (3 * ROWS, LANES), block, rim, rim, (LAT_SEND, LANES), (LAT_SEND, LANES),
         (STRIP, LANES), (STRIP, LANES)],
        [(4,) + block, (4,) + block, (2,) + block, block, (PLANES * ROWS + 16, LANES), (PLANES, 8, LANES), (PLANES, 8, LANES), block, block, block, wind.shape,
         block, (PLANES * ROWS + 16, LANES),
         pltpu.VMEM(block, jnp.int32), pltpu.SemaphoreType.DMA((8,))],
        10**7,
        vel, tra.reshape(PLANES, ROWS, LANES), active_levels, viscosity, diffusivity, ocean_depth, wind,
        far=True,
    )
    got_a = swap(send_a, lat_a)
    got_b = swap(send_b, lat_b)
    edge_a = swap(edge_a, lat_a)
    edge_b = swap(edge_b, lat_b)
    (tracer_cols,) = call(tracer_rim_kernel, [block], [], 10**5, tra)
    tall, strips, level_rows, send_a, send_b = call(
        widen_kernel,
        [(4 * TALL, LANES), (8 * STRIP, LANES), (16, LANES), (LON_SEND, LANES), (LON_SEND, LANES)],
        [(TALL, LANES)] * 2,
        10**6,
        fields, cols, tracer_cols, diffusivity, north, south, got_b, got_a,
    )
    got_a = swap(send_a, lon_a)
    got_b = swap(send_b, lon_b)
    (tracers_out,) = call(
        tracer_kernel, [(PLANES * ROWS, LANES)], [block, (4,) + block, (4,) + block, (2 * STRIP, LANES)], 10**6,
        tra, active_levels, diffusivity, level_rows, edge_b, edge_a, got_b, got_a,
    )
    padded = (2, TALL + 16, LANES)
    short = (2, ROWS + 16, LANES)
    basis, flow, partial, col_patch, row_patch = call(
        surface_kernel,
        [(SOLVE_ITERS,) + short, (2 * ROWS, LANES), (lon * lat, LANES), block, (4 * STRIP, LANES)],
        [(3,) + padded, padded, (2,) + padded, padded, padded, (4,) + padded, padded, (SOLVE_ITERS + 1,) + padded, (8,) + short, short, (2,) + padded],
        10**7,
        tall, strips, mean, got_b, got_a,
    )
    gathered = lax.all_to_all(partial, BOTH, 0, 0, tiled=True)
    (star,) = call(patch_kernel, [(PLANES * ROWS, LANES)], [], 10**6, star, col_patch, row_patch)
    velocity_out, surface = call(
        final_kernel, [(PLANES * ROWS, LANES), block],
        [short, (2,) + block], 10**6,
        gathered, basis, flow, star, active_levels,
    )
    return tracers_out.reshape(tracers.shape), velocity_out.reshape(velocity.shape), surface


def solution(mesh):
    placed = (
        P(None, None, "lat", "lon"),
        P(None, None, "lat", "lon"),
        P("lat", "lon"),
        P("lat", "lon"),
        P("lat", "lon"),
        P("lat", "lon"),
        P(None, "lat", "lon"),
    )
    return jax.shard_map(
        functools.partial(per_device, mesh.shape["lon"], mesh.shape["lat"]),
        mesh=mesh,
        in_specs=placed,
        out_specs=(P(None, None, "lat", "lon"), P(None, None, "lat", "lon"), P("lat", "lon")),
        check_vma=False,
    )
```

```python
import functools
import math

import jax
import jax.numpy as jnp
from jax import lax
from jax.experimental import pallas as pl
from jax.experimental.pallas import tpu as pltpu
from jax.sharding import PartitionSpec as P

SUBCYCLES = 8
SOLVE_ITERS = 4
LEVELS = 10
PLANES = 2 * LEVELS
ROWS = 64
LANES = 128
MARGIN = 24
TALL = ROWS + 2 * MARGIN
RIM = 32
SLOPE = 0.15
CENTRE = 5.0
RADIUS = 5.0
F32 = jnp.float32
BOTH = ("lon", "lat")

STRIP = 24
RIMS = 3 * STRIP
SENT = 20
FULL = 22
EDGE = 21
NEAR, NEXT, COLS = 3 * SENT, 3 * SENT + FULL, 3 * SENT + 2 * FULL
LAT_SEND = COLS + MARGIN
LON_SEND = 2 * TALL
WIDE = 21


def lane_ids(rows):
    return lax.broadcasted_iota(jnp.int32, (rows, LANES), 1)


def row_ids(rows):
    return lax.broadcasted_iota(jnp.int32, (rows, LANES), 0)


def turn(x, shift):
    return x if isinstance(shift, int) and shift == 0 else pltpu.roll(x, shift, 1)


def pick(x, index):
    return jnp.take_along_axis(x, index, axis=1)


def flip_lanes(x, mask=LANES - 1):
    return pick(x, lane_ids(x.shape[0]) ^ mask)


def flip_rows(x):
    rows = x.shape[0]
    ids = row_ids(rows)
    for bit in range(3):
        step = 1 << bit
        x = jnp.where((ids & step) != 0, pltpu.roll(x, step, 0), pltpu.roll(x, rows - step, 0))
    return jnp.concatenate([x[r : r + 8] for r in range(rows - 8, -8, -8)], axis=0)


def odd(axis):
    return lax.rem(lax.axis_index(axis), 2) == 1


def at_fold():
    return lax.axis_index("lat") == lax.axis_size("lat") - 1


def shifted(x):
    rows = x.shape[0]
    return (turn(x, LANES - 1), turn(x, 1), pltpu.roll(x, rows - 1, 0), pltpu.roll(x, 1, 0))


def block_kernel(
    vel_far, tra_far, lev_far, visc_far, diff_far, depth_far, wind_far,
    star, mean, fields, cols, north, south, send_a, send_b, edge_a, edge_b,
    faces, face_levels, sums, turning, vel, tra_north, tra_south, visc, diff, depth, wind, levels_kept, laps, lev, done,
):
    pairs = (
        (lev_far, lev), (visc_far, visc), (vel_far, vel), (tra_far.at[:, pl.ds(ROWS - 8, 8)], tra_north),
        (tra_far.at[:, pl.ds(0, 8)], tra_south), (wind_far, wind), (depth_far, depth), (diff_far, diff),
    )
    copies = [
        pltpu.make_async_copy(far, near.at[pl.ds(8, PLANES * ROWS)] if near is vel else near, done.at[n])
        for n, (far, near) in enumerate(pairs)
    ]
    for copy in copies:
        copy.start()
    for copy in copies[:2]:
        copy.wait()
    lanes = lane_ids(ROWS)
    ids = row_ids(ROWS)
    levels = lev[...].astype(F32)
    v = visc[...]
    inside = (lanes < LANES - 1, lanes > 0, ids < ROWS - 1, ids > 0)
    for n, (v_n, level_n) in enumerate(zip(shifted(v), shifted(levels))):
        faces[n] = 0.5 * (v + v_n)
        face_levels[n] = jnp.where(inside[n], jnp.minimum(levels, level_n), 0.0)
    row = (lax.axis_index("lat") * ROWS).astype(F32) + ids.astype(F32)
    turning[...] = 0.25 * jnp.sin(math.pi * ((row + 0.5) / (ROWS * lax.axis_size("lat")) - 0.5))
    sums[...] = jnp.zeros((2, ROWS, LANES), F32)
    levels_kept[...] = levels
    for padded in (vel, laps):
        padded[0:8, :] = jnp.zeros((8, LANES), F32)
        padded[PLANES * ROWS + 8 : PLANES * ROWS + 16, :] = jnp.zeros((8, LANES), F32)
    acc = jnp.where((lanes >> 2) == 20, turn(levels, 82), 0.0)
    cols[...] = jnp.where((lanes >> 2) == 21, turn(v, 86), acc)
    copies[2].wait()

    def lap_step(k, carry):
        level = k.astype(F32)
        open_faces = [level < face_levels[n] for n in range(4)]
        ones = [jnp.where(o, 1.0, 0.0) for o in open_faces]
        count = (ones[0] + ones[1]) + (ones[2] + ones[3])
        packed = cols[...]
        for comp in range(2):
            p = comp * LEVELS + k
            start = 8 + pl.multiple_of(p * ROWS, ROWS)
            x = vel[pl.ds(start, ROWS), :]
            around = (turn(x, LANES - 1), turn(x, 1), vel[pl.ds(start + 1, ROWS), :], vel[pl.ds(start - 1, ROWS), :])
            picked = [jnp.where(open_faces[n], around[n], 0.0) for n in range(4)]
            laps[pl.ds(start, ROWS), :] = (picked[0] + picked[1]) + (picked[2] + picked[3]) - count * x
            packed = jnp.where((lanes >> 2) == p, turn(x, 4 * p + 2), packed)
        cols[...] = packed
        return carry

    def star_step(k, carry):
        level = k.astype(F32)
        wet = level < levels_kept[...]
        weights = [jnp.where(level < face_levels[n], faces[n], 0.0) for n in range(4)]
        weight = (weights[0] + weights[1]) + (weights[2] + weights[3])
        starts = [8 + pl.multiple_of((comp * LEVELS + k) * ROWS, ROWS) for comp in range(2)]
        values = [vel[pl.ds(s, ROWS), :] for s in starts]
        for comp, x in enumerate(values):
            start = starts[comp]
            lap = laps[pl.ds(start, ROWS), :]
            around = (turn(lap, LANES - 1), turn(lap, 1), laps[pl.ds(start + 1, ROWS), :], laps[pl.ds(start - 1, ROWS), :])
            terms = [weights[n] * around[n] for n in range(4)]
            second = (terms[0] + terms[1]) + (terms[2] + terms[3]) - weight * lap
            rotated = values[1] if comp == 0 else -values[0]
            out = jnp.where(wet, x - second + turning[...] * rotated, 0.0)
            star[pl.ds(pl.multiple_of((comp * LEVELS + k) * ROWS, ROWS), ROWS), :] = out
            sums[comp] += out
        return carry

    lax.fori_loop(0, LEVELS, lap_step, 0, unroll=10)
    lax.fori_loop(0, LEVELS, star_step, 0, unroll=10)
    for copy in copies[3:]:
        copy.wait()

    ocean = levels > 0.0
    for comp in range(2):
        here = pl.ds(comp * ROWS, ROWS)
        column_mean = sums[comp] / jnp.maximum(levels, 1.0)
        mean[here, :] = column_mean
        fields[here, :] = column_mean + jnp.where(ocean, wind[here, :], 0.0)
    fields[pl.ds(2 * ROWS, ROWS), :] = jnp.where(ocean, depth[...], 0.0)
    for edge, step, out, tra in ((ROWS - 1, -1, north, tra_north), (0, 1, south, tra_south)):
        out[...] = jnp.zeros((RIMS, LANES), F32)
        for d in range(2):
            r = edge + d * step
            out[pl.ds(d * STRIP, PLANES), :] = vel[pl.ds(8 + r, PLANES, stride=ROWS), :]
            out[pl.ds(d * STRIP + 20, 1), :] = levels[r : r + 1]
            out[pl.ds(d * STRIP + 21, 1), :] = visc[pl.ds(r, 1), :]
        out[pl.ds(2 * STRIP, PLANES), :] = tra[:, edge % 8, :]
        out[pl.ds(2 * STRIP + 20, 1), :] = diff[pl.ds(edge, 1), :]
    lat_odd = odd("lat")

    def put(start, up, down):
        here = pl.ds(start, up.shape[0])
        send_a[here, :] = jnp.where(lat_odd, down, up)
        send_b[here, :] = jnp.where(lat_odd, up, down)

    for f in range(3):
        put(f * SENT, fields[pl.ds((f + 1) * ROWS - SENT, SENT), :], fields[pl.ds(f * ROWS, SENT), :])
    edge_a[...] = jnp.where(lat_odd, south[2 * STRIP : RIMS, :], north[2 * STRIP : RIMS, :])
    edge_b[...] = jnp.where(lat_odd, north[2 * STRIP : RIMS, :], south[2 * STRIP : RIMS, :])
    for start, first, count in ((NEAR, 0, FULL), (NEXT, STRIP, FULL)):
        put(start, north[pl.ds(first, count), :], south[pl.ds(first, count), :])
    put(COLS, cols[ROWS - MARGIN : ROWS, :], cols[0:MARGIN, :])

    @pl.when(at_fold())
    def _():
        for f in range(3):
            turned = flip_rows(flip_lanes(fields[pl.ds((f + 1) * ROWS - MARGIN, MARGIN), :]))[0:SENT]
            send_b[pl.ds(f * SENT, SENT), :] = turned if f == 2 else -turned
        turned = flip_lanes(north[...])
        r = row_ids(RIMS)
        is_velocity = (r < PLANES) | ((r >= STRIP) & (r < STRIP + PLANES))
        turned = jnp.where(is_velocity, -turned, turned)
        edge_b[...] = turned[2 * STRIP : RIMS]
        for start, first, count in ((NEAR, 0, FULL), (NEXT, STRIP, FULL)):
            send_b[pl.ds(start, count), :] = turned[first : first + count]
        turned = flip_rows(flip_lanes(cols[ROWS - MARGIN : ROWS, :], 3))
        send_b[pl.ds(COLS, MARGIN), :] = jnp.where(lane_ids(MARGIN) < 4 * PLANES, -turned, turned)


def tracer_rim_kernel(tra, out):
    lanes = lane_ids(ROWS)

    def tracer_step(p, acc):
        t = tra[pl.ds(pl.multiple_of(p * ROWS, ROWS), ROWS), :]
        return jnp.where((lanes >> 1) == 44 + p, turn(t, lax.rem(89 + 2 * p, LANES)), acc)

    out[...] = lax.fori_loop(0, PLANES, tracer_step, jnp.zeros((ROWS, LANES), F32), unroll=True)


def widen_kernel(fields, cols, tracer_cols, diff, north, south, recv_b, recv_a, tall, strips, level_rows, send_a, send_b, east, west):
    lat_odd = odd("lat")
    lon_odd = odd("lon")
    at_south = lax.axis_index("lat") == 0
    def received(start, count):
        here = pl.ds(start, count)
        got_a = recv_a[here, :]
        got_b = jnp.where(at_south, 0.0, recv_b[here, :])
        return jnp.where(lat_odd, got_b, got_a), jnp.where(lat_odd, got_a, got_b)

    lanes = lane_ids(TALL)
    acc_east = jnp.zeros((TALL, LANES), F32)
    acc_west = jnp.zeros((TALL, LANES), F32)
    for f in range(3):
        from_north, from_south = received(f * SENT, SENT)
        unused = jnp.zeros((MARGIN - SENT, LANES), F32)
        tall[pl.ds(f * TALL, MARGIN - SENT), :] = unused
        tall[pl.ds(f * TALL + MARGIN - SENT, SENT), :] = from_south
        tall[pl.ds(f * TALL + MARGIN, ROWS), :] = fields[pl.ds(f * ROWS, ROWS), :]
        tall[pl.ds(f * TALL + MARGIN + ROWS, SENT), :] = from_north
        tall[pl.ds(f * TALL + MARGIN + ROWS + SENT, MARGIN - SENT), :] = unused
        x = tall[pl.ds(f * TALL, TALL), :]
        here = (lanes >= f * WIDE) & (lanes < (f + 1) * WIDE)
        before = (lanes >= LANES - WIDE) if f == 0 else (lanes >= (f - 1) * WIDE) & (lanes < f * WIDE)
        acc_east = jnp.where(before, turn(x, f * WIDE), acc_east)
        acc_west = jnp.where(here, turn(x, f * WIDE), acc_west)
    from_north, from_south = received(COLS, MARGIN)
    tall[pl.ds(3 * TALL, MARGIN), :] = from_south
    tall[pl.ds(3 * TALL + MARGIN, ROWS), :] = jnp.where(lane_ids(ROWS) < 88, cols[...], tracer_cols[...])
    tall[pl.ds(3 * TALL + MARGIN + ROWS, MARGIN), :] = from_north
    for out, acc, lane, shift in ((east, acc_east, 106, 107), (west, acc_west, 63, 63)):
        out[...] = acc
        out[pl.ds(MARGIN, ROWS), :] = jnp.where(lane_ids(ROWS) == lane, turn(diff[...], shift), acc[MARGIN : MARGIN + ROWS])
    near, next_to = received(NEAR, FULL), received(NEXT, FULL)
    unused = jnp.zeros((STRIP - FULL, LANES), F32)
    group = lane_ids(STRIP) >> 5
    for s, own in enumerate((north, south)):
        pieces = (
            jnp.concatenate([next_to[s], unused], axis=0),
            jnp.concatenate([near[s], unused], axis=0),
            own[0:STRIP, :],
            own[STRIP : 2 * STRIP, :],
        )
        for r, x in enumerate(pieces):
            strips[pl.ds((4 * s + r) * STRIP, STRIP), :] = x
            block, g = divmod(4 * s + r, 2)
            here = pl.ds(block * STRIP, STRIP)
            first = 42 + 32 * g
            mine = (lane_ids(STRIP) >= first) & (lane_ids(STRIP) < first + 32)
            east[here, :] = jnp.where(mine, turn(x, first + 32), east[here, :])
            west[here, :] = jnp.where(group == 2 + g, turn(x, 64 + 32 * g), west[here, :])
        level_rows[pl.ds(8 * s, 8), :] = jnp.broadcast_to(near[s][20:21], (8, LANES))
    k = tall[pl.ds(3 * TALL, TALL), :]
    send_a[pl.ds(0, TALL), :] = k
    send_b[pl.ds(0, TALL), :] = k
    rest = pl.ds(TALL, TALL)
    e, w = east[...], west[...]
    send_a[rest, :] = jnp.where(lon_odd, w, e)
    send_b[rest, :] = jnp.where(lon_odd, e, w)


def tracer_kernel(tra, lev, diff, level_rows, edge_b, edge_a, recv_b, recv_a, out, swap, faces, face_levels, rim_rows):
    is_odd = odd("lon")
    lat_odd = odd("lat")
    from_a = edge_a[...]
    from_b = jnp.where(lax.axis_index("lat") == 0, 0.0, edge_b[...])
    rim_rows[0:STRIP, :] = jnp.where(lat_odd, from_b, from_a)
    rim_rows[STRIP : 2 * STRIP, :] = jnp.where(lat_odd, from_a, from_b)
    lanes = lane_ids(ROWS)
    ids = row_ids(ROWS)

    def received(start):
        here = pl.ds(start + MARGIN, ROWS)
        got_a = recv_a[here, :]
        got_b = recv_b[here, :]
        return jnp.where(is_odd, got_b, got_a), jnp.where(is_odd, got_a, got_b)

    east_cols, west_cols = received(0)
    east_rest, west_rest = received(TALL)
    swap[...] = jnp.where((lanes & 1) == 0, turn(east_cols, LANES - 1), turn(west_cols, 1))

    def sides(x, halo, row, rows=rim_rows, apart=STRIP):
        east, west, north, south = shifted(x)
        return (
            jnp.where(lanes == LANES - 1, halo, east),
            jnp.where(lanes == 0, halo, west),
            jnp.where(ids == ROWS - 1, rows[pl.ds(row, 1), :], north),
            jnp.where(ids == 0, rows[pl.ds(row + apart, 1), :], south),
        )

    level = lev[...].astype(F32)
    level_halo = jnp.where(lanes == LANES - 1, turn(east_cols, 45), turn(west_cols, 47))
    d = diff[...]
    d_halo = jnp.where(lanes == LANES - 1, turn(east_rest, 64), turn(west_rest, 22))
    for n, other in enumerate(sides(level, level_halo, 0, level_rows, 8)):
        face_levels[n] = jnp.minimum(level, other)
    for n, other in enumerate(sides(d, d_halo, 20)):
        faces[n] = 0.5 * (d + other)

    def level_step(k, carry):
        weights = [jnp.where(k.astype(F32) < face_levels[n], faces[n], 0.0) for n in range(4)]
        for comp in range(2):
            p = comp * LEVELS + k
            here = pl.ds(pl.multiple_of(p * ROWS, ROWS), ROWS)
            x = tra[here, :]
            around = sides(x, turn(swap[...], 39 - 2 * p), p)
            total = weights[0] * (around[0] - x)
            for n in range(1, 4):
                total += weights[n] * (around[n] - x)
            out[here, :] = x + total
        return carry

    lax.fori_loop(0, LEVELS, level_step, 0, unroll=2)


def column_strip(strip):
    rows = strip.shape[0]
    lanes = lane_ids(rows)
    ids = row_ids(rows)
    phase = lanes & 3
    group = lanes >> 2

    levels = pick(strip, phase + 80)
    v = 0.5 * pick(strip, phase + 84)
    number = jnp.where(group >= LEVELS, group - LEVELS, group)
    number = jnp.where(group < PLANES, number, LEVELS).astype(F32)
    wet = jnp.where(number < levels, 1.0, 0.0)
    x = strip
    open_e = wet * turn(wet, LANES - 1)
    open_n = wet * pltpu.roll(wet, rows - 1, 0)
    flux_e = open_e * (turn(x, LANES - 1) - x)
    flux_n = open_n * (pltpu.roll(x, rows - 1, 0) - x)
    lap = (flux_e - turn(flux_e, 1)) + (flux_n - pltpu.roll(flux_n, 1, 0))
    seam = jnp.where(phase == 1, flux_e, 0.0)
    seam_west = turn(seam, 1)
    added = seam - seam_west
    step = jnp.where(phase == 1, turn(lap, LANES - 1) - lap, turn(seam, LANES - 1) + seam_west)
    flux_e = (v + turn(v, LANES - 1)) * open_e * step
    in_block = (ids != MARGIN - 1) & (ids != MARGIN + ROWS - 1)
    face = jnp.where(in_block, (v + pltpu.roll(v, rows - 1, 0)) * open_n, 0.0)
    flux_n = face * (pltpu.roll(added, rows - 1, 0) - added)
    return (flux_e - turn(flux_e, 1)) + (flux_n - pltpu.roll(flux_n, 1, 0))


def gram_pairs():
    return [(i, j) for i in range(SOLVE_ITERS) for j in range(i, SOLVE_ITERS + 1)]


def surface_kernel(
    tall, strips, mean, recv_b, recv_a,
    basis_out, flow, partial, col_patch, row_patch,
    state, height, heights, transport, force, faces, slope, basis, weights, diagonal, sides,
):
    is_odd = odd("lon")
    rows = pl.ds(8, TALL)
    lanes = lane_ids(TALL)

    def received(start, count):
        here = pl.ds(start, count)
        got_a = recv_a[here, :]
        got_b = recv_b[here, :]
        return jnp.where(is_odd, got_b, got_a), jnp.where(is_odd, got_a, got_b)

    def ghost_strip(east, west, g):
        return jnp.where(lane_ids(STRIP) < 64, turn(east, 64 - 32 * g), turn(west, 54 - 32 * g))

    from_east, from_west = received(TALL, TALL)
    for f in range(3):
        state[f, 0, rows, :] = tall[pl.ds(f * TALL, TALL), :]
        here = (lanes >= f * WIDE) & (lanes < (f + 1) * WIDE)
        state[f, 1, rows, :] = turn(jnp.where(here, from_east, from_west), (LANES - f * WIDE) % LANES)
    last = lanes == LANES - 1
    first = lanes == 0

    def lane_sides(a, b):
        n = a.shape[0]
        ea, eb, wa, wb = turn(a, LANES - 1), turn(b, LANES - 1), turn(a, 1), turn(b, 1)
        return (
            (jnp.where(last[0:n], eb, ea), jnp.where(last[0:n], ea, eb)),
            (jnp.where(first[0:n], wb, wa), jnp.where(first[0:n], wa, wb)),
        )

    own = tall[pl.ds(3 * TALL, TALL), :]
    phase = lanes & 3
    from_east, from_west = received(0, TALL)
    to_east = column_strip(jnp.where(phase < 2, own, from_east))
    to_west = column_strip(jnp.where(phase < 2, from_west, own))
    changes = (jnp.where(phase < 2, to_east, to_west), jnp.where(phase < 2, to_west, to_east))
    deep = (own, jnp.where(phase < 2, from_west, from_east))
    col_patch[...] = changes[0][MARGIN : MARGIN + ROWS]
    to_lane = lax.broadcasted_iota(jnp.int32, (LANES, 2 * LANES), 1)
    from_lane = lax.broadcasted_iota(jnp.int32, (LANES, 2 * LANES), 0)
    column = to_lane & (LANES - 1)
    comp_of = jnp.where(from_lane < 4 * LEVELS, 0, 1)
    chosen = (
        ((column < 2) | (column >= LANES - 2))
        & ((from_lane & 3) == ((to_lane + 2) & 3))
        & (comp_of == (to_lane >> 7))
        & (from_lane < 4 * PLANES)
    )
    chooser = jnp.where(chosen, 1.0, 0.0)
    for half in range(2):
        total = lax.dot_general(
            changes[half], chooser, (((1,), (0,)), ((), ())),
            precision=lax.Precision.HIGHEST, preferred_element_type=F32,
        )
        share = 1.0 / jnp.maximum(pick(deep[half], ((lanes + 2) & 3) + 80), 1.0)
        for comp in range(2):
            change = total[:, comp * LANES : (comp + 1) * LANES] * share
            state[comp, half, rows, :] = state[comp, half, rows, :] - change
    number = lax.broadcasted_iota(jnp.int32, (STRIP, LANES), 0)
    level_of_row = jnp.where(number >= LEVELS, number - LEVELS, number).astype(F32)
    is_plane = number < PLANES
    not_last = lane_ids(STRIP) < LANES - 1
    for s in range(2):
        x, wet, v, deep = [], [], [], []
        for r in range(4):
            centre = strips[pl.ds((4 * s + r) * STRIP, STRIP), :]
            block, g = divmod(4 * s + r, 2)
            both = (centre, ghost_strip(*received(TALL + block * STRIP, STRIP), g))
            deep.append([b[20:21] for b in both])
            v.append([jnp.broadcast_to(b[21:22], (STRIP, LANES)) for b in both])
            wet.append([jnp.where(is_plane & (level_of_row < b[20:21]), 1.0, 0.0) for b in both])
            x.append([jnp.where(is_plane, b, 0.0) for b in both])
        half_range = range(2)
        lap = {}
        added = {}
        seam = [wet[1][h] * wet[2][h] * (x[2][h] - x[1][h]) for h in half_range]
        added[1] = seam
        added[2] = [-t for t in seam]
        along = {}
        for r in (1, 2):
            x_e = lane_sides(*x[r])[0]
            wet_e = lane_sides(*wet[r])[0]
            v_e = lane_sides(*v[r])[0]
            added_e = lane_sides(*added[r])[0]
            open_e = [wet[r][h] * wet_e[h] for h in half_range]
            edge = [open_e[h] * (x_e[h] - x[r][h]) for h in half_range]
            edge_w = lane_sides(*edge)[1]
            lap[r] = [
                edge[h]
                - edge_w[h]
                + wet[r][h] * (wet[r + 1][h] * (x[r + 1][h] - x[r][h]) + wet[r - 1][h] * (x[r - 1][h] - x[r][h]))
                for h in half_range
            ]
            edge = [
                jnp.where(not_last, 0.5 * (v[r][h] + v_e[h]) * open_e[h] * (added_e[h] - added[r][h]), 0.0)
                for h in half_range
            ]
            edge_w = lane_sides(*edge)[1]
            along[r] = [edge[h] - edge_w[h] for h in half_range]
        for h in half_range:
            face = [0.5 * (v[r][h] + v[r + 1][h]) * wet[r][h] * wet[r + 1][h] for r in range(3)]
            across = (face[0] * added[1][h], face[1] * (lap[2][h] - lap[1][h]), -face[2] * added[2][h])
            second = (
                across[0],
                across[1] - across[0] + along[1][h],
                across[2] - across[1] + along[2][h],
                -across[2],
            )
            for r in range(4):
                change = second[r]
                if h == 0 and r >= 2:
                    row_patch[pl.ds((2 * s + r - 2) * STRIP, STRIP), :] = change
                where = 8 + MARGIN + ((ROWS + 1 - r) if s == 0 else (r - 2))
                for comp in range(2):
                    mine = (number >= comp * LEVELS) & (number < (comp + 1) * LEVELS)
                    total = jnp.sum(jnp.where(mine, change, 0.0), axis=0, keepdims=True)
                    total = total / jnp.maximum(deep[r][h], 1.0)
                    state[comp, h, where : where + 1, :] = state[comp, h, where : where + 1, :] - total
    for comp in range(2):
        here = pl.ds(comp * ROWS, ROWS)
        started = state[comp, 0, pl.ds(8 + MARGIN, ROWS), :] - tall[pl.ds(comp * TALL + MARGIN, ROWS), :]
        flow[here, :] = -(started + mean[here, :])

    halves = range(2)
    ahead = lanes[0:8] >= LANES - 2
    behind = lanes[0:8] < 2

    def far_sides(a, b):
        ea, eb, wa, wb = turn(a, LANES - 2), turn(b, LANES - 2), turn(a, 2), turn(b, 2)
        return (
            (jnp.where(ahead, eb, ea), jnp.where(ahead, ea, eb)),
            (jnp.where(behind, wb, wa), jnp.where(behind, wa, wb)),
        )

    for half in halves:
        d = state[2, half, rows, :]
        slope[half, rows, :] = jnp.where(d > 0.0, SLOPE, 0.0)
        force[half, rows, :] = SLOPE * d
        transport[half, rows, :] = d * state[1, half, rows, :]
    tiles = range(8, 8 + TALL, 8)
    for tile in tiles:
        here, above, below = (pl.ds(tile + off, 8) for off in (0, 1, -1))
        east, west = lane_sides(force[0, here, :], force[1, here, :])
        for h in halves:
            faces[0, h, here, :] = east[h]
            faces[1, h, here, :] = west[h]
            faces[2, h, here, :] = force[h, above, :]
            faces[3, h, here, :] = force[h, below, :]
    for tile in tiles:
        here, above, below = (pl.ds(tile + off, 8) for off in (0, 1, -1))
        east, west = lane_sides(*(state[2, h, here, :] * state[0, h, here, :] for h in halves))
        for h in halves:
            divergence = (east[h] - west[h]) + (transport[h, above, :] - transport[h, below, :])
            force[h, here, :] = divergence
            new = -slope[h, here, :] * divergence
            heights[0, h, here, :] = new
            height[h, here, :] = new
    for step in range(1, SUBCYCLES):
        cut = min(8 * ((6 + 2 * step) // 8), 16)
        now, later = heights.at[(step - 1) % 2], heights.at[step % 2]
        for tile in range(8 + cut, 8 + TALL - cut, 8):
            here, above, below = (pl.ds(tile + off, 8) for off in (0, 2, -2))
            centres = [now[h, here, :] for h in halves]
            east, west = far_sides(*centres)
            for h, x in enumerate(centres):
                along = faces[0, h, here, :] * (east[h] - x) - faces[1, h, here, :] * (x - west[h])
                across = faces[2, h, here, :] * (now[h, above, :] - x) - faces[3, h, here, :] * (x - now[h, below, :])
                change = force[h, here, :] - (along + across)
                force[h, here, :] = change
                new = x - slope[h, here, :] * change
                later[h, here, :] = new
                height[h, here, :] = height[h, here, :] + new
    mine = pl.ds(8 + MARGIN, ROWS)
    east, west = lane_sides(height[0, mine, :], height[1, mine, :])
    inner = slope[0, mine, :]
    north, south = (height[0, pl.ds(8 + MARGIN + off, ROWS), :] for off in (1, -1))
    for comp, gradient in enumerate((east[0] - west[0], north - south)):
        here = pl.ds(comp * ROWS, ROWS)
        flow[here, :] = flow[here, :] + (state[comp, 0, mine, :] - inner * gradient)
    final = heights.at[(SUBCYCLES - 1) % 2]
    scale = 2.0 / RADIUS
    short = ROWS + 16
    base = MARGIN

    tiles = range(0, short, 8)

    def spin(tile, a, b):
        here = pl.ds(base + tile, 8)
        for n, pair in enumerate(lane_sides(a, b)):
            for h in halves:
                sides[n, h, here, :] = pair[h]

    def nine(read, tile, h):
        out = []
        for off in (0, 1, -1):
            where = pl.ds(base + tile + off, 8)
            out += [read(h, where), sides[0, h, where, :], sides[1, h, where, :]]
        return out

    for tile in tiles:
        here = pl.ds(base + tile, 8)
        spin(tile, state[2, 0, here, :], state[2, 1, here, :])
    for tile in tiles:
        here = pl.ds(tile, 8)
        for h in halves:
            around = nine(lambda h, where: state[2, h, where, :], tile, h)
            d = around[0]
            wet = d > 0.0
            total = jnp.where(wet, 0.05, 1.0)
            for n in range(1, 9):
                factor = 0.5 if n in (1, 2, 3, 6) else 0.25
                w = jnp.where(wet & (around[n] > 0.0), factor * (d + around[n]), 0.0)
                weights[n - 1, h, here, :] = scale * w
                total += w
            diagonal[h, here, :] = scale * (total - CENTRE)

    def applied(source, tile, h):
        around = nine(lambda h, where: basis[source, h, where, :], tile, h)
        here = pl.ds(tile, 8)
        terms = [weights[n - 1, h, here, :] * around[n] for n in range(1, 9)]
        while len(terms) > 1:
            terms = [a + b for a, b in zip(terms[::2], terms[1::2])]
        return diagonal[h, here, :] * around[0] - terms[0]

    for tile in tiles:
        here = pl.ds(base + tile, 8)
        pair = [final[h, here, :] for h in halves]
        for h in halves:
            basis[0, h, here, :] = pair[h]
        spin(tile, *pair)
    for k in range(1, SOLVE_ITERS):
        for tile in tiles:
            here = pl.ds(base + tile, 8)
            for h in halves:
                x = applied(k - 1, tile, h)
                basis[k, h, here, :] = 0.5 * x if k == 1 else x - basis[k - 2, h, here, :]
        for tile in tiles:
            here = pl.ds(base + tile, 8)
            spin(tile, basis[k, 0, here, :], basis[k, 1, here, :])
    for tile in tiles[1:-1]:
        here = pl.ds(base + tile, 8)
        basis[SOLVE_ITERS, 0, here, :] = applied(SOLVE_ITERS - 1, tile, 0) - basis[SOLVE_ITERS - 2, 0, here, :]
    lane = lane_ids(1)
    row = jnp.zeros((1, LANES), F32)
    mine = pl.ds(8 + MARGIN, ROWS)
    for n, (i, j) in enumerate(gram_pairs()):
        product = basis[i, 0, mine, :] * basis[j, 0, mine, :]
        row = jnp.where(lane == n, jnp.sum(jnp.sum(product, axis=0, keepdims=True), axis=1, keepdims=True), row)
    partial[...] = jnp.broadcast_to(row, partial.shape)
    for i in range(SOLVE_ITERS):
        for half in range(2):
            basis_out[i, half] = basis[i, half, pl.ds(base, short), :]


def solve_coefficients(gram):
    half = 0.5 * RADIUS

    def image_of(d):
        out = [None] * (len(d) + 1)

        def add(n, term):
            out[n] = term if out[n] is None else out[n] + term

        for j, value in enumerate(d):
            add(j, CENTRE * value)
            if j == 0:
                add(1, RADIUS * value)
            else:
                add(j + 1, half * value)
                add(j - 1, half * value)
        return out

    def inner(a, b):
        total = None
        for i, x in enumerate(a):
            for j, y in enumerate(b):
                term = x * y * gram[(min(i, j), max(i, j))]
                total = term if total is None else total + term
        return total

    one = jnp.ones((8, LANES), F32)
    residual, direction, surface = [one], [one], [0.0 * one]
    norm = gram[(0, 0)]
    for iteration in range(SOLVE_ITERS):
        image = image_of(direction)
        step = norm / inner(direction, image)
        surface = [a + step * b for a, b in zip(surface, direction)] + [0.0 * one]
        if iteration == SOLVE_ITERS - 1:
            break
        residual = [(residual[n] if n < len(residual) else 0.0) - step * x for n, x in enumerate(image)]
        fresh = inner(residual, residual)
        ratio = fresh / norm
        direction = [x + (ratio * direction[n] if n < len(direction) else 0.0) for n, x in enumerate(residual)]
        norm = fresh
    return surface[:SOLVE_ITERS]


def final_kernel(gathered, basis, flow, star, lev, velocity_out, surface_out, pad, change):
    sums = jnp.sum(gathered[...], axis=0, keepdims=True)
    lane = lane_ids(1)
    gram = {}
    for n, pair in enumerate(gram_pairs()):
        value = jnp.sum(jnp.where(lane == n, sums, 0.0), axis=1, keepdims=True)
        gram[pair] = jnp.broadcast_to(value, (8, LANES))
    coefficients = [c[0:1] for c in solve_coefficients(gram)]
    for half in range(2):
        total = coefficients[0] * basis[0, half]
        for i in range(1, SOLVE_ITERS):
            total += coefficients[i] * basis[i, half]
        pad[half] = total
    mine = pl.ds(8, ROWS)
    centre = pad[0, mine, :]
    ghost = pad[1, mine, :]
    surface_out[...] = centre
    lanes = lane_ids(ROWS)
    east = jnp.where(lanes == LANES - 1, turn(ghost, LANES - 1), turn(centre, LANES - 1))
    west = jnp.where(lanes == 0, turn(ghost, 1), turn(centre, 1))
    levels = lev[...]
    slope = jnp.where(levels > 0, SLOPE, 0.0)
    slopes = (east - west, pad[0, pl.ds(9, ROWS), :] - pad[0, pl.ds(7, ROWS), :])
    for comp in range(2):
        here = pl.ds(comp * ROWS, ROWS)
        change[comp] = flow[here, :] - slope * slopes[comp]


    def level_step(k, carry):
        wet = k < levels
        for comp in range(2):
            here = pl.ds(pl.multiple_of((comp * LEVELS + k) * ROWS, ROWS), ROWS)
            velocity_out[here, :] = star[here, :] + jnp.where(wet, change[comp], 0.0)
        return carry

    lax.fori_loop(0, LEVELS, level_step, 0, unroll=True)


def patch_kernel(star, col_patch, row_patch, out):
    lanes = lane_ids(ROWS)
    rims = (lanes < 2) | (lanes >= LANES - 2)
    ids = row_ids(8)

    def plane(p, carry):
        here = pl.ds(pl.multiple_of(p * ROWS, ROWS), ROWS)
        out[here, :] = star[here, :] - jnp.where(rims, turn(col_patch[...], 126 - 4 * p), 0.0)
        for first, pieces in ((ROWS - 8, ((7, 0), (6, 1))), (0, ((0, 2), (1, 3)))):
            here = pl.ds(pl.multiple_of(p * ROWS + first, 8), 8)
            x = out[here, :]
            for row, n in pieces:
                x = x - jnp.where(ids == row, row_patch[pl.ds(n * STRIP + p, 1), :], 0.0)
            out[here, :] = x
        return carry

    lax.fori_loop(0, PLANES, plane, 0, unroll=10)


def call(kernel, shapes, scratch, flops, *args, far=False):
    out = tuple(jax.ShapeDtypeStruct(s, F32) for s in shapes)
    moved = sum(4 * math.prod(a.shape) for a in args) + sum(4 * math.prod(s) for s in shapes)
    if far:
        args = [pltpu.with_memory_space_constraint(a, pltpu.HBM) for a in args]
    return pl.pallas_call(
        kernel,
        out_shape=out,
        in_specs=[pl.BlockSpec(memory_space=pltpu.HBM if far else pltpu.VMEM)] * len(args),
        scratch_shapes=[pltpu.VMEM(s, F32) if isinstance(s, tuple) else s for s in scratch],
        compiler_params=pltpu.CompilerParams(vmem_limit_bytes=32 * 1024 * 1024),
        cost_estimate=pl.CostEstimate(flops=flops, bytes_accessed=moved, transcendentals=0),
    )(*args)


def pair_tables(lon, lat):
    def index(i, j):
        return j * lat + i

    lat_a, lat_b, lon_a, lon_b = [], [], [], []
    for j in range(lon):
        for i in range(lat):
            lat_a.append((index(i, j), index(i ^ 1, j)))
            if i == lat - 1:
                lat_b.append((index(i, j), index(i, lon - 1 - j)))
            elif i > 0:
                lat_b.append((index(i, j), index(i + 1 if i % 2 else i - 1, j)))
            else:
                lat_b.append((index(i, j), index(i, j ^ 1)))
            lon_a.append((index(i, j), index(i, j ^ 1)))
            lon_b.append((index(i, j), index(i, (j + 1 if j % 2 else j - 1) % lon)))
    return lat_a, lat_b, lon_a, lon_b


def per_device(lon, lat, tracers, velocity, active_levels, diffusivity, viscosity, ocean_depth, wind_forcing):
    lat_a, lat_b, lon_a, lon_b = pair_tables(lon, lat)

    def swap(x, pairs):
        return lax.ppermute(x, BOTH, pairs)

    block = (ROWS, LANES)
    tra = tracers.reshape(PLANES * ROWS, LANES)
    vel = velocity.reshape(PLANES * ROWS, LANES)
    wind = wind_forcing.reshape(2 * ROWS, LANES)
    rim = (RIMS, LANES)
    star, mean, fields, cols, north, south, send_a, send_b, edge_a, edge_b = call(
        block_kernel,
        [(PLANES * ROWS, LANES), (2 * ROWS, LANES), (3 * ROWS, LANES), block, rim, rim, (LAT_SEND, LANES), (LAT_SEND, LANES),
         (STRIP, LANES), (STRIP, LANES)],
        [(4,) + block, (4,) + block, (2,) + block, block, (PLANES * ROWS + 16, LANES), (PLANES, 8, LANES), (PLANES, 8, LANES), block, block, block, wind.shape,
         block, (PLANES * ROWS + 16, LANES),
         pltpu.VMEM(block, jnp.int32), pltpu.SemaphoreType.DMA((8,))],
        10**7,
        vel, tra.reshape(PLANES, ROWS, LANES), active_levels, viscosity, diffusivity, ocean_depth, wind,
        far=True,
    )
    got_a = swap(send_a, lat_a)
    got_b = swap(send_b, lat_b)
    edge_a = swap(edge_a, lat_a)
    edge_b = swap(edge_b, lat_b)
    (tracer_cols,) = call(tracer_rim_kernel, [block], [], 10**5, tra)
    tall, strips, level_rows, send_a, send_b = call(
        widen_kernel,
        [(4 * TALL, LANES), (8 * STRIP, LANES), (16, LANES), (LON_SEND, LANES), (LON_SEND, LANES)],
        [(TALL, LANES)] * 2,
        10**6,
        fields, cols, tracer_cols, diffusivity, north, south, got_b, got_a,
    )
    got_a = swap(send_a, lon_a)
    got_b = swap(send_b, lon_b)
    (tracers_out,) = call(
        tracer_kernel, [(PLANES * ROWS, LANES)], [block, (4,) + block, (4,) + block, (2 * STRIP, LANES)], 10**6,
        tra, active_levels, diffusivity, level_rows, edge_b, edge_a, got_b, got_a,
    )
    padded = (2, TALL + 16, LANES)
    short = (2, ROWS + 16, LANES)
    basis, flow, partial, col_patch, row_patch = call(
        surface_kernel,
        [(SOLVE_ITERS,) + short, (2 * ROWS, LANES), (lon * lat, LANES), block, (4 * STRIP, LANES)],
        [(3,) + padded, padded, (2,) + padded, padded, padded, (4,) + padded, padded, (SOLVE_ITERS + 1,) + padded, (8,) + short, short, (2,) + padded],
        10**7,
        tall, strips, mean, got_b, got_a,
    )
    gathered = lax.all_to_all(partial, BOTH, 0, 0, tiled=True)
    (star,) = call(patch_kernel, [(PLANES * ROWS, LANES)], [], 10**6, star, col_patch, row_patch)
    velocity_out, surface = call(
        final_kernel, [(PLANES * ROWS, LANES), block],
        [short, (2,) + block], 10**6,
        gathered, basis, flow, star, active_levels,
    )
    return tracers_out.reshape(tracers.shape), velocity_out.reshape(velocity.shape), surface


def solution(mesh):
    placed = (
        P(None, None, "lat", "lon"),
        P(None, None, "lat", "lon"),
        P("lat", "lon"),
        P("lat", "lon"),
        P("lat", "lon"),
        P("lat", "lon"),
        P(None, "lat", "lon"),
    )
    return jax.shard_map(
        functools.partial(per_device, mesh.shape["lon"], mesh.shape["lat"]),
        mesh=mesh,
        in_specs=placed,
        out_specs=(P(None, None, "lat", "lon"), P(None, None, "lat", "lon"), P("lat", "lon")),
        check_vma=False,
    )
```

```python
import functools
import math

import jax
import jax.numpy as jnp
from jax import lax
from jax.experimental import pallas as pl
from jax.experimental.pallas import tpu as pltpu
from jax.sharding import PartitionSpec as P

SUBCYCLES = 8
SOLVE_ITERS = 4
LEVELS = 10
PLANES = 2 * LEVELS
ROWS = 64
LANES = 128
MARGIN = 24
TALL = ROWS + 2 * MARGIN
RIM = 32
SLOPE = 0.15
CENTRE = 5.0
RADIUS = 5.0
F32 = jnp.float32
BOTH = ("lon", "lat")

STRIP = 24
RIMS = 3 * STRIP
SENT = 20
FULL = 22
EDGE = 21
NEAR, NEXT, COLS = 3 * SENT, 3 * SENT + FULL, 3 * SENT + 2 * FULL
LAT_SEND = COLS + MARGIN
LON_SEND = 2 * TALL
WIDE = 21


def lane_ids(rows):
    return lax.broadcasted_iota(jnp.int32, (rows, LANES), 1)


def row_ids(rows):
    return lax.broadcasted_iota(jnp.int32, (rows, LANES), 0)


def turn(x, shift):
    return x if isinstance(shift, int) and shift == 0 else pltpu.roll(x, shift, 1)


def pick(x, index):
    return jnp.take_along_axis(x, index, axis=1)


def flip_lanes(x, mask=LANES - 1):
    return pick(x, lane_ids(x.shape[0]) ^ mask)


def flip_rows(x):
    rows = x.shape[0]
    ids = row_ids(rows)
    for bit in range(3):
        step = 1 << bit
        x = jnp.where((ids & step) != 0, pltpu.roll(x, step, 0), pltpu.roll(x, rows - step, 0))
    return jnp.concatenate([x[r : r + 8] for r in range(rows - 8, -8, -8)], axis=0)


def odd(axis):
    return lax.rem(lax.axis_index(axis), 2) == 1


def at_fold():
    return lax.axis_index("lat") == lax.axis_size("lat") - 1


def shifted(x):
    rows = x.shape[0]
    return (turn(x, LANES - 1), turn(x, 1), pltpu.roll(x, rows - 1, 0), pltpu.roll(x, 1, 0))


def block_kernel(
    vel_far, tra_far, lev_far, visc_far, diff_far, depth_far, wind_far,
    star, mean, fields, cols, north, south, send_a, send_b, edge_a, edge_b,
    faces, face_levels, sums, turning, vel, tra_north, tra_south, visc, diff, depth, wind, levels_kept, laps, lev, done,
):
    pairs = (
        (lev_far, lev), (visc_far, visc), (vel_far, vel), (tra_far.at[:, pl.ds(ROWS - 8, 8)], tra_north),
        (tra_far.at[:, pl.ds(0, 8)], tra_south), (wind_far, wind), (depth_far, depth), (diff_far, diff),
    )
    copies = [
        pltpu.make_async_copy(far, near.at[pl.ds(8, PLANES * ROWS)] if near is vel else near, done.at[n])
        for n, (far, near) in enumerate(pairs)
    ]
    for copy in copies:
        copy.start()
    for copy in copies[:2]:
        copy.wait()
    lanes = lane_ids(ROWS)
    ids = row_ids(ROWS)
    levels = lev[...].astype(F32)
    v = visc[...]
    inside = (lanes < LANES - 1, lanes > 0, ids < ROWS - 1, ids > 0)
    for n, (v_n, level_n) in enumerate(zip(shifted(v), shifted(levels))):
        faces[n] = 0.5 * (v + v_n)
        face_levels[n] = jnp.where(inside[n], jnp.minimum(levels, level_n), 0.0)
    row = (lax.axis_index("lat") * ROWS).astype(F32) + ids.astype(F32)
    turning[...] = 0.25 * jnp.sin(math.pi * ((row + 0.5) / (ROWS * lax.axis_size("lat")) - 0.5))
    sums[...] = jnp.zeros((2, ROWS, LANES), F32)
    levels_kept[...] = levels
    for padded in (vel, laps):
        padded[0:8, :] = jnp.zeros((8, LANES), F32)
        padded[PLANES * ROWS + 8 : PLANES * ROWS + 16, :] = jnp.zeros((8, LANES), F32)
    acc = jnp.where((lanes >> 2) == 20, turn(levels, 82), 0.0)
    cols[...] = jnp.where((lanes >> 2) == 21, turn(v, 86), acc)
    copies[2].wait()

    def lap_step(k, carry):
        level = k.astype(F32)
        open_faces = [level < face_levels[n] for n in range(4)]
        ones = [jnp.where(o, 1.0, 0.0) for o in open_faces]
        count = (ones[0] + ones[1]) + (ones[2] + ones[3])
        packed = cols[...]
        for comp in range(2):
            p = comp * LEVELS + k
            start = 8 + pl.multiple_of(p * ROWS, ROWS)
            x = vel[pl.ds(start, ROWS), :]
            around = (turn(x, LANES - 1), turn(x, 1), vel[pl.ds(start + 1, ROWS), :], vel[pl.ds(start - 1, ROWS), :])
            picked = [jnp.where(open_faces[n], around[n], 0.0) for n in range(4)]
            laps[pl.ds(start, ROWS), :] = (picked[0] + picked[1]) + (picked[2] + picked[3]) - count * x
            packed = jnp.where((lanes >> 2) == p, turn(x, 4 * p + 2), packed)
        cols[...] = packed
        return carry

    def star_step(k, carry):
        level = k.astype(F32)
        wet = level < levels_kept[...]
        weights = [jnp.where(level < face_levels[n], faces[n], 0.0) for n in range(4)]
        weight = (weights[0] + weights[1]) + (weights[2] + weights[3])
        starts = [8 + pl.multiple_of((comp * LEVELS + k) * ROWS, ROWS) for comp in range(2)]
        values = [vel[pl.ds(s, ROWS), :] for s in starts]
        for comp, x in enumerate(values):
            start = starts[comp]
            lap = laps[pl.ds(start, ROWS), :]
            around = (turn(lap, LANES - 1), turn(lap, 1), laps[pl.ds(start + 1, ROWS), :], laps[pl.ds(start - 1, ROWS), :])
            terms = [weights[n] * around[n] for n in range(4)]
            second = (terms[0] + terms[1]) + (terms[2] + terms[3]) - weight * lap
            rotated = values[1] if comp == 0 else -values[0]
            out = jnp.where(wet, x - second + turning[...] * rotated, 0.0)
            star[pl.ds(pl.multiple_of((comp * LEVELS + k) * ROWS, ROWS), ROWS), :] = out
            sums[comp] += out
        return carry

    lax.fori_loop(0, LEVELS, lap_step, 0, unroll=10)
    lax.fori_loop(0, LEVELS, star_step, 0, unroll=10)
    for copy in copies[3:]:
        copy.wait()

    ocean = levels > 0.0
    for comp in range(2):
        here = pl.ds(comp * ROWS, ROWS)
        column_mean = sums[comp] / jnp.maximum(levels, 1.0)
        mean[here, :] = column_mean
        fields[here, :] = column_mean + jnp.where(ocean, wind[here, :], 0.0)
    fields[pl.ds(2 * ROWS, ROWS), :] = jnp.where(ocean, depth[...], 0.0)
    for edge, step, out, tra in ((ROWS - 1, -1, north, tra_north), (0, 1, south, tra_south)):
        out[...] = jnp.zeros((RIMS, LANES), F32)
        for d in range(2):
            r = edge + d * step
            out[pl.ds(d * STRIP, PLANES), :] = vel[pl.ds(8 + r, PLANES, stride=ROWS), :]
            out[pl.ds(d * STRIP + 20, 1), :] = levels[r : r + 1]
            out[pl.ds(d * STRIP + 21, 1), :] = visc[pl.ds(r, 1), :]
        out[pl.ds(2 * STRIP, PLANES), :] = tra[:, edge % 8, :]
        out[pl.ds(2 * STRIP + 20, 1), :] = diff[pl.ds(edge, 1), :]
    lat_odd = odd("lat")

    def put(start, up, down):
        here = pl.ds(start, up.shape[0])
        send_a[here, :] = jnp.where(lat_odd, down, up)
        send_b[here, :] = jnp.where(lat_odd, up, down)

    for f in range(3):
        put(f * SENT, fields[pl.ds((f + 1) * ROWS - SENT, SENT), :], fields[pl.ds(f * ROWS, SENT), :])
    edge_a[...] = jnp.where(lat_odd, south[2 * STRIP : RIMS, :], north[2 * STRIP : RIMS, :])
    edge_b[...] = jnp.where(lat_odd, north[2 * STRIP : RIMS, :], south[2 * STRIP : RIMS, :])
    for start, first, count in ((NEAR, 0, FULL), (NEXT, STRIP, FULL)):
        put(start, north[pl.ds(first, count), :], south[pl.ds(first, count), :])
    put(COLS, cols[ROWS - MARGIN : ROWS, :], cols[0:MARGIN, :])

    @pl.when(at_fold())
    def _():
        for f in range(3):
            turned = flip_rows(flip_lanes(fields[pl.ds((f + 1) * ROWS - MARGIN, MARGIN), :]))[0:SENT]
            send_b[pl.ds(f * SENT, SENT), :] = turned if f == 2 else -turned
        turned = flip_lanes(north[...])
        r = row_ids(RIMS)
        is_velocity = (r < PLANES) | ((r >= STRIP) & (r < STRIP + PLANES))
        turned = jnp.where(is_velocity, -turned, turned)
        edge_b[...] = turned[2 * STRIP : RIMS]
        for start, first, count in ((NEAR, 0, FULL), (NEXT, STRIP, FULL)):
            send_b[pl.ds(start, count), :] = turned[first : first + count]
        turned = flip_rows(flip_lanes(cols[ROWS - MARGIN : ROWS, :], 3))
        send_b[pl.ds(COLS, MARGIN), :] = jnp.where(lane_ids(MARGIN) < 4 * PLANES, -turned, turned)


def tracer_rim_kernel(tra, out):
    lanes = lane_ids(ROWS)

    def tracer_step(p, acc):
        t = tra[pl.ds(pl.multiple_of(p * ROWS, ROWS), ROWS), :]
        return jnp.where((lanes >> 1) == 44 + p, turn(t, lax.rem(89 + 2 * p, LANES)), acc)

    out[...] = lax.fori_loop(0, PLANES, tracer_step, jnp.zeros((ROWS, LANES), F32), unroll=True)


def widen_kernel(fields, cols, tracer_cols, diff, north, south, recv_b, recv_a, tall, strips, level_rows, send_a, send_b, east, west):
    lat_odd = odd("lat")
    lon_odd = odd("lon")
    at_south = lax.axis_index("lat") == 0
    def received(start, count):
        here = pl.ds(start, count)
        got_a = recv_a[here, :]
        got_b = jnp.where(at_south, 0.0, recv_b[here, :])
        return jnp.where(lat_odd, got_b, got_a), jnp.where(lat_odd, got_a, got_b)

    lanes = lane_ids(TALL)
    acc_east = jnp.zeros((TALL, LANES), F32)
    acc_west = jnp.zeros((TALL, LANES), F32)
    for f in range(3):
        from_north, from_south = received(f * SENT, SENT)
        unused = jnp.zeros((MARGIN - SENT, LANES), F32)
        tall[pl.ds(f * TALL, MARGIN - SENT), :] = unused
        tall[pl.ds(f * TALL + MARGIN - SENT, SENT), :] = from_south
        tall[pl.ds(f * TALL + MARGIN, ROWS), :] = fields[pl.ds(f * ROWS, ROWS), :]
        tall[pl.ds(f * TALL + MARGIN + ROWS, SENT), :] = from_north
        tall[pl.ds(f * TALL + MARGIN + ROWS + SENT, MARGIN - SENT), :] = unused
        x = tall[pl.ds(f * TALL, TALL), :]
        here = (lanes >= f * WIDE) & (lanes < (f + 1) * WIDE)
        before = (lanes >= LANES - WIDE) if f == 0 else (lanes >= (f - 1) * WIDE) & (lanes < f * WIDE)
        acc_east = jnp.where(before, turn(x, f * WIDE), acc_east)
        acc_west = jnp.where(here, turn(x, f * WIDE), acc_west)
    from_north, from_south = received(COLS, MARGIN)
    tall[pl.ds(3 * TALL, MARGIN), :] = from_south
    tall[pl.ds(3 * TALL + MARGIN, ROWS), :] = jnp.where(lane_ids(ROWS) < 88, cols[...], tracer_cols[...])
    tall[pl.ds(3 * TALL + MARGIN + ROWS, MARGIN), :] = from_north
    for out, acc, lane, shift in ((east, acc_east, 106, 107), (west, acc_west, 63, 63)):
        out[...] = acc
        out[pl.ds(MARGIN, ROWS), :] = jnp.where(lane_ids(ROWS) == lane, turn(diff[...], shift), acc[MARGIN : MARGIN + ROWS])
    near, next_to = received(NEAR, FULL), received(NEXT, FULL)
    unused = jnp.zeros((STRIP - FULL, LANES), F32)
    group = lane_ids(STRIP) >> 5
    for s, own in enumerate((north, south)):
        pieces = (
            jnp.concatenate([next_to[s], unused], axis=0),
            jnp.concatenate([near[s], unused], axis=0),
            own[0:STRIP, :],
            own[STRIP : 2 * STRIP, :],
        )
        for r, x in enumerate(pieces):
            strips[pl.ds((4 * s + r) * STRIP, STRIP), :] = x
            block, g = divmod(4 * s + r, 2)
            here = pl.ds(block * STRIP, STRIP)
            first = 42 + 32 * g
            mine = (lane_ids(STRIP) >= first) & (lane_ids(STRIP) < first + 32)
            east[here, :] = jnp.where(mine, turn(x, first + 32), east[here, :])
            west[here, :] = jnp.where(group == 2 + g, turn(x, 64 + 32 * g), west[here, :])
        level_rows[pl.ds(8 * s, 8), :] = jnp.broadcast_to(near[s][20:21], (8, LANES))
    k = tall[pl.ds(3 * TALL, TALL), :]
    send_a[pl.ds(0, TALL), :] = k
    send_b[pl.ds(0, TALL), :] = k
    rest = pl.ds(TALL, TALL)
    e, w = east[...], west[...]
    send_a[rest, :] = jnp.where(lon_odd, w, e)
    send_b[rest, :] = jnp.where(lon_odd, e, w)


def tracer_kernel(tra, lev, diff, level_rows, edge_b, edge_a, recv_b, recv_a, out, swap, faces, face_levels, rim_rows):
    is_odd = odd("lon")
    lat_odd = odd("lat")
    from_a = edge_a[...]
    from_b = jnp.where(lax.axis_index("lat") == 0, 0.0, edge_b[...])
    rim_rows[0:STRIP, :] = jnp.where(lat_odd, from_b, from_a)
    rim_rows[STRIP : 2 * STRIP, :] = jnp.where(lat_odd, from_a, from_b)
    lanes = lane_ids(ROWS)
    ids = row_ids(ROWS)

    def received(start):
        here = pl.ds(start + MARGIN, ROWS)
        got_a = recv_a[here, :]
        got_b = recv_b[here, :]
        return jnp.where(is_odd, got_b, got_a), jnp.where(is_odd, got_a, got_b)

    east_cols, west_cols = received(0)
    east_rest, west_rest = received(TALL)
    swap[...] = jnp.where((lanes & 1) == 0, turn(east_cols, LANES - 1), turn(west_cols, 1))

    def sides(x, halo, row, rows=rim_rows, apart=STRIP):
        east, west, north, south = shifted(x)
        return (
            jnp.where(lanes == LANES - 1, halo, east),
            jnp.where(lanes == 0, halo, west),
            jnp.where(ids == ROWS - 1, rows[pl.ds(row, 1), :], north),
            jnp.where(ids == 0, rows[pl.ds(row + apart, 1), :], south),
        )

    level = lev[...].astype(F32)
    level_halo = jnp.where(lanes == LANES - 1, turn(east_cols, 45), turn(west_cols, 47))
    d = diff[...]
    d_halo = jnp.where(lanes == LANES - 1, turn(east_rest, 64), turn(west_rest, 22))
    for n, other in enumerate(sides(level, level_halo, 0, level_rows, 8)):
        face_levels[n] = jnp.minimum(level, other)
    for n, other in enumerate(sides(d, d_halo, 20)):
        faces[n] = 0.5 * (d + other)

    def level_step(k, carry):
        weights = [jnp.where(k.astype(F32) < face_levels[n], faces[n], 0.0) for n in range(4)]
        for comp in range(2):
            p = comp * LEVELS + k
            here = pl.ds(pl.multiple_of(p * ROWS, ROWS), ROWS)
            x = tra[here, :]
            around = sides(x, turn(swap[...], 39 - 2 * p), p)
            total = weights[0] * (around[0] - x)
            for n in range(1, 4):
                total += weights[n] * (around[n] - x)
            out[here, :] = x + total
        return carry

    lax.fori_loop(0, LEVELS, level_step, 0, unroll=2)


def column_strip(strip):
    rows = strip.shape[0]
    lanes = lane_ids(rows)
    ids = row_ids(rows)
    phase = lanes & 3
    group = lanes >> 2

    levels = pick(strip, phase + 80)
    v = 0.5 * pick(strip, phase + 84)
    number = jnp.where(group >= LEVELS, group - LEVELS, group)
    number = jnp.where(group < PLANES, number, LEVELS).astype(F32)
    wet = jnp.where(number < levels, 1.0, 0.0)
    x = strip
    open_e = wet * turn(wet, LANES - 1)
    open_n = wet * pltpu.roll(wet, rows - 1, 0)
    flux_e = open_e * (turn(x, LANES - 1) - x)
    flux_n = open_n * (pltpu.roll(x, rows - 1, 0) - x)
    flux_w = turn(flux_e, 1)
    lap = (flux_e - flux_w) + (flux_n - pltpu.roll(flux_n, 1, 0))
    seam = jnp.where(phase == 1, flux_e, 0.0)
    seam_west = jnp.where(phase == 2, flux_w, 0.0)
    added = seam - seam_west
    step = jnp.where(phase == 1, turn(lap, LANES - 1) - lap, turn(seam, LANES - 1) + seam_west)
    flux_e = (v + turn(v, LANES - 1)) * open_e * step
    in_block = (ids != MARGIN - 1) & (ids != MARGIN + ROWS - 1)
    face = jnp.where(in_block, (v + pltpu.roll(v, rows - 1, 0)) * open_n, 0.0)
    flux_n = face * (pltpu.roll(added, rows - 1, 0) - added)
    return (flux_e - turn(flux_e, 1)) + (flux_n - pltpu.roll(flux_n, 1, 0))


def gram_pairs():
    return [(i, j) for i in range(SOLVE_ITERS) for j in range(i, SOLVE_ITERS + 1)]


def surface_kernel(
    tall, strips, mean, recv_b, recv_a,
    basis_out, flow, partial, col_patch, row_patch,
    state, height, heights, transport, force, faces, slope, basis, weights, diagonal, sides,
):
    is_odd = odd("lon")
    rows = pl.ds(8, TALL)
    lanes = lane_ids(TALL)

    def received(start, count):
        here = pl.ds(start, count)
        got_a = recv_a[here, :]
        got_b = recv_b[here, :]
        return jnp.where(is_odd, got_b, got_a), jnp.where(is_odd, got_a, got_b)

    def ghost_strip(east, west, g):
        return jnp.where(lane_ids(STRIP) < 64, turn(east, 64 - 32 * g), turn(west, 54 - 32 * g))

    from_east, from_west = received(TALL, TALL)
    for f in range(3):
        state[f, 0, rows, :] = tall[pl.ds(f * TALL, TALL), :]
        here = (lanes >= f * WIDE) & (lanes < (f + 1) * WIDE)
        state[f, 1, rows, :] = turn(jnp.where(here, from_east, from_west), (LANES - f * WIDE) % LANES)
    last = lanes == LANES - 1
    first = lanes == 0

    def lane_sides(a, b):
        n = a.shape[0]
        ea, eb, wa, wb = turn(a, LANES - 1), turn(b, LANES - 1), turn(a, 1), turn(b, 1)
        return (
            (jnp.where(last[0:n], eb, ea), jnp.where(last[0:n], ea, eb)),
            (jnp.where(first[0:n], wb, wa), jnp.where(first[0:n], wa, wb)),
        )

    own = tall[pl.ds(3 * TALL, TALL), :]
    phase = lanes & 3
    from_east, from_west = received(0, TALL)
    to_east = column_strip(jnp.where(phase < 2, own, from_east))
    to_west = column_strip(jnp.where(phase < 2, from_west, own))
    changes = (jnp.where(phase < 2, to_east, to_west), jnp.where(phase < 2, to_west, to_east))
    deep = (own, jnp.where(phase < 2, from_west, from_east))
    col_patch[...] = changes[0][MARGIN : MARGIN + ROWS]
    to_lane = lax.broadcasted_iota(jnp.int32, (LANES, 2 * LANES), 1)
    from_lane = lax.broadcasted_iota(jnp.int32, (LANES, 2 * LANES), 0)
    column = to_lane & (LANES - 1)
    comp_of = jnp.where(from_lane < 4 * LEVELS, 0, 1)
    chosen = (
        ((column < 2) | (column >= LANES - 2))
        & ((from_lane & 3) == ((to_lane + 2) & 3))
        & (comp_of == (to_lane >> 7))
        & (from_lane < 4 * PLANES)
    )
    chooser = jnp.where(chosen, 1.0, 0.0)
    for half in range(2):
        total = lax.dot_general(
            changes[half], chooser, (((1,), (0,)), ((), ())),
            precision=lax.Precision.HIGHEST, preferred_element_type=F32,
        )
        share = 1.0 / jnp.maximum(pick(deep[half], ((lanes + 2) & 3) + 80), 1.0)
        for comp in range(2):
            change = total[:, comp * LANES : (comp + 1) * LANES] * share
            state[comp, half, rows, :] = state[comp, half, rows, :] - change
    number = lax.broadcasted_iota(jnp.int32, (STRIP, LANES), 0)
    level_of_row = jnp.where(number >= LEVELS, number - LEVELS, number).astype(F32)
    is_plane = number < PLANES
    not_last = lane_ids(STRIP) < LANES - 1
    for s in range(2):
        x, wet, v, deep = [], [], [], []
        for r in range(4):
            centre = strips[pl.ds((4 * s + r) * STRIP, STRIP), :]
            block, g = divmod(4 * s + r, 2)
            both = (centre, ghost_strip(*received(TALL + block * STRIP, STRIP), g))
            deep.append([b[20:21] for b in both])
            v.append([jnp.broadcast_to(b[21:22], (STRIP, LANES)) for b in both])
            wet.append([jnp.where(is_plane & (level_of_row < b[20:21]), 1.0, 0.0) for b in both])
            x.append([jnp.where(is_plane, b, 0.0) for b in both])
        half_range = range(2)
        lap = {}
        added = {}
        seam = [wet[1][h] * wet[2][h] * (x[2][h] - x[1][h]) for h in half_range]
        added[1] = seam
        added[2] = [-t for t in seam]
        along = {}
        for r in (1, 2):
            x_e = lane_sides(*x[r])[0]
            wet_e = lane_sides(*wet[r])[0]
            v_e = lane_sides(*v[r])[0]
            added_e = lane_sides(*added[r])[0]
            open_e = [wet[r][h] * wet_e[h] for h in half_range]
            edge = [open_e[h] * (x_e[h] - x[r][h]) for h in half_range]
            edge_w = lane_sides(*edge)[1]
            lap[r] = [
                edge[h]
                - edge_w[h]
                + wet[r][h] * (wet[r + 1][h] * (x[r + 1][h] - x[r][h]) + wet[r - 1][h] * (x[r - 1][h] - x[r][h]))
                for h in half_range
            ]
            edge = [
                jnp.where(not_last, 0.5 * (v[r][h] + v_e[h]) * open_e[h] * (added_e[h] - added[r][h]), 0.0)
                for h in half_range
            ]
            edge_w = lane_sides(*edge)[1]
            along[r] = [edge[h] - edge_w[h] for h in half_range]
        for h in half_range:
            face = [0.5 * (v[r][h] + v[r + 1][h]) * wet[r][h] * wet[r + 1][h] for r in range(3)]
            across = (face[0] * added[1][h], face[1] * (lap[2][h] - lap[1][h]), -face[2] * added[2][h])
            second = (
                across[0],
                across[1] - across[0] + along[1][h],
                across[2] - across[1] + along[2][h],
                -across[2],
            )
            for r in range(4):
                change = second[r]
                if h == 0 and r >= 2:
                    row_patch[pl.ds((2 * s + r - 2) * STRIP, STRIP), :] = change
                where = 8 + MARGIN + ((ROWS + 1 - r) if s == 0 else (r - 2))
                for comp in range(2):
                    mine = (number >= comp * LEVELS) & (number < (comp + 1) * LEVELS)
                    total = jnp.sum(jnp.where(mine, change, 0.0), axis=0, keepdims=True)
                    total = total / jnp.maximum(deep[r][h], 1.0)
                    state[comp, h, where : where + 1, :] = state[comp, h, where : where + 1, :] - total
    for comp in range(2):
        here = pl.ds(comp * ROWS, ROWS)
        started = state[comp, 0, pl.ds(8 + MARGIN, ROWS), :] - tall[pl.ds(comp * TALL + MARGIN, ROWS), :]
        flow[here, :] = -(started + mean[here, :])

    halves = range(2)
    ahead = lanes[0:8] >= LANES - 2
    behind = lanes[0:8] < 2

    def far_sides(a, b):
        ea, eb, wa, wb = turn(a, LANES - 2), turn(b, LANES - 2), turn(a, 2), turn(b, 2)
        return (
            (jnp.where(ahead, eb, ea), jnp.where(ahead, ea, eb)),
            (jnp.where(behind, wb, wa), jnp.where(behind, wa, wb)),
        )

    for half in halves:
        d = state[2, half, rows, :]
        slope[half, rows, :] = jnp.where(d > 0.0, SLOPE, 0.0)
        force[half, rows, :] = SLOPE * d
        transport[half, rows, :] = d * state[1, half, rows, :]
    tiles = range(8, 8 + TALL, 8)
    for tile in tiles:
        here, above, below = (pl.ds(tile + off, 8) for off in (0, 1, -1))
        east, west = lane_sides(force[0, here, :], force[1, here, :])
        for h in halves:
            faces[0, h, here, :] = east[h]
            faces[1, h, here, :] = west[h]
            faces[2, h, here, :] = force[h, above, :]
            faces[3, h, here, :] = force[h, below, :]
    for tile in tiles:
        here, above, below = (pl.ds(tile + off, 8) for off in (0, 1, -1))
        east, west = lane_sides(*(state[2, h, here, :] * state[0, h, here, :] for h in halves))
        for h in halves:
            divergence = (east[h] - west[h]) + (transport[h, above, :] - transport[h, below, :])
            force[h, here, :] = divergence
            new = -slope[h, here, :] * divergence
            heights[0, h, here, :] = new
            height[h, here, :] = new
    for step in range(1, SUBCYCLES):
        cut = min(8 * ((6 + 2 * step) // 8), 16)
        now, later = heights.at[(step - 1) % 2], heights.at[step % 2]
        for tile in range(8 + cut, 8 + TALL - cut, 8):
            here, above, below = (pl.ds(tile + off, 8) for off in (0, 2, -2))
            centres = [now[h, here, :] for h in halves]
            east, west = far_sides(*centres)
            for h, x in enumerate(centres):
                along = faces[0, h, here, :] * (east[h] - x) - faces[1, h, here, :] * (x - west[h])
                across = faces[2, h, here, :] * (now[h, above, :] - x) - faces[3, h, here, :] * (x - now[h, below, :])
                change = force[h, here, :] - (along + across)
                force[h, here, :] = change
                new = x - slope[h, here, :] * change
                later[h, here, :] = new
                height[h, here, :] = height[h, here, :] + new
    mine = pl.ds(8 + MARGIN, ROWS)
    east, west = lane_sides(height[0, mine, :], height[1, mine, :])
    inner = slope[0, mine, :]
    north, south = (height[0, pl.ds(8 + MARGIN + off, ROWS), :] for off in (1, -1))
    for comp, gradient in enumerate((east[0] - west[0], north - south)):
        here = pl.ds(comp * ROWS, ROWS)
        flow[here, :] = flow[here, :] + (state[comp, 0, mine, :] - inner * gradient)
    final = heights.at[(SUBCYCLES - 1) % 2]
    scale = 2.0 / RADIUS
    short = ROWS + 16
    base = MARGIN

    tiles = range(0, short, 8)

    def spin(tile, a, b):
        here = pl.ds(base + tile, 8)
        for n, pair in enumerate(lane_sides(a, b)):
            for h in halves:
                sides[n, h, here, :] = pair[h]

    def nine(read, tile, h):
        out = []
        for off in (0, 1, -1):
            where = pl.ds(base + tile + off, 8)
            out += [read(h, where), sides[0, h, where, :], sides[1, h, where, :]]
        return out

    for tile in tiles:
        here = pl.ds(base + tile, 8)
        spin(tile, state[2, 0, here, :], state[2, 1, here, :])
    for tile in tiles:
        here = pl.ds(tile, 8)
        for h in halves:
            around = nine(lambda h, where: state[2, h, where, :], tile, h)
            d = around[0]
            wet = d > 0.0
            total = jnp.where(wet, 0.05, 1.0)
            for n in range(1, 9):
                factor = 0.5 if n in (1, 2, 3, 6) else 0.25
                w = jnp.where(wet & (around[n] > 0.0), factor * (d + around[n]), 0.0)
                weights[n - 1, h, here, :] = scale * w
                total += w
            diagonal[h, here, :] = scale * (total - CENTRE)

    def applied(source, tile, h):
        around = nine(lambda h, where: basis[source, h, where, :], tile, h)
        here = pl.ds(tile, 8)
        terms = [weights[n - 1, h, here, :] * around[n] for n in range(1, 9)]
        while len(terms) > 1:
            terms = [a + b for a, b in zip(terms[::2], terms[1::2])]
        return diagonal[h, here, :] * around[0] - terms[0]

    for tile in tiles:
        here = pl.ds(base + tile, 8)
        pair = [final[h, here, :] for h in halves]
        for h in halves:
            basis[0, h, here, :] = pair[h]
        spin(tile, *pair)
    for k in range(1, SOLVE_ITERS):
        for tile in tiles:
            here = pl.ds(base + tile, 8)
            for h in halves:
                x = applied(k - 1, tile, h)
                basis[k, h, here, :] = 0.5 * x if k == 1 else x - basis[k - 2, h, here, :]
        for tile in tiles:
            here = pl.ds(base + tile, 8)
            spin(tile, basis[k, 0, here, :], basis[k, 1, here, :])
    for tile in tiles[1:-1]:
        here = pl.ds(base + tile, 8)
        basis[SOLVE_ITERS, 0, here, :] = applied(SOLVE_ITERS - 1, tile, 0) - basis[SOLVE_ITERS - 2, 0, here, :]
    lane = lane_ids(1)
    row = jnp.zeros((1, LANES), F32)
    mine = pl.ds(8 + MARGIN, ROWS)
    for n, (i, j) in enumerate(gram_pairs()):
        product = basis[i, 0, mine, :] * basis[j, 0, mine, :]
        row = jnp.where(lane == n, jnp.sum(jnp.sum(product, axis=0, keepdims=True), axis=1, keepdims=True), row)
    partial[...] = jnp.broadcast_to(row, partial.shape)
    for i in range(SOLVE_ITERS):
        for half in range(2):
            basis_out[i, half] = basis[i, half, pl.ds(base, short), :]


def solve_coefficients(gram):
    half = 0.5 * RADIUS

    def image_of(d):
        out = [None] * (len(d) + 1)

        def add(n, term):
            out[n] = term if out[n] is None else out[n] + term

        for j, value in enumerate(d):
            add(j, CENTRE * value)
            if j == 0:
                add(1, RADIUS * value)
            else:
                add(j + 1, half * value)
                add(j - 1, half * value)
        return out

    def inner(a, b):
        total = None
        for i, x in enumerate(a):
            for j, y in enumerate(b):
                term = x * y * gram[(min(i, j), max(i, j))]
                total = term if total is None else total + term
        return total

    one = jnp.ones((8, LANES), F32)
    residual, direction, surface = [one], [one], [0.0 * one]
    norm = gram[(0, 0)]
    for iteration in range(SOLVE_ITERS):
        image = image_of(direction)
        step = norm / inner(direction, image)
        surface = [a + step * b for a, b in zip(surface, direction)] + [0.0 * one]
        if iteration == SOLVE_ITERS - 1:
            break
        residual = [(residual[n] if n < len(residual) else 0.0) - step * x for n, x in enumerate(image)]
        fresh = inner(residual, residual)
        ratio = fresh / norm
        direction = [x + (ratio * direction[n] if n < len(direction) else 0.0) for n, x in enumerate(residual)]
        norm = fresh
    return surface[:SOLVE_ITERS]


def final_kernel(gathered, basis, flow, star, lev, velocity_out, surface_out, pad, change):
    sums = jnp.sum(gathered[...], axis=0, keepdims=True)
    lane = lane_ids(1)
    gram = {}
    for n, pair in enumerate(gram_pairs()):
        value = jnp.sum(jnp.where(lane == n, sums, 0.0), axis=1, keepdims=True)
        gram[pair] = jnp.broadcast_to(value, (8, LANES))
    coefficients = [c[0:1] for c in solve_coefficients(gram)]
    for half in range(2):
        total = coefficients[0] * basis[0, half]
        for i in range(1, SOLVE_ITERS):
            total += coefficients[i] * basis[i, half]
        pad[half] = total
    mine = pl.ds(8, ROWS)
    centre = pad[0, mine, :]
    ghost = pad[1, mine, :]
    surface_out[...] = centre
    lanes = lane_ids(ROWS)
    east = jnp.where(lanes == LANES - 1, turn(ghost, LANES - 1), turn(centre, LANES - 1))
    west = jnp.where(lanes == 0, turn(ghost, 1), turn(centre, 1))
    levels = lev[...]
    slope = jnp.where(levels > 0, SLOPE, 0.0)
    slopes = (east - west, pad[0, pl.ds(9, ROWS), :] - pad[0, pl.ds(7, ROWS), :])
    for comp in range(2):
        here = pl.ds(comp * ROWS, ROWS)
        change[comp] = flow[here, :] - slope * slopes[comp]


    def level_step(k, carry):
        wet = k < levels
        for comp in range(2):
            here = pl.ds(pl.multiple_of((comp * LEVELS + k) * ROWS, ROWS), ROWS)
            velocity_out[here, :] = star[here, :] + jnp.where(wet, change[comp], 0.0)
        return carry

    lax.fori_loop(0, LEVELS, level_step, 0, unroll=True)


def patch_kernel(star, col_patch, row_patch, out):
    lanes = lane_ids(ROWS)
    rims = (lanes < 2) | (lanes >= LANES - 2)
    ids = row_ids(8)

    def plane(p, carry):
        here = pl.ds(pl.multiple_of(p * ROWS, ROWS), ROWS)
        out[here, :] = star[here, :] - jnp.where(rims, turn(col_patch[...], 126 - 4 * p), 0.0)
        for first, pieces in ((ROWS - 8, ((7, 0), (6, 1))), (0, ((0, 2), (1, 3)))):
            here = pl.ds(pl.multiple_of(p * ROWS + first, 8), 8)
            x = out[here, :]
            for row, n in pieces:
                x = x - jnp.where(ids == row, row_patch[pl.ds(n * STRIP + p, 1), :], 0.0)
            out[here, :] = x
        return carry

    lax.fori_loop(0, PLANES, plane, 0, unroll=10)


def call(kernel, shapes, scratch, flops, *args, far=False):
    out = tuple(jax.ShapeDtypeStruct(s, F32) for s in shapes)
    moved = sum(4 * math.prod(a.shape) for a in args) + sum(4 * math.prod(s) for s in shapes)
    if far:
        args = [pltpu.with_memory_space_constraint(a, pltpu.HBM) for a in args]
    return pl.pallas_call(
        kernel,
        out_shape=out,
        in_specs=[pl.BlockSpec(memory_space=pltpu.HBM if far else pltpu.VMEM)] * len(args),
        scratch_shapes=[pltpu.VMEM(s, F32) if isinstance(s, tuple) else s for s in scratch],
        compiler_params=pltpu.CompilerParams(vmem_limit_bytes=32 * 1024 * 1024),
        cost_estimate=pl.CostEstimate(flops=flops, bytes_accessed=moved, transcendentals=0),
    )(*args)


def pair_tables(lon, lat):
    def index(i, j):
        return j * lat + i

    lat_a, lat_b, lon_a, lon_b = [], [], [], []
    for j in range(lon):
        for i in range(lat):
            lat_a.append((index(i, j), index(i ^ 1, j)))
            if i == lat - 1:
                lat_b.append((index(i, j), index(i, lon - 1 - j)))
            elif i > 0:
                lat_b.append((index(i, j), index(i + 1 if i % 2 else i - 1, j)))
            else:
                lat_b.append((index(i, j), index(i, j ^ 1)))
            lon_a.append((index(i, j), index(i, j ^ 1)))
            lon_b.append((index(i, j), index(i, (j + 1 if j % 2 else j - 1) % lon)))
    return lat_a, lat_b, lon_a, lon_b


def per_device(lon, lat, tracers, velocity, active_levels, diffusivity, viscosity, ocean_depth, wind_forcing):
    lat_a, lat_b, lon_a, lon_b = pair_tables(lon, lat)

    def swap(x, pairs):
        return lax.ppermute(x, BOTH, pairs)

    block = (ROWS, LANES)
    tra = tracers.reshape(PLANES * ROWS, LANES)
    vel = velocity.reshape(PLANES * ROWS, LANES)
    wind = wind_forcing.reshape(2 * ROWS, LANES)
    rim = (RIMS, LANES)
    star, mean, fields, cols, north, south, send_a, send_b, edge_a, edge_b = call(
        block_kernel,
        [(PLANES * ROWS, LANES), (2 * ROWS, LANES), (3 * ROWS, LANES), block, rim, rim, (LAT_SEND, LANES), (LAT_SEND, LANES),
         (STRIP, LANES), (STRIP, LANES)],
        [(4,) + block, (4,) + block, (2,) + block, block, (PLANES * ROWS + 16, LANES), (PLANES, 8, LANES), (PLANES, 8, LANES), block, block, block, wind.shape,
         block, (PLANES * ROWS + 16, LANES),
         pltpu.VMEM(block, jnp.int32), pltpu.SemaphoreType.DMA((8,))],
        10**7,
        vel, tra.reshape(PLANES, ROWS, LANES), active_levels, viscosity, diffusivity, ocean_depth, wind,
        far=True,
    )
    got_a = swap(send_a, lat_a)
    got_b = swap(send_b, lat_b)
    edge_a = swap(edge_a, lat_a)
    edge_b = swap(edge_b, lat_b)
    (tracer_cols,) = call(tracer_rim_kernel, [block], [], 10**5, tra)
    tall, strips, level_rows, send_a, send_b = call(
        widen_kernel,
        [(4 * TALL, LANES), (8 * STRIP, LANES), (16, LANES), (LON_SEND, LANES), (LON_SEND, LANES)],
        [(TALL, LANES)] * 2,
        10**6,
        fields, cols, tracer_cols, diffusivity, north, south, got_b, got_a,
    )
    got_a = swap(send_a, lon_a)
    got_b = swap(send_b, lon_b)
    (tracers_out,) = call(
        tracer_kernel, [(PLANES * ROWS, LANES)], [block, (4,) + block, (4,) + block, (2 * STRIP, LANES)], 10**6,
        tra, active_levels, diffusivity, level_rows, edge_b, edge_a, got_b, got_a,
    )
    padded = (2, TALL + 16, LANES)
    short = (2, ROWS + 16, LANES)
    basis, flow, partial, col_patch, row_patch = call(
        surface_kernel,
        [(SOLVE_ITERS,) + short, (2 * ROWS, LANES), (lon * lat, LANES), block, (4 * STRIP, LANES)],
        [(3,) + padded, padded, (2,) + padded, padded, padded, (4,) + padded, padded, (SOLVE_ITERS + 1,) + padded, (8,) + short, short, (2,) + padded],
        10**7,
        tall, strips, mean, got_b, got_a,
    )
    gathered = lax.all_to_all(partial, BOTH, 0, 0, tiled=True)
    (star,) = call(patch_kernel, [(PLANES * ROWS, LANES)], [], 10**6, star, col_patch, row_patch)
    velocity_out, surface = call(
        final_kernel, [(PLANES * ROWS, LANES), block],
        [short, (2,) + block], 10**6,
        gathered, basis, flow, star, active_levels,
    )
    return tracers_out.reshape(tracers.shape), velocity_out.reshape(velocity.shape), surface


def solution(mesh):
    placed = (
        P(None, None, "lat", "lon"),
        P(None, None, "lat", "lon"),
        P("lat", "lon"),
        P("lat", "lon"),
        P("lat", "lon"),
        P("lat", "lon"),
        P(None, "lat", "lon"),
    )
    return jax.shard_map(
        functools.partial(per_device, mesh.shape["lon"], mesh.shape["lat"]),
        mesh=mesh,
        in_specs=placed,
        out_specs=(P(None, None, "lat", "lon"), P(None, None, "lat", "lon"), P("lat", "lon")),
        check_vma=False,
    )
```
